32 devices in a mesh: wide: 8 (over y, x, core), narrow: 4 (over z).
Axes of the slice: x: 2, y: 2, z: 4, core: 2. Of those that a mesh axis runs over, the one named last changes fastest.
Arguments:
- coarse_basis: bfloat16 [16, 96, 3, 16, 8, 128], P('wide', None, None, 'narrow')
- material_ids: int32 [16, 16, 8, 128], P('wide', 'narrow'), may hold values from 0 to 15
- lame_table: bfloat16 [2, 16], replicated, may hold values from 0.5 to 4
- coarse_ids: int32 [16, 96], P('wide'), may hold values from 0 to 127, as said below
- coarse_slab: bfloat16 [98304, 512], P('wide', 'narrow'), may hold values from -0.5 to 2.5, as said below
- panel_owner: int32 [1], replicated, may hold values from 0 to 2
Outputs:
- factored: bfloat16 [98304, 512], P('wide', 'narrow')
- galerkin: float32 [16, 96, 96], P('wide')
The draws below stay inside these ranges and needn't reach their ends.
Inputs may be any that keep to these rules, and one draw needn't show every extreme that they name: `coarse_ids`: the 96 numbers of a row are distinct. `coarse_slab`: for every column block t, the 128 x 128 block whose rows begin at t * 2 * 12288 is symmetric positive definite.
All inputs are finite; a program needn't handle non-finite values.
Results may differ from the reference program's by a relative error of at most 0.001.
The reference program's roundings to bfloat16 on the way (of `factor`) count: a program that leaves them out, or rounds other values in their place, can miss the bound.
Values may be sent and summed in bfloat16 or wider, within the bound.
No kernel may reach another device: no remote copies, remote signals or barrier semaphores. Data moves between devices by JAX's collectives and lax.ppermute only.
A program may use at most 192 MiB of HBM per device.

```python
import math
import jax
import jax.numpy as jnp
from jax import lax

NG = 98304
NFN = 96
CB = 128
CZ = 128
NMAT = 16
SUB_W = 2
CY = 8
NXS = 16
SUBS = 16
ROWS_W = 12288
STRIDE = 2
NW = 512
OWNER_SPAN = 3


def draw_coarse_basis(key, part):
    base_key = jax.random.fold_in(jax.random.fold_in(key, 11), 0)
    field_key = jax.random.fold_in(jax.random.fold_in(key, 11), 2)
    mix_key = jax.random.fold_in(jax.random.fold_in(key, 11), 3)
    shape = (SUBS, NFN, 3, NXS, CY, CZ)
    field_shape = (6, SUBS, 3, NXS, CY, CZ)
    raw = jax.random.truncated_normal(base_key, -4.0, 4.0, shape, jnp.float32)
    shared = jax.random.truncated_normal(field_key, -4.0, 4.0, field_shape, jnp.float32)
    mixing = 0.6 * jax.random.truncated_normal(mix_key, -3.0, 3.0, (SUBS, NFN, 6), jnp.float32)
    mixed = raw
    for common in range(6):
        weight_now = mixing[:, :, common].reshape(SUBS, NFN, 1, 1, 1, 1)
        mixed = mixed + weight_now * shared[common][:, None]
    factor = (0.1 / (3.0 * NXS * CY * CZ)) ** 0.5
    return (mixed * factor).astype(jnp.bfloat16)


def one_order(order_key):
    return jax.random.permutation(order_key, CB)


def draw_coarse_ids(key, part):
    keys = jax.random.split(jax.random.fold_in(key, 23), SUBS)
    orders = jax.vmap(one_order)(keys)
    return orders[:, :NFN].astype(jnp.int32)


def draw_coarse_slab(key, part):
    entry_key, spread_key = jax.random.split(jax.random.fold_in(key, 37))
    loose = jax.random.uniform(entry_key, (NG, NW), jnp.float32, -0.5, 0.5)
    spread = jnp.exp(jax.random.uniform(spread_key, (NW // CB, CB), jnp.float32, -0.6931, 0.6931))
    distance = jnp.abs(jnp.arange(CB)[:, None] - jnp.arange(CB)[None, :]).astype(jnp.float32)
    kernel = jnp.power(0.88, distance)
    result = loose
    for column_block in range(NW // CB):
        first_row = column_block * STRIDE * ROWS_W
        scales = spread[column_block]
        tile = jnp.sqrt(scales[:, None] * scales[None, :]) * kernel + 0.5 * jnp.eye(CB, dtype=jnp.float32)
        result = result.at[first_row:first_row + CB, column_block * CB:(column_block + 1) * CB].set(tile)
    return result.astype(jnp.bfloat16)


def touch_ends(values, own_key, smallest, top_value):
    place = [jax.random.randint(jax.random.fold_in(own_key, axis), (), 0, length) for axis, length in enumerate(values.shape)]
    main_axis = values.shape.index(max(values.shape))
    neighbour = place[:main_axis] + [(place[main_axis] + 1) % values.shape[main_axis]] + place[main_axis + 1:]
    return values.at[tuple(place)].set(smallest).at[tuple(neighbour)].set(top_value)


def setup_inputs(seed: int = 0) -> dict:
    arg_keys = jax.random.split(jax.random.key(seed), 7)
    coarse_basis = draw_coarse_basis(jax.random.fold_in(arg_keys[6], 71), 0)
    material_ids = touch_ends(jax.random.randint(arg_keys[1], (SUBS, NXS, CY, CZ), 0, NMAT), jax.random.fold_in(arg_keys[1], 1), 0, NMAT - 1).astype(jnp.int32)
    lame_table = jnp.clip(jnp.exp(jax.random.uniform(arg_keys[2], (2, NMAT), jnp.float32, math.log(0.5), math.log(4.0))), 0.5, 4.0).astype(jnp.bfloat16)
    coarse_ids = draw_coarse_ids(jax.random.fold_in(arg_keys[6], 71), 0)
    coarse_slab = draw_coarse_slab(jax.random.fold_in(arg_keys[6], 71), 0)
    panel_owner = jax.random.randint(arg_keys[5], (1,), 0, OWNER_SPAN).astype(jnp.int32)
    return {"coarse_basis": coarse_basis, "material_ids": material_ids, "lame_table": lame_table, "coarse_ids": coarse_ids, "coarse_slab": coarse_slab, "panel_owner": panel_owner}


def lower_inverse(lower):
    identity = jnp.eye(lower.shape[0], dtype=lower.dtype)
    return lax.linalg.triangular_solve(lower, identity, left_side=True, lower=True)

def lame_fields(material_ids, lame_table):
    values = lame_table.astype(jnp.float32)
    shear = jnp.zeros(material_ids.shape, jnp.float32)
    dilatation = jnp.zeros(material_ids.shape, jnp.float32)
    for material in range(values.shape[1]):
        chosen = material_ids == material
        shear = jnp.where(chosen, values[0, material], shear)
        dilatation = jnp.where(chosen, values[1, material], dilatation)
    return (shear, dilatation)

def shifted(field, axis, step):
    length = field.shape[axis]
    border = jnp.zeros_like(lax.slice_in_dim(field, 0, 1, axis=axis))
    if step > 0:
        return jnp.concatenate([lax.slice_in_dim(field, 1, length, axis=axis), border], axis=axis)
    return jnp.concatenate([border, lax.slice_in_dim(field, 0, length - 1, axis=axis)], axis=axis)

def face_weight(coeff_one, coeff_two, direction):
    shear = 0.5 * (coeff_one[:, 0:1] + coeff_two[:, 0:1])
    dilate = 0.5 * (coeff_one[:, 1:2] + coeff_two[:, 1:2])
    unit = (jnp.arange(3) == direction).astype(shear.dtype).reshape(1, 1, 3, 1, 1, 1)
    return shear + unit * (dilate + shear)

def operator_image(padded, coeff):
    centre = padded[:, :, :, 1:-1]
    coeff_centre = coeff[:, :, :, 1:-1]
    pairs = [(padded[:, :, :, 2:], coeff[:, :, :, 2:], 0), (padded[:, :, :, :-2], coeff[:, :, :, :-2], 0)]
    for axis, direction in ((4, 1), (5, 2)):
        for step in (1, -1):
            pairs.append((shifted(centre, axis, step), shifted(coeff_centre, axis, step), direction))
    image = jnp.zeros(centre.shape, centre.dtype)
    for other, other_coeff, direction in pairs:
        image = image + face_weight(coeff_centre, other_coeff, direction) * (centre - other)
    return image

def galerkin_of(left_field, right_field):
    subs, funcs = (left_field.shape[0], left_field.shape[1])
    return jnp.einsum('sak,sbk->sab', left_field.reshape(subs, funcs, -1), right_field.reshape(subs, funcs, -1), precision=lax.Precision.HIGHEST)

def one_subdomain(items):
    field, coeff = items
    widths = ((0, 0), (0, 0), (0, 0), (1, 1), (0, 0), (0, 0))
    padded = jnp.pad(field.astype(jnp.float32)[None], widths)
    coeff_padded = jnp.pad(coeff[None], widths)
    image = operator_image(padded, coeff_padded)
    return galerkin_of(padded[:, :, :, 1:-1], image)[0]

def reference(coarse_basis, material_ids, lame_table, coarse_ids, coarse_slab, panel_owner):
    shear, dilatation = lame_fields(material_ids, lame_table)
    coeff = jnp.stack([shear, dilatation], 1)[:, :, None]
    galerkin = lax.map(one_subdomain, (coarse_basis, coeff))
    owner = panel_owner[0].astype(jnp.int32)
    added_blocks = []
    for column_block in range(NW // CB):
        first_sub = column_block * STRIDE * SUB_W
        members = galerkin[first_sub:first_sub + SUB_W]
        slots = (coarse_ids[first_sub:first_sub + SUB_W][:, :, None] == jnp.arange(CB)[None, None, :]).astype(jnp.float32)
        spread = jnp.einsum('sab,sbc->sac', members, slots, precision=lax.Precision.HIGHEST)
        added_blocks.append(jnp.einsum('sar,sac->rc', slots, spread, precision=lax.Precision.HIGHEST))
    stacked = jnp.stack(added_blocks, 0)
    added_owner = lax.dynamic_index_in_dim(stacked, owner, 0, keepdims=False)
    start_row = (owner * STRIDE * ROWS_W).astype(jnp.int32)
    diagonal = lax.dynamic_slice(coarse_slab, (start_row, (owner * CB).astype(jnp.int32)), (CB, CB)).astype(jnp.float32)
    diagonal = diagonal + added_owner
    diagonal = 0.5 * (diagonal + diagonal.T)
    lower = jnp.linalg.cholesky(diagonal)
    inverse = lower_inverse(lower)
    column = lax.dynamic_slice_in_dim(coarse_slab, (owner * CB).astype(jnp.int32), CB, axis=1)
    solved = jnp.dot(column.astype(jnp.float32), inverse.T, precision=lax.Precision.HIGHEST)
    rows = lax.broadcasted_iota(jnp.int32, (NG, CB), 0)
    wide_of = rows // ROWS_W
    head = rows % ROWS_W < CB
    diagonal_rows = head & (wide_of == owner * STRIDE)
    earlier = head & (wide_of % STRIDE == 0) & (wide_of // STRIDE < owner)
    own_block = lax.dynamic_update_slice(jnp.zeros((NG, CB), jnp.float32), lower, (start_row, jnp.int32(0)))
    solved = jnp.where(diagonal_rows, own_block, solved)
    solved = jnp.where(earlier, 0.0, solved)
    factor = solved.astype(jnp.bfloat16)
    blocks = []
    for column_block in range(NW // CB):
        first_row = column_block * STRIDE * ROWS_W
        added = added_blocks[column_block]
        base = coarse_slab[:, column_block * CB:(column_block + 1) * CB].astype(jnp.float32)
        base = base.at[first_row:first_row + CB].add(jnp.where(column_block >= owner, added, 0.0))
        rows_needed = factor[first_row:first_row + CB]
        update = jnp.dot(factor.astype(jnp.float32), rows_needed.T.astype(jnp.float32), preferred_element_type=jnp.float32)
        result = jnp.where(column_block > owner, base - update, base)
        result = jnp.where(column_block == owner, factor.astype(jnp.float32), result)
        blocks.append(result.astype(jnp.bfloat16))
    return (jnp.concatenate(blocks, axis=1), galerkin)
```

```python
import functools

import jax
import jax.numpy as jnp
from jax import lax
from jax.experimental import pallas as pl
from jax.experimental.pallas import tpu as pltpu
from jax.sharding import PartitionSpec as P

F32, BF16 = jnp.float32, jnp.bfloat16
NT = (((1,), (1,)), ((), ()))
TN = (((0,), (0,)), ((), ()))
CHUNKS = 8
BLOCK = 16


def exact_dot(left, right, dims=(((1,), (0,)), ((), ()))):
    return lax.dot_general(
        left, right, dims, precision=lax.Precision.HIGHEST, preferred_element_type=F32
    )


def dot(left, right, dims=(((1,), (0,)), ((), ()))):
    return lax.dot_general(left, right, dims, preferred_element_type=F32)


def split_two(value):
    high = value.astype(BF16)
    return high, (value - high.astype(F32)).astype(BF16)


def lame_of(ids, table_ref):
    shear = jnp.zeros(ids.shape, F32)
    dilate = jnp.zeros(ids.shape, F32)
    for material in range(table_ref.shape[1]):
        chosen = ids == material
        shear = jnp.where(chosen, table_ref[0, material], shear)
        dilate = jnp.where(chosen, table_ref[1, material], dilate)
    return shear, dilate


def interior_kernel(edge_ref, table_ref, ids_ref, basis_ref, out_ref, fields, coef, left, right, acc):
    comp = pl.program_id(1)
    layers, ny, nz = basis_ref.shape[3:]
    funcs = basis_ref.shape[1]
    row = lax.broadcasted_iota(jnp.int32, (ny, nz), 0)
    lane = lax.broadcasted_iota(jnp.int32, (ny, nz), 1)
    table = [lame_of(ids_ref[0, x], table_ref) for x in range(layers)]

    def weight(one, two, direction):
        shear = 0.5 * (one[0] + two[0])
        dilate = 0.5 * (one[1] + two[1])
        return shear + jnp.where(comp == direction, shear + dilate, 0.0)

    def ahead(field, axis):
        size = field.shape[axis]
        index = row if axis == 0 else lane
        return jnp.where(index == size - 1, 0.0, pltpu.roll(field, size - 1, axis=axis))

    def behind(field, axis):
        index = row if axis == 0 else lane
        return jnp.where(index == 0, 0.0, pltpu.roll(field, 1, axis=axis))

    nothing = (jnp.zeros((ny, nz), F32),) * 2
    previous = weight(table[0], nothing, 0) * edge_ref[0].astype(F32)
    for x in range(layers):
        diagonal = previous
        forward = []
        if x + 1 < layers:
            face = weight(table[x], table[x + 1], 0)
            diagonal = diagonal + face
            previous = face
            forward.append(face)
        else:
            forward.append(jnp.zeros((ny, nz), F32))
        for axis in (0, 1):
            index, size = (row, ny) if axis == 0 else (lane, nz)
            other = tuple(ahead(value, axis) for value in table[x])
            face = weight(table[x], other, axis + 1)
            before = tuple(behind(value, axis) for value in table[x])
            diagonal = diagonal + face + weight(table[x], before, axis + 1)
            forward.append(jnp.where(index == size - 1, 0.0, face))
        coef[x, 0] = 0.5 * diagonal
        for kind in range(3):
            coef[x, kind + 1] = forward[kind]
        fields[x] = basis_ref[0, :, 0, x].astype(F32).reshape(funcs * ny, nz)

    total = None
    for x in range(layers):
        values = [fields[x, pl.ds(y, funcs, stride=ny), :] for y in range(ny)]
        for y in range(ny):
            value = values[y]
            image = coef[x, 0, y : y + 1, :] * value
            image = image - coef[x, 3, y : y + 1, :] * pltpu.roll(value, nz - 1, axis=1)
            if y + 1 < ny:
                image = image - coef[x, 2, y : y + 1, :] * values[y + 1]
            if x + 1 < layers:
                image = image - coef[x, 1, y : y + 1, :] * fields[x + 1, pl.ds(y, funcs, stride=ny), :]
            high, low = split_two(image)
            left[:, y * nz : (y + 1) * nz] = value.astype(BF16)
            right[0:funcs, y * nz : (y + 1) * nz] = high
            right[funcs : 2 * funcs, y * nz : (y + 1) * nz] = low
        product = dot(left[...], right[...], NT)
        total = product if total is None else total + product

    @pl.when(comp == 0)
    def _():
        acc[...] = total

    @pl.when(comp > 0)
    def _():
        acc[...] += total

    @pl.when(comp == pl.num_programs(1) - 1)
    def _():
        out_ref[0] = acc[:, 0:funcs] + acc[:, funcs : 2 * funcs]


def interior(edge, table, ids, basis):
    subs, funcs, comps, layers, ny, nz = basis.shape
    return pl.pallas_call(
        interior_kernel,
        grid=(subs, comps),
        in_specs=[
            pl.BlockSpec(memory_space=pltpu.SMEM),
            pl.BlockSpec(memory_space=pltpu.SMEM),
            pl.BlockSpec((1, layers, ny, nz), lambda s, c: (s, 0, 0, 0)),
            pl.BlockSpec((1, funcs, 1, layers, ny, nz), lambda s, c: (s, 0, c, 0, 0, 0)),
        ],
        out_specs=pl.BlockSpec((1, funcs, funcs), lambda s, c: (s, 0, 0)),
        out_shape=jax.ShapeDtypeStruct((subs, funcs, funcs), F32),
        scratch_shapes=[
            pltpu.VMEM((layers, funcs * ny, nz), F32),
            pltpu.VMEM((layers, 4, ny, nz), F32),
            pltpu.VMEM((funcs, ny * nz), BF16),
            pltpu.VMEM((2 * funcs, ny * nz), BF16),
            pltpu.VMEM((funcs, 2 * funcs), F32),
        ],
        compiler_params=pltpu.CompilerParams(vmem_limit_bytes=32 * 2**20),
        cost_estimate=pl.CostEstimate(flops=4 * basis.size * funcs, bytes_accessed=2 * basis.size, transcendentals=0),
        name="interior",
    )(edge, table, ids, basis)


def face_kernel(table_ref, ids_ref, basis_ref, halo_ref, coef_ref, inner_ref, out_ref, mine, theirs, left, right, acc):
    comp = pl.program_id(1)
    funcs = basis_ref.shape[1]
    ny, nz = basis_ref.shape[4:]
    shear, dilate = lame_of(ids_ref[0, 0], table_ref)
    shear = 0.5 * (shear + coef_ref[0, 0].astype(F32))
    dilate = 0.5 * (dilate + coef_ref[0, 1].astype(F32))
    weight = shear + jnp.where(comp == 0, shear + dilate, 0.0)
    mine[...] = basis_ref[0, :, 0, 0].astype(F32).reshape(funcs * ny, nz)
    theirs[...] = halo_ref[0].astype(F32).reshape(funcs * ny, nz)
    for y in range(ny):
        here = mine[pl.ds(y, funcs, stride=ny), :]
        there = theirs[pl.ds(y, funcs, stride=ny), :]
        high, low = split_two(weight[y : y + 1, :] * (here - there))
        left[0:funcs, y * nz : (y + 1) * nz] = here.astype(BF16)
        left[funcs : 2 * funcs, y * nz : (y + 1) * nz] = there.astype(BF16)
        right[0:funcs, y * nz : (y + 1) * nz] = high
        right[funcs : 2 * funcs, y * nz : (y + 1) * nz] = low
    product = dot(left[...], right[...], NT)
    product = product[0:funcs] - product[funcs : 2 * funcs]
    total = product[:, 0:funcs] + product[:, funcs : 2 * funcs]

    @pl.when(comp == 0)
    def _():
        acc[...] = total

    @pl.when(comp > 0)
    def _():
        acc[...] += total

    @pl.when(comp == pl.num_programs(1) - 1)
    def _():
        half = inner_ref[0] + 0.5 * acc[...]
        out_ref[0] = half + half.T


def face(table, ids, basis, halo, inner):
    subs, funcs, comps, layers, ny, nz = basis.shape
    return pl.pallas_call(
        face_kernel,
        grid=(subs, comps),
        in_specs=[
            pl.BlockSpec(memory_space=pltpu.SMEM),
            pl.BlockSpec((1, 1, ny, nz), lambda s, c: (s, layers - 1, 0, 0)),
            pl.BlockSpec((1, funcs, 1, 1, ny, nz), lambda s, c: (s, 0, c, layers - 1, 0, 0)),
            pl.BlockSpec((1, funcs, ny, nz), lambda s, c: (s, c, 0, 0)),
            pl.BlockSpec((1, 2, ny, nz), lambda s, c: (s, comps * funcs // 2, 0, 0)),
            pl.BlockSpec((1, funcs, funcs), lambda s, c: (s, 0, 0)),
        ],
        out_specs=pl.BlockSpec((1, funcs, funcs), lambda s, c: (s, 0, 0)),
        out_shape=jax.ShapeDtypeStruct((subs, funcs, funcs), F32),
        scratch_shapes=[
            pltpu.VMEM((funcs * ny, nz), F32),
            pltpu.VMEM((funcs * ny, nz), F32),
            pltpu.VMEM((2 * funcs, ny * nz), BF16),
            pltpu.VMEM((2 * funcs, ny * nz), BF16),
            pltpu.VMEM((funcs, funcs), F32),
        ],
        compiler_params=pltpu.CompilerParams(vmem_limit_bytes=32 * 2**20),
        cost_estimate=pl.CostEstimate(flops=basis.size * funcs * 2, bytes_accessed=basis.size, transcendentals=0),
        name="face",
    )(table, ids, basis, halo, halo, inner)


def assemble_kernel(flags_ref, gal_ref, column_ids_ref, row_ids_ref, head_ref, added_ref, message_ref):
    subs, funcs = gal_ref.shape[0:2]
    size = added_ref.shape[0]
    added = jnp.zeros((size, size), F32)
    for sub in range(subs):
        lane = lax.broadcasted_iota(jnp.int32, (funcs, size), 1)
        slots = (column_ids_ref[sub] == lane).astype(F32)
        row = lax.broadcasted_iota(jnp.int32, (size, funcs), 0)
        slots_t = (row_ids_ref[sub] == row).astype(F32)
        added = added + exact_dot(slots_t, exact_dot(gal_ref[sub], slots))
    head = head_ref[...].astype(F32)
    added_ref[...] = added
    message_ref[0:size] = jnp.where(flags_ref[0] == 1, added + head, 0.0)
    message_ref[size : 2 * size] = jnp.where(flags_ref[1] == 1, head, 0.0)


def assemble(flags, galerkin, ids, head):
    size = head.shape[0]
    whole = pl.BlockSpec(memory_space=pltpu.VMEM)
    return pl.pallas_call(
        assemble_kernel,
        in_specs=[pl.BlockSpec(memory_space=pltpu.SMEM)] + [whole] * 4,
        out_specs=[whole, whole],
        out_shape=[
            jax.ShapeDtypeStruct((size, size), F32),
            jax.ShapeDtypeStruct((2 * size, size), F32),
        ],
        cost_estimate=pl.CostEstimate(flops=10**8, bytes_accessed=4 * 10**5, transcendentals=0),
        name="assemble",
    )(flags, galerkin, ids[:, :, None], ids[:, None, :], head)


def factor_kernel(message_ref, lower_ref, pieces_ref, rows_ref, work):
    size = lower_ref.shape[0]
    diagonal = message_ref[0:size]
    row = lax.broadcasted_iota(jnp.int32, (size, size), 0)
    lane = lax.broadcasted_iota(jnp.int32, (size, size), 1)
    work[:, 0:size] = 0.5 * (diagonal + diagonal.T)
    work[:, size : 2 * size] = (row == lane).astype(F32)
    index = lax.broadcasted_iota(jnp.int32, (BLOCK, 1), 0)
    for start in range(0, size, BLOCK):
        panel = work[start : start + BLOCK, :]
        for step in range(BLOCK):
            spot = start + step
            column = panel[:, spot : spot + 1]
            scale = lax.rsqrt(panel[step : step + 1, spot : spot + 1])
            pivot = panel[step : step + 1, :] * scale
            scaled = column * scale
            panel = jnp.where(
                index == step, pivot, panel - jnp.where(index > step, scaled, 0.0) * pivot
            )
        work[start : start + BLOCK, :] = panel
        rest = start + BLOCK
        if rest < size:
            work[rest:size, :] -= exact_dot(panel[:, rest:size], panel, TN)
    upper = jnp.where(row <= lane, work[:, 0:size], 0.0)
    lower_ref[...] = upper.T
    inverse = jnp.where(row >= lane, work[:, size : 2 * size], 0.0)
    high = inverse.astype(BF16)
    left = inverse - high.astype(F32)
    middle = left.astype(BF16)
    pieces_ref[0] = high
    pieces_ref[1] = middle
    pieces_ref[2] = (left - middle.astype(F32)).astype(BF16)
    rows_ref[...] = exact_dot(message_ref[size : 2 * size], inverse, NT).astype(BF16)


def factorize(message):
    size = message.shape[1]
    whole = pl.BlockSpec(memory_space=pltpu.VMEM)
    return pl.pallas_call(
        factor_kernel,
        in_specs=[whole],
        out_specs=[whole] * 3,
        out_shape=[
            jax.ShapeDtypeStruct((size, size), F32),
            jax.ShapeDtypeStruct((3, size, size), BF16),
            jax.ShapeDtypeStruct((size, size), BF16),
        ],
        scratch_shapes=[pltpu.VMEM((size, 2 * size), F32)],
        cost_estimate=pl.CostEstimate(flops=10**9, bytes_accessed=4 * 10**5, transcendentals=0),
        name="factorize",
    )(message)


def panel_kernel(
    flags_ref, lower_ref, pieces_ref, rows_ref, added_ref, slab_ref, even_ref, odd_ref, old_ref, out_ref,
    slab, column, result, sems,
):
    size = lower_ref.shape[0]
    length = slab.shape[0]
    valid, index, mode = flags_ref[0], flags_ref[1], flags_ref[2]
    parity, head, own = flags_ref[3], flags_ref[4], flags_ref[5]
    here = pl.ds(index * length, length)

    @pl.when(valid == 1)
    def _():
        fetch = pltpu.make_async_copy(slab_ref.at[here], slab, sems.at[0])
        fetch.start()

        @pl.when((mode == 2) & (parity == 0))
        def _():
            other = pltpu.make_async_copy(even_ref, column, sems.at[1])
            other.start()
            other.wait()

        @pl.when((mode == 2) & (parity == 1))
        def _():
            other = pltpu.make_async_copy(odd_ref, column, sems.at[1])
            other.start()
            other.wait()

        fetch.wait()

        def factor_of(piece):
            solved = dot(piece, pieces_ref[0], NT) + dot(piece, pieces_ref[1], NT)
            return solved + dot(piece, pieces_ref[2], NT)

        def head_of(solved):
            solved = jnp.where(head == 1, lower_ref[...], solved)
            return jnp.where(head == 2, 0.0, solved).astype(BF16)

        @pl.when(mode == 0)
        def _():
            result[...] = slab[...]

        @pl.when(mode == 1)
        def _():
            result[...] = factor_of(slab[...]).astype(BF16)

            @pl.when(index == 0)
            def _():
                result[0:size] = head_of(factor_of(slab[0:size]))

        @pl.when(mode == 2)
        def _():
            factor = factor_of(column[...]).astype(BF16)
            result[...] = (slab[...].astype(F32) - dot(factor, rows_ref[...], NT)).astype(BF16)

            @pl.when(index == 0)
            def _():
                first = head_of(factor_of(column[0:size]))
                base = slab[0:size].astype(F32) + jnp.where(own == 1, added_ref[...], 0.0)
                result[0:size] = (base - dot(first, rows_ref[...], NT)).astype(BF16)

        store = pltpu.make_async_copy(result, out_ref.at[here], sems.at[2])
        store.start()
        store.wait()


def panel(flags, lower, pieces, rows, added, slab, even, odd, old):
    length, size = even.shape
    whole = pl.BlockSpec(memory_space=pltpu.VMEM)
    anywhere = pl.BlockSpec(memory_space=pl.ANY)
    return pl.pallas_call(
        panel_kernel,
        in_specs=[pl.BlockSpec(memory_space=pltpu.SMEM)] + [whole] * 4 + [anywhere] * 4,
        out_specs=anywhere,
        out_shape=jax.ShapeDtypeStruct(slab.shape, BF16),
        input_output_aliases={8: 0},
        scratch_shapes=[pltpu.VMEM((length, size), BF16)] * 3 + [pltpu.SemaphoreType.DMA((3,))],
        compiler_params=pltpu.CompilerParams(vmem_limit_bytes=32 * 2**20),
        cost_estimate=pl.CostEstimate(flops=8 * length * size * size, bytes_accessed=6 * length * size, transcendentals=0),
        name="panel",
    )(flags, lower, pieces, rows, added, slab, even, odd, old)


def both(axes, pairs_of):
    return functools.partial(lax.ppermute, axis_name=axes, perm=pairs_of)


def doubling_sum(value, axis):
    count = lax.axis_size(axis)
    if count & (count - 1):
        return lax.psum(value, axis)
    distance = 1
    while distance < count:
        pairs = [(i, i ^ distance) for i in range(count)]
        value = value + lax.ppermute(value, axis, pairs)
        distance *= 2
    return value


def on_device(coarse_basis, material_ids, lame_table, coarse_ids, coarse_slab, panel_owner):
    narrow, wide = lax.axis_size("narrow"), lax.axis_size("wide")
    stride = wide // narrow
    wide_index, narrow_index = lax.axis_index("wide"), lax.axis_index("narrow")
    owner = panel_owner[0]
    block = coarse_slab.shape[1]
    length = coarse_slab.shape[0] // CHUNKS
    subs, funcs, comps, layers, ny, nz = coarse_basis.shape
    table = lame_table.astype(F32)
    axes = ("wide", "narrow")

    def pairs(parity):
        return [
            (w * narrow + i, w * narrow + i + 1)
            for w in range(wide)
            if w % 2 == parity
            for i in range(narrow - 1)
        ]

    is_owner = narrow_index == owner
    received = {0: [], 1: []}

    def send_step(step, parity):
        chunk = jnp.clip(step - narrow_index, 0, CHUNKS - 1)
        mine = lax.dynamic_slice_in_dim(coarse_slab, chunk * length, length, axis=0)
        if step > 0:
            mine = jnp.where(is_owner, mine, received[parity][-1])
        received[parity].append(lax.ppermute(mine, axes, pairs(parity)))

    steps = CHUNKS + narrow - 2
    for step in range(steps):
        send_step(step, 0)
        send_step(step, 1)

    first_ids = material_ids[:, 0]
    shear = jnp.zeros(first_ids.shape, BF16)
    dilate = jnp.zeros(first_ids.shape, BF16)
    for material in range(lame_table.shape[1]):
        shear = jnp.where(first_ids == material, lame_table[0, material], shear)
        dilate = jnp.where(first_ids == material, lame_table[1, material], dilate)
    first = coarse_basis[:, :, :, 0].transpose(0, 2, 1, 3, 4).reshape(subs, comps * funcs, ny, nz)
    first = jnp.concatenate([first, jnp.stack([shear, dilate], 1)], axis=1)
    halo = lax.ppermute(first, "narrow", [(i + 1, i) for i in range(narrow - 1)])

    edge = (narrow_index == 0).astype(jnp.int32).reshape(1)
    inner = interior(edge, table, material_ids, coarse_basis)
    galerkin = doubling_sum(face(table, material_ids, coarse_basis, halo, inner), "narrow")

    got = jnp.where(wide_index % 2 == 0, received[0][0][:block], received[1][0][:block])
    for step in range(1, narrow - 1):
        later = jnp.where(wide_index % 2 == 0, received[0][step][:block], received[1][step][:block])
        got = jnp.where(narrow_index == step + 1, later, got)
    head = jnp.where(is_owner, coarse_slab[:block], got)
    source = (wide_index == owner * stride) & (narrow_index >= owner)
    own = wide_index == narrow_index * stride
    flags = jnp.stack([source, own]).astype(jnp.int32)
    added, message = assemble(flags, galerkin, coarse_ids, head)
    message = doubling_sum(message, "wide")
    lower, pieces, rows = factorize(message)

    mode = jnp.where(narrow_index == owner, 1, jnp.where(narrow_index > owner, 2, 0))
    earlier = (wide_index % stride == 0) & (wide_index // stride < owner)
    kind = jnp.where(wide_index == owner * stride, 1, jnp.where(earlier, 2, 0))
    result = jnp.zeros(coarse_slab.shape, BF16)
    for step in range(steps):
        index = step - jnp.maximum(narrow_index - 1, 0)
        valid = (index >= 0) & (index < CHUNKS)
        settings = jnp.stack(
            [valid, jnp.clip(index, 0, CHUNKS - 1), mode, wide_index % 2, kind, own]
        ).astype(jnp.int32)
        result = panel(
            settings, lower, pieces, rows, added, coarse_slab,
            received[0][step], received[1][step], result,
        )
    return result, galerkin


def solution(mesh):
    return jax.shard_map(
        on_device,
        mesh=mesh,
        in_specs=(
            P("wide", None, None, "narrow", None, None),
            P("wide", "narrow", None, None),
            P(),
            P("wide", None),
            P("wide", "narrow"),
            P(),
        ),
        out_specs=(P("wide", "narrow"), P("wide", None, None)),
        check_vma=False,
    )
```

```python
import functools

import jax
import jax.numpy as jnp
from jax import lax
from jax.experimental import pallas as pl
from jax.experimental.pallas import tpu as pltpu
from jax.sharding import PartitionSpec as P

F32, BF16 = jnp.float32, jnp.bfloat16
NT = (((1,), (1,)), ((), ()))
TN = (((0,), (0,)), ((), ()))
UNITS = (6, 6, 6, 6)
MOST_BRANCHES = 4
BLOCK = 16


def exact_dot(left, right, dims=(((1,), (0,)), ((), ()))):
    return lax.dot_general(
        left, right, dims, precision=lax.Precision.HIGHEST, preferred_element_type=F32
    )


def dot(left, right, dims=(((1,), (0,)), ((), ()))):
    return lax.dot_general(left, right, dims, preferred_element_type=F32)


def split_two(value):
    high = value.astype(BF16)
    return high, (value - high.astype(F32)).astype(BF16)


def lame_of(ids, table_ref):
    shear = jnp.zeros(ids.shape, F32)
    dilate = jnp.zeros(ids.shape, F32)
    for material in range(table_ref.shape[1]):
        chosen = ids == material
        shear = jnp.where(chosen, table_ref[0, material], shear)
        dilate = jnp.where(chosen, table_ref[1, material], dilate)
    return shear, dilate


def interior_kernel(edge_ref, table_ref, ids_ref, basis_ref, out_ref, fields, coef, left, right, acc):
    comp = pl.program_id(1)
    layers, ny, nz = basis_ref.shape[3:]
    funcs = basis_ref.shape[1]
    row = lax.broadcasted_iota(jnp.int32, (ny, nz), 0)
    lane = lax.broadcasted_iota(jnp.int32, (ny, nz), 1)
    table = [lame_of(ids_ref[0, x], table_ref) for x in range(layers)]

    def weight(one, two, direction):
        shear = 0.5 * (one[0] + two[0])
        dilate = 0.5 * (one[1] + two[1])
        return shear + jnp.where(comp == direction, shear + dilate, 0.0)

    def ahead(field, axis):
        size = field.shape[axis]
        index = row if axis == 0 else lane
        return jnp.where(index == size - 1, 0.0, pltpu.roll(field, size - 1, axis=axis))

    def behind(field, axis):
        index = row if axis == 0 else lane
        return jnp.where(index == 0, 0.0, pltpu.roll(field, 1, axis=axis))

    nothing = (jnp.zeros((ny, nz), F32),) * 2
    previous = weight(table[0], nothing, 0) * edge_ref[0].astype(F32)
    for x in range(layers):
        diagonal = previous
        forward = []
        if x + 1 < layers:
            face = weight(table[x], table[x + 1], 0)
            diagonal = diagonal + face
            previous = face
            forward.append(face)
        else:
            forward.append(jnp.zeros((ny, nz), F32))
        for axis in (0, 1):
            index, size = (row, ny) if axis == 0 else (lane, nz)
            other = tuple(ahead(value, axis) for value in table[x])
            face = weight(table[x], other, axis + 1)
            before = tuple(behind(value, axis) for value in table[x])
            diagonal = diagonal + face + weight(table[x], before, axis + 1)
            forward.append(jnp.where(index == size - 1, 0.0, face))
        coef[x, 0] = 0.5 * diagonal
        for kind in range(3):
            coef[x, kind + 1] = forward[kind]
        fields[x] = basis_ref[0, :, 0, x].astype(F32).reshape(funcs * ny, nz)

    total = None
    for x in range(layers):
        values = [fields[x, pl.ds(y, funcs, stride=ny), :] for y in range(ny)]
        for y in range(ny):
            value = values[y]
            image = coef[x, 0, y : y + 1, :] * value
            image = image - coef[x, 3, y : y + 1, :] * pltpu.roll(value, nz - 1, axis=1)
            if y + 1 < ny:
                image = image - coef[x, 2, y : y + 1, :] * values[y + 1]
            if x + 1 < layers:
                image = image - coef[x, 1, y : y + 1, :] * fields[x + 1, pl.ds(y, funcs, stride=ny), :]
            high, low = split_two(image)
            left[:, y * nz : (y + 1) * nz] = value.astype(BF16)
            right[0:funcs, y * nz : (y + 1) * nz] = high
            right[funcs : 2 * funcs, y * nz : (y + 1) * nz] = low
        product = dot(left[...], right[...], NT)
        total = product if total is None else total + product

    @pl.when(comp == 0)
    def _():
        acc[...] = total

    @pl.when(comp > 0)
    def _():
        acc[...] += total

    @pl.when(comp == pl.num_programs(1) - 1)
    def _():
        out_ref[0] = acc[:, 0:funcs] + acc[:, funcs : 2 * funcs]


def interior(edge, table, ids, basis):
    subs, funcs, comps, layers, ny, nz = basis.shape
    return pl.pallas_call(
        interior_kernel,
        grid=(subs, comps),
        in_specs=[
            pl.BlockSpec(memory_space=pltpu.SMEM),
            pl.BlockSpec(memory_space=pltpu.SMEM),
            pl.BlockSpec((1, layers, ny, nz), lambda s, c: (s, 0, 0, 0)),
            pl.BlockSpec((1, funcs, 1, layers, ny, nz), lambda s, c: (s, 0, c, 0, 0, 0)),
        ],
        out_specs=pl.BlockSpec((1, funcs, funcs), lambda s, c: (s, 0, 0)),
        out_shape=jax.ShapeDtypeStruct((subs, funcs, funcs), F32),
        scratch_shapes=[
            pltpu.VMEM((layers, funcs * ny, nz), F32),
            pltpu.VMEM((layers, 4, ny, nz), F32),
            pltpu.VMEM((funcs, ny * nz), BF16),
            pltpu.VMEM((2 * funcs, ny * nz), BF16),
            pltpu.VMEM((funcs, 2 * funcs), F32),
        ],
        compiler_params=pltpu.CompilerParams(vmem_limit_bytes=32 * 2**20),
        cost_estimate=pl.CostEstimate(flops=4 * basis.size * funcs, bytes_accessed=2 * basis.size, transcendentals=0),
        name="interior",
    )(edge, table, ids, basis)


def face_kernel(table_ref, ids_ref, basis_ref, halo_ref, coef_ref, inner_ref, out_ref, mine, theirs, left, right, acc):
    comp = pl.program_id(1)
    funcs = basis_ref.shape[1]
    ny, nz = basis_ref.shape[4:]
    shear, dilate = lame_of(ids_ref[0, 0], table_ref)
    shear = 0.5 * (shear + coef_ref[0, 0].astype(F32))
    dilate = 0.5 * (dilate + coef_ref[0, 1].astype(F32))
    weight = shear + jnp.where(comp == 0, shear + dilate, 0.0)
    mine[...] = basis_ref[0, :, 0, 0].astype(F32).reshape(funcs * ny, nz)
    theirs[...] = halo_ref[0].astype(F32).reshape(funcs * ny, nz)
    for y in range(ny):
        here = mine[pl.ds(y, funcs, stride=ny), :]
        there = theirs[pl.ds(y, funcs, stride=ny), :]
        high, low = split_two(weight[y : y + 1, :] * (here - there))
        left[0:funcs, y * nz : (y + 1) * nz] = here.astype(BF16)
        left[funcs : 2 * funcs, y * nz : (y + 1) * nz] = there.astype(BF16)
        right[0:funcs, y * nz : (y + 1) * nz] = high
        right[funcs : 2 * funcs, y * nz : (y + 1) * nz] = low
    product = dot(left[...], right[...], NT)
    product = product[0:funcs] - product[funcs : 2 * funcs]
    total = product[:, 0:funcs] + product[:, funcs : 2 * funcs]

    @pl.when(comp == 0)
    def _():
        acc[...] = total

    @pl.when(comp > 0)
    def _():
        acc[...] += total

    @pl.when(comp == pl.num_programs(1) - 1)
    def _():
        half = inner_ref[0] + 0.5 * acc[...]
        out_ref[0] = half + half.T


def face(table, ids, basis, halo, inner):
    subs, funcs, comps, layers, ny, nz = basis.shape
    return pl.pallas_call(
        face_kernel,
        grid=(subs, comps),
        in_specs=[
            pl.BlockSpec(memory_space=pltpu.SMEM),
            pl.BlockSpec((1, 1, ny, nz), lambda s, c: (s, layers - 1, 0, 0)),
            pl.BlockSpec((1, funcs, 1, 1, ny, nz), lambda s, c: (s, 0, c, layers - 1, 0, 0)),
            pl.BlockSpec((1, funcs, ny, nz), lambda s, c: (s, c, 0, 0)),
            pl.BlockSpec((1, 2, ny, nz), lambda s, c: (s, comps * funcs // 2, 0, 0)),
            pl.BlockSpec((1, funcs, funcs), lambda s, c: (s, 0, 0)),
        ],
        out_specs=pl.BlockSpec((1, funcs, funcs), lambda s, c: (s, 0, 0)),
        out_shape=jax.ShapeDtypeStruct((subs, funcs, funcs), F32),
        scratch_shapes=[
            pltpu.VMEM((funcs * ny, nz), F32),
            pltpu.VMEM((funcs * ny, nz), F32),
            pltpu.VMEM((2 * funcs, ny * nz), BF16),
            pltpu.VMEM((2 * funcs, ny * nz), BF16),
            pltpu.VMEM((funcs, funcs), F32),
        ],
        compiler_params=pltpu.CompilerParams(vmem_limit_bytes=32 * 2**20),
        cost_estimate=pl.CostEstimate(flops=basis.size * funcs * 2, bytes_accessed=basis.size, transcendentals=0),
        name="face",
    )(table, ids, basis, halo, halo, inner)


def assemble_kernel(flags_ref, gal_ref, column_ids_ref, row_ids_ref, head_ref, added_ref, message_ref):
    subs, funcs = gal_ref.shape[0:2]
    size = added_ref.shape[0]
    added = jnp.zeros((size, size), F32)
    for sub in range(subs):
        lane = lax.broadcasted_iota(jnp.int32, (funcs, size), 1)
        slots = (column_ids_ref[sub] == lane).astype(F32)
        row = lax.broadcasted_iota(jnp.int32, (size, funcs), 0)
        slots_t = (row_ids_ref[sub] == row).astype(F32)
        added = added + exact_dot(slots_t, exact_dot(gal_ref[sub], slots))
    head = head_ref[...].astype(F32)
    added_ref[...] = added
    message_ref[0:size] = jnp.where(flags_ref[0] == 1, added + head, 0.0)
    message_ref[size : 2 * size] = jnp.where(flags_ref[1] == 1, head, 0.0)


def assemble(flags, galerkin, ids, head):
    size = head.shape[0]
    whole = pl.BlockSpec(memory_space=pltpu.VMEM)
    return pl.pallas_call(
        assemble_kernel,
        in_specs=[pl.BlockSpec(memory_space=pltpu.SMEM)] + [whole] * 4,
        out_specs=[whole, whole],
        out_shape=[
            jax.ShapeDtypeStruct((size, size), F32),
            jax.ShapeDtypeStruct((2 * size, size), F32),
        ],
        cost_estimate=pl.CostEstimate(flops=10**8, bytes_accessed=4 * 10**5, transcendentals=0),
        name="assemble",
    )(flags, galerkin, ids[:, :, None], ids[:, None, :], head)


def factor_kernel(message_ref, lower_ref, pieces_ref, rows_ref, work):
    size = lower_ref.shape[0]
    diagonal = message_ref[0:size]
    row = lax.broadcasted_iota(jnp.int32, (size, size), 0)
    lane = lax.broadcasted_iota(jnp.int32, (size, size), 1)
    work[:, 0:size] = 0.5 * (diagonal + diagonal.T)
    work[:, size : 2 * size] = (row == lane).astype(F32)
    index = lax.broadcasted_iota(jnp.int32, (BLOCK, 1), 0)
    for start in range(0, size, BLOCK):
        panel = work[start : start + BLOCK, :]
        for step in range(BLOCK):
            spot = start + step
            column = panel[:, spot : spot + 1]
            scale = lax.rsqrt(panel[step : step + 1, spot : spot + 1])
            pivot = panel[step : step + 1, :] * scale
            scaled = column * scale
            panel = jnp.where(
                index == step, pivot, panel - jnp.where(index > step, scaled, 0.0) * pivot
            )
        work[start : start + BLOCK, :] = panel
        rest = start + BLOCK
        if rest < size:
            work[rest:size, :] -= exact_dot(panel[:, rest:size], panel, TN)
    upper = jnp.where(row <= lane, work[:, 0:size], 0.0)
    lower_ref[...] = upper.T
    inverse = jnp.where(row >= lane, work[:, size : 2 * size], 0.0)
    high = inverse.astype(BF16)
    left = inverse - high.astype(F32)
    middle = left.astype(BF16)
    pieces_ref[0] = high
    pieces_ref[1] = middle
    pieces_ref[2] = (left - middle.astype(F32)).astype(BF16)
    rows_ref[...] = exact_dot(message_ref[size : 2 * size], inverse, NT).astype(BF16)


def factorize(message):
    size = message.shape[1]
    whole = pl.BlockSpec(memory_space=pltpu.VMEM)
    return pl.pallas_call(
        factor_kernel,
        in_specs=[whole],
        out_specs=[whole] * 3,
        out_shape=[
            jax.ShapeDtypeStruct((size, size), F32),
            jax.ShapeDtypeStruct((3, size, size), BF16),
            jax.ShapeDtypeStruct((size, size), BF16),
        ],
        scratch_shapes=[pltpu.VMEM((size, 2 * size), F32)],
        cost_estimate=pl.CostEstimate(flops=10**9, bytes_accessed=4 * 10**5, transcendentals=0),
        name="factorize",
    )(message)


def panel_kernel(
    flags_ref, lower_ref, pieces_ref, rows_ref, added_ref, slab_ref, *rest, received, first
):
    others, out_ref = rest[:received], rest[-1]
    size = lower_ref.shape[0]
    mode, head, own, which = flags_ref[0], flags_ref[1], flags_ref[2], flags_ref[3]
    top = first & (pl.program_id(0) == 0)

    def factor_of(piece):
        twice = jnp.concatenate([piece, piece], axis=1)
        weights = jnp.concatenate([pieces_ref[0], pieces_ref[1]], axis=1)
        return dot(twice, weights, NT) + dot(piece, pieces_ref[2], NT)

    def head_of(solved):
        solved = jnp.where(head == 1, lower_ref[...], solved)
        return jnp.where(head == 2, 0.0, solved).astype(BF16)

    @pl.when(mode == 0)
    def _():
        out_ref[...] = slab_ref[...]

    @pl.when(mode == 1)
    def _():
        out_ref[...] = factor_of(slab_ref[...]).astype(BF16)

        @pl.when(top)
        def _():
            out_ref[0:size] = head_of(factor_of(slab_ref[0:size]))

    for number, other_ref in enumerate(others):

        @pl.when((mode == 2) & (which == number))
        def _(other_ref=other_ref):
            factor = factor_of(other_ref[...]).astype(BF16)
            out_ref[...] = (slab_ref[...].astype(F32) - dot(factor, rows_ref[...], NT)).astype(BF16)

            @pl.when(top)
            def _():
                begin = head_of(factor_of(other_ref[0:size]))
                base = slab_ref[0:size].astype(F32) + jnp.where(own == 1, added_ref[...], 0.0)
                out_ref[0:size] = (base - dot(begin, rows_ref[...], NT)).astype(BF16)


def panel(flags, lower, pieces, rows, added, slab, others, old, start, tile):
    length, size = others[0].shape
    offset = start // tile

    def chosen(number):
        return lambda i, flags: (jnp.where(flags[3] == number, i, 0), 0)

    def fixed(rank):
        return lambda i, flags: (0,) * rank

    blocks = [
        pl.BlockSpec((size, size), fixed(2)),
        pl.BlockSpec((3, size, size), fixed(3)),
        pl.BlockSpec((size, size), fixed(2)),
        pl.BlockSpec((size, size), fixed(2)),
        pl.BlockSpec((tile, size), lambda i, flags: (i + offset, 0)),
    ] + [pl.BlockSpec((tile, size), chosen(number)) for number in range(len(others))]
    operands = [flags, lower, pieces, rows, added, slab] + others
    aliases = {}
    if old is not None:
        aliases = {len(operands): 0}
        blocks.append(pl.BlockSpec(memory_space=pl.ANY))
        operands.append(old)
    return pl.pallas_call(
        functools.partial(panel_kernel, received=len(others), first=start == 0),
        grid_spec=pltpu.PrefetchScalarGridSpec(
            num_scalar_prefetch=1,
            grid=(length // tile,),
            in_specs=blocks,
            out_specs=pl.BlockSpec((tile, size), lambda i, flags: (i + offset, 0)),
        ),
        out_shape=jax.ShapeDtypeStruct(slab.shape, BF16),
        input_output_aliases=aliases,
        compiler_params=pltpu.CompilerParams(vmem_limit_bytes=32 * 2**20),
        cost_estimate=pl.CostEstimate(flops=8 * length * size * size, bytes_accessed=6 * length * size, transcendentals=0),
        name="panel",
    )(*operands)


def halo_kernel(table_ref, ids_ref, basis_ref, out_ref, coefs, sems):
    subs, funcs, comps = basis_ref.shape[0:3]
    copies = []
    for sub in range(subs):
        for comp in range(comps):
            copies.append(
                pltpu.make_async_copy(
                    basis_ref.at[sub, :, comp, 0],
                    out_ref.at[sub, pl.ds(comp * funcs, funcs)],
                    sems.at[sub, comp],
                )
            )
            copies[-1].start()
    for sub in range(subs):
        shear, dilate = lame_of(ids_ref[sub, 0], table_ref)
        coefs[sub, 0] = shear.astype(BF16)
        coefs[sub, 1] = dilate.astype(BF16)
        copies.append(
            pltpu.make_async_copy(
                coefs.at[sub], out_ref.at[sub, pl.ds(comps * funcs, 2)], sems.at[sub, comps]
            )
        )
        copies[-1].start()
    for copy in copies:
        copy.wait()


def halo_message(table, ids, basis):
    subs, funcs, comps, layers, ny, nz = basis.shape
    return pl.pallas_call(
        halo_kernel,
        in_specs=[
            pl.BlockSpec(memory_space=pltpu.SMEM),
            pl.BlockSpec(memory_space=pltpu.VMEM),
            pl.BlockSpec(memory_space=pl.ANY),
        ],
        out_specs=pl.BlockSpec(memory_space=pl.ANY),
        out_shape=jax.ShapeDtypeStruct((subs, comps * funcs + 2, ny, nz), BF16),
        scratch_shapes=[pltpu.VMEM((subs, 2, ny, nz), BF16), pltpu.SemaphoreType.DMA((subs, comps + 1))],
        cost_estimate=pl.CostEstimate(flops=0, bytes_accessed=basis.size, transcendentals=0),
        name="halo_message",
    )(table, ids, basis)


def broadcast(value, axis, source):
    kept = jnp.where(lax.axis_index(axis) == source, value, 0).astype(value.dtype)
    return lax.psum(kept, axis)


def doubling_sum(value, axis):
    count = lax.axis_size(axis)
    if count & (count - 1):
        return lax.psum(value, axis)
    distance = 1
    while distance < count:
        pairs = [(i, i ^ distance) for i in range(count)]
        value = value + lax.ppermute(value, axis, pairs)
        distance *= 2
    return value


def tied(value, *earlier):
    return lax.optimization_barrier((value, *earlier))[0]


def column_pieces(coarse_slab, owner, bounds):
    narrow = lax.axis_size("narrow")
    if not isinstance(owner, int):
        column = broadcast(coarse_slab, "narrow", owner)
        return [[column[low:high]] for low, high in bounds]
    pieces = []
    for number, (low, high) in enumerate(bounds):
        moving = coarse_slab[low:high]
        if number >= 2:
            moving = tied(moving, pieces[number - 2][0])
        hops = []
        for place in range(owner, narrow - 1):
            moving = lax.ppermute(moving, "narrow", [(place, place + 1)])
            hops.append(moving)
        pieces.append(hops)
    return pieces


def body(owner, coarse_basis, material_ids, lame_table, coarse_ids, coarse_slab):
    narrow, wide = lax.axis_size("narrow"), lax.axis_size("wide")
    stride = wide // narrow
    wide_index, narrow_index = lax.axis_index("wide"), lax.axis_index("narrow")
    height, block = coarse_slab.shape
    unit = height // sum(UNITS)
    bounds, low = [], 0
    for units in UNITS:
        bounds.append((low, low + units * unit))
        low += units * unit
    table = lame_table.astype(F32)

    pieces = column_pieces(coarse_slab, owner, bounds)
    later = narrow_index > owner
    which = jnp.where(later, narrow_index - owner - 1, -1) if isinstance(owner, int) else jnp.where(later, 0, -1)

    first = halo_message(table, material_ids, coarse_basis)
    halo = lax.ppermute(first, "narrow", [(i + 1, i) for i in range(narrow - 1)])

    edge = (narrow_index == 0).astype(jnp.int32).reshape(1)
    inner = interior(edge, table, material_ids, coarse_basis)
    galerkin = doubling_sum(face(table, material_ids, coarse_basis, halo, inner), "narrow")

    head = coarse_slab[:block]
    for number, piece in enumerate(pieces[0]):
        head = jnp.where(which == number, piece[:block], head)
    source = (wide_index == owner * stride) & (narrow_index >= owner)
    own = wide_index == narrow_index * stride
    added, message = assemble(jnp.stack([source, own]).astype(jnp.int32), galerkin, coarse_ids, head)
    lower, inverse, rows = factorize(doubling_sum(message, "wide"))

    mode = jnp.where(narrow_index == owner, 1, jnp.where(later, 2, 0))
    earlier = (wide_index % stride == 0) & (wide_index // stride < owner)
    kind = jnp.where(wide_index == owner * stride, 1, jnp.where(earlier, 2, 0))
    settings = jnp.stack([mode, kind, own, which]).astype(jnp.int32)
    result = None
    for (low, high), hops in zip(bounds, pieces):
        result = panel(settings, lower, inverse, rows, added, coarse_slab, hops, result, low, 2 * unit)
    return result, galerkin


def on_device(coarse_basis, material_ids, lame_table, coarse_ids, coarse_slab, panel_owner):
    narrow = lax.axis_size("narrow")
    arrays = (coarse_basis, material_ids, lame_table, coarse_ids, coarse_slab)
    owner = panel_owner[0]
    if narrow > MOST_BRANCHES:
        return body(owner, *arrays)
    branches = [functools.partial(body, place) for place in range(narrow - 1)]
    return lax.switch(owner, branches, *arrays)


def solution(mesh):
    return jax.shard_map(
        on_device,
        mesh=mesh,
        in_specs=(
            P("wide", None, None, "narrow", None, None),
            P("wide", "narrow", None, None),
            P(),
            P("wide", None),
            P("wide", "narrow"),
            P(),
        ),
        out_specs=(P("wide", "narrow"), P("wide", None, None)),
        check_vma=False,
    )
```

```python
import functools

import jax
import jax.numpy as jnp
from jax import lax
from jax.experimental import pallas as pl
from jax.experimental.pallas import tpu as pltpu
from jax.sharding import PartitionSpec as P

F32, BF16 = jnp.float32, jnp.bfloat16
NT = (((1,), (1,)), ((), ()))
TN = (((0,), (0,)), ((), ()))
VMEM = pl.BlockSpec(memory_space=pltpu.VMEM)
SMEM = pl.BlockSpec(memory_space=pltpu.SMEM)
UNITS = {1: (2, 8, 8, 4, 2), 2: (2, 6, 6, 6, 4), 3: (2, 4, 4, 4, 4, 4, 2)}
BLOCK = 16


def exact_dot(left, right, dims=(((1,), (0,)), ((), ()))):
    return lax.dot_general(
        left, right, dims, precision=lax.Precision.HIGHEST, preferred_element_type=F32
    )


def dot(left, right, dims=(((1,), (0,)), ((), ()))):
    return lax.dot_general(left, right, dims, preferred_element_type=F32)


def split_two(value):
    high = value.astype(BF16)
    return high, (value - high.astype(F32)).astype(BF16)


def lame_of(ids, table_ref):
    shear = jnp.zeros(ids.shape, F32)
    dilate = jnp.zeros(ids.shape, F32)
    for material in range(table_ref.shape[1]):
        chosen = ids == material
        shear = jnp.where(chosen, table_ref[0, material], shear)
        dilate = jnp.where(chosen, table_ref[1, material], dilate)
    return shear, dilate


def halo_kernel(table_ref, ids_ref, basis_ref, out_ref):
    subs, funcs, comps = basis_ref.shape[0:3]
    for sub in range(subs):
        for comp in range(comps):
            out_ref[sub, comp * funcs : (comp + 1) * funcs] = basis_ref[sub, :, comp, 0]
        shear, dilate = lame_of(ids_ref[sub, 0], table_ref)
        out_ref[sub, comps * funcs] = shear.astype(BF16)
        out_ref[sub, comps * funcs + 1] = dilate.astype(BF16)


def halo_message(table, ids, basis):
    subs, funcs, comps, layers, ny, nz = basis.shape
    return pl.pallas_call(
        halo_kernel,
        in_specs=[SMEM, VMEM, VMEM],
        out_specs=VMEM,
        out_shape=jax.ShapeDtypeStruct((subs, comps * funcs + 2, ny, nz), BF16),
        compiler_params=pltpu.CompilerParams(vmem_limit_bytes=32 * 2**20),
        cost_estimate=pl.CostEstimate(flops=0, bytes_accessed=basis.size, transcendentals=0),
        name="halo_message",
    )(table, ids, basis)


def interior_kernel(edge_ref, table_ref, ids_ref, basis_ref, out_ref, fields, coef, left, right, acc):
    sub, comp = pl.program_id(0), pl.program_id(1)
    layers, ny, nz = basis_ref.shape[3:]
    funcs = basis_ref.shape[1]
    row = lax.broadcasted_iota(jnp.int32, (ny, nz), 0)
    lane = lax.broadcasted_iota(jnp.int32, (ny, nz), 1)
    table = [lame_of(ids_ref[sub, x], table_ref) for x in range(layers)]

    def weight(one, two, direction):
        shear = 0.5 * (one[0] + two[0])
        dilate = 0.5 * (one[1] + two[1])
        return shear + jnp.where(comp == direction, shear + dilate, 0.0)

    def ahead(field, axis):
        size = field.shape[axis]
        index = row if axis == 0 else lane
        return jnp.where(index == size - 1, 0.0, pltpu.roll(field, size - 1, axis=axis))

    def behind(field, axis):
        index = row if axis == 0 else lane
        return jnp.where(index == 0, 0.0, pltpu.roll(field, 1, axis=axis))

    nothing = (jnp.zeros((ny, nz), F32),) * 2
    previous = weight(table[0], nothing, 0) * edge_ref[0].astype(F32)
    for x in range(layers):
        diagonal = previous
        forward = []
        if x + 1 < layers:
            face = weight(table[x], table[x + 1], 0)
            diagonal = diagonal + face
            previous = face
            forward.append(face)
        else:
            forward.append(jnp.zeros((ny, nz), F32))
        for axis in (0, 1):
            index, size = (row, ny) if axis == 0 else (lane, nz)
            other = tuple(ahead(value, axis) for value in table[x])
            face = weight(table[x], other, axis + 1)
            before = tuple(behind(value, axis) for value in table[x])
            diagonal = diagonal + face + weight(table[x], before, axis + 1)
            forward.append(jnp.where(index == size - 1, 0.0, face))
        coef[x, 0] = 0.5 * diagonal
        for kind in range(3):
            coef[x, kind + 1] = forward[kind]
        fields[x] = basis_ref[sub, :, comp, x].astype(F32).reshape(funcs * ny, nz)

    total = None
    for x in range(layers):
        values = [fields[x, pl.ds(y, funcs, stride=ny), :] for y in range(ny)]
        for y in range(ny):
            value = values[y]
            image = coef[x, 0, y : y + 1, :] * value
            image = image - coef[x, 3, y : y + 1, :] * pltpu.roll(value, nz - 1, axis=1)
            if y + 1 < ny:
                image = image - coef[x, 2, y : y + 1, :] * values[y + 1]
            if x + 1 < layers:
                image = image - coef[x, 1, y : y + 1, :] * fields[x + 1, pl.ds(y, funcs, stride=ny), :]
            high, low = split_two(image)
            left[:, y * nz : (y + 1) * nz] = value.astype(BF16)
            right[0:funcs, y * nz : (y + 1) * nz] = high
            right[funcs : 2 * funcs, y * nz : (y + 1) * nz] = low
        product = dot(right[...], left[...], NT)
        total = product if total is None else total + product

    @pl.when(comp == 0)
    def _():
        acc[...] = total

    @pl.when(comp > 0)
    def _():
        acc[...] += total

    @pl.when(comp == pl.num_programs(1) - 1)
    def _():
        out_ref[0] = acc[0:funcs] + acc[funcs : 2 * funcs]


def interior(edge, table, ids, basis):
    subs, funcs, comps, layers, ny, nz = basis.shape
    return pl.pallas_call(
        interior_kernel,
        grid=(subs, comps),
        in_specs=[SMEM, SMEM, VMEM, VMEM],
        out_specs=pl.BlockSpec((1, funcs, funcs), lambda s, c: (s, 0, 0)),
        out_shape=jax.ShapeDtypeStruct((subs, funcs, funcs), F32),
        scratch_shapes=[
            pltpu.VMEM((layers, funcs * ny, nz), F32),
            pltpu.VMEM((layers, 4, ny, nz), F32),
            pltpu.VMEM((funcs, ny * nz), BF16),
            pltpu.VMEM((2 * funcs, ny * nz), BF16),
            pltpu.VMEM((2 * funcs, funcs), F32),
        ],
        compiler_params=pltpu.CompilerParams(vmem_limit_bytes=32 * 2**20),
        cost_estimate=pl.CostEstimate(flops=20 * basis.size * funcs, bytes_accessed=2 * basis.size, transcendentals=0),
        name="interior",
    )(edge, table, ids, basis)


def face_kernel(table_ref, ids_ref, basis_ref, halo_ref, inner_ref, out_ref, mine, theirs, left, right):
    subs, funcs, comps, layers, ny, nz = basis_ref.shape
    for sub in range(subs):
        shear, dilate = lame_of(ids_ref[sub, layers - 1], table_ref)
        shear = 0.5 * (shear + halo_ref[sub, comps * funcs].astype(F32))
        dilate = 0.5 * (dilate + halo_ref[sub, comps * funcs + 1].astype(F32))
        total = None
        for comp in range(comps):
            weight = shear + (shear + dilate) if comp == 0 else shear
            slot = (sub * comps + comp) % 2
            mine[slot] = basis_ref[sub, :, comp, layers - 1].astype(F32).reshape(funcs * ny, nz)
            theirs[slot] = halo_ref[sub, comp * funcs : (comp + 1) * funcs].astype(F32).reshape(funcs * ny, nz)
            for y in range(ny):
                here = mine[slot, pl.ds(y, funcs, stride=ny), :]
                there = theirs[slot, pl.ds(y, funcs, stride=ny), :]
                high, low = split_two(weight[y : y + 1, :] * (here - there))
                left[slot, 0:funcs, y * nz : (y + 1) * nz] = here.astype(BF16)
                left[slot, funcs : 2 * funcs, y * nz : (y + 1) * nz] = there.astype(BF16)
                right[slot, 0:funcs, y * nz : (y + 1) * nz] = high
                right[slot, funcs : 2 * funcs, y * nz : (y + 1) * nz] = low
            product = dot(right[slot], left[slot], NT)
            total = product if total is None else total + product
        total = total[:, 0:funcs] - total[:, funcs : 2 * funcs]
        half = inner_ref[sub] + 0.5 * (total[0:funcs] + total[funcs : 2 * funcs])
        out_ref[sub] = half + half.T


def face(table, ids, basis, halo, inner):
    subs, funcs, comps, layers, ny, nz = basis.shape
    return pl.pallas_call(
        face_kernel,
        in_specs=[SMEM] + [VMEM] * 4,
        out_specs=VMEM,
        out_shape=jax.ShapeDtypeStruct((subs, funcs, funcs), F32),
        scratch_shapes=[
            pltpu.VMEM((2, funcs * ny, nz), F32),
            pltpu.VMEM((2, funcs * ny, nz), F32),
            pltpu.VMEM((2, 2 * funcs, ny * nz), BF16),
            pltpu.VMEM((2, 2 * funcs, ny * nz), BF16),
        ],
        compiler_params=pltpu.CompilerParams(vmem_limit_bytes=32 * 2**20),
        cost_estimate=pl.CostEstimate(flops=basis.size * funcs * 4, bytes_accessed=basis.size, transcendentals=0),
        name="face",
    )(table, ids, basis, halo, inner)


def spread(gal_ref, column_ids_ref, row_ids_ref, size):
    subs, funcs = column_ids_ref.shape[0:2]
    added = jnp.zeros((size, size), F32)
    lane = lax.broadcasted_iota(jnp.int32, (funcs, size), 1)
    row = lax.broadcasted_iota(jnp.int32, (size, funcs), 0)
    for sub in range(subs):
        slots = (column_ids_ref[sub] == lane).astype(F32)
        slots_t = (row_ids_ref[sub] == row).astype(F32)
        added = added + exact_dot(slots_t, exact_dot(gal_ref[sub], slots))
    return added


def assemble_kernel(flags_ref, column_ids_ref, row_ids_ref, slab_ref, *rest, parts, heads):
    gal_refs, head_refs = rest[:parts], rest[parts : parts + heads]
    sum_ref, message_ref = rest[parts + heads :]
    size = message_ref.shape[0]
    which, mode = flags_ref[0], flags_ref[1]
    total = gal_refs[0][...]
    for gal_ref in gal_refs[1:]:
        total = total + gal_ref[...]
    sum_ref[...] = total

    @pl.when(mode != 2)
    def _():
        added = spread(sum_ref, column_ids_ref, row_ids_ref, size)
        message_ref[...] = added + slab_ref[...].astype(F32)

    for number, head_ref in enumerate(head_refs):

        @pl.when((mode == 2) & (which == number))
        def _(head_ref=head_ref):
            message_ref[...] = head_ref[...].astype(F32)


def assemble(flags, ids, slab, parts, heads):
    size = slab.shape[1]
    block = pl.BlockSpec((size, size), lambda i: (0, 0))
    return pl.pallas_call(
        functools.partial(assemble_kernel, parts=len(parts), heads=len(heads)),
        grid=(1,),
        in_specs=[SMEM, VMEM, VMEM, block] + [VMEM] * len(parts) + [block] * len(heads),
        out_specs=[VMEM, VMEM],
        out_shape=[
            jax.ShapeDtypeStruct(parts[0].shape, F32),
            jax.ShapeDtypeStruct((size, size), F32),
        ],
        cost_estimate=pl.CostEstimate(flops=10**9, bytes_accessed=4 * 10**5, transcendentals=0),
        name="assemble",
    )(flags, ids[:, :, None], ids[:, None, :], slab, *parts, *heads)


def factor_kernel(*refs, parts, rows):
    message_refs, gal_ref = refs[:parts], refs[parts]
    summary_ref, block_ref, work = refs[parts + 1 :]
    subs, funcs = gal_ref.shape[0:2]
    size = summary_ref.shape[1]
    diagonal = message_refs[0][...]
    for message_ref in message_refs[1:]:
        diagonal = diagonal + message_ref[...]
    block_ref[...] = diagonal
    row = lax.broadcasted_iota(jnp.int32, (size, size), 0)
    lane = lax.broadcasted_iota(jnp.int32, (size, size), 1)
    work[:, 0:size] = 0.5 * (diagonal + diagonal.T)
    work[:, size : 2 * size] = (row == lane).astype(F32)
    index = lax.broadcasted_iota(jnp.int32, (BLOCK, 1), 0)
    for start in range(0, size, BLOCK):
        panel = work[start : start + BLOCK, :]
        for step in range(0, BLOCK, 2):
            spot = start + step
            column, next_column = panel[:, spot : spot + 1], panel[:, spot + 1 : spot + 2]
            one, mixed = column[step : step + 1], column[step + 1 : step + 2]
            two = next_column[step + 1 : step + 2]
            scale = lax.rsqrt(one)
            next_scale = lax.rsqrt(one * two - mixed * mixed) * (one * scale)
            mixed = mixed * scale
            pivot = panel[step : step + 1, :] * scale
            next_pivot = (panel[step + 1 : step + 2, :] - mixed * pivot) * next_scale
            column = column * scale
            next_column = (next_column - column * mixed) * next_scale
            rest = panel - column * pivot - next_column * next_pivot
            panel = jnp.where(index > step + 1, rest, panel)
            panel = jnp.where(index == step, pivot, panel)
            panel = jnp.where(index == step + 1, next_pivot, panel)
        work[start : start + BLOCK, :] = panel
        rest = start + BLOCK
        if rest < size:
            work[rest:size, :] -= exact_dot(panel[:, rest:size], panel, TN)
    upper = jnp.where(row <= lane, work[:, 0:size], 0.0)
    summary_ref[0:size] = jnp.where(row >= lane, work[:, size : 2 * size], 0.0).T
    summary_ref[size : 2 * size] = upper.T
    for sub in range(subs):
        summary_ref[rows + sub * funcs : rows + (sub + 1) * funcs, 0:funcs] = gal_ref[sub]
        summary_ref[rows + sub * funcs : rows + (sub + 1) * funcs, funcs:size] = jnp.zeros(
            (funcs, size - funcs), F32
        )


def factorize(messages, galerkin):
    size = messages[0].shape[1]
    subs, funcs = galerkin.shape[0:2]
    return pl.pallas_call(
        functools.partial(factor_kernel, parts=len(messages), rows=2 * size),
        in_specs=[VMEM] * (len(messages) + 1),
        out_specs=[VMEM] * 2,
        out_shape=[
            jax.ShapeDtypeStruct((2 * size + subs * funcs, size), F32),
            jax.ShapeDtypeStruct((size, size), F32),
        ],
        scratch_shapes=[pltpu.VMEM((size, 2 * size), F32)],
        cost_estimate=pl.CostEstimate(flops=5 * 10**9, bytes_accessed=4 * 10**5, transcendentals=0),
        name="factorize",
    )(*messages, galerkin)


def prepare_kernel(flags_ref, column_ids_ref, row_ids_ref, head_ref, *rest, sources):
    summary_refs = rest[:sources]
    weights_ref, rows_ref, lower_ref, added_ref, gal_ref, summary = rest[sources:]
    subs, funcs = gal_ref.shape[0:2]
    size = head_ref.shape[0]
    choice, mode, own = flags_ref[0], flags_ref[1], flags_ref[2]
    for number, summary_ref in enumerate(summary_refs):

        @pl.when(choice == number)
        def _(summary_ref=summary_ref):
            summary[...] = summary_ref[...]

    for sub in range(subs):
        begin = 2 * size + sub * funcs
        gal_ref[sub] = summary[begin : begin + funcs, 0:funcs]

    def doubled(block):
        nothing = jnp.zeros((size, size), BF16)
        top = jnp.concatenate([block, nothing], axis=1)
        return jnp.concatenate([top, jnp.concatenate([nothing, block], axis=1)], axis=0)

    @pl.when(mode > 0)
    def _():
        inverse = summary[0:size]
        high = inverse.astype(BF16)
        left = inverse - high.astype(F32)
        middle = left.astype(BF16)
        weights_ref[0] = doubled(high)
        weights_ref[1] = doubled(middle)
        weights_ref[2] = doubled((left - middle.astype(F32)).astype(BF16))
        lower_ref[...] = summary[size : 2 * size]

    @pl.when(mode == 2)
    def _():
        solved = exact_dot(head_ref[...], summary[0:size])
        rows_ref[...] = doubled(solved.T.astype(BF16))

    @pl.when((mode == 2) & (own == 1))
    def _():
        added_ref[...] = spread(gal_ref, column_ids_ref, row_ids_ref, size)


def prepare(flags, ids, head, summaries):
    size = head.shape[0]
    subs, funcs = ids.shape
    return pl.pallas_call(
        functools.partial(prepare_kernel, sources=len(summaries)),
        in_specs=[SMEM] + [VMEM] * (3 + len(summaries)),
        out_specs=[VMEM] * 5,
        out_shape=[
            jax.ShapeDtypeStruct((3, 2 * size, 2 * size), BF16),
            jax.ShapeDtypeStruct((2 * size, 2 * size), BF16),
            jax.ShapeDtypeStruct((size, size), F32),
            jax.ShapeDtypeStruct((size, size), F32),
            jax.ShapeDtypeStruct((subs, funcs, funcs), F32),
        ],
        scratch_shapes=[pltpu.VMEM(summaries[0].shape, F32)],
        compiler_params=pltpu.CompilerParams(vmem_limit_bytes=32 * 2**20),
        cost_estimate=pl.CostEstimate(flops=10**9, bytes_accessed=4 * 10**5, transcendentals=0),
        name="prepare",
    )(flags, ids[:, :, None], ids[:, None, :], head, *summaries)


def panel_kernel(
    flags_ref, lower_ref, weights_ref, rows_ref, added_ref, slab_ref, *rest, received, first
):
    others, out_ref = rest[:received], rest[-1]
    size = lower_ref.shape[0]
    half = out_ref.shape[0] // 2
    mode, head, own, which = flags_ref[0], flags_ref[1], flags_ref[2], flags_ref[3]
    top = first & (pl.program_id(0) == 0)

    def side_by_side(ref):
        return jnp.concatenate([ref[0:half], ref[half : 2 * half]], axis=1)

    def factor_of(pair):
        solved = dot(pair, weights_ref[0]) + dot(pair, weights_ref[1])
        return solved + dot(pair, weights_ref[2])

    def head_of(ref):
        solved = factor_of(jnp.concatenate([ref[0:size]] * 2, axis=1))[:, 0:size]
        solved = jnp.where(head == 1, lower_ref[...], solved)
        return jnp.where(head == 2, 0.0, solved).astype(BF16)

    @pl.when(mode == 0)
    def _():
        out_ref[...] = slab_ref[...]

    @pl.when(mode == 1)
    def _():
        factor = factor_of(side_by_side(slab_ref)).astype(BF16)
        out_ref[0:half] = factor[:, 0:size]
        out_ref[half : 2 * half] = factor[:, size : 2 * size]

        @pl.when(top)
        def _():
            out_ref[0:size] = head_of(slab_ref)

    for number, other_ref in enumerate(others):

        @pl.when((mode == 2) & (which == number))
        def _(other_ref=other_ref):
            factor = factor_of(side_by_side(other_ref)).astype(BF16)
            update = dot(factor, rows_ref[...])
            out_ref[0:half] = (slab_ref[0:half].astype(F32) - update[:, 0:size]).astype(BF16)
            out_ref[half : 2 * half] = (
                slab_ref[half : 2 * half].astype(F32) - update[:, size : 2 * size]
            ).astype(BF16)

            @pl.when(top)
            def _():
                begin = head_of(other_ref)
                update = dot(begin, rows_ref[0:size, 0:size])
                base = slab_ref[0:size].astype(F32)
                out_ref[0:size] = (base - update).astype(BF16)

                @pl.when(own == 1)
                def _():
                    out_ref[0:size] = (base + added_ref[...] - update).astype(BF16)


def panel(flags, lower, weights, rows, added, slab, others, old, start, tile):
    length, size = others[0].shape
    offset = start // tile

    def chosen(number):
        return lambda i, flags: (jnp.where(flags[3] == number, i, 0), 0)

    def fixed(rank):
        return lambda i, flags: (0,) * rank

    blocks = [
        pl.BlockSpec((size, size), fixed(2)),
        pl.BlockSpec(weights.shape, fixed(3)),
        pl.BlockSpec(rows.shape, fixed(2)),
        pl.BlockSpec((size, size), fixed(2)),
        pl.BlockSpec((tile, size), lambda i, flags: (i + offset, 0)),
    ] + [pl.BlockSpec((tile, size), chosen(number)) for number in range(len(others))]
    operands = [flags, lower, weights, rows, added, slab] + others
    aliases = {}
    if old is not None:
        aliases = {len(operands): 0}
        blocks.append(pl.BlockSpec(memory_space=pl.ANY))
        operands.append(old)
    return pl.pallas_call(
        functools.partial(panel_kernel, received=len(others), first=start == 0),
        grid_spec=pltpu.PrefetchScalarGridSpec(
            num_scalar_prefetch=1,
            grid=(length // tile,),
            in_specs=blocks,
            out_specs=pl.BlockSpec((tile, size), lambda i, flags: (i + offset, 0)),
        ),
        out_shape=jax.ShapeDtypeStruct(slab.shape, BF16),
        input_output_aliases=aliases,
        compiler_params=pltpu.CompilerParams(vmem_limit_bytes=32 * 2**20),
        cost_estimate=pl.CostEstimate(flops=8 * length * size * size, bytes_accessed=6 * length * size, transcendentals=0),
        name="panel",
    )(*operands)


def broadcast(value, axis, source):
    kept = jnp.where(lax.axis_index(axis) == source, value, 0).astype(value.dtype)
    return lax.psum(kept, axis)


def tied(value, *earlier):
    return lax.optimization_barrier((value, *earlier))[0]


def settings(*values):
    return jnp.stack([jnp.asarray(value).astype(jnp.int32) for value in values])


def holder_to_all(message, wide, narrow):
    stride = wide // narrow
    axes = ("wide", "narrow")

    def pairs(step, spread_out):
        found = []
        for n in range(narrow):
            for start in range(0, wide if spread_out else 1, 2):
                source = (n * stride) ^ start
                found.append((source * narrow + n, (source ^ step) * narrow + n))
        return found

    parts = [lax.ppermute(message, axes, pairs(step, False)) for step in range(2, wide, 2)]
    holds = lax.axis_index("wide") == lax.axis_index("narrow") * stride
    message = jnp.where(holds, message, sum(parts))
    other = lax.ppermute(message, axes, pairs(1, True))
    return [message, other]


def body(owner, coarse_basis, material_ids, lame_table, coarse_ids, coarse_slab):
    narrow, wide = lax.axis_size("narrow"), lax.axis_size("wide")
    static = isinstance(owner, int)
    stride = wide // narrow
    wide_index, narrow_index = lax.axis_index("wide"), lax.axis_index("narrow")
    height, block = coarse_slab.shape
    own = wide_index == narrow_index * stride
    later = narrow_index > owner
    mode = jnp.where(narrow_index == owner, 1, jnp.where(later, 2, 0))
    earlier = (wide_index % stride == 0) & (wide_index // stride < owner)
    kind = jnp.where(wide_index == owner * stride, 1, jnp.where(earlier, 2, 0))
    table = lame_table.astype(F32)

    first = halo_message(table, material_ids, coarse_basis)
    halo = lax.ppermute(first, "narrow", [(i + 1, i) for i in range(narrow - 1)])
    edge = tied((narrow_index == 0).astype(jnp.int32).reshape(1), first)
    inner = interior(edge, table, material_ids, coarse_basis)

    if static:
        units = UNITS[narrow - 1 - owner]
        which = jnp.where(later, narrow_index - owner - 1, -1)
        unit = height // sum(units)
        bounds, low, pieces = [], 0, []
        for number, count in enumerate(units):
            bounds.append((low, low + count * unit))
            low += count * unit
            moving = coarse_slab[bounds[-1][0] : bounds[-1][1]]
            if number == 1:
                moving = tied(moving, first)
            if number >= 2:
                moving = tied(moving, pieces[number - 2][0])
            hops = []
            for place in range(owner, narrow - 1):
                if place > owner and number == 0:
                    moving = tied(moving, inner)
                moving = lax.ppermute(moving, "narrow", [(place, place + 1)])
                hops.append(moving)
            pieces.append(hops)
    else:
        column = broadcast(coarse_slab, "narrow", owner)
        unit, bounds, pieces = height // 24, [(0, height)], [[column]]
        which = jnp.where(later, 0, -1)

    partial = face(table, material_ids, coarse_basis, halo, inner)
    if static:
        parts = [partial] + [
            lax.ppermute(partial, "narrow", [(n, owner)]) for n in range(narrow) if n != owner
        ]
    else:
        parts = [lax.psum(partial, "narrow")]
    galerkin, message = assemble(settings(which, mode), coarse_ids, coarse_slab, parts, pieces[0])
    if static:
        messages = holder_to_all(message, wide, narrow)
        summary, head = factorize(messages, galerkin)
        summaries = [summary]
        moving = summary
        for place in range(owner, narrow - 1):
            moving = lax.ppermute(moving, "narrow", [(place, place + 1)])
            summaries.append(moving)
        for place in range(owner):
            summaries.append(lax.ppermute(summary, "narrow", [(owner, place)]))
        choice = jnp.where(narrow_index >= owner, narrow_index - owner, narrow - owner + narrow_index)
    else:
        diagonal = broadcast(jnp.where(wide_index == owner * stride, message, 0.0), "narrow", owner)
        summary, _ = factorize([lax.psum(diagonal, "wide")], galerkin)
        head = broadcast(message, "wide", narrow_index * stride)
        summaries, choice = [summary], jnp.int32(0)

    weights, rows, lower, added, galerkin = prepare(settings(choice, mode, own), coarse_ids, head, summaries)
    flags = settings(mode, kind, own, which)
    result = None
    for (low, high), hops in zip(bounds, pieces):
        result = panel(flags, lower, weights, rows, added, coarse_slab, hops, result, low, 2 * unit)
    return result, galerkin


def on_device(coarse_basis, material_ids, lame_table, coarse_ids, coarse_slab, panel_owner):
    narrow, wide = lax.axis_size("narrow"), lax.axis_size("wide")
    arrays = (coarse_basis, material_ids, lame_table, coarse_ids, coarse_slab)
    owner = panel_owner[0]
    if narrow - 1 > len(UNITS) or wide % 2:
        return body(owner, *arrays)
    branches = [functools.partial(body, place) for place in range(narrow - 1)]
    return lax.switch(owner, branches, *arrays)


def solution(mesh):
    return jax.shard_map(
        on_device,
        mesh=mesh,
        in_specs=(
            P("wide", None, None, "narrow", None, None),
            P("wide", "narrow", None, None),
            P(),
            P("wide", None),
            P("wide", "narrow"),
            P(),
        ),
        out_specs=(P("wide", "narrow"), P("wide", None, None)),
        check_vma=False,
    )
```

```python
import functools

import jax
import jax.numpy as jnp
from jax import lax
from jax.experimental import pallas as pl
from jax.experimental.pallas import tpu as pltpu
from jax.sharding import PartitionSpec as P

F32, BF16 = jnp.float32, jnp.bfloat16
NT = (((1,), (1,)), ((), ()))
TN = (((0,), (0,)), ((), ()))
VMEM = pl.BlockSpec(memory_space=pltpu.VMEM)
ANY = pl.BlockSpec(memory_space=pl.ANY)
SMEM = pl.BlockSpec(memory_space=pltpu.SMEM)
UNITS = {1: (8, 8, 4, 4), 2: (6, 6, 6, 6), 3: (4, 4, 4, 4, 4, 4)}
BLOCK = 16
LIGHT = pl.CostEstimate(flops=1, bytes_accessed=1, transcendentals=0)


def exact_dot(left, right, dims=(((1,), (0,)), ((), ()))):
    return lax.dot_general(
        left, right, dims, precision=lax.Precision.HIGHEST, preferred_element_type=F32
    )


def dot(left, right, dims=(((1,), (0,)), ((), ()))):
    return lax.dot_general(left, right, dims, preferred_element_type=F32)


def split_two(value):
    high = value.astype(BF16)
    return high, (value - high.astype(F32)).astype(BF16)


def lame_of(ids, table_ref):
    shear = jnp.zeros(ids.shape, F32)
    dilate = jnp.zeros(ids.shape, F32)
    for material in range(table_ref.shape[1]):
        chosen = ids == material
        shear = jnp.where(chosen, table_ref[0, material], shear)
        dilate = jnp.where(chosen, table_ref[1, material], dilate)
    return shear, dilate


def halo_kernel(table_ref, ids_ref, basis_ref, out_ref):
    subs, funcs, comps = basis_ref.shape[0:3]
    for sub in range(subs):
        for comp in range(comps):
            out_ref[sub, comp * funcs : (comp + 1) * funcs] = basis_ref[sub, :, comp, 0]
        shear, dilate = lame_of(ids_ref[sub, 0], table_ref)
        out_ref[sub, comps * funcs] = shear.astype(BF16)
        out_ref[sub, comps * funcs + 1] = dilate.astype(BF16)


def halo_message(table, ids, basis):
    subs, funcs, comps, layers, ny, nz = basis.shape
    return pl.pallas_call(
        halo_kernel,
        in_specs=[SMEM, VMEM, VMEM],
        out_specs=VMEM,
        out_shape=jax.ShapeDtypeStruct((subs, comps * funcs + 2, ny, nz), BF16),
        compiler_params=pltpu.CompilerParams(vmem_limit_bytes=32 * 2**20),
        cost_estimate=LIGHT,
        name="halo_message",
    )(table, ids, basis)


def interior_kernel(edge_ref, table_ref, ids_ref, basis_ref, token_ref, out_ref, fields, turned, coef, left, right, acc, *, sub, lowest):
    comp = pl.program_id(0) + lowest
    layers, ny, nz = basis_ref.shape[3:]
    funcs = basis_ref.shape[1]
    row = lax.broadcasted_iota(jnp.int32, (ny, nz), 0)
    lane = lax.broadcasted_iota(jnp.int32, (ny, nz), 1)
    table = [lame_of(ids_ref[sub, x], table_ref) for x in range(layers)]

    def weight(one, two, direction):
        shear = 0.5 * (one[0] + two[0])
        dilate = 0.5 * (one[1] + two[1])
        return shear + jnp.where(comp == direction, shear + dilate, 0.0)

    def ahead(field, axis):
        size = field.shape[axis]
        index = row if axis == 0 else lane
        return jnp.where(index == size - 1, 0.0, pltpu.roll(field, size - 1, axis=axis))

    def behind(field, axis):
        index = row if axis == 0 else lane
        return jnp.where(index == 0, 0.0, pltpu.roll(field, 1, axis=axis))

    nothing = (jnp.zeros((ny, nz), F32),) * 2
    previous = weight(table[0], nothing, 0) * edge_ref[0].astype(F32)
    for x in range(layers):
        diagonal = previous
        forward = []
        if x + 1 < layers:
            face = weight(table[x], table[x + 1], 0)
            diagonal = diagonal + face
            previous = face
            forward.append(face)
        else:
            forward.append(jnp.zeros((ny, nz), F32))
        for axis in (0, 1):
            index, size = (row, ny) if axis == 0 else (lane, nz)
            other = tuple(ahead(value, axis) for value in table[x])
            face = weight(table[x], other, axis + 1)
            before = tuple(behind(value, axis) for value in table[x])
            diagonal = diagonal + face + weight(table[x], before, axis + 1)
            forward.append(jnp.where(index == size - 1, 0.0, face))
        coef[x, 0] = 0.5 * diagonal
        for kind in range(3):
            coef[x, kind + 1] = forward[kind]
        fields[x] = basis_ref[sub, :, comp, x].astype(F32).reshape(funcs * ny, nz)

    total = None
    for x in reversed(range(layers)):
        values = [fields[x, pl.ds(y, funcs, stride=ny), :] for y in range(ny)]
        for y in range(ny):
            value = values[y]
            turned[x % 2, y] = value
            image = coef[x, 0, y : y + 1, :] * value
            image = image - coef[x, 3, y : y + 1, :] * pltpu.roll(value, nz - 1, axis=1)
            if y + 1 < ny:
                image = image - coef[x, 2, y : y + 1, :] * values[y + 1]
            if x + 1 < layers:
                image = image - coef[x, 1, y : y + 1, :] * turned[(x + 1) % 2, y]
            high, low = split_two(image)
            left[:, y * nz : (y + 1) * nz] = value.astype(BF16)
            right[0:funcs, y * nz : (y + 1) * nz] = high
            right[funcs : 2 * funcs, y * nz : (y + 1) * nz] = low
        product = dot(right[...], left[...], NT)
        total = product if total is None else total + product

    @pl.when(comp == lowest)
    def _():
        acc[...] = total

    @pl.when(comp > lowest)
    def _():
        acc[...] += total

    @pl.when(comp == lowest + pl.num_programs(0) - 1)
    def _():
        out_ref[...] = acc[0:funcs] + acc[funcs : 2 * funcs]


def interior(edge, table, ids, basis, token, sub, low, high):
    subs, funcs, comps, layers, ny, nz = basis.shape
    return pl.pallas_call(
        functools.partial(interior_kernel, sub=sub, lowest=low),
        grid=(high - low,),
        in_specs=[SMEM, SMEM, VMEM, VMEM, ANY],
        out_specs=VMEM,
        out_shape=jax.ShapeDtypeStruct((funcs, funcs), F32),
        scratch_shapes=[
            pltpu.VMEM((layers, funcs * ny, nz), F32),
            pltpu.VMEM((2, ny, funcs, nz), F32),
            pltpu.VMEM((layers, 4, ny, nz), F32),
            pltpu.VMEM((funcs, ny * nz), BF16),
            pltpu.VMEM((2 * funcs, ny * nz), BF16),
            pltpu.VMEM((2 * funcs, funcs), F32),
        ],
        compiler_params=pltpu.CompilerParams(vmem_limit_bytes=32 * 2**20),
        cost_estimate=LIGHT,
        name="interior",
    )(edge, table, ids, basis, token)


def face_kernel(table_ref, ids_ref, basis_ref, halo_ref, token_ref, *rest, owners):
    inner_refs, (out_ref, mine, theirs, left, right) = rest[: len(owners)], rest[len(owners) :]
    subs, funcs, comps, layers, ny, nz = basis_ref.shape
    for sub in range(subs):
        shear, dilate = lame_of(ids_ref[sub, layers - 1], table_ref)
        shear = 0.5 * (shear + halo_ref[sub, comps * funcs].astype(F32))
        dilate = 0.5 * (dilate + halo_ref[sub, comps * funcs + 1].astype(F32))
        total = None
        for comp in range(comps):
            weight = shear + (shear + dilate) if comp == 0 else shear
            slot = (sub * comps + comp) % 2
            mine[slot] = basis_ref[sub, :, comp, layers - 1].astype(F32).reshape(funcs * ny, nz)
            theirs[slot] = halo_ref[sub, comp * funcs : (comp + 1) * funcs].astype(F32).reshape(funcs * ny, nz)
            for y in range(ny):
                here = mine[slot, pl.ds(y, funcs, stride=ny), :]
                there = theirs[slot, pl.ds(y, funcs, stride=ny), :]
                high, low = split_two(weight[y : y + 1, :] * (here - there))
                left[slot, 0:funcs, y * nz : (y + 1) * nz] = here.astype(BF16)
                left[slot, funcs : 2 * funcs, y * nz : (y + 1) * nz] = there.astype(BF16)
                right[slot, 0:funcs, y * nz : (y + 1) * nz] = high
                right[slot, funcs : 2 * funcs, y * nz : (y + 1) * nz] = low
            product = dot(right[slot], left[slot], NT)
            total = product if total is None else total + product
        total = total[:, 0:funcs] - total[:, funcs : 2 * funcs]
        half = 0.5 * (total[0:funcs] + total[funcs : 2 * funcs])
        for number, inner_ref in zip(owners, inner_refs):
            if number == sub:
                half = half + inner_ref[...]
        out_ref[sub] = half + half.T


def face(table, ids, basis, halo, token, inner, owners):
    subs, funcs, comps, layers, ny, nz = basis.shape
    return pl.pallas_call(
        functools.partial(face_kernel, owners=owners),
        in_specs=[SMEM] + [VMEM] * 3 + [ANY] + [VMEM] * len(inner),
        out_specs=VMEM,
        out_shape=jax.ShapeDtypeStruct((subs, funcs, funcs), F32),
        scratch_shapes=[
            pltpu.VMEM((2, funcs * ny, nz), F32),
            pltpu.VMEM((2, funcs * ny, nz), F32),
            pltpu.VMEM((2, 2 * funcs, ny * nz), BF16),
            pltpu.VMEM((2, 2 * funcs, ny * nz), BF16),
        ],
        compiler_params=pltpu.CompilerParams(vmem_limit_bytes=32 * 2**20),
        cost_estimate=LIGHT,
        name="face",
    )(table, ids, basis, halo, token, *inner)


def spread(gal_ref, column_ids_ref, row_ids_ref, size):
    subs, funcs = column_ids_ref.shape[0:2]
    added = jnp.zeros((size, size), F32)
    lane = lax.broadcasted_iota(jnp.int32, (funcs, size), 1)
    row = lax.broadcasted_iota(jnp.int32, (size, funcs), 0)
    for sub in range(subs):
        slots = (column_ids_ref[sub] == lane).astype(F32)
        slots_t = (row_ids_ref[sub] == row).astype(F32)
        added = added + exact_dot(slots_t, exact_dot(gal_ref[sub], slots))
    return added


def assemble_kernel(flags_ref, token_ref, column_ids_ref, row_ids_ref, slab_ref, *rest, heads):
    head_refs, gal_refs, (sum_ref, message_ref) = rest[:heads], rest[heads:-2], rest[-2:]
    size = message_ref.shape[0]
    mode, own, which = flags_ref[0], flags_ref[1], flags_ref[2]
    total = gal_refs[0][...]
    for gal_ref in gal_refs[1:]:
        total = total + gal_ref[...]
    sum_ref[...] = total

    message_ref[...] = jnp.zeros_like(message_ref)

    @pl.when((mode == 1) & (own == 1))
    def _():
        added = spread(sum_ref, column_ids_ref, row_ids_ref, size)
        message_ref[...] = added + slab_ref[...].astype(F32)

    for number, head_ref in enumerate(head_refs):

        @pl.when((mode == 2) & (own == 1) & (which == number))
        def _(head_ref=head_ref):
            message_ref[...] = head_ref[...].astype(F32)


def assemble(flags, token, ids, slab, heads, parts):
    size = slab.shape[1]
    block = pl.BlockSpec((size, size), lambda i: (0, 0))
    return pl.pallas_call(
        functools.partial(assemble_kernel, heads=len(heads)),
        grid=(1,),
        in_specs=[SMEM, ANY, VMEM, VMEM, block] + [block] * len(heads) + [VMEM] * len(parts),
        out_specs=[VMEM, VMEM],
        out_shape=[
            jax.ShapeDtypeStruct(parts[0].shape, F32),
            jax.ShapeDtypeStruct((size, size), F32),
        ],
        cost_estimate=LIGHT,
        name="assemble",
    )(flags, token, ids[:, :, None], ids[:, None, :], slab, *heads, *parts)


def factor_kernel(flags_ref, token_ref, *refs, parts):
    message_refs, gal_ref = refs[:parts], refs[parts]
    summary_ref, block_ref, work = refs[parts + 1 :]
    subs, funcs = gal_ref.shape[0:2]
    size = summary_ref.shape[1]
    rows = 2 * size
    diagonal = message_refs[0][...]
    for message_ref in message_refs[1:]:
        diagonal = diagonal + message_ref[...]
    block_ref[...] = diagonal

    @pl.when(flags_ref[0] == 1)
    def _():
        row = lax.broadcasted_iota(jnp.int32, (size, size), 0)
        lane = lax.broadcasted_iota(jnp.int32, (size, size), 1)
        work[:, 0:size] = 0.5 * (diagonal + diagonal.T)
        work[:, size : 2 * size] = (row == lane).astype(F32)
        index = lax.broadcasted_iota(jnp.int32, (BLOCK, size), 0)
        for start in range(0, size, BLOCK):
            panel = work[start : start + BLOCK, 0:size]
            extra = work[start : start + BLOCK, size : 2 * size]
            columns = [
                jnp.broadcast_to(panel[:, start + step : start + step + 1], (BLOCK, size))
                for step in range(BLOCK)
            ]
            for step in range(BLOCK):
                scale = lax.rsqrt(columns[step][step : step + 1, :])
                column = jnp.where(index > step, columns[step] * scale, 0.0)
                for later in range(step + 1, BLOCK):
                    columns[later] = columns[later] - column * column[later : later + 1, :]
                pivot = panel[step : step + 1, :] * scale
                panel = jnp.where(index == step, pivot, panel - column * pivot)
                pivot = extra[step : step + 1, :] * scale
                extra = jnp.where(index == step, pivot, extra - column * pivot)
            work[start : start + BLOCK, 0:size] = panel
            work[start : start + BLOCK, size : 2 * size] = extra
            rest = start + BLOCK
            if rest < size:
                both = jnp.concatenate([panel, extra], axis=1)
                work[rest:size, :] -= exact_dot(panel[:, rest:size], both, TN)
        upper = jnp.where(row <= lane, work[:, 0:size], 0.0)
        summary_ref[0:size] = jnp.where(row >= lane, work[:, size : 2 * size], 0.0).T
        summary_ref[size : 2 * size] = upper.T
        for sub in range(subs):
            begin = rows + sub * funcs
            summary_ref[begin : begin + funcs, 0:funcs] = gal_ref[sub]
            summary_ref[begin : begin + funcs, funcs:size] = jnp.zeros((funcs, size - funcs), F32)


def factorize(flags, token, messages, galerkin):
    size = messages[0].shape[1]
    subs, funcs = galerkin.shape[0:2]
    return pl.pallas_call(
        functools.partial(factor_kernel, parts=len(messages)),
        in_specs=[SMEM, ANY] + [VMEM] * (len(messages) + 1),
        out_specs=[VMEM] * 2,
        out_shape=[
            jax.ShapeDtypeStruct((2 * size + subs * funcs, size), F32),
            jax.ShapeDtypeStruct((size, size), F32),
        ],
        scratch_shapes=[pltpu.VMEM((size, 2 * size), F32)],
        cost_estimate=LIGHT,
        name="factorize",
    )(flags, token, *messages, galerkin)


def prepare_kernel(flags_ref, column_ids_ref, row_ids_ref, head_ref, *rest, sources):
    summary_refs = rest[:sources]
    weights_ref, rows_ref, lower_ref, added_ref, gal_ref, summary = rest[sources:]
    subs, funcs = gal_ref.shape[0:2]
    size = head_ref.shape[0]
    choice, mode, own = flags_ref[0], flags_ref[1], flags_ref[2]
    for number, summary_ref in enumerate(summary_refs):

        @pl.when(choice == number)
        def _(summary_ref=summary_ref):
            summary[...] = summary_ref[...]

    for sub in range(subs):
        begin = 2 * size + sub * funcs
        gal_ref[sub] = summary[begin : begin + funcs, 0:funcs]

    def doubled(block):
        nothing = jnp.zeros((size, size), BF16)
        top = jnp.concatenate([block, nothing], axis=1)
        return jnp.concatenate([top, jnp.concatenate([nothing, block], axis=1)], axis=0)

    @pl.when(mode > 0)
    def _():
        inverse = summary[0:size]
        high = inverse.astype(BF16)
        left = inverse - high.astype(F32)
        middle = left.astype(BF16)
        weights_ref[0] = doubled(high)
        weights_ref[1] = doubled(middle)
        weights_ref[2] = doubled((left - middle.astype(F32)).astype(BF16))
        lower_ref[...] = summary[size : 2 * size]

    @pl.when(mode == 2)
    def _():
        solved = exact_dot(head_ref[...], summary[0:size])
        rows_ref[...] = doubled(solved.T.astype(BF16))

    @pl.when((mode == 2) & (own == 1))
    def _():
        added_ref[...] = spread(gal_ref, column_ids_ref, row_ids_ref, size)


def prepare(flags, ids, head, summaries):
    size = head.shape[0]
    subs, funcs = ids.shape
    return pl.pallas_call(
        functools.partial(prepare_kernel, sources=len(summaries)),
        in_specs=[SMEM] + [VMEM] * (3 + len(summaries)),
        out_specs=[VMEM] * 5,
        out_shape=[
            jax.ShapeDtypeStruct((3, 2 * size, 2 * size), BF16),
            jax.ShapeDtypeStruct((2 * size, 2 * size), BF16),
            jax.ShapeDtypeStruct((size, size), F32),
            jax.ShapeDtypeStruct((size, size), F32),
            jax.ShapeDtypeStruct((subs, funcs, funcs), F32),
        ],
        scratch_shapes=[pltpu.VMEM(summaries[0].shape, F32)],
        compiler_params=pltpu.CompilerParams(vmem_limit_bytes=32 * 2**20),
        cost_estimate=LIGHT,
        name="prepare",
    )(flags, ids[:, :, None], ids[:, None, :], head, *summaries)


def panel_kernel(
    flags_ref, lower_ref, weights_ref, rows_ref, added_ref, slab_ref, *rest, pieces, spans, first
):
    hops = len(pieces) // len(spans)
    others = rest[: len(pieces)]
    out_ref, column, sems = rest[-3:]
    tile, size = out_ref.shape
    half = tile // 2
    mode, head, own, which = flags_ref[0], flags_ref[1], flags_ref[2], flags_ref[3]
    step, steps = pl.program_id(0), pl.num_programs(0)
    top = first & (step == 0)

    def copy_of(at, act):
        for number, (begin, end) in enumerate(spans):
            for hop in range(hops):

                @pl.when((mode == 2) & (which == hop) & (at >= begin) & (at < end))
                def _(other_ref=others[number * hops + hop], begin=begin):
                    source = other_ref.at[pl.ds(pl.multiple_of((at - begin) * tile, tile), tile)]
                    act(pltpu.make_async_copy(source, column.at[at % 2], sems.at[at % 2]))

    @pl.when(step == 0)
    def _():
        copy_of(step, lambda copy: copy.start())

    @pl.when(step + 1 < steps)
    def _():
        copy_of(step + 1, lambda copy: copy.start())

    def side_by_side(value):
        return jnp.concatenate([value[0:half], value[half:tile]], axis=1)

    def factor_of(pair):
        solved = dot(pair, weights_ref[0]) + dot(pair, weights_ref[1])
        return solved + dot(pair, weights_ref[2])

    def head_of(value):
        solved = factor_of(jnp.concatenate([value] * 2, axis=1))[:, 0:size]
        solved = jnp.where(head == 1, lower_ref[...], solved)
        return jnp.where(head == 2, 0.0, solved).astype(BF16)

    @pl.when(mode == 0)
    def _():
        out_ref[...] = slab_ref[...]

    @pl.when(mode == 1)
    def _():
        factor = factor_of(side_by_side(slab_ref[...])).astype(BF16)
        out_ref[0:half] = factor[:, 0:size]
        out_ref[half:tile] = factor[:, size : 2 * size]

        @pl.when(top)
        def _():
            out_ref[0:size] = head_of(slab_ref[0:size])

    @pl.when(mode == 2)
    def _():
        copy_of(step, lambda copy: copy.wait())
        factor = factor_of(side_by_side(column[step % 2])).astype(BF16)
        update = dot(factor, rows_ref[...])
        out_ref[0:half] = (slab_ref[0:half].astype(F32) - update[:, 0:size]).astype(BF16)
        out_ref[half:tile] = (slab_ref[half:tile].astype(F32) - update[:, size : 2 * size]).astype(BF16)

        @pl.when(top)
        def _():
            begin = head_of(column[0, 0:size])
            update = dot(begin, rows_ref[0:size, 0:size])
            base = slab_ref[0:size].astype(F32)
            out_ref[0:size] = (base - update).astype(BF16)

            @pl.when(own == 1)
            def _():
                out_ref[0:size] = (base + added_ref[...] - update).astype(BF16)


def panel(flags, lower, weights, rows, added, slab, parts, old, start, tile):
    size = slab.shape[1]
    offset = start // tile
    spans, begin, operands = [], 0, []
    for hops in parts:
        end = begin + hops[0].shape[0] // tile
        spans.append((begin, end))
        begin = end
        operands += hops
    blocks = [
        SMEM,
        pl.BlockSpec((size, size), lambda i: (0, 0)),
        pl.BlockSpec(weights.shape, lambda i: (0, 0, 0)),
        pl.BlockSpec(rows.shape, lambda i: (0, 0)),
        pl.BlockSpec((size, size), lambda i: (0, 0)),
        pl.BlockSpec((tile, size), lambda i: (i + offset, 0)),
    ] + [ANY] * len(operands)
    pieces = len(operands)
    operands = [flags, lower, weights, rows, added, slab] + operands
    aliases = {}
    if old is not None:
        aliases = {len(operands): 0}
        blocks.append(ANY)
        operands.append(old)
    return pl.pallas_call(
        functools.partial(panel_kernel, pieces=range(pieces), spans=spans, first=start == 0),
        grid=(begin,),
        in_specs=blocks,
        out_specs=pl.BlockSpec((tile, size), lambda i: (i + offset, 0)),
        out_shape=jax.ShapeDtypeStruct(slab.shape, BF16),
        input_output_aliases=aliases,
        scratch_shapes=[pltpu.VMEM((2, tile, size), BF16), pltpu.SemaphoreType.DMA((2,))],
        compiler_params=pltpu.CompilerParams(vmem_limit_bytes=32 * 2**20),
        cost_estimate=LIGHT,
        name="panel",
    )(*operands)


def broadcast(value, axis, source):
    kept = jnp.where(lax.axis_index(axis) == source, value, 0).astype(value.dtype)
    return lax.psum(kept, axis)


def tied(value, *earlier):
    return lax.optimization_barrier((value, *earlier))[0]


def settings(*values):
    return jnp.stack([jnp.asarray(value).astype(jnp.int32) for value in values])


def holder_pairs(wide, narrow, distance):
    stride = wide // narrow
    found = []
    for n in range(narrow):
        for start in range(0, wide, 2 * distance):
            source = (n * stride) ^ start
            found.append((source * narrow + n, (source ^ distance) * narrow + n))
    return found


class Order:
    def __init__(self, value):
        self.last = value

    def gate(self, value):
        return lax.optimization_barrier((value, self.last))[0]


def known_owner(owner, coarse_basis, material_ids, lame_table, coarse_ids, coarse_slab):
    narrow, wide = lax.axis_size("narrow"), lax.axis_size("wide")
    stride = wide // narrow
    wide_index, narrow_index = lax.axis_index("wide"), lax.axis_index("narrow")
    height, block = coarse_slab.shape
    own = wide_index == narrow_index * stride
    later = narrow_index > owner
    which = jnp.where(later, narrow_index - owner - 1, -1)
    mode = jnp.where(narrow_index == owner, 1, jnp.where(later, 2, 0))
    earlier = (wide_index % stride == 0) & (wide_index // stride < owner)
    kind = jnp.where(wide_index == owner * stride, 1, jnp.where(earlier, 2, 0))
    table = lame_table.astype(F32)
    hops = narrow - 1 - owner
    units = UNITS[hops]
    unit = height // sum(units)
    count = len(units)
    bounds, low = [], 0
    for number in units:
        bounds.append((low, low + number * unit))
        low += number * unit

    def hop(value, place):
        return lax.ppermute(value, "narrow", [(place, place + 1)])

    def rows_of(number):
        low, high = bounds[number]
        return coarse_slab[low:high]

    pieces = [[hop(rows_of(0), owner)]]
    first = halo_message(table, material_ids, coarse_basis)
    halo = lax.ppermute(first, "narrow", [(i + 1, i) for i in range(narrow - 1)])
    order = Order(first)
    axes = ("wide", "narrow")
    edge = (narrow_index == 0).astype(jnp.int32).reshape(1)
    inner, owners, found = [], [], {}

    def nearest(base, extent):
        return min(range(base, min(base + extent, narrow)), key=lambda n: abs(n - owner))

    def arrive(number, place):
        moving = order.gate(pieces[number][place])
        order.last = moving
        if place + 1 < hops:
            pieces[number].append(hop(moving, owner + place + 1))
        if place == 0 and number + 2 < count - 1:
            pieces.append([hop(order.gate(rows_of(number + 2)), owner)])

    def interior_step(sub, low, high):
        inner.append(interior(edge, table, material_ids, coarse_basis, order.last, sub, low, high))
        owners.append(sub)
        order.last = inner[-1]
        if len(pieces) == 1:
            pieces.append([hop(order.gate(rows_of(1)), owner)])

    def face_step():
        found["partial"] = face(table, material_ids, coarse_basis, halo, order.last, inner, owners)
        order.last = found["partial"]
        total, distance = found["partial"], 1
        while True:
            pairs = []
            for n in range(narrow):
                base = n // (2 * distance) * 2 * distance
                one, two = nearest(base, distance), nearest(base + distance, distance)
                if n == base and base + distance < narrow:
                    pairs.append((two, one) if nearest(base, 2 * distance) == one else (one, two))
            received = lax.ppermute(total, "narrow", pairs)
            distance *= 2
            if distance >= narrow:
                break
            total = total + received
        found["sums"] = [total, received]

    def assemble_step():
        found["galerkin"], found["message"] = assemble(
            settings(mode, own, which), order.last, coarse_ids, coarse_slab, pieces[0], found["sums"]
        )
        order.last = found["message"]

    def spread_step(distance):
        message = found["message"]
        pairs = holder_pairs(wide, narrow, distance)
        received = lax.ppermute(order.gate(message), axes, pairs)
        if distance > 1:
            found["message"] = message + received
            order.last = found["message"]
        else:
            found["messages"] = [message, received]

    def factor_step():
        summary, found["head"] = factorize(
            settings(mode), order.last, found["messages"], found["galerkin"]
        )
        order.last = summary
        found["summaries"] = [summary, hop(summary, owner)]
        pieces.append([hop(tied(rows_of(count - 1), summary), owner)])
        for place in range(owner):
            found["summaries"].append(lax.ppermute(summary, "narrow", [(owner, place)]))

    def pass_summary(place):
        moving = order.gate(found["summaries"][place + 1])
        found["summaries"].insert(place + 2, hop(moving, owner + place + 1))
        order.last = moving

    rate = 2.62
    comps = coarse_basis.shape[2]
    steps = [(7.0, functools.partial(interior_step, 0, 0, 1)), (8.0, functools.partial(interior_step, 0, 1, comps))]
    steps += [(9.0, functools.partial(interior_step, sub, 0, comps)) for sub in range(1, coarse_basis.shape[0])]
    steps += [(32.5, face_step), (40.0, assemble_step)]
    distance, late = wide // 2, 45.0
    while distance:
        steps.append((late, functools.partial(spread_step, distance)))
        distance, late = distance // 2, late + 3.0
    steps.append((late, factor_step))
    waves = [8.0 + rate * sum(units[: number + 1]) for number in range(count)]
    waves[-1] = max(waves[-1], late + 10.0)
    for place in range(1, hops):
        waves.append(waves[-1] + max(units) * rate)
    for number in range(count):
        for place in range(hops):
            steps.append((waves[number + place] + 0.1 * place, functools.partial(arrive, number, place)))
    for place in range(hops - 1):
        steps.append((max(waves[count - 2], late) + 5.0 * (place + 1), functools.partial(pass_summary, place)))
    for _, step in sorted(steps, key=lambda item: item[0]):
        step()

    choice = jnp.where(narrow_index >= owner, narrow_index - owner, narrow - owner + narrow_index)
    weights, rows, lower, added, galerkin = prepare(
        settings(choice, mode, own), coarse_ids, found["head"], found["summaries"]
    )
    flags = settings(mode, kind, own, which)
    result = None
    for begin, end in ((0, count - 2), (count - 2, count - 1), (count - 1, count)):
        result = panel(
            flags, lower, weights, rows, added, coarse_slab, pieces[begin:end], result, bounds[begin][0], 2 * unit
        )
    return result, galerkin


def any_owner(owner, coarse_basis, material_ids, lame_table, coarse_ids, coarse_slab):
    narrow, wide = lax.axis_size("narrow"), lax.axis_size("wide")
    stride = wide // narrow
    wide_index, narrow_index = lax.axis_index("wide"), lax.axis_index("narrow")
    own = wide_index == narrow_index * stride
    later = narrow_index > owner
    which = jnp.where(later, 0, -1)
    mode = jnp.where(narrow_index == owner, 1, jnp.where(later, 2, 0))
    earlier = (wide_index % stride == 0) & (wide_index // stride < owner)
    kind = jnp.where(wide_index == owner * stride, 1, jnp.where(earlier, 2, 0))
    table = lame_table.astype(F32)
    column = broadcast(coarse_slab, "narrow", owner)
    first = halo_message(table, material_ids, coarse_basis)
    halo = lax.ppermute(first, "narrow", [(i + 1, i) for i in range(narrow - 1)])
    edge = (narrow_index == 0).astype(jnp.int32).reshape(1)
    subs, comps = coarse_basis.shape[0], coarse_basis.shape[2]
    inner = [interior(edge, table, material_ids, coarse_basis, first, sub, 0, comps) for sub in range(subs)]
    partial = face(table, material_ids, coarse_basis, halo, first, inner, list(range(subs)))
    parts = [lax.psum(partial, "narrow")]
    galerkin, message = assemble(settings(mode, own, which), first, coarse_ids, coarse_slab, [column], parts)
    at_owner = (wide_index == owner * stride) & (narrow_index == owner)
    diagonal = lax.psum(jnp.where(at_owner, message, 0.0), ("wide", "narrow"))
    summary, _ = factorize(settings(1), first, [diagonal], galerkin)
    head = broadcast(message, "wide", narrow_index * stride)
    weights, rows, lower, added, galerkin = prepare(settings(0, mode, own), coarse_ids, head, [summary])
    flags = settings(mode, kind, own, which)
    tile = coarse_slab.shape[0] // 12
    result = panel(flags, lower, weights, rows, added, coarse_slab, [[column]], None, 0, tile)
    return result, galerkin


def on_device(coarse_basis, material_ids, lame_table, coarse_ids, coarse_slab, panel_owner):
    narrow, wide = lax.axis_size("narrow"), lax.axis_size("wide")
    arrays = (coarse_basis, material_ids, lame_table, coarse_ids, coarse_slab)
    owner = panel_owner[0]
    if narrow - 1 > len(UNITS) or wide & (wide - 1):
        return any_owner(owner, *arrays)
    branches = [functools.partial(known_owner, place) for place in range(narrow - 1)]
    return lax.switch(owner, branches, *arrays)


def solution(mesh):
    return jax.shard_map(
        on_device,
        mesh=mesh,
        in_specs=(
            P("wide", None, None, "narrow", None, None),
            P("wide", "narrow", None, None),
            P(),
            P("wide", None),
            P("wide", "narrow"),
            P(),
        ),
        out_specs=(P("wide", "narrow"), P("wide", None, None)),
        check_vma=False,
    )
```

```python
import functools

import jax
import jax.numpy as jnp
from jax import lax
from jax.experimental import pallas as pl
from jax.experimental.pallas import tpu as pltpu
from jax.sharding import PartitionSpec as P

F32, BF16 = jnp.float32, jnp.bfloat16
NT = (((1,), (1,)), ((), ()))
TN = (((0,), (0,)), ((), ()))
VMEM = pl.BlockSpec(memory_space=pltpu.VMEM)
ANY = pl.BlockSpec(memory_space=pl.ANY)
SMEM = pl.BlockSpec(memory_space=pltpu.SMEM)
PLANS = {
    1: ((14, 8, 2), ("assemble", "spread", "factor")),
    2: (
        (8, 6, 4, 4, 2),
        ((0, 0), "assemble", (1, 0), "spread", (2, 0), "factor", ("s", 0), (3, 0), (4, 0)),
    ),
    3: (
        (8, 6, 4, 4, 2),
        (
            (0, 0), "assemble", (1, 0), "spread", (2, 0), "factor", (0, 1), (1, 1), ("s", 0), (3, 0), (2, 1),
            ("s", 1), (4, 0), (3, 1), (4, 1),
        ),
    ),
}
BLOCK = 16
LIGHT = pl.CostEstimate(flops=1, bytes_accessed=1, transcendentals=0)


def exact_dot(left, right, dims=(((1,), (0,)), ((), ()))):
    return lax.dot_general(
        left, right, dims, precision=lax.Precision.HIGHEST, preferred_element_type=F32
    )


def dot(left, right, dims=(((1,), (0,)), ((), ()))):
    return lax.dot_general(left, right, dims, preferred_element_type=F32)


def split_two(value):
    high = value.astype(BF16)
    return high, (value - high.astype(F32)).astype(BF16)


def lame_of(ids, table_ref):
    shear = jnp.zeros(ids.shape, F32)
    dilate = jnp.zeros(ids.shape, F32)
    for material in range(table_ref.shape[1]):
        chosen = ids == material
        shear = jnp.where(chosen, table_ref[0, material], shear)
        dilate = jnp.where(chosen, table_ref[1, material], dilate)
    return shear, dilate


def halo_kernel(table_ref, ids_ref, basis_ref, out_ref):
    subs, funcs, comps = basis_ref.shape[0:3]
    for sub in range(subs):
        for comp in range(comps):
            out_ref[sub, comp * funcs : (comp + 1) * funcs] = basis_ref[sub, :, comp, 0]
        shear, dilate = lame_of(ids_ref[sub, 0], table_ref)
        out_ref[sub, comps * funcs] = shear.astype(BF16)
        out_ref[sub, comps * funcs + 1] = dilate.astype(BF16)


def halo_message(table, ids, basis):
    subs, funcs, comps, layers, ny, nz = basis.shape
    return pl.pallas_call(
        halo_kernel,
        in_specs=[SMEM, VMEM, VMEM],
        out_specs=VMEM,
        out_shape=jax.ShapeDtypeStruct((subs, comps * funcs + 2, ny, nz), BF16),
        compiler_params=pltpu.CompilerParams(vmem_limit_bytes=32 * 2**20),
        cost_estimate=LIGHT,
        name="halo_message",
    )(table, ids, basis)


def interior_kernel(edge_ref, table_ref, ids_ref, basis_ref, token_ref, out_ref, fields, turned, coef, left, right, acc):
    sub, comp = pl.program_id(0), pl.program_id(1)
    layers, ny, nz = basis_ref.shape[3:]
    funcs = basis_ref.shape[1]
    row = lax.broadcasted_iota(jnp.int32, (ny, nz), 0)
    lane = lax.broadcasted_iota(jnp.int32, (ny, nz), 1)
    table = [lame_of(ids_ref[sub, x], table_ref) for x in range(layers)]

    def weight(one, two, direction):
        shear = 0.5 * (one[0] + two[0])
        dilate = 0.5 * (one[1] + two[1])
        return shear + jnp.where(comp == direction, shear + dilate, 0.0)

    def ahead(field, axis):
        size = field.shape[axis]
        index = row if axis == 0 else lane
        return jnp.where(index == size - 1, 0.0, pltpu.roll(field, size - 1, axis=axis))

    def behind(field, axis):
        index = row if axis == 0 else lane
        return jnp.where(index == 0, 0.0, pltpu.roll(field, 1, axis=axis))

    nothing = (jnp.zeros((ny, nz), F32),) * 2
    previous = weight(table[0], nothing, 0) * edge_ref[0].astype(F32)
    for x in range(layers):
        diagonal = previous
        forward = []
        if x + 1 < layers:
            face = weight(table[x], table[x + 1], 0)
            diagonal = diagonal + face
            previous = face
            forward.append(face)
        else:
            forward.append(jnp.zeros((ny, nz), F32))
        for axis in (0, 1):
            index, size = (row, ny) if axis == 0 else (lane, nz)
            other = tuple(ahead(value, axis) for value in table[x])
            face = weight(table[x], other, axis + 1)
            before = tuple(behind(value, axis) for value in table[x])
            diagonal = diagonal + face + weight(table[x], before, axis + 1)
            forward.append(jnp.where(index == size - 1, 0.0, face))
        coef[x, 0] = 0.5 * diagonal
        for kind in range(3):
            coef[x, kind + 1] = forward[kind]
        fields[x] = basis_ref[sub, :, comp, x].astype(F32).reshape(funcs * ny, nz)

    total = None
    for x in reversed(range(layers)):
        values = [fields[x, pl.ds(y, funcs, stride=ny), :] for y in range(ny)]
        for y in range(ny):
            value = values[y]
            turned[x % 2, y] = value
            image = coef[x, 0, y : y + 1, :] * value
            image = image - coef[x, 3, y : y + 1, :] * pltpu.roll(value, nz - 1, axis=1)
            if y + 1 < ny:
                image = image - coef[x, 2, y : y + 1, :] * values[y + 1]
            if x + 1 < layers:
                image = image - coef[x, 1, y : y + 1, :] * turned[(x + 1) % 2, y]
            high, low = split_two(image)
            left[:, y * nz : (y + 1) * nz] = value.astype(BF16)
            right[0:funcs, y * nz : (y + 1) * nz] = high
            right[funcs : 2 * funcs, y * nz : (y + 1) * nz] = low
        product = dot(right[...], left[...], NT)
        total = product if total is None else total + product

    @pl.when(comp == 0)
    def _():
        acc[...] = total

    @pl.when(comp > 0)
    def _():
        acc[...] += total

    @pl.when(comp == pl.num_programs(1) - 1)
    def _():
        out_ref[0] = acc[0:funcs] + acc[funcs : 2 * funcs]


def interior(edge, table, ids, basis, token):
    subs, funcs, comps, layers, ny, nz = basis.shape
    return pl.pallas_call(
        interior_kernel,
        grid=(subs, comps),
        in_specs=[SMEM, SMEM, VMEM, VMEM, ANY],
        out_specs=pl.BlockSpec((1, funcs, funcs), lambda s, c: (s, 0, 0)),
        out_shape=jax.ShapeDtypeStruct((subs, funcs, funcs), F32),
        scratch_shapes=[
            pltpu.VMEM((layers, funcs * ny, nz), F32),
            pltpu.VMEM((2, ny, funcs, nz), F32),
            pltpu.VMEM((layers, 4, ny, nz), F32),
            pltpu.VMEM((funcs, ny * nz), BF16),
            pltpu.VMEM((2 * funcs, ny * nz), BF16),
            pltpu.VMEM((2 * funcs, funcs), F32),
        ],
        compiler_params=pltpu.CompilerParams(vmem_limit_bytes=32 * 2**20),
        cost_estimate=LIGHT,
        name="interior",
    )(edge, table, ids, basis, token)


def face_kernel(table_ref, ids_ref, basis_ref, halo_ref, token_ref, inner_ref, out_ref, mine, theirs, left, right):
    subs, funcs, comps, layers, ny, nz = basis_ref.shape
    for sub in range(subs):
        shear, dilate = lame_of(ids_ref[sub, layers - 1], table_ref)
        shear = 0.5 * (shear + halo_ref[sub, comps * funcs].astype(F32))
        dilate = 0.5 * (dilate + halo_ref[sub, comps * funcs + 1].astype(F32))
        total = None
        for comp in range(comps):
            weight = shear + (shear + dilate) if comp == 0 else shear
            slot = (sub * comps + comp) % 2
            mine[slot] = basis_ref[sub, :, comp, layers - 1].astype(F32).reshape(funcs * ny, nz)
            theirs[slot] = halo_ref[sub, comp * funcs : (comp + 1) * funcs].astype(F32).reshape(funcs * ny, nz)
            for y in range(ny):
                here = mine[slot, pl.ds(y, funcs, stride=ny), :]
                there = theirs[slot, pl.ds(y, funcs, stride=ny), :]
                high, low = split_two(weight[y : y + 1, :] * (here - there))
                left[slot, 0:funcs, y * nz : (y + 1) * nz] = here.astype(BF16)
                left[slot, funcs : 2 * funcs, y * nz : (y + 1) * nz] = there.astype(BF16)
                right[slot, 0:funcs, y * nz : (y + 1) * nz] = high
                right[slot, funcs : 2 * funcs, y * nz : (y + 1) * nz] = low
            product = dot(right[slot], left[slot], NT)
            total = product if total is None else total + product
        total = total[:, 0:funcs] - total[:, funcs : 2 * funcs]
        half = inner_ref[sub] + 0.5 * (total[0:funcs] + total[funcs : 2 * funcs])
        out_ref[sub] = half + half.T


def face(table, ids, basis, halo, token, inner):
    subs, funcs, comps, layers, ny, nz = basis.shape
    return pl.pallas_call(
        face_kernel,
        in_specs=[SMEM] + [VMEM] * 3 + [ANY, VMEM],
        out_specs=VMEM,
        out_shape=jax.ShapeDtypeStruct((subs, funcs, funcs), F32),
        scratch_shapes=[
            pltpu.VMEM((2, funcs * ny, nz), F32),
            pltpu.VMEM((2, funcs * ny, nz), F32),
            pltpu.VMEM((2, 2 * funcs, ny * nz), BF16),
            pltpu.VMEM((2, 2 * funcs, ny * nz), BF16),
        ],
        compiler_params=pltpu.CompilerParams(vmem_limit_bytes=32 * 2**20),
        cost_estimate=LIGHT,
        name="face",
    )(table, ids, basis, halo, token, inner)


def spread(gal_ref, column_ids_ref, row_ids_ref, size):
    subs, funcs = column_ids_ref.shape[0:2]
    added = jnp.zeros((size, size), F32)
    lane = lax.broadcasted_iota(jnp.int32, (funcs, size), 1)
    row = lax.broadcasted_iota(jnp.int32, (size, funcs), 0)
    for sub in range(subs):
        slots = (column_ids_ref[sub] == lane).astype(F32)
        slots_t = (row_ids_ref[sub] == row).astype(F32)
        added = added + exact_dot(slots_t, exact_dot(gal_ref[sub], slots))
    return added


def assemble_kernel(flags_ref, token_ref, column_ids_ref, row_ids_ref, slab_ref, head_ref, *rest):
    gal_refs, (sum_ref, message_ref) = rest[:-2], rest[-2:]
    size = message_ref.shape[0]
    mode, own = flags_ref[0], flags_ref[1]
    total = gal_refs[0][...]
    for gal_ref in gal_refs[1:]:
        total = total + gal_ref[...]
    sum_ref[...] = total

    message_ref[...] = jnp.zeros_like(message_ref)

    @pl.when((mode == 1) & (own == 1))
    def _():
        added = spread(sum_ref, column_ids_ref, row_ids_ref, size)
        message_ref[...] = added + slab_ref[...].astype(F32)

    @pl.when((mode == 2) & (own == 1))
    def _():
        message_ref[...] = head_ref[...].astype(F32)


def assemble(flags, token, ids, slab, head, parts):
    size = slab.shape[1]
    block = pl.BlockSpec((size, size), lambda i: (0, 0))
    return pl.pallas_call(
        assemble_kernel,
        grid=(1,),
        in_specs=[SMEM, ANY, VMEM, VMEM, block, block] + [VMEM] * len(parts),
        out_specs=[VMEM, VMEM],
        out_shape=[
            jax.ShapeDtypeStruct(parts[0].shape, F32),
            jax.ShapeDtypeStruct((size, size), F32),
        ],
        cost_estimate=LIGHT,
        name="assemble",
    )(flags, token, ids[:, :, None], ids[:, None, :], slab, head, *parts)


def factor_kernel(flags_ref, token_ref, *refs, parts):
    message_refs, gal_ref = refs[:parts], refs[parts]
    summary_ref, block_ref, work = refs[parts + 1 :]
    subs, funcs = gal_ref.shape[0:2]
    size = summary_ref.shape[1]
    rows = 2 * size
    diagonal = message_refs[0][...]
    for message_ref in message_refs[1:]:
        diagonal = diagonal + message_ref[...]
    block_ref[...] = diagonal

    @pl.when(flags_ref[0] == 1)
    def _():
        row = lax.broadcasted_iota(jnp.int32, (size, size), 0)
        lane = lax.broadcasted_iota(jnp.int32, (size, size), 1)
        work[:, 0:size] = 0.5 * (diagonal + diagonal.T)
        work[:, size : 2 * size] = (row == lane).astype(F32)
        index = lax.broadcasted_iota(jnp.int32, (BLOCK, size), 0)
        for start in range(0, size, BLOCK):
            panel = work[start : start + BLOCK, 0:size]
            extra = work[start : start + BLOCK, size : 2 * size]
            columns = [
                jnp.broadcast_to(panel[:, start + step : start + step + 1], (BLOCK, size))
                for step in range(BLOCK)
            ]
            for step in range(BLOCK):
                scale = lax.rsqrt(columns[step][step : step + 1, :])
                column = jnp.where(index > step, columns[step] * scale, 0.0)
                for later in range(step + 1, BLOCK):
                    columns[later] = columns[later] - column * column[later : later + 1, :]
                pivot = panel[step : step + 1, :] * scale
                panel = jnp.where(index == step, pivot, panel - column * pivot)
                pivot = extra[step : step + 1, :] * scale
                extra = jnp.where(index == step, pivot, extra - column * pivot)
            work[start : start + BLOCK, 0:size] = panel
            work[start : start + BLOCK, size : 2 * size] = extra
            rest = start + BLOCK
            if rest < size:
                both = jnp.concatenate([panel, extra], axis=1)
                work[rest:size, :] -= exact_dot(panel[:, rest:size], both, TN)
        upper = jnp.where(row <= lane, work[:, 0:size], 0.0)
        summary_ref[0:size] = jnp.where(row >= lane, work[:, size : 2 * size], 0.0).T
        summary_ref[size : 2 * size] = upper.T
        for sub in range(subs):
            begin = rows + sub * funcs
            summary_ref[begin : begin + funcs, 0:funcs] = gal_ref[sub]
            summary_ref[begin : begin + funcs, funcs:size] = jnp.zeros((funcs, size - funcs), F32)


def factorize(flags, token, messages, galerkin):
    size = messages[0].shape[1]
    subs, funcs = galerkin.shape[0:2]
    return pl.pallas_call(
        functools.partial(factor_kernel, parts=len(messages)),
        in_specs=[SMEM, ANY] + [VMEM] * (len(messages) + 1),
        out_specs=[VMEM] * 2,
        out_shape=[
            jax.ShapeDtypeStruct((2 * size + subs * funcs, size), F32),
            jax.ShapeDtypeStruct((size, size), F32),
        ],
        scratch_shapes=[pltpu.VMEM((size, 2 * size), F32)],
        cost_estimate=LIGHT,
        name="factorize",
    )(flags, token, *messages, galerkin)


def prepare_kernel(flags_ref, column_ids_ref, row_ids_ref, head_ref, *rest, sources):
    summary_refs = rest[:sources]
    weights_ref, rows_ref, lower_ref, added_ref, gal_ref, summary = rest[sources:]
    subs, funcs = gal_ref.shape[0:2]
    size = head_ref.shape[0]
    choice, mode, own = flags_ref[0], flags_ref[1], flags_ref[2]
    for number, summary_ref in enumerate(summary_refs):

        @pl.when(choice == number)
        def _(summary_ref=summary_ref):
            summary[...] = summary_ref[...]

    for sub in range(subs):
        begin = 2 * size + sub * funcs
        gal_ref[sub] = summary[begin : begin + funcs, 0:funcs]

    def doubled(block):
        nothing = jnp.zeros((size, size), BF16)
        top = jnp.concatenate([block, nothing], axis=1)
        return jnp.concatenate([top, jnp.concatenate([nothing, block], axis=1)], axis=0)

    @pl.when(mode > 0)
    def _():
        inverse = summary[0:size]
        high = inverse.astype(BF16)
        left = inverse - high.astype(F32)
        middle = left.astype(BF16)
        weights_ref[0] = doubled(high)
        weights_ref[1] = doubled(middle)
        weights_ref[2] = doubled((left - middle.astype(F32)).astype(BF16))
        lower_ref[...] = summary[size : 2 * size]

    @pl.when(mode == 2)
    def _():
        solved = exact_dot(head_ref[...], summary[0:size])
        rows_ref[...] = doubled(solved.T.astype(BF16))

    @pl.when((mode == 2) & (own == 1))
    def _():
        added_ref[...] = spread(gal_ref, column_ids_ref, row_ids_ref, size)


def prepare(flags, ids, head, summaries):
    size = head.shape[0]
    subs, funcs = ids.shape
    return pl.pallas_call(
        functools.partial(prepare_kernel, sources=len(summaries)),
        in_specs=[SMEM] + [VMEM] * (3 + len(summaries)),
        out_specs=[VMEM] * 5,
        out_shape=[
            jax.ShapeDtypeStruct((3, 2 * size, 2 * size), BF16),
            jax.ShapeDtypeStruct((2 * size, 2 * size), BF16),
            jax.ShapeDtypeStruct((size, size), F32),
            jax.ShapeDtypeStruct((size, size), F32),
            jax.ShapeDtypeStruct((subs, funcs, funcs), F32),
        ],
        scratch_shapes=[pltpu.VMEM(summaries[0].shape, F32)],
        compiler_params=pltpu.CompilerParams(vmem_limit_bytes=32 * 2**20),
        cost_estimate=LIGHT,
        name="prepare",
    )(flags, ids[:, :, None], ids[:, None, :], head, *summaries)


def panel_kernel(
    flags_ref, lower_ref, weights_ref, rows_ref, added_ref, slab_ref, *rest, pieces, spans, first
):
    hops = len(pieces) // len(spans)
    others = rest[: len(pieces)]
    out_ref, column, sems = rest[-3:]
    tile, size = out_ref.shape
    half = tile // 2
    mode, head, own, which = flags_ref[0], flags_ref[1], flags_ref[2], flags_ref[3]
    step, steps = pl.program_id(0), pl.num_programs(0)
    top = first & (step == 0)

    def copy_of(at, act):
        for number, (begin, end) in enumerate(spans):
            for hop in range(hops):

                @pl.when((mode == 2) & (which == hop) & (at >= begin) & (at < end))
                def _(other_ref=others[number * hops + hop], begin=begin):
                    source = other_ref.at[pl.ds(pl.multiple_of((at - begin) * tile, tile), tile)]
                    act(pltpu.make_async_copy(source, column.at[at % 2], sems.at[at % 2]))

    @pl.when(step == 0)
    def _():
        copy_of(step, lambda copy: copy.start())

    @pl.when(step + 1 < steps)
    def _():
        copy_of(step + 1, lambda copy: copy.start())

    def side_by_side(value):
        return jnp.concatenate([value[0:half], value[half:tile]], axis=1)

    def factor_of(pair):
        solved = dot(pair, weights_ref[0]) + dot(pair, weights_ref[1])
        return solved + dot(pair, weights_ref[2])

    def head_of(value):
        solved = factor_of(jnp.concatenate([value] * 2, axis=1))[:, 0:size]
        solved = jnp.where(head == 1, lower_ref[...], solved)
        return jnp.where(head == 2, 0.0, solved).astype(BF16)

    @pl.when(mode == 0)
    def _():
        out_ref[...] = slab_ref[...]

    @pl.when(mode == 1)
    def _():
        factor = factor_of(side_by_side(slab_ref[...])).astype(BF16)
        out_ref[0:half] = factor[:, 0:size]
        out_ref[half:tile] = factor[:, size : 2 * size]

        @pl.when(top)
        def _():
            out_ref[0:size] = head_of(slab_ref[0:size])

    @pl.when(mode == 2)
    def _():
        copy_of(step, lambda copy: copy.wait())
        factor = factor_of(side_by_side(column[step % 2])).astype(BF16)
        update = dot(factor, rows_ref[...])
        out_ref[0:half] = (slab_ref[0:half].astype(F32) - update[:, 0:size]).astype(BF16)
        out_ref[half:tile] = (slab_ref[half:tile].astype(F32) - update[:, size : 2 * size]).astype(BF16)

        @pl.when(top)
        def _():
            begin = head_of(column[0, 0:size])
            update = dot(begin, rows_ref[0:size, 0:size])
            base = slab_ref[0:size].astype(F32)
            out_ref[0:size] = (base - update).astype(BF16)

            @pl.when(own == 1)
            def _():
                out_ref[0:size] = (base + added_ref[...] - update).astype(BF16)


def panel(flags, lower, weights, rows, added, slab, parts, old, start, tile):
    size = slab.shape[1]
    offset = start // tile
    spans, begin, operands = [], 0, []
    for hops in parts:
        end = begin + hops[0].shape[0] // tile
        spans.append((begin, end))
        begin = end
        operands += hops
    blocks = [
        SMEM,
        pl.BlockSpec((size, size), lambda i: (0, 0)),
        pl.BlockSpec(weights.shape, lambda i: (0, 0, 0)),
        pl.BlockSpec(rows.shape, lambda i: (0, 0)),
        pl.BlockSpec((size, size), lambda i: (0, 0)),
        pl.BlockSpec((tile, size), lambda i: (i + offset, 0)),
    ] + [ANY] * len(operands)
    pieces = len(operands)
    operands = [flags, lower, weights, rows, added, slab] + operands
    aliases = {}
    if old is not None:
        aliases = {len(operands): 0}
        blocks.append(ANY)
        operands.append(old)
    return pl.pallas_call(
        functools.partial(panel_kernel, pieces=range(pieces), spans=spans, first=start == 0),
        grid=(begin,),
        in_specs=blocks,
        out_specs=pl.BlockSpec((tile, size), lambda i: (i + offset, 0)),
        out_shape=jax.ShapeDtypeStruct(slab.shape, BF16),
        input_output_aliases=aliases,
        scratch_shapes=[pltpu.VMEM((2, tile, size), BF16), pltpu.SemaphoreType.DMA((2,))],
        compiler_params=pltpu.CompilerParams(vmem_limit_bytes=32 * 2**20),
        cost_estimate=LIGHT,
        name="panel",
    )(*operands)


def broadcast(value, axis, source):
    kept = jnp.where(lax.axis_index(axis) == source, value, 0).astype(value.dtype)
    return lax.psum(kept, axis)


def tied(value, *earlier):
    return lax.optimization_barrier((value, *earlier))[0]


def settings(*values):
    return jnp.stack([jnp.asarray(value).astype(jnp.int32) for value in values])


def holder_pairs(wide, narrow, distance):
    stride = wide // narrow
    found = []
    for n in range(narrow):
        for start in range(0, wide, 2 * distance):
            source = (n * stride) ^ start
            found.append((source * narrow + n, (source ^ distance) * narrow + n))
    return found


class Order:
    def __init__(self, value):
        self.last = value

    def gate(self, value):
        return lax.optimization_barrier((value, self.last))[0]


def known_owner(owner, coarse_basis, material_ids, lame_table, coarse_ids, coarse_slab):
    narrow, wide = lax.axis_size("narrow"), lax.axis_size("wide")
    stride = wide // narrow
    wide_index, narrow_index = lax.axis_index("wide"), lax.axis_index("narrow")
    height, block = coarse_slab.shape
    own = wide_index == narrow_index * stride
    later = narrow_index > owner
    which = jnp.where(later, narrow_index - owner - 1, -1)
    mode = jnp.where(narrow_index == owner, 1, jnp.where(later, 2, 0))
    earlier = (wide_index % stride == 0) & (wide_index // stride < owner)
    kind = jnp.where(wide_index == owner * stride, 1, jnp.where(earlier, 2, 0))
    table = lame_table.astype(F32)
    hops = narrow - 1 - owner
    units, plan = PLANS[hops]
    unit = height // sum(units)
    count = len(units)
    bounds, low = [], 0
    for number in units:
        bounds.append((low, low + number * unit))
        low += number * unit
    axes = ("wide", "narrow")

    def rows_of(number):
        low, high = bounds[number]
        return coarse_slab[low:high]

    def send(value, source, target):
        return lax.ppermute(value, "narrow", [(owner + source, owner + target)])

    ways = [((n * stride) * narrow + owner, (n * stride) * narrow + n) for n in range(owner + 1, narrow)]
    head = lax.ppermute(coarse_slab[:block], axes, ways)
    first = halo_message(table, material_ids, coarse_basis)
    halo = lax.ppermute(first, "narrow", [(i + 1, i) for i in range(narrow - 1)])
    order = Order(tied(head, first))
    moved = {0: [send(order.gate(rows_of(0)), 0, hops)]}
    for number in range(1, count - 1):
        moved[number] = [send(order.gate(rows_of(number)), 0, 1)]

    edge = (narrow_index == 0).astype(jnp.int32).reshape(1)
    inner = interior(edge, table, material_ids, coarse_basis, order.last)
    partial = face(table, material_ids, coarse_basis, halo, inner, inner)

    def nearest(base, extent):
        return min(range(base, min(base + extent, narrow)), key=lambda n: abs(n - owner))

    total, distance = partial, 1
    while True:
        pairs = []
        for base in range(0, narrow - distance, 2 * distance):
            one, two = nearest(base, distance), nearest(base + distance, distance)
            pairs.append((two, one) if nearest(base, 2 * distance) == one else (one, two))
        received = lax.ppermute(total, "narrow", pairs)
        distance *= 2
        if distance >= narrow:
            break
        total = total + received
    order.last = total

    for step in plan:
        if step == "assemble":
            galerkin, message = assemble(
                settings(mode, own), order.last, coarse_ids, coarse_slab, head, [total, received]
            )
            order.last = message
        elif step == "spread":
            distance = wide // 2
            while distance > 1:
                message = message + lax.ppermute(message, axes, holder_pairs(wide, narrow, distance))
                distance //= 2
            order.last = message
        elif step == "factor":
            messages = [message, lax.ppermute(order.gate(message), axes, holder_pairs(wide, narrow, 1))]
            summary, head = factorize(settings(mode), order.last, messages, galerkin)
            order.last = summary
            moved["s"] = [send(summary, 0, 1)]
            backward = [lax.ppermute(summary, "narrow", [(owner, place)]) for place in range(owner)]
            moved[count - 1] = [send(tied(rows_of(count - 1), summary), 0, 1)]
        else:
            number, hop = step
            moving = order.gate(moved[number][hop])
            order.last = moving
            if number == 0:
                moved[number].append(send(moving, hops - hop, hops - hop - 1))
            else:
                moved[number].append(send(moving, hop + 1, hop + 2))
    pieces = [moved[0][::-1]] + [moved[number] for number in range(1, count)]
    summaries = [summary] + moved["s"] + backward

    choice = jnp.where(narrow_index >= owner, narrow_index - owner, narrow - owner + narrow_index)
    weights, rows, lower, added, galerkin = prepare(
        settings(choice, mode, own), coarse_ids, head, summaries
    )
    flags = settings(mode, kind, own, which)
    result = None
    for begin, end in ((0, count - 2), (count - 2, count - 1), (count - 1, count)):
        result = panel(
            flags, lower, weights, rows, added, coarse_slab, pieces[begin:end], result, bounds[begin][0], 2 * unit
        )
    return result, galerkin


def any_owner(owner, coarse_basis, material_ids, lame_table, coarse_ids, coarse_slab):
    narrow, wide = lax.axis_size("narrow"), lax.axis_size("wide")
    stride = wide // narrow
    wide_index, narrow_index = lax.axis_index("wide"), lax.axis_index("narrow")
    own = wide_index == narrow_index * stride
    later = narrow_index > owner
    which = jnp.where(later, 0, -1)
    mode = jnp.where(narrow_index == owner, 1, jnp.where(later, 2, 0))
    earlier = (wide_index % stride == 0) & (wide_index // stride < owner)
    kind = jnp.where(wide_index == owner * stride, 1, jnp.where(earlier, 2, 0))
    table = lame_table.astype(F32)
    column = broadcast(coarse_slab, "narrow", owner)
    first = halo_message(table, material_ids, coarse_basis)
    halo = lax.ppermute(first, "narrow", [(i + 1, i) for i in range(narrow - 1)])
    edge = (narrow_index == 0).astype(jnp.int32).reshape(1)
    inner = interior(edge, table, material_ids, coarse_basis, first)
    partial = face(table, material_ids, coarse_basis, halo, first, inner)
    parts = [lax.psum(partial, "narrow")]
    galerkin, message = assemble(settings(mode, own), first, coarse_ids, coarse_slab, column, parts)
    at_owner = (wide_index == owner * stride) & (narrow_index == owner)
    diagonal = lax.psum(jnp.where(at_owner, message, 0.0), ("wide", "narrow"))
    summary, _ = factorize(settings(1), first, [diagonal], galerkin)
    head = broadcast(message, "wide", narrow_index * stride)
    weights, rows, lower, added, galerkin = prepare(settings(0, mode, own), coarse_ids, head, [summary])
    flags = settings(mode, kind, own, which)
    tile = coarse_slab.shape[0] // 12
    result = panel(flags, lower, weights, rows, added, coarse_slab, [[column]], None, 0, tile)
    return result, galerkin


def on_device(coarse_basis, material_ids, lame_table, coarse_ids, coarse_slab, panel_owner):
    narrow, wide = lax.axis_size("narrow"), lax.axis_size("wide")
    arrays = (coarse_basis, material_ids, lame_table, coarse_ids, coarse_slab)
    owner = panel_owner[0]
    if narrow - 1 > len(PLANS) or wide & (wide - 1):
        return any_owner(owner, *arrays)
    branches = [functools.partial(known_owner, place) for place in range(narrow - 1)]
    return lax.switch(owner, branches, *arrays)


def solution(mesh):
    return jax.shard_map(
        on_device,
        mesh=mesh,
        in_specs=(
            P("wide", None, None, "narrow", None, None),
            P("wide", "narrow", None, None),
            P(),
            P("wide", None),
            P("wide", "narrow"),
            P(),
        ),
        out_specs=(P("wide", "narrow"), P("wide", None, None)),
        check_vma=False,
    )
```

```python
import functools

import jax
import jax.numpy as jnp
from jax import lax
from jax.experimental import pallas as pl
from jax.experimental.pallas import tpu as pltpu
from jax.sharding import PartitionSpec as P

F32, BF16 = jnp.float32, jnp.bfloat16
NT = (((1,), (1,)), ((), ()))
TN = (((0,), (0,)), ((), ()))
VMEM = pl.BlockSpec(memory_space=pltpu.VMEM)
ANY = pl.BlockSpec(memory_space=pl.ANY)
SMEM = pl.BlockSpec(memory_space=pltpu.SMEM)
PLANS = {
    1: ((14, 8, 2), ("assemble", "others", "spread", "spread", "spread", "factor")),
    2: (
        (8, 6, 4, 4, 2),
        (
            (0, 0), "assemble", "others", "spread", (1, 0), "spread", "spread", (2, 0), (1, 1), "factor",
            ("s", 0), (3, 0), (2, 1), (4, 0),
        ),
    ),
    3: (
        (8, 6, 4, 4, 2),
        (
            (0, 0), "assemble", "others", "spread", (1, 0), "spread", "spread", (2, 0), (0, 1), (1, 1), "factor",
            ("s", 0), (3, 0), ("s", 1), (2, 1), (4, 0), (3, 1), (4, 1),
        ),
    ),
}
BLOCK = 16
LIGHT = pl.CostEstimate(flops=1, bytes_accessed=1, transcendentals=0)


def exact_dot(left, right, dims=(((1,), (0,)), ((), ()))):
    return lax.dot_general(
        left, right, dims, precision=lax.Precision.HIGHEST, preferred_element_type=F32
    )


def dot(left, right, dims=(((1,), (0,)), ((), ()))):
    return lax.dot_general(left, right, dims, preferred_element_type=F32)


def split_two(value):
    high = value.astype(BF16)
    return high, (value - high.astype(F32)).astype(BF16)


def lame_of(ids, table_ref):
    shear = jnp.zeros(ids.shape, F32)
    dilate = jnp.zeros(ids.shape, F32)
    for material in range(table_ref.shape[1]):
        chosen = ids == material
        shear = jnp.where(chosen, table_ref[0, material], shear)
        dilate = jnp.where(chosen, table_ref[1, material], dilate)
    return shear, dilate


def halo_kernel(table_ref, ids_ref, basis_ref, out_ref):
    subs, funcs, comps = basis_ref.shape[0:3]
    for sub in range(subs):
        for comp in range(comps):
            out_ref[sub, comp * funcs : (comp + 1) * funcs] = basis_ref[sub, :, comp, 0]
        shear, dilate = lame_of(ids_ref[sub, 0], table_ref)
        out_ref[sub, comps * funcs] = shear.astype(BF16)
        out_ref[sub, comps * funcs + 1] = dilate.astype(BF16)


def halo_message(table, ids, basis):
    subs, funcs, comps, layers, ny, nz = basis.shape
    return pl.pallas_call(
        halo_kernel,
        in_specs=[SMEM, VMEM, VMEM],
        out_specs=VMEM,
        out_shape=jax.ShapeDtypeStruct((subs, comps * funcs + 2, ny, nz), BF16),
        compiler_params=pltpu.CompilerParams(vmem_limit_bytes=16 * 2**20),
        cost_estimate=LIGHT,
        name="halo_message",
    )(table, ids, basis)


def interior_kernel(edge_ref, table_ref, ids_ref, basis_ref, token_ref, out_ref, fields, turned, coef, left, right, acc):
    sub, comp = pl.program_id(0), pl.program_id(1)
    layers, ny, nz = basis_ref.shape[3:]
    funcs = basis_ref.shape[1]
    row = lax.broadcasted_iota(jnp.int32, (ny, nz), 0)
    lane = lax.broadcasted_iota(jnp.int32, (ny, nz), 1)
    table = [lame_of(ids_ref[sub, x], table_ref) for x in range(layers)]

    def weight(one, two, direction):
        shear = 0.5 * (one[0] + two[0])
        dilate = 0.5 * (one[1] + two[1])
        return shear + jnp.where(comp == direction, shear + dilate, 0.0)

    def ahead(field, axis):
        size = field.shape[axis]
        index = row if axis == 0 else lane
        return jnp.where(index == size - 1, 0.0, pltpu.roll(field, size - 1, axis=axis))

    def behind(field, axis):
        index = row if axis == 0 else lane
        return jnp.where(index == 0, 0.0, pltpu.roll(field, 1, axis=axis))

    nothing = (jnp.zeros((ny, nz), F32),) * 2
    previous = weight(table[0], nothing, 0) * edge_ref[0].astype(F32)
    for x in range(layers):
        diagonal = previous
        forward = []
        if x + 1 < layers:
            face = weight(table[x], table[x + 1], 0)
            diagonal = diagonal + face
            previous = face
            forward.append(face)
        else:
            forward.append(jnp.zeros((ny, nz), F32))
        for axis in (0, 1):
            index, size = (row, ny) if axis == 0 else (lane, nz)
            other = tuple(ahead(value, axis) for value in table[x])
            face = weight(table[x], other, axis + 1)
            before = tuple(behind(value, axis) for value in table[x])
            diagonal = diagonal + face + weight(table[x], before, axis + 1)
            forward.append(jnp.where(index == size - 1, 0.0, face))
        coef[x, 0] = 0.5 * diagonal
        for kind in range(3):
            coef[x, kind + 1] = forward[kind]
        fields[x] = basis_ref[sub, :, comp, x].astype(F32).reshape(funcs * ny, nz)

    total = None
    for x in reversed(range(layers)):
        values = [fields[x, pl.ds(y, funcs, stride=ny), :] for y in range(ny)]
        for y in range(ny):
            value = values[y]
            turned[x % 2, y] = value
            image = coef[x, 0, y : y + 1, :] * value
            image = image - coef[x, 3, y : y + 1, :] * pltpu.roll(value, nz - 1, axis=1)
            if y + 1 < ny:
                image = image - coef[x, 2, y : y + 1, :] * values[y + 1]
            if x + 1 < layers:
                image = image - coef[x, 1, y : y + 1, :] * turned[(x + 1) % 2, y]
            high, low = split_two(image)
            left[:, y * nz : (y + 1) * nz] = value.astype(BF16)
            right[0:funcs, y * nz : (y + 1) * nz] = high
            right[funcs : 2 * funcs, y * nz : (y + 1) * nz] = low
        product = dot(right[...], left[...], NT)
        total = product if total is None else total + product

    @pl.when(comp == 0)
    def _():
        acc[...] = total

    @pl.when(comp > 0)
    def _():
        acc[...] += total

    @pl.when(comp == pl.num_programs(1) - 1)
    def _():
        out_ref[0] = acc[0:funcs] + acc[funcs : 2 * funcs]


def interior(edge, table, ids, basis, token):
    subs, funcs, comps, layers, ny, nz = basis.shape
    return pl.pallas_call(
        interior_kernel,
        grid=(subs, comps),
        in_specs=[SMEM, SMEM, VMEM, VMEM, ANY],
        out_specs=pl.BlockSpec((1, funcs, funcs), lambda s, c: (s, 0, 0)),
        out_shape=jax.ShapeDtypeStruct((subs, funcs, funcs), F32),
        scratch_shapes=[
            pltpu.VMEM((layers, funcs * ny, nz), F32),
            pltpu.VMEM((2, ny, funcs, nz), F32),
            pltpu.VMEM((layers, 4, ny, nz), F32),
            pltpu.VMEM((funcs, ny * nz), BF16),
            pltpu.VMEM((2 * funcs, ny * nz), BF16),
            pltpu.VMEM((2 * funcs, funcs), F32),
        ],
        compiler_params=pltpu.CompilerParams(vmem_limit_bytes=16 * 2**20),
        cost_estimate=LIGHT,
        name="interior",
    )(edge, table, ids, basis, token)


def face_kernel(flags_ref, *refs):
    @pl.when(flags_ref[0] == 1)
    def _():
        face_sums(*refs)


def face_sums(table_ref, ids_ref, basis_ref, halo_ref, token_ref, inner_ref, out_ref, mine, theirs, left, right):
    subs, funcs, comps, layers, ny, nz = basis_ref.shape
    for sub in range(subs):
        shear, dilate = lame_of(ids_ref[sub, layers - 1], table_ref)
        shear = 0.5 * (shear + halo_ref[sub, comps * funcs].astype(F32))
        dilate = 0.5 * (dilate + halo_ref[sub, comps * funcs + 1].astype(F32))
        total = None
        for comp in range(comps):
            weight = shear + (shear + dilate) if comp == 0 else shear
            slot = (sub * comps + comp) % 2
            mine[slot] = basis_ref[sub, :, comp, layers - 1].astype(F32).reshape(funcs * ny, nz)
            theirs[slot] = halo_ref[sub, comp * funcs : (comp + 1) * funcs].astype(F32).reshape(funcs * ny, nz)
            for y in range(ny):
                here = mine[slot, pl.ds(y, funcs, stride=ny), :]
                there = theirs[slot, pl.ds(y, funcs, stride=ny), :]
                high, low = split_two(weight[y : y + 1, :] * (here - there))
                left[slot, 0:funcs, y * nz : (y + 1) * nz] = here.astype(BF16)
                left[slot, funcs : 2 * funcs, y * nz : (y + 1) * nz] = there.astype(BF16)
                right[slot, 0:funcs, y * nz : (y + 1) * nz] = high
                right[slot, funcs : 2 * funcs, y * nz : (y + 1) * nz] = low
            product = dot(right[slot], left[slot], NT)
            total = product if total is None else total + product
        total = total[:, 0:funcs] - total[:, funcs : 2 * funcs]
        half = inner_ref[sub] + 0.5 * (total[0:funcs] + total[funcs : 2 * funcs])
        out_ref[sub] = half + half.T


def face(flags, table, ids, basis, halo, token, inner):
    subs, funcs, comps, layers, ny, nz = basis.shape
    return pl.pallas_call(
        face_kernel,
        in_specs=[SMEM, SMEM] + [VMEM] * 3 + [ANY, VMEM],
        out_specs=VMEM,
        out_shape=jax.ShapeDtypeStruct((subs, funcs, funcs), F32),
        scratch_shapes=[
            pltpu.VMEM((2, funcs * ny, nz), F32),
            pltpu.VMEM((2, funcs * ny, nz), F32),
            pltpu.VMEM((2, 2 * funcs, ny * nz), BF16),
            pltpu.VMEM((2, 2 * funcs, ny * nz), BF16),
        ],
        compiler_params=pltpu.CompilerParams(vmem_limit_bytes=16 * 2**20),
        cost_estimate=LIGHT,
        name="face",
    )(flags, table, ids, basis, halo, token, inner)


def spread(gal_ref, column_ids_ref, row_ids_ref, size):
    subs, funcs = column_ids_ref.shape[0:2]
    added = jnp.zeros((size, size), F32)
    lane = lax.broadcasted_iota(jnp.int32, (funcs, size), 1)
    row = lax.broadcasted_iota(jnp.int32, (size, funcs), 0)
    for sub in range(subs):
        slots = (column_ids_ref[sub] == lane).astype(F32)
        slots_t = (row_ids_ref[sub] == row).astype(F32)
        added = added + exact_dot(slots_t, exact_dot(gal_ref[sub], slots))
    return added


def assemble_kernel(flags_ref, token_ref, column_ids_ref, row_ids_ref, slab_ref, head_ref, *rest):
    gal_refs, (message_ref, sum_ref) = rest[:-2], rest[-2:]
    size = message_ref.shape[0]
    mode, own = flags_ref[0], flags_ref[1]
    message_ref[...] = jnp.zeros_like(message_ref)

    @pl.when((mode == 1) & (own == 1))
    def _():
        total = gal_refs[0][...]
        for gal_ref in gal_refs[1:]:
            total = total + gal_ref[...]
        sum_ref[...] = total
        added = spread(sum_ref, column_ids_ref, row_ids_ref, size)
        message_ref[...] = added + slab_ref[...].astype(F32)

    @pl.when((mode == 2) & (own == 1))
    def _():
        message_ref[...] = head_ref[...].astype(F32)


def assemble(flags, token, ids, slab, head, parts):
    size = slab.shape[1]
    block = pl.BlockSpec((size, size), lambda i: (0, 0))
    return pl.pallas_call(
        assemble_kernel,
        grid=(1,),
        in_specs=[SMEM, ANY, VMEM, VMEM, block, block] + [VMEM] * len(parts),
        out_specs=VMEM,
        out_shape=jax.ShapeDtypeStruct((size, size), F32),
        scratch_shapes=[pltpu.VMEM(parts[0].shape, F32)],
        cost_estimate=LIGHT,
        name="assemble",
    )(flags, token, ids[:, :, None], ids[:, None, :], slab, head, *parts)


def factor_kernel(flags_ref, token_ref, *refs, parts, groups):
    message_refs, gal_refs = refs[:parts], refs[parts:-3]
    summary_ref, block_ref, work = refs[-3:]
    subs, funcs = gal_refs[0].shape[0:2]
    size = summary_ref.shape[1]
    rows = 2 * size
    diagonal = message_refs[0][...]
    for message_ref in message_refs[1:]:
        diagonal = diagonal + message_ref[...]
    block_ref[...] = diagonal

    @pl.when(flags_ref[0] == 1)
    def _():
        row = lax.broadcasted_iota(jnp.int32, (size, size), 0)
        lane = lax.broadcasted_iota(jnp.int32, (size, size), 1)
        work[:, 0:size] = 0.5 * (diagonal + diagonal.T)
        work[:, size : 2 * size] = (row == lane).astype(F32)
        index = lax.broadcasted_iota(jnp.int32, (BLOCK, size), 0)
        for start in range(0, size, BLOCK):
            panel = work[start : start + BLOCK, 0:size]
            extra = work[start : start + BLOCK, size : 2 * size]
            columns = [
                jnp.broadcast_to(panel[:, start + step : start + step + 1], (BLOCK, size))
                for step in range(BLOCK)
            ]
            for step in range(BLOCK):
                scale = lax.rsqrt(columns[step][step : step + 1, :])
                column = jnp.where(index > step, columns[step] * scale, 0.0)
                for later in range(step + 1, BLOCK):
                    columns[later] = columns[later] - column * column[later : later + 1, :]
                pivot = panel[step : step + 1, :] * scale
                panel = jnp.where(index == step, pivot, panel - column * pivot)
                pivot = extra[step : step + 1, :] * scale
                extra = jnp.where(index == step, pivot, extra - column * pivot)
            work[start : start + BLOCK, 0:size] = panel
            work[start : start + BLOCK, size : 2 * size] = extra
            rest = start + BLOCK
            if rest < size:
                both = jnp.concatenate([panel, extra], axis=1)
                work[rest:size, :] -= exact_dot(panel[:, rest:size], both, TN)
        upper = jnp.where(row <= lane, work[:, 0:size], 0.0)
        summary_ref[0:size] = jnp.where(row >= lane, work[:, size : 2 * size], 0.0).T
        summary_ref[size : 2 * size] = upper.T
        each = len(gal_refs) // groups
        for group in range(groups):

            @pl.when(flags_ref[1] == group)
            def _(chosen=gal_refs[group * each : (group + 1) * each]):
                for sub in range(subs):
                    begin = rows + sub * funcs
                    total = chosen[0][sub]
                    for gal_ref in chosen[1:]:
                        total = total + gal_ref[sub]
                    summary_ref[begin : begin + funcs, 0:funcs] = total
                    summary_ref[begin : begin + funcs, funcs:size] = jnp.zeros((funcs, size - funcs), F32)


def factorize(flags, token, messages, groups):
    size = messages[0].shape[1]
    subs, funcs = groups[0][0].shape[0:2]
    parts = [part for group in groups for part in group]
    return pl.pallas_call(
        functools.partial(factor_kernel, parts=len(messages), groups=len(groups)),
        in_specs=[SMEM, ANY] + [VMEM] * (len(messages) + len(parts)),
        out_specs=[VMEM] * 2,
        out_shape=[
            jax.ShapeDtypeStruct((2 * size + subs * funcs, size), F32),
            jax.ShapeDtypeStruct((size, size), F32),
        ],
        scratch_shapes=[pltpu.VMEM((size, 2 * size), F32)],
        cost_estimate=LIGHT,
        name="factorize",
    )(flags, token, *messages, *parts)


def prepare_kernel(flags_ref, column_ids_ref, row_ids_ref, head_ref, *rest, sources):
    summary_refs = rest[:sources]
    weights_ref, rows_ref, lower_ref, added_ref, gal_ref, summary, sem = rest[sources:]
    subs, funcs = gal_ref.shape[0:2]
    size = head_ref.shape[0]
    choice, mode, own = flags_ref[0], flags_ref[1], flags_ref[2]
    for number, summary_ref in enumerate(summary_refs):

        @pl.when(choice == number)
        def _(summary_ref=summary_ref):
            copy = pltpu.make_async_copy(summary_ref, summary, sem)
            copy.start()
            copy.wait()

    for sub in range(subs):
        begin = 2 * size + sub * funcs
        gal_ref[sub] = summary[begin : begin + funcs, 0:funcs]

    def doubled(block):
        nothing = jnp.zeros((size, size), BF16)
        top = jnp.concatenate([block, nothing], axis=1)
        return jnp.concatenate([top, jnp.concatenate([nothing, block], axis=1)], axis=0)

    @pl.when(mode > 0)
    def _():
        inverse = summary[0:size]
        high = inverse.astype(BF16)
        weights_ref[0 : 2 * size] = doubled(high)
        weights_ref[2 * size : 4 * size] = doubled((inverse - high.astype(F32)).astype(BF16))
        lower_ref[...] = summary[size : 2 * size]

    @pl.when(mode == 2)
    def _():
        solved = exact_dot(head_ref[...], summary[0:size])
        rows_ref[...] = doubled(solved.T.astype(BF16))

    @pl.when((mode == 2) & (own == 1))
    def _():
        added_ref[...] = spread(gal_ref, column_ids_ref, row_ids_ref, size)


def prepare(flags, ids, head, summaries):
    size = head.shape[0]
    subs, funcs = ids.shape
    return pl.pallas_call(
        functools.partial(prepare_kernel, sources=len(summaries)),
        in_specs=[SMEM] + [VMEM] * 3 + [ANY] * len(summaries),
        out_specs=[VMEM] * 5,
        out_shape=[
            jax.ShapeDtypeStruct((4 * size, 2 * size), BF16),
            jax.ShapeDtypeStruct((2 * size, 2 * size), BF16),
            jax.ShapeDtypeStruct((size, size), F32),
            jax.ShapeDtypeStruct((size, size), F32),
            jax.ShapeDtypeStruct((subs, funcs, funcs), F32),
        ],
        scratch_shapes=[pltpu.VMEM(summaries[0].shape, F32), pltpu.SemaphoreType.DMA],
        compiler_params=pltpu.CompilerParams(vmem_limit_bytes=16 * 2**20),
        cost_estimate=LIGHT,
        name="prepare",
    )(flags, ids[:, :, None], ids[:, None, :], head, *summaries)


def panel_kernel(
    flags_ref, lower_ref, weights_ref, rows_ref, added_ref, slab_ref, *rest, pieces, spans, first
):
    hops = len(pieces) // len(spans)
    others = rest[: len(pieces)]
    out_ref, column, sems = rest[-3:]
    tile, size = out_ref.shape
    half = tile // 2
    mode, head, own, which = flags_ref[0], flags_ref[1], flags_ref[2], flags_ref[3]
    step, steps = pl.program_id(0), pl.num_programs(0)
    top = first & (step == 0)

    def copy_of(at, act):
        for number, (begin, end) in enumerate(spans):
            for hop in range(hops):

                @pl.when((mode == 2) & (which == hop) & (at >= begin) & (at < end))
                def _(other_ref=others[number * hops + hop], begin=begin):
                    source = other_ref.at[pl.ds(pl.multiple_of((at - begin) * tile, tile), tile)]
                    act(pltpu.make_async_copy(source, column.at[at % 2], sems.at[at % 2]))

    @pl.when(step == 0)
    def _():
        copy_of(step, lambda copy: copy.start())

    @pl.when(step + 1 < steps)
    def _():
        copy_of(step + 1, lambda copy: copy.start())

    def side_by_side(value):
        return jnp.concatenate([value[0:half], value[half:tile]], axis=1)

    def factor_of(pair):
        return dot(jnp.concatenate([pair, pair], axis=1), weights_ref[...])

    def head_of(value):
        solved = factor_of(jnp.concatenate([value] * 2, axis=1))[:, 0:size]
        solved = jnp.where(head == 1, lower_ref[...], solved)
        return jnp.where(head == 2, 0.0, solved).astype(BF16)

    @pl.when(mode == 0)
    def _():
        out_ref[...] = slab_ref[...]

    @pl.when(mode == 1)
    def _():
        factor = factor_of(side_by_side(slab_ref[...])).astype(BF16)
        out_ref[0:half] = factor[:, 0:size]
        out_ref[half:tile] = factor[:, size : 2 * size]

        @pl.when(top)
        def _():
            out_ref[0:size] = head_of(slab_ref[0:size])

    @pl.when(mode == 2)
    def _():
        copy_of(step, lambda copy: copy.wait())
        factor = factor_of(side_by_side(column[step % 2])).astype(BF16)
        update = dot(factor, rows_ref[...])
        out_ref[0:half] = (slab_ref[0:half].astype(F32) - update[:, 0:size]).astype(BF16)
        out_ref[half:tile] = (slab_ref[half:tile].astype(F32) - update[:, size : 2 * size]).astype(BF16)

        @pl.when(top)
        def _():
            begin = head_of(column[0, 0:size])
            update = dot(begin, rows_ref[0:size, 0:size])
            base = slab_ref[0:size].astype(F32)
            out_ref[0:size] = (base - update).astype(BF16)

            @pl.when(own == 1)
            def _():
                out_ref[0:size] = (base + added_ref[...] - update).astype(BF16)


def panel(flags, lower, weights, rows, added, slab, parts, old, start, tile):
    size = slab.shape[1]
    offset = start // tile
    spans, begin, operands = [], 0, []
    for hops in parts:
        end = begin + hops[0].shape[0] // tile
        spans.append((begin, end))
        begin = end
        operands += hops
    blocks = [
        SMEM,
        pl.BlockSpec((size, size), lambda i: (0, 0)),
        pl.BlockSpec(weights.shape, lambda i: (0, 0)),
        pl.BlockSpec(rows.shape, lambda i: (0, 0)),
        pl.BlockSpec((size, size), lambda i: (0, 0)),
        pl.BlockSpec((tile, size), lambda i: (i + offset, 0)),
    ] + [ANY] * len(operands)
    pieces = len(operands)
    operands = [flags, lower, weights, rows, added, slab] + operands
    aliases = {}
    if old is not None:
        aliases = {len(operands): 0}
        blocks.append(ANY)
        operands.append(old)
    return pl.pallas_call(
        functools.partial(panel_kernel, pieces=range(pieces), spans=spans, first=start == 0),
        grid=(begin,),
        in_specs=blocks,
        out_specs=pl.BlockSpec((tile, size), lambda i: (i + offset, 0)),
        out_shape=jax.ShapeDtypeStruct(slab.shape, BF16),
        input_output_aliases=aliases,
        scratch_shapes=[pltpu.VMEM((2, tile, size), BF16), pltpu.SemaphoreType.DMA((2,))],
        compiler_params=pltpu.CompilerParams(vmem_limit_bytes=16 * 2**20),
        cost_estimate=LIGHT,
        name="panel",
    )(*operands)


def broadcast(value, axis, source):
    kept = jnp.where(lax.axis_index(axis) == source, value, 0).astype(value.dtype)
    return lax.psum(kept, axis)


def tied(value, *earlier):
    return lax.optimization_barrier((value, *earlier))[0]


def settings(*values):
    return jnp.stack([jnp.asarray(value).astype(jnp.int32) for value in values])


def holder_pairs(wide, narrow, distance):
    stride = wide // narrow
    found = []
    for n in range(narrow):
        for start in range(0, wide, 2 * distance):
            source = (n * stride) ^ start
            found.append((source * narrow + n, (source ^ distance) * narrow + n))
    return found


class Order:
    def __init__(self, value):
        self.last = value

    def gate(self, value):
        return lax.optimization_barrier((value, self.last))[0]


def known_owner(owner, coarse_basis, material_ids, lame_table, coarse_ids, coarse_slab):
    narrow, wide = lax.axis_size("narrow"), lax.axis_size("wide")
    stride = wide // narrow
    wide_index, narrow_index = lax.axis_index("wide"), lax.axis_index("narrow")
    height, block = coarse_slab.shape
    own = wide_index == narrow_index * stride
    later = narrow_index > owner
    which = jnp.where(later, narrow_index - owner - 1, -1)
    mode = jnp.where(narrow_index == owner, 1, jnp.where(later, 2, 0))
    earlier = (wide_index % stride == 0) & (wide_index // stride < owner)
    kind = jnp.where(wide_index == owner * stride, 1, jnp.where(earlier, 2, 0))
    table = lame_table.astype(F32)
    hops = narrow - 1 - owner
    units, plan = PLANS[hops]
    unit = height // sum(units)
    count = len(units)
    bounds, low = [], 0
    for number in units:
        bounds.append((low, low + number * unit))
        low += number * unit
    axes = ("wide", "narrow")

    def rows_of(number):
        low, high = bounds[number]
        return coarse_slab[low:high]

    def send(value, source, target):
        return lax.ppermute(value, "narrow", [(owner + source, owner + target)])

    ways = [((n * stride) * narrow + owner, (n * stride) * narrow + n) for n in range(owner + 1, narrow)]
    head = lax.ppermute(coarse_slab[:block], axes, ways)
    first = halo_message(table, material_ids, coarse_basis)
    groups = [[w for w in range(wide) if w % stride == 0], [w for w in range(wide) if w % stride]]
    groups = [group for group in groups if group]
    member = jnp.where(wide_index % stride == 0, 0, 1)

    def within(group, pairs):
        return [(w * narrow + one, w * narrow + two) for w in group for one, two in pairs]

    def halo_of(group, message):
        return lax.ppermute(message, axes, within(group, [(i + 1, i) for i in range(narrow - 1)]))

    halos = [halo_of(groups[0], first)]
    order = Order(tied(head, first))
    moved = {0: [send(order.gate(rows_of(0)), 0, hops)]}
    for number in range(1, count - 1):
        moved[number] = [send(order.gate(rows_of(number)), 0, 1)]

    edge = (narrow_index == 0).astype(jnp.int32).reshape(1)
    inner = interior(edge, table, material_ids, coarse_basis, order.last)
    for group in groups[1:]:
        halos.append(halo_of(group, tied(first, halos[-1], inner)))
    def nearest(base, extent):
        return min(range(base, min(base + extent, narrow)), key=lambda n: abs(n - owner))

    def sums_of(number, token):
        flag = settings(member == number)
        total = face(flag, table, material_ids, coarse_basis, halos[number], token, inner)
        distance = 1
        while True:
            pairs = []
            for base in range(0, narrow - distance, 2 * distance):
                one, two = nearest(base, distance), nearest(base + distance, distance)
                pairs.append((two, one) if nearest(base, 2 * distance) == one else (one, two))
            received = lax.ppermute(total, axes, within(groups[number], pairs))
            distance *= 2
            if distance >= narrow:
                return [total, received]
            total = total + received

    sums = [sums_of(0, inner)]
    order.last = sums[0][0]
    distance, messages, left = wide // 2, [], plan.count("spread")
    for step in plan:
        if step == "assemble":
            message = assemble(settings(mode, own), order.last, coarse_ids, coarse_slab, head, sums[0])
            order.last = message
        elif step == "others":
            for number in range(1, len(groups)):
                sums.append(sums_of(number, order.last))
        elif step == "spread":
            left -= 1
            while distance:
                received = lax.ppermute(order.gate(message), axes, holder_pairs(wide, narrow, distance))
                messages = [message, received]
                if distance > 1:
                    message = message + received
                    order.last = message
                distance //= 2
                if left:
                    break
        elif step == "factor":
            summary, head = factorize(settings(mode, member), order.last, messages, sums)
            order.last = summary
            moved["s"] = [send(summary, 0, 1)]
            backward = [lax.ppermute(summary, "narrow", [(owner, place)]) for place in range(owner)]
            moved[count - 1] = [send(tied(rows_of(count - 1), summary), 0, 1)]
        else:
            number, hop = step
            moving = order.gate(moved[number][hop])
            order.last = moving
            if number == 0 and hop + 1 < hops:
                moved[number].append(send(moving, hops - hop, hops - hop - 1))
            elif number != 0 and hop + 1 < hops:
                moved[number].append(send(moving, hop + 1, hop + 2))
    pieces = [moved[0][::-1]] + [moved[number] for number in range(1, count)]
    summaries = [summary] + moved["s"] + backward

    choice = jnp.where(narrow_index >= owner, narrow_index - owner, narrow - owner + narrow_index)
    weights, rows, lower, added, galerkin = prepare(
        settings(choice, mode, own), coarse_ids, head, summaries
    )
    flags = settings(mode, kind, own, which)
    result = None
    for begin, end in ((0, count - 2), (count - 2, count - 1), (count - 1, count)):
        result = panel(
            flags, lower, weights, rows, added, coarse_slab, pieces[begin:end], result, bounds[begin][0], 2 * unit
        )
    return result, galerkin


def any_owner(owner, coarse_basis, material_ids, lame_table, coarse_ids, coarse_slab):
    narrow, wide = lax.axis_size("narrow"), lax.axis_size("wide")
    stride = wide // narrow
    wide_index, narrow_index = lax.axis_index("wide"), lax.axis_index("narrow")
    own = wide_index == narrow_index * stride
    later = narrow_index > owner
    which = jnp.where(later, 0, -1)
    mode = jnp.where(narrow_index == owner, 1, jnp.where(later, 2, 0))
    earlier = (wide_index % stride == 0) & (wide_index // stride < owner)
    kind = jnp.where(wide_index == owner * stride, 1, jnp.where(earlier, 2, 0))
    table = lame_table.astype(F32)
    column = broadcast(coarse_slab, "narrow", owner)
    first = halo_message(table, material_ids, coarse_basis)
    halo = lax.ppermute(first, "narrow", [(i + 1, i) for i in range(narrow - 1)])
    edge = (narrow_index == 0).astype(jnp.int32).reshape(1)
    inner = interior(edge, table, material_ids, coarse_basis, first)
    partial = face(settings(1), table, material_ids, coarse_basis, halo, first, inner)
    parts = [lax.psum(partial, "narrow")]
    message = assemble(settings(mode, own), first, coarse_ids, coarse_slab, column, parts)
    at_owner = (wide_index == owner * stride) & (narrow_index == owner)
    diagonal = lax.psum(jnp.where(at_owner, message, 0.0), ("wide", "narrow"))
    summary, _ = factorize(settings(1, 0), first, [diagonal], [parts])
    head = broadcast(message, "wide", narrow_index * stride)
    weights, rows, lower, added, galerkin = prepare(settings(0, mode, own), coarse_ids, head, [summary])
    flags = settings(mode, kind, own, which)
    tile = coarse_slab.shape[0] // 12
    result = panel(flags, lower, weights, rows, added, coarse_slab, [[column]], None, 0, tile)
    return result, galerkin


def on_device(coarse_basis, material_ids, lame_table, coarse_ids, coarse_slab, panel_owner):
    narrow, wide = lax.axis_size("narrow"), lax.axis_size("wide")
    arrays = (coarse_basis, material_ids, lame_table, coarse_ids, coarse_slab)
    owner = panel_owner[0]
    if narrow - 1 > len(PLANS) or wide & (wide - 1):
        return any_owner(owner, *arrays)
    branches = [functools.partial(known_owner, place) for place in range(narrow - 1)]
    return lax.switch(owner, branches, *arrays)


def solution(mesh):
    return jax.shard_map(
        on_device,
        mesh=mesh,
        in_specs=(
            P("wide", None, None, "narrow", None, None),
            P("wide", "narrow", None, None),
            P(),
            P("wide", None),
            P("wide", "narrow"),
            P(),
        ),
        out_specs=(P("wide", "narrow"), P("wide", None, None)),
        check_vma=False,
    )
```

```python
import functools

import jax
import jax.numpy as jnp
from jax import lax
from jax.experimental import pallas as pl
from jax.experimental.pallas import tpu as pltpu
from jax.sharding import PartitionSpec as P

F32, BF16 = jnp.float32, jnp.bfloat16
NT = (((1,), (1,)), ((), ()))
TN = (((0,), (0,)), ((), ()))
VMEM = pl.BlockSpec(memory_space=pltpu.VMEM)
ANY = pl.BlockSpec(memory_space=pl.ANY)
SMEM = pl.BlockSpec(memory_space=pltpu.SMEM)
PLANS = {
    1: ((14, 8, 2), (), ("assemble", "spread", "others", "spread", "more", "spread", "factor")),
    2: (
        (14, 4, 4, 2),
        (),
        (
            "assemble", "spread", "others", "spread", "more", (0, 0), "spread", (1, 0), (1, 1), "factor",
            (2, 0), (2, 1), (3, 0),
        ),
    ),
    3: (
        (12, 4, 4, 2, 2),
        (1, 2, 3),
        (
            "assemble", "spread", "others", (0, 0), "spread", "more", "spread", "factor",
            (1, 0), (1, 1), (0, 1), (2, 0), (1, 2), (2, 1), (3, 0), (3, 1), (4, 0), (2, 2), (4, 1),
        ),
    ),
}
BLOCK = 16
LIGHT = pl.CostEstimate(flops=1, bytes_accessed=1, transcendentals=0)


def exact_dot(left, right, dims=(((1,), (0,)), ((), ()))):
    return lax.dot_general(
        left, right, dims, precision=lax.Precision.HIGHEST, preferred_element_type=F32
    )


def dot(left, right, dims=(((1,), (0,)), ((), ()))):
    return lax.dot_general(left, right, dims, preferred_element_type=F32)


def split_two(value):
    high = value.astype(BF16)
    return high, (value - high.astype(F32)).astype(BF16)


def lame_of(ids, table_ref):
    shear = jnp.zeros(ids.shape, F32)
    dilate = jnp.zeros(ids.shape, F32)
    for material in range(table_ref.shape[1]):
        chosen = ids == material
        shear = jnp.where(chosen, table_ref[0, material], shear)
        dilate = jnp.where(chosen, table_ref[1, material], dilate)
    return shear, dilate


def halo_kernel(table_ref, ids_ref, token_ref, basis_ref, out_ref, last_ref):
    subs, funcs, comps, layers = basis_ref.shape[0:4]
    for sub in range(subs):
        for comp in range(comps):
            out_ref[sub, comp * funcs : (comp + 1) * funcs] = basis_ref[sub, :, comp, 0]
            last_ref[sub, comp * funcs : (comp + 1) * funcs] = basis_ref[sub, :, comp, layers - 1]
        shear, dilate = lame_of(ids_ref[sub, 0], table_ref)
        out_ref[sub, comps * funcs] = shear.astype(BF16)
        out_ref[sub, comps * funcs + 1] = dilate.astype(BF16)


def halo_message(table, ids, token, basis):
    subs, funcs, comps, layers, ny, nz = basis.shape
    return pl.pallas_call(
        halo_kernel,
        in_specs=[SMEM, VMEM, ANY, VMEM],
        out_specs=[VMEM, VMEM],
        out_shape=[
            jax.ShapeDtypeStruct((subs, comps * funcs + 2, ny, nz), BF16),
            jax.ShapeDtypeStruct((subs, comps * funcs, ny, nz), BF16),
        ],
        compiler_params=pltpu.CompilerParams(vmem_limit_bytes=16 * 2**20),
        cost_estimate=LIGHT,
        name="halo_message",
    )(table, ids, token, basis)


def interior_kernel(edge_ref, table_ref, ids_ref, basis_ref, token_ref, out_ref, fields, turned, coef, left, right, acc):
    sub, comp = pl.program_id(0), pl.program_id(1)
    layers, ny, nz = basis_ref.shape[3:]
    funcs = basis_ref.shape[1]
    row = lax.broadcasted_iota(jnp.int32, (ny, nz), 0)
    lane = lax.broadcasted_iota(jnp.int32, (ny, nz), 1)
    table = [lame_of(ids_ref[sub, x], table_ref) for x in range(layers)]

    def weight(one, two, direction):
        shear = 0.5 * (one[0] + two[0])
        dilate = 0.5 * (one[1] + two[1])
        return shear + jnp.where(comp == direction, shear + dilate, 0.0)

    def ahead(field, axis):
        size = field.shape[axis]
        index = row if axis == 0 else lane
        return jnp.where(index == size - 1, 0.0, pltpu.roll(field, size - 1, axis=axis))

    def behind(field, axis):
        index = row if axis == 0 else lane
        return jnp.where(index == 0, 0.0, pltpu.roll(field, 1, axis=axis))

    nothing = (jnp.zeros((ny, nz), F32),) * 2
    previous = weight(table[0], nothing, 0) * edge_ref[0].astype(F32)
    for x in range(layers):
        diagonal = previous
        forward = []
        if x + 1 < layers:
            face = weight(table[x], table[x + 1], 0)
            diagonal = diagonal + face
            previous = face
            forward.append(face)
        else:
            forward.append(jnp.zeros((ny, nz), F32))
        for axis in (0, 1):
            index, size = (row, ny) if axis == 0 else (lane, nz)
            other = tuple(ahead(value, axis) for value in table[x])
            face = weight(table[x], other, axis + 1)
            before = tuple(behind(value, axis) for value in table[x])
            diagonal = diagonal + face + weight(table[x], before, axis + 1)
            forward.append(jnp.where(index == size - 1, 0.0, face))
        coef[x, 0] = 0.5 * diagonal
        for kind in range(3):
            coef[x, kind + 1] = forward[kind]
        fields[x] = basis_ref[sub, :, comp, x].astype(F32).reshape(funcs * ny, nz)

    total = None
    for x in reversed(range(layers)):
        values = [fields[x, pl.ds(y, funcs, stride=ny), :] for y in range(ny)]
        for y in range(ny):
            value = values[y]
            turned[x % 2, y] = value
            image = coef[x, 0, y : y + 1, :] * value
            image = image - coef[x, 3, y : y + 1, :] * pltpu.roll(value, nz - 1, axis=1)
            if y + 1 < ny:
                image = image - coef[x, 2, y : y + 1, :] * values[y + 1]
            if x + 1 < layers:
                image = image - coef[x, 1, y : y + 1, :] * turned[(x + 1) % 2, y]
            high, low = split_two(image)
            left[:, y * nz : (y + 1) * nz] = value.astype(BF16)
            right[0:funcs, y * nz : (y + 1) * nz] = high
            right[funcs : 2 * funcs, y * nz : (y + 1) * nz] = low
        product = dot(right[...], left[...], NT)
        total = product if total is None else total + product

    @pl.when(comp == 0)
    def _():
        acc[...] = total

    @pl.when(comp > 0)
    def _():
        acc[...] += total

    @pl.when(comp == pl.num_programs(1) - 1)
    def _():
        out_ref[0] = acc[0:funcs] + acc[funcs : 2 * funcs]


def interior(edge, table, ids, basis, token):
    subs, funcs, comps, layers, ny, nz = basis.shape
    return pl.pallas_call(
        interior_kernel,
        grid=(subs, comps),
        in_specs=[SMEM, SMEM, VMEM, VMEM, ANY],
        out_specs=pl.BlockSpec((1, funcs, funcs), lambda s, c: (s, 0, 0)),
        out_shape=jax.ShapeDtypeStruct((subs, funcs, funcs), F32),
        scratch_shapes=[
            pltpu.VMEM((layers, funcs * ny, nz), F32),
            pltpu.VMEM((2, ny, funcs, nz), F32),
            pltpu.VMEM((layers, 4, ny, nz), F32),
            pltpu.VMEM((funcs, ny * nz), BF16),
            pltpu.VMEM((2 * funcs, ny * nz), BF16),
            pltpu.VMEM((2 * funcs, funcs), F32),
        ],
        compiler_params=pltpu.CompilerParams(vmem_limit_bytes=16 * 2**20),
        cost_estimate=LIGHT,
        name="interior",
    )(edge, table, ids, basis, token)


def face_kernel(flags_ref, table_ref, ids_ref, last_ref, halo_ref, token_ref, inner_ref, out_ref, *scratch):
    @pl.when(flags_ref[0] == 1)
    def _():
        last, halo, sems = scratch[-3:]
        copies = [
            pltpu.make_async_copy(last_ref, last, sems.at[0]),
            pltpu.make_async_copy(halo_ref, halo, sems.at[1]),
        ]
        for copy in copies:
            copy.start()
        for copy in copies:
            copy.wait()
        face_sums(table_ref, ids_ref, last, halo, inner_ref, out_ref, *scratch[:-3])


def face_sums(table_ref, ids_ref, last_ref, halo_ref, inner_ref, out_ref, mine, theirs, left, right):
    subs, layers, ny, nz = ids_ref.shape
    funcs = inner_ref.shape[1]
    comps = last_ref.shape[1] // funcs
    for sub in range(subs):
        shear, dilate = lame_of(ids_ref[sub, layers - 1], table_ref)
        shear = 0.5 * (shear + halo_ref[sub, comps * funcs].astype(F32))
        dilate = 0.5 * (dilate + halo_ref[sub, comps * funcs + 1].astype(F32))
        total = None
        for comp in range(comps):
            weight = shear + (shear + dilate) if comp == 0 else shear
            slot = (sub * comps + comp) % 2
            mine[slot] = last_ref[sub, comp * funcs : (comp + 1) * funcs].astype(F32).reshape(funcs * ny, nz)
            theirs[slot] = halo_ref[sub, comp * funcs : (comp + 1) * funcs].astype(F32).reshape(funcs * ny, nz)
            for y in range(ny):
                here = mine[slot, pl.ds(y, funcs, stride=ny), :]
                there = theirs[slot, pl.ds(y, funcs, stride=ny), :]
                high, low = split_two(weight[y : y + 1, :] * (here - there))
                left[slot, 0:funcs, y * nz : (y + 1) * nz] = here.astype(BF16)
                left[slot, funcs : 2 * funcs, y * nz : (y + 1) * nz] = there.astype(BF16)
                right[slot, 0:funcs, y * nz : (y + 1) * nz] = high
                right[slot, funcs : 2 * funcs, y * nz : (y + 1) * nz] = low
            product = dot(right[slot], left[slot], NT)
            total = product if total is None else total + product
        total = total[:, 0:funcs] - total[:, funcs : 2 * funcs]
        half = inner_ref[sub] + 0.5 * (total[0:funcs] + total[funcs : 2 * funcs])
        out_ref[sub] = half + half.T


def face(flags, table, ids, last, halo, token, inner):
    subs, layers, ny, nz = ids.shape
    funcs = inner.shape[1]
    return pl.pallas_call(
        face_kernel,
        in_specs=[SMEM, SMEM, VMEM, ANY, ANY, ANY, VMEM],
        out_specs=VMEM,
        out_shape=jax.ShapeDtypeStruct((subs, funcs, funcs), F32),
        scratch_shapes=[
            pltpu.VMEM((2, funcs * ny, nz), F32),
            pltpu.VMEM((2, funcs * ny, nz), F32),
            pltpu.VMEM((2, 2 * funcs, ny * nz), BF16),
            pltpu.VMEM((2, 2 * funcs, ny * nz), BF16),
            pltpu.VMEM(last.shape, BF16),
            pltpu.VMEM(halo.shape, BF16),
            pltpu.SemaphoreType.DMA((2,)),
        ],
        compiler_params=pltpu.CompilerParams(vmem_limit_bytes=16 * 2**20),
        cost_estimate=LIGHT,
        name="face",
    )(flags, table, ids, last, halo, token, inner)


def spread(gal_ref, column_ids_ref, row_ids_ref, size):
    subs, funcs = column_ids_ref.shape[0:2]
    added = jnp.zeros((size, size), F32)
    lane = lax.broadcasted_iota(jnp.int32, (funcs, size), 1)
    row = lax.broadcasted_iota(jnp.int32, (size, funcs), 0)
    for sub in range(subs):
        slots = (column_ids_ref[sub] == lane).astype(F32)
        slots_t = (row_ids_ref[sub] == row).astype(F32)
        added = added + exact_dot(slots_t, exact_dot(gal_ref[sub], slots))
    return added


def assemble_kernel(flags_ref, token_ref, column_ids_ref, row_ids_ref, slab_ref, head_ref, *rest):
    gal_refs, (message_ref, sum_ref) = rest[:-2], rest[-2:]
    size = message_ref.shape[0]
    mode, own = flags_ref[0], flags_ref[1]
    message_ref[...] = jnp.zeros_like(message_ref)

    @pl.when((mode == 1) & (own == 1))
    def _():
        total = gal_refs[0][...]
        for gal_ref in gal_refs[1:]:
            total = total + gal_ref[...]
        sum_ref[...] = total
        added = spread(sum_ref, column_ids_ref, row_ids_ref, size)
        message_ref[...] = added + slab_ref[...].astype(F32)

    @pl.when((mode == 2) & (own == 1))
    def _():
        message_ref[...] = head_ref[...].astype(F32)


def assemble(flags, token, ids, slab, head, parts):
    size = slab.shape[1]
    block = pl.BlockSpec((size, size), lambda i: (0, 0))
    return pl.pallas_call(
        assemble_kernel,
        grid=(1,),
        in_specs=[SMEM, ANY, VMEM, VMEM, block, block] + [VMEM] * len(parts),
        out_specs=VMEM,
        out_shape=jax.ShapeDtypeStruct((size, size), F32),
        scratch_shapes=[pltpu.VMEM(parts[0].shape, F32)],
        cost_estimate=LIGHT,
        name="assemble",
    )(flags, token, ids[:, :, None], ids[:, None, :], slab, head, *parts)


def factor_kernel(flags_ref, token_ref, *refs, parts, groups):
    message_refs, gal_refs = refs[:parts], refs[parts:-3]
    summary_ref, block_ref, work = refs[-3:]
    subs, funcs = gal_refs[0].shape[0:2]
    size = summary_ref.shape[1]
    rows = 2 * size
    diagonal = message_refs[0][...]
    for message_ref in message_refs[1:]:
        diagonal = diagonal + message_ref[...]
    block_ref[...] = diagonal

    @pl.when(flags_ref[0] == 1)
    def _():
        row = lax.broadcasted_iota(jnp.int32, (size, size), 0)
        lane = lax.broadcasted_iota(jnp.int32, (size, size), 1)
        work[:, 0:size] = 0.5 * (diagonal + diagonal.T)
        work[:, size : 2 * size] = (row == lane).astype(F32)
        index = lax.broadcasted_iota(jnp.int32, (BLOCK, size), 0)
        for start in range(0, size, BLOCK):
            panel = work[start : start + BLOCK, 0:size]
            extra = work[start : start + BLOCK, size : 2 * size]
            columns = [
                jnp.broadcast_to(panel[:, start + step : start + step + 1], (BLOCK, size))
                for step in range(BLOCK)
            ]
            for step in range(BLOCK):
                scale = lax.rsqrt(columns[step][step : step + 1, :])
                column = jnp.where(index > step, columns[step] * scale, 0.0)
                for later in range(step + 1, BLOCK):
                    columns[later] = columns[later] - column * column[later : later + 1, :]
                pivot = panel[step : step + 1, :] * scale
                panel = jnp.where(index == step, pivot, panel - column * pivot)
                pivot = extra[step : step + 1, :] * scale
                extra = jnp.where(index == step, pivot, extra - column * pivot)
            work[start : start + BLOCK, 0:size] = panel
            work[start : start + BLOCK, size : 2 * size] = extra
            rest = start + BLOCK
            if rest < size:
                both = jnp.concatenate([panel, extra], axis=1)
                work[rest:size, :] -= exact_dot(panel[:, rest:size], both, TN)
        upper = jnp.where(row <= lane, work[:, 0:size], 0.0)
        summary_ref[0:size] = jnp.where(row >= lane, work[:, size : 2 * size], 0.0).T
        summary_ref[size : 2 * size] = upper.T
        each = len(gal_refs) // groups
        for group in range(groups):

            @pl.when(flags_ref[1] == group)
            def _(chosen=gal_refs[group * each : (group + 1) * each]):
                for sub in range(subs):
                    begin = rows + sub * funcs
                    total = chosen[0][sub]
                    for gal_ref in chosen[1:]:
                        total = total + gal_ref[sub]
                    summary_ref[begin : begin + funcs, 0:funcs] = total
                    summary_ref[begin : begin + funcs, funcs:size] = jnp.zeros((funcs, size - funcs), F32)


def factorize(flags, token, messages, groups):
    size = messages[0].shape[1]
    subs, funcs = groups[0][0].shape[0:2]
    parts = [part for group in groups for part in group]
    return pl.pallas_call(
        functools.partial(factor_kernel, parts=len(messages), groups=len(groups)),
        in_specs=[SMEM, ANY] + [VMEM] * (len(messages) + len(parts)),
        out_specs=[VMEM] * 2,
        out_shape=[
            jax.ShapeDtypeStruct((2 * size + subs * funcs, size), F32),
            jax.ShapeDtypeStruct((size, size), F32),
        ],
        scratch_shapes=[pltpu.VMEM((size, 2 * size), F32)],
        cost_estimate=LIGHT,
        name="factorize",
    )(flags, token, *messages, *parts)


def prepare_kernel(flags_ref, token_ref, column_ids_ref, row_ids_ref, head_ref, *rest, sources):
    summary_refs = rest[:sources]
    weights_ref, rows_ref, lower_ref, added_ref, gal_ref, summary, sem = rest[sources:]
    subs, funcs = gal_ref.shape[0:2]
    size = head_ref.shape[0]
    choice, mode, own = flags_ref[0], flags_ref[1], flags_ref[2]
    for number, summary_ref in enumerate(summary_refs):

        @pl.when(choice == number)
        def _(summary_ref=summary_ref):
            copy = pltpu.make_async_copy(summary_ref, summary, sem)
            copy.start()
            copy.wait()

    for sub in range(subs):
        begin = 2 * size + sub * funcs
        gal_ref[sub] = summary[begin : begin + funcs, 0:funcs]

    def doubled(block):
        nothing = jnp.zeros((size, size), BF16)
        top = jnp.concatenate([block, nothing], axis=1)
        return jnp.concatenate([top, jnp.concatenate([nothing, block], axis=1)], axis=0)

    @pl.when(mode > 0)
    def _():
        inverse = summary[0:size]
        high = inverse.astype(BF16)
        weights_ref[0 : 2 * size] = doubled(high)
        weights_ref[2 * size : 4 * size] = doubled((inverse - high.astype(F32)).astype(BF16))
        lower_ref[...] = summary[size : 2 * size]

    @pl.when(mode == 2)
    def _():
        solved = exact_dot(head_ref[...], summary[0:size])
        rows_ref[...] = doubled(solved.T.astype(BF16))

    @pl.when((mode == 2) & (own == 1))
    def _():
        added_ref[...] = spread(gal_ref, column_ids_ref, row_ids_ref, size)


def prepare(flags, token, ids, head, summaries):
    size = head.shape[0]
    subs, funcs = ids.shape
    return pl.pallas_call(
        functools.partial(prepare_kernel, sources=len(summaries)),
        in_specs=[SMEM, ANY] + [VMEM] * 3 + [ANY] * len(summaries),
        out_specs=[VMEM] * 5,
        out_shape=[
            jax.ShapeDtypeStruct((4 * size, 2 * size), BF16),
            jax.ShapeDtypeStruct((2 * size, 2 * size), BF16),
            jax.ShapeDtypeStruct((size, size), F32),
            jax.ShapeDtypeStruct((size, size), F32),
            jax.ShapeDtypeStruct((subs, funcs, funcs), F32),
        ],
        scratch_shapes=[pltpu.VMEM(summaries[0].shape, F32), pltpu.SemaphoreType.DMA],
        compiler_params=pltpu.CompilerParams(vmem_limit_bytes=16 * 2**20),
        cost_estimate=LIGHT,
        name="prepare",
    )(flags, token, ids[:, :, None], ids[:, None, :], head, *summaries)


def panel_kernel(
    flags_ref, lower_ref, weights_ref, rows_ref, added_ref, slab_ref, *rest, pieces, spans, first
):
    hops = len(pieces) // len(spans)
    others = rest[: len(pieces)]
    out_ref, column, sems = rest[-3:]
    tile, size = out_ref.shape
    half = tile // 2
    mode, head, own, which = flags_ref[0], flags_ref[1], flags_ref[2], flags_ref[3]
    step, steps = pl.program_id(0), pl.num_programs(0)
    top = first & (step == 0)

    def copy_of(at, act):
        for number, (begin, end) in enumerate(spans):
            for hop in range(hops):

                @pl.when((mode == 2) & (which == hop) & (at >= begin) & (at < end))
                def _(other_ref=others[number * hops + hop], begin=begin):
                    source = other_ref.at[pl.ds(pl.multiple_of((at - begin) * tile, tile), tile)]
                    act(pltpu.make_async_copy(source, column.at[at % 2], sems.at[at % 2]))

    @pl.when(step == 0)
    def _():
        copy_of(step, lambda copy: copy.start())

    @pl.when(step + 1 < steps)
    def _():
        copy_of(step + 1, lambda copy: copy.start())

    def side_by_side(value):
        return jnp.concatenate([value[0:half], value[half:tile]], axis=1)

    def factor_of(pair):
        return dot(jnp.concatenate([pair, pair], axis=1), weights_ref[...])

    def head_of(value):
        solved = factor_of(jnp.concatenate([value] * 2, axis=1))[:, 0:size]
        solved = jnp.where(head == 1, lower_ref[...], solved)
        return jnp.where(head == 2, 0.0, solved).astype(BF16)

    @pl.when(mode == 0)
    def _():
        out_ref[...] = slab_ref[...]

    @pl.when(mode == 1)
    def _():
        factor = factor_of(side_by_side(slab_ref[...])).astype(BF16)
        out_ref[0:half] = factor[:, 0:size]
        out_ref[half:tile] = factor[:, size : 2 * size]

        @pl.when(top)
        def _():
            out_ref[0:size] = head_of(slab_ref[0:size])

    @pl.when(mode == 2)
    def _():
        copy_of(step, lambda copy: copy.wait())
        factor = factor_of(side_by_side(column[step % 2])).astype(BF16)
        update = dot(factor, rows_ref[...])
        out_ref[0:half] = (slab_ref[0:half].astype(F32) - update[:, 0:size]).astype(BF16)
        out_ref[half:tile] = (slab_ref[half:tile].astype(F32) - update[:, size : 2 * size]).astype(BF16)

        @pl.when(top)
        def _():
            begin = head_of(column[0, 0:size])
            update = dot(begin, rows_ref[0:size, 0:size])
            base = slab_ref[0:size].astype(F32)
            out_ref[0:size] = (base - update).astype(BF16)

            @pl.when(own == 1)
            def _():
                out_ref[0:size] = (base + added_ref[...] - update).astype(BF16)


def panel(flags, lower, weights, rows, added, slab, parts, old, start, tile):
    size = slab.shape[1]
    offset = start // tile
    spans, begin, operands = [], 0, []
    for hops in parts:
        end = begin + hops[0].shape[0] // tile
        spans.append((begin, end))
        begin = end
        operands += hops
    blocks = [
        SMEM,
        pl.BlockSpec((size, size), lambda i: (0, 0)),
        pl.BlockSpec(weights.shape, lambda i: (0, 0)),
        pl.BlockSpec(rows.shape, lambda i: (0, 0)),
        pl.BlockSpec((size, size), lambda i: (0, 0)),
        pl.BlockSpec((tile, size), lambda i: (i + offset, 0)),
    ] + [ANY] * len(operands)
    pieces = len(operands)
    operands = [flags, lower, weights, rows, added, slab] + operands
    aliases = {}
    if old is not None:
        aliases = {len(operands): 0}
        blocks.append(ANY)
        operands.append(old)
    return pl.pallas_call(
        functools.partial(panel_kernel, pieces=range(pieces), spans=spans, first=start == 0),
        grid=(begin,),
        in_specs=blocks,
        out_specs=pl.BlockSpec((tile, size), lambda i: (i + offset, 0)),
        out_shape=jax.ShapeDtypeStruct(slab.shape, BF16),
        input_output_aliases=aliases,
        scratch_shapes=[pltpu.VMEM((2, tile, size), BF16), pltpu.SemaphoreType.DMA((2,))],
        compiler_params=pltpu.CompilerParams(vmem_limit_bytes=16 * 2**20),
        cost_estimate=LIGHT,
        name="panel",
    )(*operands)


def broadcast(value, axis, source):
    kept = jnp.where(lax.axis_index(axis) == source, value, 0).astype(value.dtype)
    return lax.psum(kept, axis)


def settings(*values):
    return jnp.stack([jnp.asarray(value).astype(jnp.int32) for value in values])


def holder_pairs(wide, narrow, distance):
    stride = wide // narrow
    found = []
    for n in range(narrow):
        for start in range(0, wide, 2 * distance):
            source = (n * stride) ^ start
            found.append((source * narrow + n, (source ^ distance) * narrow + n))
    return found


class Order:
    def __init__(self, token):
        self.token = token

    def after(self, value):
        value, self.token = lax.optimization_barrier((value, self.token))
        return value


def known_owner(owner, coarse_basis, material_ids, lame_table, coarse_ids, coarse_slab):
    narrow, wide = lax.axis_size("narrow"), lax.axis_size("wide")
    stride = wide // narrow
    wide_index, narrow_index = lax.axis_index("wide"), lax.axis_index("narrow")
    height, block = coarse_slab.shape
    own = wide_index == narrow_index * stride
    later = narrow_index > owner
    which = jnp.where(later, narrow_index - owner - 1, -1)
    mode = jnp.where(narrow_index == owner, 1, jnp.where(later, 2, 0))
    earlier = (wide_index % stride == 0) & (wide_index // stride < owner)
    kind = jnp.where(wide_index == owner * stride, 1, jnp.where(earlier, 2, 0))
    table = lame_table.astype(F32)
    hops = narrow - 1 - owner
    units, joined, plan = PLANS[hops]
    unit = height // sum(units)
    count = len(units)
    bounds, low = [], 0
    for number in units:
        bounds.append((low, low + number * unit))
        low += number * unit
    axes = ("wide", "narrow")

    def rows_of(number):
        low, high = bounds[number]
        return coarse_slab[low:high]

    def send(value, source, target):
        return lax.ppermute(value, "narrow", [(owner + source, owner + target)])

    order = Order(settings(mode))

    ways = [((n * stride) * narrow + owner, (n * stride) * narrow + n) for n in range(owner + 1, narrow)]
    head = order.after(lax.ppermute(coarse_slab[:block], axes, ways))
    moved = {0: [send(order.after(rows_of(0)), 0, hops)]}

    groups = [[w for w in range(wide) if w % stride == 0], [w for w in range(wide) if w % stride]]
    groups = [group for group in groups if group]
    member = jnp.where(wide_index % stride == 0, 0, 1)

    def within(group, pairs):
        return [(w * narrow + one, w * narrow + two) for w in group for one, two in pairs]

    def halo_of(group, message):
        return lax.ppermute(message, axes, within(group, [(i + 1, i) for i in range(narrow - 1)]))

    first, last = halo_message(table, material_ids, order.token, coarse_basis)
    first = order.after(first)
    halos = [halo_of(groups[0], first)]
    edge = (narrow_index == 0).astype(jnp.int32).reshape(1)
    inner = order.after(interior(edge, table, material_ids, coarse_basis, order.token))
    if joined:
        whole = send(order.after(coarse_slab[bounds[joined[0]][0] : bounds[joined[-1]][1]]), 0, 1)
    else:
        moved[1] = [send(order.after(rows_of(1)), 0, 1)]
    halos[0] = order.after(halos[0])
    for group in groups[1:]:
        halos.append(halo_of(group, order.after(first)))

    def nearest(base, extent):
        return min(range(base, min(base + extent, narrow)), key=lambda n: abs(n - owner))

    def summed(parts, distance, group):
        total = parts[0] if len(parts) == 1 else parts[0] + parts[1]
        pairs = []
        for base in range(0, narrow - distance, 2 * distance):
            one, two = nearest(base, distance), nearest(base + distance, distance)
            pairs.append((two, one) if nearest(base, 2 * distance) == one else (one, two))
        return [total, lax.ppermute(total, axes, within(group, pairs))], 2 * distance

    def faces_of(number):
        flag = settings(member == number)
        return [order.after(face(flag, table, material_ids, last, halos[number], order.token, inner))]

    sums, reach = [faces_of(0)], [1]
    while reach[0] < narrow:
        sums[0], reach[0] = summed(sums[0], reach[0], groups[0])
    if not joined:
        for number in range(2, count - 1):
            moved[number] = [send(order.after(rows_of(number)), 0, 1)]
    distance, messages, left = wide // 2, [], plan.count("spread")
    for step in plan:
        if step == "assemble":
            message = assemble(settings(mode, own), order.token, coarse_ids, coarse_slab, head, sums[0])
            message = order.after(message)
        elif step == "others":
            for number in range(1, len(groups)):
                halos[number] = order.after(halos[number])
                parts, far = summed(faces_of(number), 1, groups[number])
                sums.append(parts)
                reach.append(far)
        elif step == "more":
            for number in range(1, len(groups)):
                while reach[number] < narrow:
                    sums[number][1] = order.after(sums[number][1])
                    sums[number], reach[number] = summed(sums[number], reach[number], groups[number])
        elif step == "spread":
            left -= 1
            while distance:
                received = order.after(lax.ppermute(message, axes, holder_pairs(wide, narrow, distance)))
                messages = [message, received]
                if distance > 1:
                    message = message + received
                distance //= 2
                if left:
                    break
        elif step == "factor":
            summary, head = factorize(settings(mode, member), order.token, messages, sums)
            summary = order.after(summary)
            summaries = [summary] + [
                lax.ppermute(summary, "narrow", [(owner, (owner + place) % narrow)]) for place in range(1, narrow)
            ]
            moved[count - 1] = [send(order.after(rows_of(count - 1)), 0, 1)]
            for place in range(1, hops + 1):
                summaries[place] = order.after(summaries[place])
        else:
            number, hop = step
            if joined and step == (joined[0], 0):
                whole = order.after(whole)
                for part in joined:
                    low, high = (bound - bounds[joined[0]][0] for bound in bounds[part])
                    moved[part] = [whole[low:high]]
            moving = moved[number][hop] = order.after(moved[number][hop])
            if number == 0 and hop + 1 < hops:
                moved[number].append(send(moving, hops - hop, hops - hop - 1))
            elif number != 0 and hop + 1 < hops:
                moved[number].append(send(moving, hop + 1, hop + 2))
    pieces = [moved[0][::-1]] + [moved[number] for number in range(1, count)]

    choice = (narrow_index - owner) % narrow
    weights, rows, lower, added, galerkin = prepare(
        settings(choice, mode, own), order.token, coarse_ids, head, summaries
    )
    flags = settings(mode, kind, own, which)
    result = None
    for begin, end in ((0, count - 2), (count - 2, count - 1), (count - 1, count)):
        result = panel(
            flags, lower, weights, rows, added, coarse_slab, pieces[begin:end], result, bounds[begin][0], 2 * unit
        )
    return result, galerkin


def any_owner(owner, coarse_basis, material_ids, lame_table, coarse_ids, coarse_slab):
    narrow, wide = lax.axis_size("narrow"), lax.axis_size("wide")
    stride = wide // narrow
    wide_index, narrow_index = lax.axis_index("wide"), lax.axis_index("narrow")
    own = wide_index == narrow_index * stride
    later = narrow_index > owner
    which = jnp.where(later, 0, -1)
    mode = jnp.where(narrow_index == owner, 1, jnp.where(later, 2, 0))
    earlier = (wide_index % stride == 0) & (wide_index // stride < owner)
    kind = jnp.where(wide_index == owner * stride, 1, jnp.where(earlier, 2, 0))
    table = lame_table.astype(F32)
    column = broadcast(coarse_slab, "narrow", owner)
    first, last = halo_message(table, material_ids, table, coarse_basis)
    halo = lax.ppermute(first, "narrow", [(i + 1, i) for i in range(narrow - 1)])
    edge = (narrow_index == 0).astype(jnp.int32).reshape(1)
    inner = interior(edge, table, material_ids, coarse_basis, first)
    partial = face(settings(1), table, material_ids, last, halo, first, inner)
    parts = [lax.psum(partial, "narrow")]
    message = assemble(settings(mode, own), first, coarse_ids, coarse_slab, column, parts)
    at_owner = (wide_index == owner * stride) & (narrow_index == owner)
    diagonal = lax.psum(jnp.where(at_owner, message, 0.0), ("wide", "narrow"))
    summary, _ = factorize(settings(1, 0), first, [diagonal], [parts])
    head = broadcast(message, "wide", narrow_index * stride)
    weights, rows, lower, added, galerkin = prepare(settings(0, mode, own), settings(mode), coarse_ids, head, [summary])
    flags = settings(mode, kind, own, which)
    tile = coarse_slab.shape[0] // 12
    result = panel(flags, lower, weights, rows, added, coarse_slab, [[column]], None, 0, tile)
    return result, galerkin


def on_device(coarse_basis, material_ids, lame_table, coarse_ids, coarse_slab, panel_owner):
    narrow, wide = lax.axis_size("narrow"), lax.axis_size("wide")
    arrays = (coarse_basis, material_ids, lame_table, coarse_ids, coarse_slab)
    owner = panel_owner[0]
    if narrow - 1 > len(PLANS) or wide & (wide - 1):
        return any_owner(owner, *arrays)
    branches = [functools.partial(known_owner, place) for place in range(narrow - 1)]
    return lax.switch(owner, branches, *arrays)


def solution(mesh):
    return jax.shard_map(
        on_device,
        mesh=mesh,
        in_specs=(
            P("wide", None, None, "narrow", None, None),
            P("wide", "narrow", None, None),
            P(),
            P("wide", None),
            P("wide", "narrow"),
            P(),
        ),
        out_specs=(P("wide", "narrow"), P("wide", None, None)),
        check_vma=False,
    )
```

```python
import functools

import jax
import jax.numpy as jnp
from jax import lax
from jax.experimental import pallas as pl
from jax.experimental.pallas import tpu as pltpu
from jax.sharding import PartitionSpec as P

F32, BF16 = jnp.float32, jnp.bfloat16
NT = (((1,), (1,)), ((), ()))
TN = (((0,), (0,)), ((), ()))
VMEM = pl.BlockSpec(memory_space=pltpu.VMEM)
ANY = pl.BlockSpec(memory_space=pl.ANY)
SMEM = pl.BlockSpec(memory_space=pltpu.SMEM)
PLANS = {
    1: (
        (14, 8, 2),
        (),
        ("assemble", "spread", "others", "spread", "more", "spread", "factor", ("panel", 0, 2), ("panel", 2, 3)),
    ),
    2: (
        (14, 4, 4, 2),
        (),
        (
            "assemble", "spread", "others", "spread", "more", (0, 0), "spread", (1, 0), "factor",
            (2, 0), ("panel", 1, 2), (3, 0), ("panel", 2, 3), ("panel", 0, 1), ("panel", 3, 4),
        ),
    ),
    3: (
        (12, 4, 4, 2, 2),
        (1, 2, 3),
        (
            "assemble", "spread", "others", (0, 0), "spread", "more", "spread", "factor",
            (1, 0), (1, 1), (0, 1), (2, 0), (2, 1), (3, 0), ("panel", 1, 2), (3, 1), (4, 0), ("panel", 2, 3), (4, 1),
            ("panel", 0, 1), ("panel", 3, 5),
        ),
    ),
}
BLOCK = 16
LIGHT = pl.CostEstimate(flops=1, bytes_accessed=1, transcendentals=0)


def exact_dot(left, right, dims=(((1,), (0,)), ((), ()))):
    return lax.dot_general(
        left, right, dims, precision=lax.Precision.HIGHEST, preferred_element_type=F32
    )


def dot(left, right, dims=(((1,), (0,)), ((), ()))):
    return lax.dot_general(left, right, dims, preferred_element_type=F32)


def split_two(value):
    high = value.astype(BF16)
    return high, (value - high.astype(F32)).astype(BF16)


def lame_of(ids, table_ref):
    shear = jnp.zeros(ids.shape, F32)
    dilate = jnp.zeros(ids.shape, F32)
    for material in range(table_ref.shape[1]):
        chosen = ids == material
        shear = jnp.where(chosen, table_ref[0, material], shear)
        dilate = jnp.where(chosen, table_ref[1, material], dilate)
    return shear, dilate


def halo_kernel(table_ref, ids_ref, token_ref, basis_ref, slab_ref, out_ref, last_ref, *rest, spans):
    piece_refs, sems = rest[:-1], rest[-1]
    subs, funcs, comps, layers = basis_ref.shape[0:4]
    copies = []
    for number, ((low, high), piece_ref) in enumerate(zip(spans, piece_refs)):
        copies.append(pltpu.make_async_copy(slab_ref.at[pl.ds(low, high - low)], piece_ref, sems.at[number]))
        copies[-1].start()
    for sub in range(subs):
        for comp in range(comps):
            out_ref[sub, comp * funcs : (comp + 1) * funcs] = basis_ref[sub, :, comp, 0]
            last_ref[sub, comp * funcs : (comp + 1) * funcs] = basis_ref[sub, :, comp, layers - 1]
        shear, dilate = lame_of(ids_ref[sub, 0], table_ref)
        out_ref[sub, comps * funcs] = shear.astype(BF16)
        out_ref[sub, comps * funcs + 1] = dilate.astype(BF16)
    for copy in copies:
        copy.wait()


def halo_message(table, ids, token, basis, slab, spans):
    subs, funcs, comps, layers, ny, nz = basis.shape
    return pl.pallas_call(
        functools.partial(halo_kernel, spans=spans),
        in_specs=[SMEM, VMEM, ANY, VMEM, ANY],
        out_specs=[VMEM, VMEM] + [ANY] * len(spans),
        out_shape=[
            jax.ShapeDtypeStruct((subs, comps * funcs + 2, ny, nz), BF16),
            jax.ShapeDtypeStruct((subs, comps * funcs, ny, nz), BF16),
        ]
        + [jax.ShapeDtypeStruct((high - low, slab.shape[1]), BF16) for low, high in spans],
        scratch_shapes=[pltpu.SemaphoreType.DMA((max(1, len(spans)),))],
        compiler_params=pltpu.CompilerParams(vmem_limit_bytes=16 * 2**20),
        cost_estimate=LIGHT,
        name="halo_message",
    )(table, ids, token, basis, slab)


def interior_kernel(edge_ref, table_ref, ids_ref, basis_ref, token_ref, out_ref, fields, turned, coef, left, right, acc):
    sub, comp = pl.program_id(0), pl.program_id(1)
    layers, ny, nz = basis_ref.shape[3:]
    funcs = basis_ref.shape[1]
    row = lax.broadcasted_iota(jnp.int32, (ny, nz), 0)
    lane = lax.broadcasted_iota(jnp.int32, (ny, nz), 1)
    table = [lame_of(ids_ref[sub, x], table_ref) for x in range(layers)]

    def weight(one, two, direction):
        shear = 0.5 * (one[0] + two[0])
        dilate = 0.5 * (one[1] + two[1])
        return shear + jnp.where(comp == direction, shear + dilate, 0.0)

    def ahead(field, axis):
        size = field.shape[axis]
        index = row if axis == 0 else lane
        return jnp.where(index == size - 1, 0.0, pltpu.roll(field, size - 1, axis=axis))

    def behind(field, axis):
        index = row if axis == 0 else lane
        return jnp.where(index == 0, 0.0, pltpu.roll(field, 1, axis=axis))

    nothing = (jnp.zeros((ny, nz), F32),) * 2
    previous = weight(table[0], nothing, 0) * edge_ref[0].astype(F32)
    for x in range(layers):
        diagonal = previous
        forward = []
        if x + 1 < layers:
            face = weight(table[x], table[x + 1], 0)
            diagonal = diagonal + face
            previous = face
            forward.append(face)
        else:
            forward.append(jnp.zeros((ny, nz), F32))
        for axis in (0, 1):
            index, size = (row, ny) if axis == 0 else (lane, nz)
            other = tuple(ahead(value, axis) for value in table[x])
            face = weight(table[x], other, axis + 1)
            before = tuple(behind(value, axis) for value in table[x])
            diagonal = diagonal + face + weight(table[x], before, axis + 1)
            forward.append(jnp.where(index == size - 1, 0.0, face))
        coef[x, 0] = 0.5 * diagonal
        for kind in range(3):
            coef[x, kind + 1] = forward[kind]
        fields[x] = basis_ref[sub, :, comp, x].astype(F32).reshape(funcs * ny, nz)

    total = None
    for x in reversed(range(layers)):
        values = [fields[x, pl.ds(y, funcs, stride=ny), :] for y in range(ny)]
        for y in range(ny):
            value = values[y]
            turned[x % 2, y] = value
            image = coef[x, 0, y : y + 1, :] * value
            image = image - coef[x, 3, y : y + 1, :] * pltpu.roll(value, nz - 1, axis=1)
            if y + 1 < ny:
                image = image - coef[x, 2, y : y + 1, :] * values[y + 1]
            if x + 1 < layers:
                image = image - coef[x, 1, y : y + 1, :] * turned[(x + 1) % 2, y]
            high, low = split_two(image)
            left[:, y * nz : (y + 1) * nz] = value.astype(BF16)
            right[0:funcs, y * nz : (y + 1) * nz] = high
            right[funcs : 2 * funcs, y * nz : (y + 1) * nz] = low
        product = dot(right[...], left[...], NT)
        total = product if total is None else total + product

    @pl.when(comp == 0)
    def _():
        acc[...] = total

    @pl.when(comp > 0)
    def _():
        acc[...] += total

    @pl.when(comp == pl.num_programs(1) - 1)
    def _():
        out_ref[0] = acc[0:funcs] + acc[funcs : 2 * funcs]


def interior(edge, table, ids, basis, token):
    subs, funcs, comps, layers, ny, nz = basis.shape
    return pl.pallas_call(
        interior_kernel,
        grid=(subs, comps),
        in_specs=[SMEM, SMEM, VMEM, VMEM, ANY],
        out_specs=pl.BlockSpec((1, funcs, funcs), lambda s, c: (s, 0, 0)),
        out_shape=jax.ShapeDtypeStruct((subs, funcs, funcs), F32),
        scratch_shapes=[
            pltpu.VMEM((layers, funcs * ny, nz), F32),
            pltpu.VMEM((2, ny, funcs, nz), F32),
            pltpu.VMEM((layers, 4, ny, nz), F32),
            pltpu.VMEM((funcs, ny * nz), BF16),
            pltpu.VMEM((2 * funcs, ny * nz), BF16),
            pltpu.VMEM((2 * funcs, funcs), F32),
        ],
        compiler_params=pltpu.CompilerParams(vmem_limit_bytes=16 * 2**20),
        cost_estimate=LIGHT,
        name="interior",
    )(edge, table, ids, basis, token)


def face_kernel(flags_ref, table_ref, ids_ref, last_ref, halo_ref, token_ref, inner_ref, out_ref, *scratch):
    @pl.when(flags_ref[0] == 1)
    def _():
        last, halo, sems = scratch[-3:]
        copies = [
            pltpu.make_async_copy(last_ref, last, sems.at[0]),
            pltpu.make_async_copy(halo_ref, halo, sems.at[1]),
        ]
        for copy in copies:
            copy.start()
        for copy in copies:
            copy.wait()
        face_sums(table_ref, ids_ref, last, halo, inner_ref, out_ref, *scratch[:-3])


def face_sums(table_ref, ids_ref, last_ref, halo_ref, inner_ref, out_ref, mine, theirs, left, right, weights, acc):
    subs, layers, ny, nz = ids_ref.shape
    funcs = inner_ref.shape[1]
    comps = last_ref.shape[1] // funcs

    @pl.loop(0, subs)
    def _(sub):
        shear, dilate = lame_of(ids_ref[sub, layers - 1], table_ref)
        weights[0] = 0.5 * (shear + halo_ref[sub, comps * funcs].astype(F32))
        weights[1] = 0.5 * (dilate + halo_ref[sub, comps * funcs + 1].astype(F32))

        @pl.loop(0, comps)
        def _(comp):
            weight = weights[0] + jnp.where(comp == 0, weights[0] + weights[1], 0.0)
            rows = pl.ds(comp * funcs, funcs)
            mine[...] = last_ref[sub, rows].astype(F32).reshape(funcs * ny, nz)
            theirs[...] = halo_ref[sub, rows].astype(F32).reshape(funcs * ny, nz)
            for y in range(ny):
                here = mine[pl.ds(y, funcs, stride=ny), :]
                there = theirs[pl.ds(y, funcs, stride=ny), :]
                high, low = split_two(weight[y : y + 1, :] * (here - there))
                left[0:funcs, y * nz : (y + 1) * nz] = here.astype(BF16)
                left[funcs : 2 * funcs, y * nz : (y + 1) * nz] = there.astype(BF16)
                right[0:funcs, y * nz : (y + 1) * nz] = high
                right[funcs : 2 * funcs, y * nz : (y + 1) * nz] = low
            product = dot(right[...], left[...], NT)

            @pl.when(comp == 0)
            def _():
                acc[...] = product

            @pl.when(comp > 0)
            def _():
                acc[...] += product

        total = acc[:, 0:funcs] - acc[:, funcs : 2 * funcs]
        half = inner_ref[sub] + 0.5 * (total[0:funcs] + total[funcs : 2 * funcs])
        out_ref[sub] = half + half.T


def face(flags, table, ids, last, halo, token, inner):
    subs, layers, ny, nz = ids.shape
    funcs = inner.shape[1]
    return pl.pallas_call(
        face_kernel,
        in_specs=[SMEM, SMEM, VMEM, ANY, ANY, ANY, VMEM],
        out_specs=VMEM,
        out_shape=jax.ShapeDtypeStruct((subs, funcs, funcs), F32),
        scratch_shapes=[
            pltpu.VMEM((funcs * ny, nz), F32),
            pltpu.VMEM((funcs * ny, nz), F32),
            pltpu.VMEM((2 * funcs, ny * nz), BF16),
            pltpu.VMEM((2 * funcs, ny * nz), BF16),
            pltpu.VMEM((2, ny, nz), F32),
            pltpu.VMEM((2 * funcs, 2 * funcs), F32),
            pltpu.VMEM(last.shape, BF16),
            pltpu.VMEM(halo.shape, BF16),
            pltpu.SemaphoreType.DMA((2,)),
        ],
        compiler_params=pltpu.CompilerParams(vmem_limit_bytes=16 * 2**20),
        cost_estimate=LIGHT,
        name="face",
    )(flags, table, ids, last, halo, token, inner)


def spread(gal_ref, column_ids_ref, row_ids_ref, size):
    subs, funcs = column_ids_ref.shape[0:2]
    added = jnp.zeros((size, size), F32)
    lane = lax.broadcasted_iota(jnp.int32, (funcs, size), 1)
    row = lax.broadcasted_iota(jnp.int32, (size, funcs), 0)
    for sub in range(subs):
        slots = (column_ids_ref[sub] == lane).astype(F32)
        slots_t = (row_ids_ref[sub] == row).astype(F32)
        added = added + exact_dot(slots_t, exact_dot(gal_ref[sub], slots))
    return added


def assemble_kernel(flags_ref, token_ref, column_ids_ref, row_ids_ref, slab_ref, head_ref, *rest):
    gal_refs, (message_ref, sum_ref) = rest[:-2], rest[-2:]
    size = message_ref.shape[0]
    mode, own = flags_ref[0], flags_ref[1]
    message_ref[...] = jnp.zeros_like(message_ref)

    @pl.when((mode == 1) & (own == 1))
    def _():
        total = gal_refs[0][...]
        for gal_ref in gal_refs[1:]:
            total = total + gal_ref[...]
        sum_ref[...] = total
        added = spread(sum_ref, column_ids_ref, row_ids_ref, size)
        message_ref[...] = added + slab_ref[...].astype(F32)

    @pl.when((mode == 2) & (own == 1))
    def _():
        message_ref[...] = head_ref[...].astype(F32)


def assemble(flags, token, ids, slab, head, parts):
    size = slab.shape[1]
    block = pl.BlockSpec((size, size), lambda i: (0, 0))
    return pl.pallas_call(
        assemble_kernel,
        grid=(1,),
        in_specs=[SMEM, ANY, VMEM, VMEM, block, block] + [VMEM] * len(parts),
        out_specs=VMEM,
        out_shape=jax.ShapeDtypeStruct((size, size), F32),
        scratch_shapes=[pltpu.VMEM(parts[0].shape, F32)],
        cost_estimate=LIGHT,
        name="assemble",
    )(flags, token, ids[:, :, None], ids[:, None, :], slab, head, *parts)


def factor_kernel(flags_ref, token_ref, *refs, parts, groups):
    message_refs, gal_refs = refs[:parts], refs[parts:-3]
    summary_ref, block_ref, work = refs[-3:]
    subs, funcs = gal_refs[0].shape[0:2]
    size = summary_ref.shape[1]
    rows = 2 * size
    diagonal = message_refs[0][...]
    for message_ref in message_refs[1:]:
        diagonal = diagonal + message_ref[...]
    block_ref[...] = diagonal

    @pl.when(flags_ref[0] == 1)
    def _():
        row = lax.broadcasted_iota(jnp.int32, (size, size), 0)
        lane = lax.broadcasted_iota(jnp.int32, (size, size), 1)
        work[:, 0:size] = 0.5 * (diagonal + diagonal.T)
        work[:, size : 2 * size] = (row == lane).astype(F32)
        index = lax.broadcasted_iota(jnp.int32, (BLOCK, size), 0)
        for start in range(0, size, BLOCK):
            panel = work[start : start + BLOCK, 0:size]
            extra = work[start : start + BLOCK, size : 2 * size]
            columns = [
                jnp.broadcast_to(panel[:, start + step : start + step + 1], (BLOCK, size))
                for step in range(BLOCK)
            ]
            for step in range(BLOCK):
                scale = lax.rsqrt(columns[step][step : step + 1, :])
                column = jnp.where(index > step, columns[step] * scale, 0.0)
                for later in range(step + 1, BLOCK):
                    columns[later] = columns[later] - column * column[later : later + 1, :]
                pivot = panel[step : step + 1, :] * scale
                panel = jnp.where(index == step, pivot, panel - column * pivot)
                pivot = extra[step : step + 1, :] * scale
                extra = jnp.where(index == step, pivot, extra - column * pivot)
            work[start : start + BLOCK, 0:size] = panel
            work[start : start + BLOCK, size : 2 * size] = extra
            rest = start + BLOCK
            if rest < size:
                both = jnp.concatenate([panel, extra], axis=1)
                work[rest:size, :] -= exact_dot(panel[:, rest:size], both, TN)
        upper = jnp.where(row <= lane, work[:, 0:size], 0.0)
        summary_ref[0:size] = jnp.where(row >= lane, work[:, size : 2 * size], 0.0).T
        summary_ref[size : 2 * size] = upper.T
        each = len(gal_refs) // groups
        for group in range(groups):

            @pl.when(flags_ref[1] == group)
            def _(chosen=gal_refs[group * each : (group + 1) * each]):
                for sub in range(subs):
                    begin = rows + sub * funcs
                    total = chosen[0][sub]
                    for gal_ref in chosen[1:]:
                        total = total + gal_ref[sub]
                    summary_ref[begin : begin + funcs, 0:funcs] = total
                    summary_ref[begin : begin + funcs, funcs:size] = jnp.zeros((funcs, size - funcs), F32)


def factorize(flags, token, messages, groups):
    size = messages[0].shape[1]
    subs, funcs = groups[0][0].shape[0:2]
    parts = [part for group in groups for part in group]
    return pl.pallas_call(
        functools.partial(factor_kernel, parts=len(messages), groups=len(groups)),
        in_specs=[SMEM, ANY] + [VMEM] * (len(messages) + len(parts)),
        out_specs=[VMEM] * 2,
        out_shape=[
            jax.ShapeDtypeStruct((2 * size + subs * funcs, size), F32),
            jax.ShapeDtypeStruct((size, size), F32),
        ],
        scratch_shapes=[pltpu.VMEM((size, 2 * size), F32)],
        cost_estimate=LIGHT,
        name="factorize",
    )(flags, token, *messages, *parts)


def prepare_kernel(flags_ref, token_ref, column_ids_ref, row_ids_ref, head_ref, *rest, sources):
    summary_refs = rest[:sources]
    weights_ref, rows_ref, lower_ref, added_ref, gal_ref, summary, sem = rest[sources:]
    subs, funcs = gal_ref.shape[0:2]
    size = head_ref.shape[0]
    choice, mode, own = flags_ref[0], flags_ref[1], flags_ref[2]
    for number, summary_ref in enumerate(summary_refs):

        @pl.when(choice == number)
        def _(summary_ref=summary_ref):
            copy = pltpu.make_async_copy(summary_ref, summary, sem)
            copy.start()
            copy.wait()

    for sub in range(subs):
        begin = 2 * size + sub * funcs
        gal_ref[sub] = summary[begin : begin + funcs, 0:funcs]

    def doubled(block):
        nothing = jnp.zeros((size, size), BF16)
        top = jnp.concatenate([block, nothing], axis=1)
        return jnp.concatenate([top, jnp.concatenate([nothing, block], axis=1)], axis=0)

    @pl.when(mode > 0)
    def _():
        inverse = summary[0:size]
        high = inverse.astype(BF16)
        weights_ref[0 : 2 * size] = doubled(high)
        weights_ref[2 * size : 4 * size] = doubled((inverse - high.astype(F32)).astype(BF16))
        lower_ref[...] = summary[size : 2 * size]

    @pl.when(mode == 2)
    def _():
        solved = exact_dot(head_ref[...], summary[0:size])
        rows_ref[...] = doubled(solved.T.astype(BF16))

    @pl.when((mode == 2) & (own == 1))
    def _():
        added_ref[...] = spread(gal_ref, column_ids_ref, row_ids_ref, size)


def prepare(flags, token, ids, head, summaries):
    size = head.shape[0]
    subs, funcs = ids.shape
    return pl.pallas_call(
        functools.partial(prepare_kernel, sources=len(summaries)),
        in_specs=[SMEM, ANY] + [VMEM] * 3 + [ANY] * len(summaries),
        out_specs=[VMEM] * 5,
        out_shape=[
            jax.ShapeDtypeStruct((4 * size, 2 * size), BF16),
            jax.ShapeDtypeStruct((2 * size, 2 * size), BF16),
            jax.ShapeDtypeStruct((size, size), F32),
            jax.ShapeDtypeStruct((size, size), F32),
            jax.ShapeDtypeStruct((subs, funcs, funcs), F32),
        ],
        scratch_shapes=[pltpu.VMEM(summaries[0].shape, F32), pltpu.SemaphoreType.DMA],
        compiler_params=pltpu.CompilerParams(vmem_limit_bytes=16 * 2**20),
        cost_estimate=LIGHT,
        name="prepare",
    )(flags, token, ids[:, :, None], ids[:, None, :], head, *summaries)


def panel_kernel(
    flags_ref, token_ref, lower_ref, weights_ref, rows_ref, added_ref, slab_ref, *rest, pieces, spans, first
):
    hops = len(pieces) // len(spans)
    others = rest[: len(pieces)]
    out_ref, done_ref, column, factor, sems = rest[-5:]
    done_ref[0] = flags_ref[0]
    tile, size = out_ref.shape
    half = tile // 2
    mode, head, own, which = flags_ref[0], flags_ref[1], flags_ref[2], flags_ref[3]
    step, steps = pl.program_id(0), pl.num_programs(0)
    top = first & (step == 0)

    def copy_of(at, act):
        for number, (begin, end) in enumerate(spans):
            for hop in range(hops):

                @pl.when((mode == 2) & (which == hop) & (at >= begin) & (at < end))
                def _(other_ref=others[number * hops + hop], begin=begin):
                    source = other_ref.at[pl.ds(pl.multiple_of((at - begin) * tile, tile), tile)]
                    act(pltpu.make_async_copy(source, column.at[at % 2], sems.at[at % 2]))

    @pl.when(step == 0)
    def _():
        copy_of(step, lambda copy: copy.start())

    @pl.when(step + 1 < steps)
    def _():
        copy_of(step + 1, lambda copy: copy.start())

    @pl.when(mode == 0)
    def _():
        out_ref[...] = slab_ref[...]

    @pl.when(mode == 1)
    def _():
        column[step % 2] = slab_ref[...]

    @pl.when(mode == 2)
    def _():
        copy_of(step, lambda copy: copy.wait())

    @pl.when(mode > 0)
    def _():
        value = column[step % 2]
        pair = jnp.concatenate([value[0:half], value[half:tile]], axis=1)
        factor[...] = dot(jnp.concatenate([pair, pair], axis=1), weights_ref[...]).astype(BF16)

        @pl.when(top & (head == 1))
        def _():
            factor[0:size, 0:size] = lower_ref[...].astype(BF16)

        @pl.when(top & (head == 2))
        def _():
            factor[0:size, 0:size] = jnp.zeros((size, size), BF16)

    @pl.when(mode == 1)
    def _():
        out_ref[0:half] = factor[:, 0:size]
        out_ref[half:tile] = factor[:, size : 2 * size]

    @pl.when(mode == 2)
    def _():
        update = dot(factor[...], rows_ref[...])
        out_ref[0:half] = (slab_ref[0:half].astype(F32) - update[:, 0:size]).astype(BF16)
        out_ref[half:tile] = (slab_ref[half:tile].astype(F32) - update[:, size : 2 * size]).astype(BF16)

        @pl.when(top & (own == 1))
        def _():
            base = slab_ref[0:size].astype(F32) + added_ref[...]
            out_ref[0:size] = (base - update[0:size, 0:size]).astype(BF16)


def panel(flags, token, lower, weights, rows, added, slab, parts, old, start, tile):
    size = slab.shape[1]
    offset = start // tile
    spans, begin, operands = [], 0, []
    for hops in parts:
        end = begin + hops[0].shape[0] // tile
        spans.append((begin, end))
        begin = end
        operands += hops
    blocks = [
        SMEM,
        ANY,
        pl.BlockSpec((size, size), lambda i: (0, 0)),
        pl.BlockSpec(weights.shape, lambda i: (0, 0)),
        pl.BlockSpec(rows.shape, lambda i: (0, 0)),
        pl.BlockSpec((size, size), lambda i: (0, 0)),
        pl.BlockSpec((tile, size), lambda i: (i + offset, 0)),
    ] + [ANY] * len(operands)
    pieces = len(operands)
    operands = [flags, token, lower, weights, rows, added, slab] + operands
    aliases = {}
    if old is not None:
        aliases = {len(operands): 0}
        blocks.append(ANY)
        operands.append(old)
    return pl.pallas_call(
        functools.partial(panel_kernel, pieces=range(pieces), spans=spans, first=start == 0),
        grid=(begin,),
        in_specs=blocks,
        out_specs=[pl.BlockSpec((tile, size), lambda i: (i + offset, 0)), SMEM],
        out_shape=[jax.ShapeDtypeStruct(slab.shape, BF16), jax.ShapeDtypeStruct((1,), jnp.int32)],
        input_output_aliases=aliases,
        scratch_shapes=[
            pltpu.VMEM((2, tile, size), BF16),
            pltpu.VMEM((tile // 2, 2 * size), BF16),
            pltpu.SemaphoreType.DMA((2,)),
        ],
        compiler_params=pltpu.CompilerParams(vmem_limit_bytes=16 * 2**20),
        cost_estimate=LIGHT,
        name="panel",
    )(*operands)


def broadcast(value, axis, source):
    kept = jnp.where(lax.axis_index(axis) == source, value, 0).astype(value.dtype)
    return lax.psum(kept, axis)


def settings(*values):
    return jnp.stack([jnp.asarray(value).astype(jnp.int32) for value in values])


def holder_pairs(wide, narrow, distance):
    stride = wide // narrow
    found = []
    for n in range(narrow):
        for start in range(0, wide, 2 * distance):
            source = (n * stride) ^ start
            found.append((source * narrow + n, (source ^ distance) * narrow + n))
    return found


class Order:
    def __init__(self, token):
        self.token = token

    def after(self, value):
        value, self.token = lax.optimization_barrier((value, self.token))
        return value


def known_owner(owner, coarse_basis, material_ids, lame_table, coarse_ids, coarse_slab):
    narrow, wide = lax.axis_size("narrow"), lax.axis_size("wide")
    stride = wide // narrow
    wide_index, narrow_index = lax.axis_index("wide"), lax.axis_index("narrow")
    height, block = coarse_slab.shape
    own = wide_index == narrow_index * stride
    later = narrow_index > owner
    which = jnp.where(later, narrow_index - owner - 1, -1)
    mode = jnp.where(narrow_index == owner, 1, jnp.where(later, 2, 0))
    earlier = (wide_index % stride == 0) & (wide_index // stride < owner)
    kind = jnp.where(wide_index == owner * stride, 1, jnp.where(earlier, 2, 0))
    table = lame_table.astype(F32)
    hops = narrow - 1 - owner
    units, joined, plan = PLANS[hops]
    unit = height // sum(units)
    count = len(units)
    bounds, low = [], 0
    for number in units:
        bounds.append((low, low + number * unit))
        low += number * unit
    axes = ("wide", "narrow")

    def rows_of(number):
        low, high = bounds[number]
        return coarse_slab[low:high]

    def send(value, source, target):
        return lax.ppermute(value, "narrow", [(owner + source, owner + target)])

    order = Order(settings(mode))

    ways = [((n * stride) * narrow + owner, (n * stride) * narrow + n) for n in range(owner + 1, narrow)]
    head = order.after(lax.ppermute(coarse_slab[:block], axes, ways))
    moved = {}

    groups = [[w for w in range(wide) if w % stride == 0], [w for w in range(wide) if w % stride]]
    groups = [group for group in groups if group]
    member = jnp.where(wide_index % stride == 0, 0, 1)

    def within(group, pairs):
        return [(w * narrow + one, w * narrow + two) for w in group for one, two in pairs]

    def halo_of(group, message):
        return lax.ppermute(message, axes, within(group, [(i + 1, i) for i in range(narrow - 1)]))

    spans = [bounds[0], (bounds[joined[0]][0], bounds[joined[-1]][1]) if joined else bounds[1]]
    first, last, *begun = halo_message(table, material_ids, order.token, coarse_basis, coarse_slab, spans)
    first = order.after(first)
    halos = [halo_of(groups[0], first)]
    moved[0] = [send(order.after(begun[0]), 0, hops)]
    edge = (narrow_index == 0).astype(jnp.int32).reshape(1)
    inner = order.after(interior(edge, table, material_ids, coarse_basis, order.token))
    if joined:
        whole = send(order.after(begun[1]), 0, 1)
    else:
        moved[1] = [send(order.after(begun[1]), 0, 1)]
    halos[0] = order.after(halos[0])
    for group in groups[1:]:
        halos.append(halo_of(group, order.after(first)))

    def nearest(base, extent):
        return min(range(base, min(base + extent, narrow)), key=lambda n: abs(n - owner))

    def summed(parts, distance, group):
        total = parts[0] if len(parts) == 1 else parts[0] + parts[1]
        pairs = []
        for base in range(0, narrow - distance, 2 * distance):
            one, two = nearest(base, distance), nearest(base + distance, distance)
            pairs.append((two, one) if nearest(base, 2 * distance) == one else (one, two))
        return [total, lax.ppermute(total, axes, within(group, pairs))], 2 * distance

    def faces_of(number):
        flag = settings(member == number)
        return [order.after(face(flag, table, material_ids, last, halos[number], order.token, inner))]

    sums, reach = [faces_of(0)], [1]
    while reach[0] < narrow:
        sums[0], reach[0] = summed(sums[0], reach[0], groups[0])
    if not joined:
        for number in range(2, count - 1):
            moved[number] = [send(order.after(rows_of(number)), 0, 1)]
    distance, messages, left = wide // 2, [], plan.count("spread")
    result, prepared = None, None
    choice = (narrow_index - owner) % narrow
    flags = settings(mode, kind, own, which)
    for step in plan:
        if step[0] == "panel":
            if prepared is None:
                prepared = prepare(settings(choice, mode, own), order.token, coarse_ids, head, summaries)
            weights, rows, lower, added, galerkin = prepared
            begin, end = step[1:]
            parts = [moved[number][:: 1 if number else -1] for number in range(begin, end)]
            result, order.token = panel(
                flags, order.token, lower, weights, rows, added, coarse_slab, parts, result, bounds[begin][0], 2 * unit
            )
        elif step == "assemble":
            message = assemble(settings(mode, own), order.token, coarse_ids, coarse_slab, head, sums[0])
            message = order.after(message)
        elif step == "others":
            for number in range(1, len(groups)):
                halos[number] = order.after(halos[number])
                parts, far = summed(faces_of(number), 1, groups[number])
                sums.append(parts)
                reach.append(far)
        elif step == "more":
            for number in range(1, len(groups)):
                while reach[number] < narrow:
                    sums[number][1] = order.after(sums[number][1])
                    sums[number], reach[number] = summed(sums[number], reach[number], groups[number])
        elif step == "spread":
            left -= 1
            while distance:
                received = order.after(lax.ppermute(message, axes, holder_pairs(wide, narrow, distance)))
                messages = [message, received]
                if distance > 1:
                    message = message + received
                distance //= 2
                if left:
                    break
        elif step == "factor":
            summary, head = factorize(settings(mode, member), order.token, messages, sums)
            summary = order.after(summary)
            summaries = [summary] + [
                lax.ppermute(summary, "narrow", [(owner, (owner + place) % narrow)]) for place in range(1, narrow)
            ]
            moved[count - 1] = [send(order.after(rows_of(count - 1)), 0, 1)]
            for place in range(1, narrow):
                summaries[place] = order.after(summaries[place])
        else:
            number, hop = step
            if joined and step == (joined[0], 0):
                whole = order.after(whole)
                for part in joined:
                    low, high = (bound - bounds[joined[0]][0] for bound in bounds[part])
                    moved[part] = [whole[low:high]]
            moving = moved[number][hop] = order.after(moved[number][hop])
            if number == 0 and hop + 1 < hops:
                moved[number].append(send(moving, hops - hop, hops - hop - 1))
            elif number != 0 and hop + 1 < hops:
                moved[number].append(send(moving, hop + 1, hop + 2))
    return result, galerkin


def any_owner(owner, coarse_basis, material_ids, lame_table, coarse_ids, coarse_slab):
    narrow, wide = lax.axis_size("narrow"), lax.axis_size("wide")
    stride = wide // narrow
    wide_index, narrow_index = lax.axis_index("wide"), lax.axis_index("narrow")
    own = wide_index == narrow_index * stride
    later = narrow_index > owner
    which = jnp.where(later, 0, -1)
    mode = jnp.where(narrow_index == owner, 1, jnp.where(later, 2, 0))
    earlier = (wide_index % stride == 0) & (wide_index // stride < owner)
    kind = jnp.where(wide_index == owner * stride, 1, jnp.where(earlier, 2, 0))
    table = lame_table.astype(F32)
    column = broadcast(coarse_slab, "narrow", owner)
    first, last = halo_message(table, material_ids, table, coarse_basis, coarse_slab, ())
    halo = lax.ppermute(first, "narrow", [(i + 1, i) for i in range(narrow - 1)])
    edge = (narrow_index == 0).astype(jnp.int32).reshape(1)
    inner = interior(edge, table, material_ids, coarse_basis, first)
    partial = face(settings(1), table, material_ids, last, halo, first, inner)
    parts = [lax.psum(partial, "narrow")]
    message = assemble(settings(mode, own), first, coarse_ids, coarse_slab, column, parts)
    at_owner = (wide_index == owner * stride) & (narrow_index == owner)
    diagonal = lax.psum(jnp.where(at_owner, message, 0.0), ("wide", "narrow"))
    summary, _ = factorize(settings(1, 0), first, [diagonal], [parts])
    head = broadcast(message, "wide", narrow_index * stride)
    weights, rows, lower, added, galerkin = prepare(settings(0, mode, own), settings(mode), coarse_ids, head, [summary])
    flags = settings(mode, kind, own, which)
    tile = coarse_slab.shape[0] // 12
    result, _ = panel(flags, flags, lower, weights, rows, added, coarse_slab, [[column]], None, 0, tile)
    return result, galerkin


def on_device(coarse_basis, material_ids, lame_table, coarse_ids, coarse_slab, panel_owner):
    narrow, wide = lax.axis_size("narrow"), lax.axis_size("wide")
    arrays = (coarse_basis, material_ids, lame_table, coarse_ids, coarse_slab)
    owner = panel_owner[0]
    if narrow - 1 > len(PLANS) or wide & (wide - 1):
        return any_owner(owner, *arrays)
    branches = [functools.partial(known_owner, place) for place in range(narrow - 1)]
    return lax.switch(owner, branches, *arrays)


def solution(mesh):
    return jax.shard_map(
        on_device,
        mesh=mesh,
        in_specs=(
            P("wide", None, None, "narrow", None, None),
            P("wide", "narrow", None, None),
            P(),
            P("wide", None),
            P("wide", "narrow"),
            P(),
        ),
        out_specs=(P("wide", "narrow"), P("wide", None, None)),
        check_vma=False,
    )
```

```python
import functools

import jax
import jax.numpy as jnp
from jax import lax
from jax.experimental import pallas as pl
from jax.experimental.pallas import tpu as pltpu
from jax.sharding import PartitionSpec as P

F32, BF16 = jnp.float32, jnp.bfloat16
NT = (((1,), (1,)), ((), ()))
TN = (((0,), (0,)), ((), ()))
VMEM = pl.BlockSpec(memory_space=pltpu.VMEM)
ANY = pl.BlockSpec(memory_space=pl.ANY)
SMEM = pl.BlockSpec(memory_space=pltpu.SMEM)
PLANS = {
    1: (
        (12, 10, 2),
        (),
        ((0, 0), "assemble", "spread", "others", "spread", "more", "spread", "factor", ("panel", 1, 2), ("panel", 0, 1), ("panel", 2, 3)),
    ),
    2: (
        (12, 6, 4, 2),
        (),
        (
            (0, 0), "assemble", "spread", "others", "spread", "more", "spread", (1, 0), "factor",
            (2, 0), ("panel", 1, 2), (3, 0), ("panel", 2, 3), ("panel", 0, 1), ("panel", 3, 4),
        ),
    ),
    3: (
        (12, 4, 4, 2, 2),
        (1, 2, 3),
        (
            (0, 0), "assemble", "spread", "others", "spread", "more", "spread", "factor",
            (1, 0), (1, 1), (0, 1), (2, 0), (2, 1), (3, 0), ("panel", 1, 2), (3, 1), (4, 0), ("panel", 2, 3), (4, 1),
            ("panel", 0, 1), ("panel", 3, 5),
        ),
    ),
}
BLOCK = 16
LIGHT = pl.CostEstimate(flops=1, bytes_accessed=1, transcendentals=0)


def exact_dot(left, right, dims=(((1,), (0,)), ((), ()))):
    return lax.dot_general(
        left, right, dims, precision=lax.Precision.HIGHEST, preferred_element_type=F32
    )


def dot(left, right, dims=(((1,), (0,)), ((), ()))):
    return lax.dot_general(left, right, dims, preferred_element_type=F32)


def split_two(value):
    high = value.astype(BF16)
    return high, (value - high.astype(F32)).astype(BF16)


def lame_of(ids, table_ref):
    shear = jnp.zeros(ids.shape, F32)
    dilate = jnp.zeros(ids.shape, F32)
    for material in range(table_ref.shape[1]):
        chosen = ids == material
        shear = jnp.where(chosen, table_ref[0, material], shear)
        dilate = jnp.where(chosen, table_ref[1, material], dilate)
    return shear, dilate


def halo_kernel(table_ref, ids_ref, token_ref, basis_ref, slab_ref, out_ref, last_ref, *rest, spans):
    piece_refs, sems = rest[:-1], rest[-1]
    subs, funcs, comps, layers = basis_ref.shape[0:4]
    copies = []
    for number, ((low, high), piece_ref) in enumerate(zip(spans, piece_refs)):
        copies.append(pltpu.make_async_copy(slab_ref.at[pl.ds(low, high - low)], piece_ref, sems.at[number]))
        copies[-1].start()
    for sub in range(subs):
        for comp in range(comps):
            out_ref[sub, comp * funcs : (comp + 1) * funcs] = basis_ref[sub, :, comp, 0]
            last_ref[sub, comp * funcs : (comp + 1) * funcs] = basis_ref[sub, :, comp, layers - 1]
        shear, dilate = lame_of(ids_ref[sub, 0], table_ref)
        out_ref[sub, comps * funcs] = shear.astype(BF16)
        out_ref[sub, comps * funcs + 1] = dilate.astype(BF16)
    for copy in copies:
        copy.wait()


def halo_message(table, ids, token, basis, slab, spans):
    subs, funcs, comps, layers, ny, nz = basis.shape
    return pl.pallas_call(
        functools.partial(halo_kernel, spans=spans),
        in_specs=[SMEM, VMEM, ANY, VMEM, ANY],
        out_specs=[VMEM] * (2 + len(spans)),
        out_shape=[
            jax.ShapeDtypeStruct((subs, comps * funcs + 2, ny, nz), BF16),
            jax.ShapeDtypeStruct((subs, comps * funcs, ny, nz), BF16),
        ]
        + [jax.ShapeDtypeStruct((high - low, slab.shape[1]), BF16) for low, high in spans],
        scratch_shapes=[pltpu.SemaphoreType.DMA((max(1, len(spans)),))],
        compiler_params=pltpu.CompilerParams(vmem_limit_bytes=16 * 2**20),
        cost_estimate=LIGHT,
        name="halo_message",
    )(table, ids, token, basis, slab)


def interior_kernel(edge_ref, table_ref, ids_ref, basis_ref, token_ref, out_ref, fields, turned, coef, left, right, acc):
    sub, comp = pl.program_id(0), pl.program_id(1)
    layers, ny, nz = basis_ref.shape[3:]
    funcs = basis_ref.shape[1]
    row = lax.broadcasted_iota(jnp.int32, (ny, nz), 0)
    lane = lax.broadcasted_iota(jnp.int32, (ny, nz), 1)
    table = [lame_of(ids_ref[sub, x], table_ref) for x in range(layers)]

    def weight(one, two, direction):
        shear = 0.5 * (one[0] + two[0])
        dilate = 0.5 * (one[1] + two[1])
        return shear + jnp.where(comp == direction, shear + dilate, 0.0)

    def ahead(field, axis):
        size = field.shape[axis]
        index = row if axis == 0 else lane
        return jnp.where(index == size - 1, 0.0, pltpu.roll(field, size - 1, axis=axis))

    def behind(field, axis):
        index = row if axis == 0 else lane
        return jnp.where(index == 0, 0.0, pltpu.roll(field, 1, axis=axis))

    nothing = (jnp.zeros((ny, nz), F32),) * 2
    previous = weight(table[0], nothing, 0) * edge_ref[0].astype(F32)
    for x in range(layers):
        diagonal = previous
        forward = []
        if x + 1 < layers:
            face = weight(table[x], table[x + 1], 0)
            diagonal = diagonal + face
            previous = face
            forward.append(face)
        else:
            forward.append(jnp.zeros((ny, nz), F32))
        for axis in (0, 1):
            index, size = (row, ny) if axis == 0 else (lane, nz)
            other = tuple(ahead(value, axis) for value in table[x])
            face = weight(table[x], other, axis + 1)
            before = tuple(behind(value, axis) for value in table[x])
            diagonal = diagonal + face + weight(table[x], before, axis + 1)
            forward.append(jnp.where(index == size - 1, 0.0, face))
        coef[x, 0] = 0.5 * diagonal
        for kind in range(3):
            coef[x, kind + 1] = forward[kind]
        fields[x] = basis_ref[sub, :, comp, x].astype(F32).reshape(funcs * ny, nz)

    total = None
    for x in reversed(range(layers)):
        values = [fields[x, pl.ds(y, funcs, stride=ny), :] for y in range(ny)]
        for y in range(ny):
            value = values[y]
            turned[x % 2, y] = value
            image = coef[x, 0, y : y + 1, :] * value
            image = image - coef[x, 3, y : y + 1, :] * pltpu.roll(value, nz - 1, axis=1)
            if y + 1 < ny:
                image = image - coef[x, 2, y : y + 1, :] * values[y + 1]
            if x + 1 < layers:
                image = image - coef[x, 1, y : y + 1, :] * turned[(x + 1) % 2, y]
            high, low = split_two(image)
            left[:, y * nz : (y + 1) * nz] = value.astype(BF16)
            right[0:funcs, y * nz : (y + 1) * nz] = high
            right[funcs : 2 * funcs, y * nz : (y + 1) * nz] = low
        product = dot(right[...], left[...], NT)
        total = product if total is None else total + product

    @pl.when(comp == 0)
    def _():
        acc[...] = total

    @pl.when(comp > 0)
    def _():
        acc[...] += total

    @pl.when(comp == pl.num_programs(1) - 1)
    def _():
        out_ref[0] = acc[0:funcs] + acc[funcs : 2 * funcs]


def interior(edge, table, ids, basis, token):
    subs, funcs, comps, layers, ny, nz = basis.shape
    return pl.pallas_call(
        interior_kernel,
        grid=(subs, comps),
        in_specs=[SMEM, SMEM, VMEM, VMEM, ANY],
        out_specs=pl.BlockSpec((1, funcs, funcs), lambda s, c: (s, 0, 0)),
        out_shape=jax.ShapeDtypeStruct((subs, funcs, funcs), F32),
        scratch_shapes=[
            pltpu.VMEM((layers, funcs * ny, nz), F32),
            pltpu.VMEM((2, ny, funcs, nz), F32),
            pltpu.VMEM((layers, 4, ny, nz), F32),
            pltpu.VMEM((funcs, ny * nz), BF16),
            pltpu.VMEM((2 * funcs, ny * nz), BF16),
            pltpu.VMEM((2 * funcs, funcs), F32),
        ],
        compiler_params=pltpu.CompilerParams(vmem_limit_bytes=16 * 2**20),
        cost_estimate=LIGHT,
        name="interior",
    )(edge, table, ids, basis, token)


def face_kernel(flags_ref, table_ref, ids_ref, last_ref, halo_ref, token_ref, inner_ref, out_ref, *scratch):
    @pl.when(flags_ref[0] == 1)
    def _():
        last, halo, sems = scratch[-3:]
        copies = [
            pltpu.make_async_copy(last_ref, last, sems.at[0]),
            pltpu.make_async_copy(halo_ref, halo, sems.at[1]),
        ]
        for copy in copies:
            copy.start()
        for copy in copies:
            copy.wait()
        face_sums(table_ref, ids_ref, last, halo, inner_ref, out_ref, *scratch[:-3])


def face_sums(table_ref, ids_ref, last_ref, halo_ref, inner_ref, out_ref, mine, theirs, left, right, weights, acc):
    subs, layers, ny, nz = ids_ref.shape
    funcs = inner_ref.shape[1]
    comps = last_ref.shape[1] // funcs

    @pl.loop(0, subs)
    def _(sub):
        shear, dilate = lame_of(ids_ref[sub, layers - 1], table_ref)
        weights[0] = 0.5 * (shear + halo_ref[sub, comps * funcs].astype(F32))
        weights[1] = 0.5 * (dilate + halo_ref[sub, comps * funcs + 1].astype(F32))

        @pl.loop(0, comps)
        def _(comp):
            weight = weights[0] + jnp.where(comp == 0, weights[0] + weights[1], 0.0)
            rows = pl.ds(comp * funcs, funcs)
            mine[...] = last_ref[sub, rows].astype(F32).reshape(funcs * ny, nz)
            theirs[...] = halo_ref[sub, rows].astype(F32).reshape(funcs * ny, nz)
            for y in range(ny):
                here = mine[pl.ds(y, funcs, stride=ny), :]
                there = theirs[pl.ds(y, funcs, stride=ny), :]
                high, low = split_two(weight[y : y + 1, :] * (here - there))
                left[0:funcs, y * nz : (y + 1) * nz] = here.astype(BF16)
                left[funcs : 2 * funcs, y * nz : (y + 1) * nz] = there.astype(BF16)
                right[0:funcs, y * nz : (y + 1) * nz] = high
                right[funcs : 2 * funcs, y * nz : (y + 1) * nz] = low
            product = dot(right[...], left[...], NT)

            @pl.when(comp == 0)
            def _():
                acc[...] = product

            @pl.when(comp > 0)
            def _():
                acc[...] += product

        total = acc[:, 0:funcs] - acc[:, funcs : 2 * funcs]
        half = inner_ref[sub] + 0.5 * (total[0:funcs] + total[funcs : 2 * funcs])
        out_ref[sub] = half + half.T


def face(flags, table, ids, last, halo, token, inner):
    subs, layers, ny, nz = ids.shape
    funcs = inner.shape[1]
    return pl.pallas_call(
        face_kernel,
        in_specs=[SMEM, SMEM, VMEM, ANY, ANY, ANY, VMEM],
        out_specs=VMEM,
        out_shape=jax.ShapeDtypeStruct((subs, funcs, funcs), F32),
        scratch_shapes=[
            pltpu.VMEM((funcs * ny, nz), F32),
            pltpu.VMEM((funcs * ny, nz), F32),
            pltpu.VMEM((2 * funcs, ny * nz), BF16),
            pltpu.VMEM((2 * funcs, ny * nz), BF16),
            pltpu.VMEM((2, ny, nz), F32),
            pltpu.VMEM((2 * funcs, 2 * funcs), F32),
            pltpu.VMEM(last.shape, BF16),
            pltpu.VMEM(halo.shape, BF16),
            pltpu.SemaphoreType.DMA((2,)),
        ],
        compiler_params=pltpu.CompilerParams(vmem_limit_bytes=16 * 2**20),
        cost_estimate=LIGHT,
        name="face",
    )(flags, table, ids, last, halo, token, inner)


def spread(gal_ref, column_ids_ref, row_ids_ref, size):
    subs, funcs = column_ids_ref.shape[0:2]
    added = jnp.zeros((size, size), F32)
    lane = lax.broadcasted_iota(jnp.int32, (funcs, size), 1)
    row = lax.broadcasted_iota(jnp.int32, (size, funcs), 0)
    for sub in range(subs):
        slots = (column_ids_ref[sub] == lane).astype(F32)
        slots_t = (row_ids_ref[sub] == row).astype(F32)
        added = added + exact_dot(slots_t, exact_dot(gal_ref[sub], slots))
    return added


def assemble_kernel(flags_ref, token_ref, column_ids_ref, row_ids_ref, slab_ref, head_ref, *rest):
    gal_refs, (message_ref, sum_ref) = rest[:-2], rest[-2:]
    size = message_ref.shape[0]
    mode, own = flags_ref[0], flags_ref[1]
    message_ref[...] = jnp.zeros_like(message_ref)

    @pl.when((mode == 1) & (own == 1))
    def _():
        total = gal_refs[0][...]
        for gal_ref in gal_refs[1:]:
            total = total + gal_ref[...]
        sum_ref[...] = total
        added = spread(sum_ref, column_ids_ref, row_ids_ref, size)
        message_ref[...] = added + slab_ref[...].astype(F32)

    @pl.when((mode == 2) & (own == 1))
    def _():
        message_ref[...] = head_ref[...].astype(F32)


def assemble(flags, token, ids, slab, head, parts):
    size = slab.shape[1]
    block = pl.BlockSpec((size, size), lambda i: (0, 0))
    return pl.pallas_call(
        assemble_kernel,
        grid=(1,),
        in_specs=[SMEM, ANY, VMEM, VMEM, block, block] + [VMEM] * len(parts),
        out_specs=VMEM,
        out_shape=jax.ShapeDtypeStruct((size, size), F32),
        scratch_shapes=[pltpu.VMEM(parts[0].shape, F32)],
        cost_estimate=LIGHT,
        name="assemble",
    )(flags, token, ids[:, :, None], ids[:, None, :], slab, head, *parts)


def factor_kernel(flags_ref, token_ref, *refs, parts, groups):
    message_refs, gal_refs = refs[:parts], refs[parts:-4]
    summary_ref, block_ref, sum_ref, work = refs[-4:]
    subs, funcs = gal_refs[0].shape[0:2]
    size = summary_ref.shape[1]
    diagonal = message_refs[0][...]
    for message_ref in message_refs[1:]:
        diagonal = diagonal + message_ref[...]
    block_ref[...] = diagonal

    @pl.when(flags_ref[0] == 1)
    def _():
        row = lax.broadcasted_iota(jnp.int32, (size, size), 0)
        lane = lax.broadcasted_iota(jnp.int32, (size, size), 1)
        work[:, 0:size] = 0.5 * (diagonal + diagonal.T)
        work[:, size : 2 * size] = (row == lane).astype(F32)
        index = lax.broadcasted_iota(jnp.int32, (BLOCK, size), 0)
        for start in range(0, size, BLOCK):
            panel = work[start : start + BLOCK, 0:size]
            extra = work[start : start + BLOCK, size : 2 * size]
            columns = [
                jnp.broadcast_to(panel[:, start + step : start + step + 1], (BLOCK, size))
                for step in range(BLOCK)
            ]
            for step in range(BLOCK):
                scale = lax.rsqrt(columns[step][step : step + 1, :])
                column = jnp.where(index > step, columns[step] * scale, 0.0)
                for later in range(step + 1, BLOCK):
                    columns[later] = columns[later] - column * column[later : later + 1, :]
                pivot = panel[step : step + 1, :] * scale
                panel = jnp.where(index == step, pivot, panel - column * pivot)
                pivot = extra[step : step + 1, :] * scale
                extra = jnp.where(index == step, pivot, extra - column * pivot)
            work[start : start + BLOCK, 0:size] = panel
            work[start : start + BLOCK, size : 2 * size] = extra
            rest = start + BLOCK
            if rest < size:
                both = jnp.concatenate([panel, extra], axis=1)
                work[rest:size, :] -= exact_dot(panel[:, rest:size], both, TN)
        upper = jnp.where(row <= lane, work[:, 0:size], 0.0)
        inverse = jnp.where(row >= lane, work[:, size : 2 * size], 0.0).T
        high = inverse.astype(BF16)
        summary_ref[0:size] = high
        summary_ref[size : 2 * size] = (inverse - high.astype(F32)).astype(BF16)
        summary_ref[2 * size : 3 * size] = upper.T.astype(BF16)
        each = len(gal_refs) // groups
        for group in range(groups):

            @pl.when(flags_ref[1] == group)
            def _(chosen=gal_refs[group * each : (group + 1) * each]):
                total = chosen[0][...]
                for gal_ref in chosen[1:]:
                    total = total + gal_ref[...]
                sum_ref[...] = total


def factorize(flags, token, messages, groups):
    size = messages[0].shape[1]
    subs, funcs = groups[0][0].shape[0:2]
    parts = [part for group in groups for part in group]
    return pl.pallas_call(
        functools.partial(factor_kernel, parts=len(messages), groups=len(groups)),
        in_specs=[SMEM, ANY] + [VMEM] * (len(messages) + len(parts)),
        out_specs=[VMEM] * 3,
        out_shape=[
            jax.ShapeDtypeStruct((3 * size, size), BF16),
            jax.ShapeDtypeStruct((size, size), F32),
            jax.ShapeDtypeStruct(groups[0][0].shape, F32),
        ],
        scratch_shapes=[pltpu.VMEM((size, 2 * size), F32)],
        cost_estimate=LIGHT,
        name="factorize",
    )(flags, token, *messages, *parts)


def prepare_kernel(flags_ref, token_ref, head_ref, *rest, sources):
    summary_refs = rest[:sources]
    weights_ref, rows_ref, lower_ref, summary, sem = rest[sources:]
    size = head_ref.shape[0]
    choice, mode = flags_ref[0], flags_ref[1]
    for number, summary_ref in enumerate(summary_refs):

        @pl.when(choice == number)
        def _(summary_ref=summary_ref):
            copy = pltpu.make_async_copy(summary_ref, summary, sem)
            copy.start()
            copy.wait()

    def doubled(block):
        nothing = jnp.zeros((size, size), BF16)
        top = jnp.concatenate([block, nothing], axis=1)
        return jnp.concatenate([top, jnp.concatenate([nothing, block], axis=1)], axis=0)

    @pl.when(mode > 0)
    def _():
        weights_ref[0 : 2 * size] = doubled(summary[0:size])
        weights_ref[2 * size : 4 * size] = doubled(summary[size : 2 * size])
        lower_ref[...] = summary[2 * size : 3 * size]

    @pl.when(mode == 2)
    def _():
        inverse = summary[0:size].astype(F32) + summary[size : 2 * size].astype(F32)
        solved = exact_dot(head_ref[...], inverse)
        rows_ref[...] = doubled(solved.T.astype(BF16))


def prepare(flags, token, head, summaries):
    size = head.shape[0]
    return pl.pallas_call(
        functools.partial(prepare_kernel, sources=len(summaries)),
        in_specs=[SMEM, ANY, VMEM] + [ANY] * len(summaries),
        out_specs=[VMEM] * 3,
        out_shape=[
            jax.ShapeDtypeStruct((4 * size, 2 * size), BF16),
            jax.ShapeDtypeStruct((2 * size, 2 * size), BF16),
            jax.ShapeDtypeStruct((size, size), BF16),
        ],
        scratch_shapes=[pltpu.VMEM(summaries[0].shape, BF16), pltpu.SemaphoreType.DMA],
        compiler_params=pltpu.CompilerParams(vmem_limit_bytes=16 * 2**20),
        cost_estimate=LIGHT,
        name="prepare",
    )(flags, token, head, *summaries)


def added_kernel(flags_ref, token_ref, column_ids_ref, row_ids_ref, *rest, sources):
    sum_refs, (added_ref, gal_ref) = rest[:sources], rest[sources:]
    for number, sum_ref in enumerate(sum_refs):

        @pl.when(flags_ref[0] == number)
        def _(sum_ref=sum_ref):
            gal_ref[...] = sum_ref[...]

    @pl.when((flags_ref[1] == 2) & (flags_ref[2] == 1))
    def _():
        added_ref[...] = spread(gal_ref, column_ids_ref, row_ids_ref, added_ref.shape[0])


def added_of(flags, token, ids, sums, size):
    return pl.pallas_call(
        functools.partial(added_kernel, sources=len(sums)),
        in_specs=[SMEM, ANY] + [VMEM] * (2 + len(sums)),
        out_specs=[VMEM] * 2,
        out_shape=[jax.ShapeDtypeStruct((size, size), F32), jax.ShapeDtypeStruct(sums[0].shape, F32)],
        cost_estimate=LIGHT,
        name="added",
    )(flags, token, ids[:, :, None], ids[:, None, :], *sums)


def panel_kernel(
    flags_ref, token_ref, lower_ref, weights_ref, rows_ref, added_ref, slab_ref, *rest, pieces, spans, first
):
    hops = len(pieces) // len(spans)
    others = rest[: len(pieces)]
    out_ref, done_ref, column, factor, sems = rest[-5:]
    done_ref[0] = flags_ref[0]
    tile, size = out_ref.shape
    half = tile // 2
    mode, head, own, which = flags_ref[0], flags_ref[1], flags_ref[2], flags_ref[3]
    step, steps = pl.program_id(0), pl.num_programs(0)
    top = first & (step == 0)

    def copy_of(at, act):
        for number, (begin, end) in enumerate(spans):
            for hop in range(hops):

                @pl.when((mode == 2) & (which == hop) & (at >= begin) & (at < end))
                def _(other_ref=others[number * hops + hop], begin=begin):
                    source = other_ref.at[pl.ds(pl.multiple_of((at - begin) * tile, tile), tile)]
                    act(pltpu.make_async_copy(source, column.at[at % 2], sems.at[at % 2]))

    @pl.when(step == 0)
    def _():
        copy_of(step, lambda copy: copy.start())

    @pl.when(step + 1 < steps)
    def _():
        copy_of(step + 1, lambda copy: copy.start())

    @pl.when(mode == 0)
    def _():
        out_ref[...] = slab_ref[...]

    @pl.when(mode == 1)
    def _():
        column[step % 2] = slab_ref[...]

    @pl.when(mode == 2)
    def _():
        copy_of(step, lambda copy: copy.wait())

    @pl.when(mode > 0)
    def _():
        value = column[step % 2]
        pair = jnp.concatenate([value[0:half], value[half:tile]], axis=1)
        factor[...] = dot(jnp.concatenate([pair, pair], axis=1), weights_ref[...]).astype(BF16)

        @pl.when(top & (head == 1))
        def _():
            factor[0:size, 0:size] = lower_ref[...]

        @pl.when(top & (head == 2))
        def _():
            factor[0:size, 0:size] = jnp.zeros((size, size), BF16)

    @pl.when(mode == 1)
    def _():
        out_ref[0:half] = factor[:, 0:size]
        out_ref[half:tile] = factor[:, size : 2 * size]

    @pl.when(mode == 2)
    def _():
        update = dot(factor[...], rows_ref[...])
        out_ref[0:half] = (slab_ref[0:half].astype(F32) - update[:, 0:size]).astype(BF16)
        out_ref[half:tile] = (slab_ref[half:tile].astype(F32) - update[:, size : 2 * size]).astype(BF16)

        @pl.when(top & (own == 1))
        def _():
            base = slab_ref[0:size].astype(F32) + added_ref[...]
            out_ref[0:size] = (base - update[0:size, 0:size]).astype(BF16)


def panel(flags, token, lower, weights, rows, added, slab, parts, old, start, tile):
    size = slab.shape[1]
    offset = start // tile
    spans, begin, operands = [], 0, []
    for hops in parts:
        end = begin + hops[0].shape[0] // tile
        spans.append((begin, end))
        begin = end
        operands += hops
    blocks = [
        SMEM,
        ANY,
        pl.BlockSpec((size, size), lambda i: (0, 0)),
        pl.BlockSpec(weights.shape, lambda i: (0, 0)),
        pl.BlockSpec(rows.shape, lambda i: (0, 0)),
        pl.BlockSpec((size, size), lambda i: (0, 0)),
        pl.BlockSpec((tile, size), lambda i: (i + offset, 0)),
    ] + [ANY] * len(operands)
    pieces = len(operands)
    operands = [flags, token, lower, weights, rows, added, slab] + operands
    aliases = {}
    if old is not None:
        aliases = {len(operands): 0}
        blocks.append(ANY)
        operands.append(old)
    return pl.pallas_call(
        functools.partial(panel_kernel, pieces=range(pieces), spans=spans, first=start == 0),
        grid=(begin,),
        in_specs=blocks,
        out_specs=[pl.BlockSpec((tile, size), lambda i: (i + offset, 0)), SMEM],
        out_shape=[jax.ShapeDtypeStruct(slab.shape, BF16), jax.ShapeDtypeStruct((1,), jnp.int32)],
        input_output_aliases=aliases,
        scratch_shapes=[
            pltpu.VMEM((2, tile, size), BF16),
            pltpu.VMEM((tile // 2, 2 * size), BF16),
            pltpu.SemaphoreType.DMA((2,)),
        ],
        compiler_params=pltpu.CompilerParams(vmem_limit_bytes=16 * 2**20),
        cost_estimate=LIGHT,
        name="panel",
    )(*operands)


def broadcast(value, axis, source):
    kept = jnp.where(lax.axis_index(axis) == source, value, 0).astype(value.dtype)
    return lax.psum(kept, axis)


def settings(*values):
    return jnp.stack([jnp.asarray(value).astype(jnp.int32) for value in values])


def holder_pairs(wide, narrow, distance):
    stride = wide // narrow
    found = []
    for n in range(narrow):
        for start in range(0, wide, 2 * distance):
            source = (n * stride) ^ start
            found.append((source * narrow + n, (source ^ distance) * narrow + n))
    return found


class Order:
    def __init__(self, token):
        self.token = token

    def after(self, value):
        value, self.token = lax.optimization_barrier((value, self.token))
        return value


def known_owner(owner, coarse_basis, material_ids, lame_table, coarse_ids, coarse_slab):
    narrow, wide = lax.axis_size("narrow"), lax.axis_size("wide")
    stride = wide // narrow
    wide_index, narrow_index = lax.axis_index("wide"), lax.axis_index("narrow")
    height, block = coarse_slab.shape
    own = wide_index == narrow_index * stride
    later = narrow_index > owner
    which = jnp.where(later, narrow_index - owner - 1, -1)
    mode = jnp.where(narrow_index == owner, 1, jnp.where(later, 2, 0))
    earlier = (wide_index % stride == 0) & (wide_index // stride < owner)
    kind = jnp.where(wide_index == owner * stride, 1, jnp.where(earlier, 2, 0))
    table = lame_table.astype(F32)
    hops = narrow - 1 - owner
    units, joined, plan = PLANS[hops]
    unit = height // sum(units)
    count = len(units)
    bounds, low = [], 0
    for number in units:
        bounds.append((low, low + number * unit))
        low += number * unit
    axes = ("wide", "narrow")

    def rows_of(number):
        low, high = bounds[number]
        return coarse_slab[low:high]

    def send(value, source, target):
        return lax.ppermute(value, "narrow", [(owner + source, owner + target)])

    order = Order(settings(mode))

    ways = [((n * stride) * narrow + owner, (n * stride) * narrow + n) for n in range(owner + 1, narrow)]
    head = order.after(lax.ppermute(coarse_slab[:block], axes, ways))
    moved = {}

    groups = [[w for w in range(wide) if w % stride == 0], [w for w in range(wide) if w % stride]]
    groups = [group for group in groups if group]
    member = jnp.where(wide_index % stride == 0, 0, 1)

    def within(group, pairs):
        return [(w * narrow + one, w * narrow + two) for w in group for one, two in pairs]

    def halo_of(group, message):
        return lax.ppermute(message, axes, within(group, [(i + 1, i) for i in range(narrow - 1)]))

    spans = [bounds[0], (bounds[joined[0]][0], bounds[joined[-1]][1]) if joined else bounds[1]]
    first, last, *begun = halo_message(table, material_ids, order.token, coarse_basis, coarse_slab, spans)
    first = order.after(first)
    halos = [halo_of(groups[0], first)]
    moved[0] = [send(order.after(begun[0]), 0, hops)]
    edge = (narrow_index == 0).astype(jnp.int32).reshape(1)
    inner = order.after(interior(edge, table, material_ids, coarse_basis, order.token))
    if joined:
        whole = send(order.after(begun[1]), 0, 1)
    else:
        moved[1] = [send(order.after(begun[1]), 0, 1)]
    halos[0] = order.after(halos[0])
    for group in groups[1:]:
        halos.append(halo_of(group, order.after(first)))

    def nearest(base, extent):
        return min(range(base, min(base + extent, narrow)), key=lambda n: abs(n - owner))

    def summed(parts, distance, group):
        total = parts[0] if len(parts) == 1 else parts[0] + parts[1]
        pairs = []
        for base in range(0, narrow - distance, 2 * distance):
            one, two = nearest(base, distance), nearest(base + distance, distance)
            pairs.append((two, one) if nearest(base, 2 * distance) == one else (one, two))
        return [total, lax.ppermute(total, axes, within(group, pairs))], 2 * distance

    def faces_of(number):
        flag = settings(member == number)
        return [order.after(face(flag, table, material_ids, last, halos[number], order.token, inner))]

    sums, reach = [faces_of(0)], [1]
    while reach[0] < narrow:
        sums[0], reach[0] = summed(sums[0], reach[0], groups[0])
    sums[0][1] = order.after(sums[0][1])
    if not joined:
        for number in range(2, count - 1):
            moved[number] = [send(order.after(rows_of(number)), 0, 1)]
    distance, messages, left = wide // 2, [], plan.count("spread")
    result, prepared = None, None
    choice = (narrow_index - owner) % narrow
    flags = settings(mode, kind, own, which)
    for step in plan:
        if step[0] == "panel":
            if prepared is None:
                prepared = prepare(settings(choice, mode), order.token, head, summaries)
                added, galerkin = added_of(
                    settings(choice, mode, own), prepared[0], coarse_ids, galerkins, block
                )
            weights, rows, lower = prepared
            begin, end = step[1:]
            parts = [moved[number][:: 1 if number else -1] for number in range(begin, end)]
            result, order.token = panel(
                flags, order.token, lower, weights, rows, added if begin == 0 else head, coarse_slab, parts, result, bounds[begin][0], 2 * unit
            )
        elif step == "assemble":
            message = assemble(settings(mode, own), order.token, coarse_ids, coarse_slab, head, sums[0])
            message = order.after(message)
        elif step == "others":
            for number in range(1, len(groups)):
                halos[number] = order.after(halos[number])
                parts, far = summed(faces_of(number), 1, groups[number])
                sums.append(parts)
                reach.append(far)
        elif step == "more":
            for number in range(1, len(groups)):
                while reach[number] < narrow:
                    sums[number][1] = order.after(sums[number][1])
                    sums[number], reach[number] = summed(sums[number], reach[number], groups[number])
        elif step == "spread":
            left -= 1
            while distance:
                received = order.after(lax.ppermute(message, axes, holder_pairs(wide, narrow, distance)))
                messages = [message, received]
                if distance > 1:
                    message = message + received
                distance //= 2
                if left:
                    break
        elif step == "factor":
            summary, head, galerkin = factorize(settings(mode, member), order.token, messages, sums)
            summary = order.after(summary)
            ways = [[(owner, (owner + place) % narrow)] for place in range(1, narrow)]
            summaries = [summary] + [lax.ppermute(summary, "narrow", way) for way in ways]
            moved[count - 1] = [send(order.after(rows_of(count - 1)), 0, 1)]
            for place in range(1, narrow):
                summaries[place] = order.after(summaries[place])
            galerkin = order.after(galerkin)
            galerkins = [galerkin] + [lax.ppermute(galerkin, "narrow", way) for way in ways]
        else:
            number, hop = step
            if joined and step == (joined[0], 0):
                whole = order.after(whole)
                for part in joined:
                    low, high = (bound - bounds[joined[0]][0] for bound in bounds[part])
                    moved[part] = [whole[low:high]]
            moving = moved[number][hop] = order.after(moved[number][hop])
            if number == 0 and hop + 1 < hops:
                moved[number].append(send(moving, hops - hop, hops - hop - 1))
            elif number != 0 and hop + 1 < hops:
                moved[number].append(send(moving, hop + 1, hop + 2))
    return result, galerkin


def any_owner(owner, coarse_basis, material_ids, lame_table, coarse_ids, coarse_slab):
    narrow, wide = lax.axis_size("narrow"), lax.axis_size("wide")
    stride = wide // narrow
    wide_index, narrow_index = lax.axis_index("wide"), lax.axis_index("narrow")
    own = wide_index == narrow_index * stride
    later = narrow_index > owner
    which = jnp.where(later, 0, -1)
    mode = jnp.where(narrow_index == owner, 1, jnp.where(later, 2, 0))
    earlier = (wide_index % stride == 0) & (wide_index // stride < owner)
    kind = jnp.where(wide_index == owner * stride, 1, jnp.where(earlier, 2, 0))
    table = lame_table.astype(F32)
    column = broadcast(coarse_slab, "narrow", owner)
    first, last = halo_message(table, material_ids, table, coarse_basis, coarse_slab, ())
    halo = lax.ppermute(first, "narrow", [(i + 1, i) for i in range(narrow - 1)])
    edge = (narrow_index == 0).astype(jnp.int32).reshape(1)
    inner = interior(edge, table, material_ids, coarse_basis, first)
    partial = face(settings(1), table, material_ids, last, halo, first, inner)
    parts = [lax.psum(partial, "narrow")]
    message = assemble(settings(mode, own), first, coarse_ids, coarse_slab, column, parts)
    at_owner = (wide_index == owner * stride) & (narrow_index == owner)
    diagonal = lax.psum(jnp.where(at_owner, message, 0.0), ("wide", "narrow"))
    summary, _, galerkin = factorize(settings(1, 0), first, [diagonal], [parts])
    head = broadcast(message, "wide", narrow_index * stride)
    weights, rows, lower = prepare(settings(0, mode), settings(mode), head, [summary])
    added, galerkin = added_of(settings(0, mode, own), weights, coarse_ids, [galerkin], head.shape[0])
    flags = settings(mode, kind, own, which)
    tile = coarse_slab.shape[0] // 12
    result, _ = panel(flags, flags, lower, weights, rows, added, coarse_slab, [[column]], None, 0, tile)
    return result, galerkin


def on_device(coarse_basis, material_ids, lame_table, coarse_ids, coarse_slab, panel_owner):
    narrow, wide = lax.axis_size("narrow"), lax.axis_size("wide")
    arrays = (coarse_basis, material_ids, lame_table, coarse_ids, coarse_slab)
    owner = panel_owner[0]
    if narrow - 1 > len(PLANS) or wide & (wide - 1):
        return any_owner(owner, *arrays)
    branches = [functools.partial(known_owner, place) for place in range(narrow - 1)]
    return lax.switch(owner, branches, *arrays)


def solution(mesh):
    return jax.shard_map(
        on_device,
        mesh=mesh,
        in_specs=(
            P("wide", None, None, "narrow", None, None),
            P("wide", "narrow", None, None),
            P(),
            P("wide", None),
            P("wide", "narrow"),
            P(),
        ),
        out_specs=(P("wide", "narrow"), P("wide", None, None)),
        check_vma=False,
    )
```

```python
import functools

import jax
import jax.numpy as jnp
from jax import lax
from jax.experimental import pallas as pl
from jax.experimental.pallas import tpu as pltpu
from jax.sharding import PartitionSpec as P

F32, BF16 = jnp.float32, jnp.bfloat16
NT = (((1,), (1,)), ((), ()))
TN = (((0,), (0,)), ((), ()))
VMEM = pl.BlockSpec(memory_space=pltpu.VMEM)
ANY = pl.BlockSpec(memory_space=pl.ANY)
SMEM = pl.BlockSpec(memory_space=pltpu.SMEM)
PLANS = {
    1: (
        (14, 8, 2),
        (),
        (
            (0, 0), "assemble", "spread", "next", "others", "spread", "more", "spread", "factor",
            ("panel", 1, 2), ("panel", 0, 1), ("panel", 2, 3),
        ),
    ),
    2: (
        (14, 4, 4, 2),
        (),
        (
            (0, 0), "next", "assemble", "spread", "others", "spread", "more", "spread", (1, 0), "factor",
            (2, 0), ("panel", 1, 2), (3, 0), ("panel", 2, 3), ("panel", 0, 1), ("panel", 3, 4),
        ),
    ),
    3: (
        (12, 4, 4, 2, 2),
        (1, 2, 3),
        (
            (0, 0), "next", "assemble", "spread", "others", "spread", "more", "spread", "factor",
            (1, 0), (1, 1), (0, 1), (2, 0), (2, 1), (3, 0), ("panel", 1, 2), (3, 1), (4, 0), ("panel", 2, 3), (4, 1),
            ("panel", 0, 1), ("panel", 3, 5),
        ),
    ),
}
BLOCK = 16
LIGHT = pl.CostEstimate(flops=1, bytes_accessed=1, transcendentals=0)


def exact_dot(left, right, dims=(((1,), (0,)), ((), ()))):
    return lax.dot_general(
        left, right, dims, precision=lax.Precision.HIGHEST, preferred_element_type=F32
    )


def dot(left, right, dims=(((1,), (0,)), ((), ()))):
    return lax.dot_general(left, right, dims, preferred_element_type=F32)


def split_two(value):
    high = value.astype(BF16)
    return high, (value - high.astype(F32)).astype(BF16)


def lame_of(ids, table_ref):
    shear = jnp.zeros(ids.shape, F32)
    dilate = jnp.zeros(ids.shape, F32)
    for material in range(table_ref.shape[1]):
        chosen = ids == material
        shear = jnp.where(chosen, table_ref[0, material], shear)
        dilate = jnp.where(chosen, table_ref[1, material], dilate)
    return shear, dilate


def halo_kernel(table_ref, ids_ref, token_ref, basis_ref, slab_ref, out_ref, last_ref, *rest, spans):
    piece_refs, sems = rest[:-1], rest[-1]
    subs, funcs, comps, layers = basis_ref.shape[0:4]
    copies = []
    for number, ((low, high), piece_ref) in enumerate(zip(spans, piece_refs)):
        copies.append(pltpu.make_async_copy(slab_ref.at[pl.ds(low, high - low)], piece_ref, sems.at[number]))
        copies[-1].start()
    for sub in range(subs):
        for comp in range(comps):
            out_ref[sub, comp * funcs : (comp + 1) * funcs] = basis_ref[sub, :, comp, 0]
            last_ref[sub, comp * funcs : (comp + 1) * funcs] = basis_ref[sub, :, comp, layers - 1]
        shear, dilate = lame_of(ids_ref[sub, 0], table_ref)
        out_ref[sub, comps * funcs] = shear.astype(BF16)
        out_ref[sub, comps * funcs + 1] = dilate.astype(BF16)
    for copy in copies:
        copy.wait()


def halo_message(table, ids, token, basis, slab, spans):
    subs, funcs, comps, layers, ny, nz = basis.shape
    return pl.pallas_call(
        functools.partial(halo_kernel, spans=spans),
        in_specs=[SMEM, VMEM, ANY, VMEM, ANY],
        out_specs=[VMEM] * (2 + len(spans)),
        out_shape=[
            jax.ShapeDtypeStruct((subs, comps * funcs + 2, ny, nz), BF16),
            jax.ShapeDtypeStruct((subs, comps * funcs, ny, nz), BF16),
        ]
        + [jax.ShapeDtypeStruct((high - low, slab.shape[1]), BF16) for low, high in spans],
        scratch_shapes=[pltpu.SemaphoreType.DMA((max(1, len(spans)),))],
        compiler_params=pltpu.CompilerParams(vmem_limit_bytes=16 * 2**20),
        cost_estimate=LIGHT,
        name="halo_message",
    )(table, ids, token, basis, slab)


def interior_kernel(edge_ref, table_ref, ids_ref, basis_ref, token_ref, out_ref, fields, turned, coef, left, right, acc):
    sub, comp = pl.program_id(0), pl.program_id(1)
    layers, ny, nz = basis_ref.shape[3:]
    funcs = basis_ref.shape[1]
    row = lax.broadcasted_iota(jnp.int32, (ny, nz), 0)
    lane = lax.broadcasted_iota(jnp.int32, (ny, nz), 1)
    table = [lame_of(ids_ref[sub, x], table_ref) for x in range(layers)]

    def weight(one, two, direction):
        shear = 0.5 * (one[0] + two[0])
        dilate = 0.5 * (one[1] + two[1])
        return shear + jnp.where(comp == direction, shear + dilate, 0.0)

    def ahead(field, axis):
        size = field.shape[axis]
        index = row if axis == 0 else lane
        return jnp.where(index == size - 1, 0.0, pltpu.roll(field, size - 1, axis=axis))

    def behind(field, axis):
        index = row if axis == 0 else lane
        return jnp.where(index == 0, 0.0, pltpu.roll(field, 1, axis=axis))

    nothing = (jnp.zeros((ny, nz), F32),) * 2
    previous = weight(table[0], nothing, 0) * edge_ref[0].astype(F32)
    for x in range(layers):
        diagonal = previous
        forward = []
        if x + 1 < layers:
            face = weight(table[x], table[x + 1], 0)
            diagonal = diagonal + face
            previous = face
            forward.append(face)
        else:
            forward.append(jnp.zeros((ny, nz), F32))
        for axis in (0, 1):
            index, size = (row, ny) if axis == 0 else (lane, nz)
            other = tuple(ahead(value, axis) for value in table[x])
            face = weight(table[x], other, axis + 1)
            before = tuple(behind(value, axis) for value in table[x])
            diagonal = diagonal + face + weight(table[x], before, axis + 1)
            forward.append(jnp.where(index == size - 1, 0.0, face))
        coef[x, 0] = 0.5 * diagonal
        for kind in range(3):
            coef[x, kind + 1] = forward[kind]
        fields[x] = basis_ref[sub, :, comp, x].astype(F32).reshape(funcs * ny, nz)

    total = None
    for x in reversed(range(layers)):
        values = [fields[x, pl.ds(y, funcs, stride=ny), :] for y in range(ny)]
        for y in range(ny):
            value = values[y]
            turned[x % 2, y] = value
            image = coef[x, 0, y : y + 1, :] * value
            image = image - coef[x, 3, y : y + 1, :] * pltpu.roll(value, nz - 1, axis=1)
            if y + 1 < ny:
                image = image - coef[x, 2, y : y + 1, :] * values[y + 1]
            if x + 1 < layers:
                image = image - coef[x, 1, y : y + 1, :] * turned[(x + 1) % 2, y]
            high, low = split_two(image)
            left[:, y * nz : (y + 1) * nz] = value.astype(BF16)
            right[0:funcs, y * nz : (y + 1) * nz] = high
            right[funcs : 2 * funcs, y * nz : (y + 1) * nz] = low
        product = dot(right[...], left[...], NT)
        total = product if total is None else total + product

    @pl.when(comp == 0)
    def _():
        acc[...] = total

    @pl.when(comp > 0)
    def _():
        acc[...] += total

    @pl.when(comp == pl.num_programs(1) - 1)
    def _():
        out_ref[0] = acc[0:funcs] + acc[funcs : 2 * funcs]


def interior(edge, table, ids, basis, token):
    subs, funcs, comps, layers, ny, nz = basis.shape
    return pl.pallas_call(
        interior_kernel,
        grid=(subs, comps),
        in_specs=[SMEM, SMEM, VMEM, VMEM, ANY],
        out_specs=pl.BlockSpec((1, funcs, funcs), lambda s, c: (s, 0, 0)),
        out_shape=jax.ShapeDtypeStruct((subs, funcs, funcs), F32),
        scratch_shapes=[
            pltpu.VMEM((layers, funcs * ny, nz), F32),
            pltpu.VMEM((2, ny, funcs, nz), F32),
            pltpu.VMEM((layers, 4, ny, nz), F32),
            pltpu.VMEM((funcs, ny * nz), BF16),
            pltpu.VMEM((2 * funcs, ny * nz), BF16),
            pltpu.VMEM((2 * funcs, funcs), F32),
        ],
        compiler_params=pltpu.CompilerParams(vmem_limit_bytes=16 * 2**20),
        cost_estimate=LIGHT,
        name="interior",
    )(edge, table, ids, basis, token)


def face_kernel(flags_ref, table_ref, ids_ref, last_ref, halo_ref, token_ref, inner_ref, out_ref, *scratch):
    @pl.when(flags_ref[0] == 1)
    def _():
        last, halo, sems = scratch[-3:]
        copies = [
            pltpu.make_async_copy(last_ref, last, sems.at[0]),
            pltpu.make_async_copy(halo_ref, halo, sems.at[1]),
        ]
        for copy in copies:
            copy.start()
        for copy in copies:
            copy.wait()
        face_sums(table_ref, ids_ref, last, halo, inner_ref, out_ref, *scratch[:-3])


def face_sums(table_ref, ids_ref, last_ref, halo_ref, inner_ref, out_ref, mine, theirs, left, right, weights, acc):
    subs, layers, ny, nz = ids_ref.shape
    funcs = inner_ref.shape[1]
    comps = last_ref.shape[1] // funcs

    @pl.loop(0, subs)
    def _(sub):
        shear, dilate = lame_of(ids_ref[sub, layers - 1], table_ref)
        weights[0] = 0.5 * (shear + halo_ref[sub, comps * funcs].astype(F32))
        weights[1] = 0.5 * (dilate + halo_ref[sub, comps * funcs + 1].astype(F32))

        @pl.loop(0, comps)
        def _(comp):
            weight = weights[0] + jnp.where(comp == 0, weights[0] + weights[1], 0.0)
            rows = pl.ds(comp * funcs, funcs)
            mine[...] = last_ref[sub, rows].astype(F32).reshape(funcs * ny, nz)
            theirs[...] = halo_ref[sub, rows].astype(F32).reshape(funcs * ny, nz)
            for y in range(ny):
                here = mine[pl.ds(y, funcs, stride=ny), :]
                there = theirs[pl.ds(y, funcs, stride=ny), :]
                high, low = split_two(weight[y : y + 1, :] * (here - there))
                left[0:funcs, y * nz : (y + 1) * nz] = here.astype(BF16)
                left[funcs : 2 * funcs, y * nz : (y + 1) * nz] = there.astype(BF16)
                right[0:funcs, y * nz : (y + 1) * nz] = high
                right[funcs : 2 * funcs, y * nz : (y + 1) * nz] = low
            product = dot(right[...], left[...], NT)

            @pl.when(comp == 0)
            def _():
                acc[...] = product

            @pl.when(comp > 0)
            def _():
                acc[...] += product

        total = acc[:, 0:funcs] - acc[:, funcs : 2 * funcs]
        half = inner_ref[sub] + 0.5 * (total[0:funcs] + total[funcs : 2 * funcs])
        out_ref[sub] = half + half.T


def face(flags, table, ids, last, halo, token, inner):
    subs, layers, ny, nz = ids.shape
    funcs = inner.shape[1]
    return pl.pallas_call(
        face_kernel,
        in_specs=[SMEM, SMEM, VMEM, ANY, ANY, ANY, VMEM],
        out_specs=VMEM,
        out_shape=jax.ShapeDtypeStruct((subs, funcs, funcs), F32),
        scratch_shapes=[
            pltpu.VMEM((funcs * ny, nz), F32),
            pltpu.VMEM((funcs * ny, nz), F32),
            pltpu.VMEM((2 * funcs, ny * nz), BF16),
            pltpu.VMEM((2 * funcs, ny * nz), BF16),
            pltpu.VMEM((2, ny, nz), F32),
            pltpu.VMEM((2 * funcs, 2 * funcs), F32),
            pltpu.VMEM(last.shape, BF16),
            pltpu.VMEM(halo.shape, BF16),
            pltpu.SemaphoreType.DMA((2,)),
        ],
        compiler_params=pltpu.CompilerParams(vmem_limit_bytes=16 * 2**20),
        cost_estimate=LIGHT,
        name="face",
    )(flags, table, ids, last, halo, token, inner)


def spread(gal_ref, column_ids_ref, row_ids_ref, size):
    subs, funcs = column_ids_ref.shape[0:2]
    added = jnp.zeros((size, size), F32)
    lane = lax.broadcasted_iota(jnp.int32, (funcs, size), 1)
    row = lax.broadcasted_iota(jnp.int32, (size, funcs), 0)
    for sub in range(subs):
        slots = (column_ids_ref[sub] == lane).astype(F32)
        slots_t = (row_ids_ref[sub] == row).astype(F32)
        added = added + exact_dot(slots_t, exact_dot(gal_ref[sub], slots))
    return added


def assemble_kernel(flags_ref, token_ref, column_ids_ref, row_ids_ref, slab_ref, head_ref, *rest):
    gal_refs, (message_ref, sum_ref) = rest[:-2], rest[-2:]
    size = message_ref.shape[0]
    mode, own = flags_ref[0], flags_ref[1]
    message_ref[...] = jnp.zeros_like(message_ref)

    @pl.when((mode == 1) & (own == 1))
    def _():
        total = gal_refs[0][...]
        for gal_ref in gal_refs[1:]:
            total = total + gal_ref[...]
        sum_ref[...] = total
        added = spread(sum_ref, column_ids_ref, row_ids_ref, size)
        message_ref[...] = added + slab_ref[...].astype(F32)

    @pl.when((mode == 2) & (own == 1))
    def _():
        message_ref[...] = head_ref[...].astype(F32)


def assemble(flags, token, ids, slab, head, parts):
    size = slab.shape[1]
    block = pl.BlockSpec((size, size), lambda i: (0, 0))
    return pl.pallas_call(
        assemble_kernel,
        grid=(1,),
        in_specs=[SMEM, ANY, VMEM, VMEM, block, block] + [VMEM] * len(parts),
        out_specs=VMEM,
        out_shape=jax.ShapeDtypeStruct((size, size), F32),
        scratch_shapes=[pltpu.VMEM(parts[0].shape, F32)],
        cost_estimate=LIGHT,
        name="assemble",
    )(flags, token, ids[:, :, None], ids[:, None, :], slab, head, *parts)


def factor_kernel(flags_ref, token_ref, *refs, parts, groups):
    message_refs, gal_refs = refs[:parts], refs[parts:-4]
    summary_ref, block_ref, sum_ref, work = refs[-4:]
    subs, funcs = gal_refs[0].shape[0:2]
    size = summary_ref.shape[1]
    diagonal = message_refs[0][...]
    for message_ref in message_refs[1:]:
        diagonal = diagonal + message_ref[...]
    block_ref[...] = diagonal

    @pl.when(flags_ref[0] == 1)
    def _():
        row = lax.broadcasted_iota(jnp.int32, (size, size), 0)
        lane = lax.broadcasted_iota(jnp.int32, (size, size), 1)
        work[:, 0:size] = 0.5 * (diagonal + diagonal.T)
        work[:, size : 2 * size] = (row == lane).astype(F32)
        index = lax.broadcasted_iota(jnp.int32, (BLOCK, size), 0)
        for start in range(0, size, BLOCK):
            panel = work[start : start + BLOCK, 0:size]
            extra = work[start : start + BLOCK, size : 2 * size]
            columns = [
                jnp.broadcast_to(panel[:, start + step : start + step + 1], (BLOCK, size))
                for step in range(BLOCK)
            ]
            for step in range(BLOCK):
                scale = lax.rsqrt(columns[step][step : step + 1, :])
                column = jnp.where(index > step, columns[step] * scale, 0.0)
                for later in range(step + 1, BLOCK):
                    columns[later] = columns[later] - column * column[later : later + 1, :]
                pivot = panel[step : step + 1, :] * scale
                panel = jnp.where(index == step, pivot, panel - column * pivot)
                pivot = extra[step : step + 1, :] * scale
                extra = jnp.where(index == step, pivot, extra - column * pivot)
            work[start : start + BLOCK, 0:size] = panel
            work[start : start + BLOCK, size : 2 * size] = extra
            rest = start + BLOCK
            if rest < size:
                both = jnp.concatenate([panel, extra], axis=1)
                work[rest:size, :] -= exact_dot(panel[:, rest:size], both, TN)
        upper = jnp.where(row <= lane, work[:, 0:size], 0.0)
        inverse = jnp.where(row >= lane, work[:, size : 2 * size], 0.0).T
        high = inverse.astype(BF16)
        summary_ref[0:size] = high
        summary_ref[size : 2 * size] = (inverse - high.astype(F32)).astype(BF16)
        summary_ref[2 * size : 3 * size] = upper.T.astype(BF16)
        each = len(gal_refs) // groups
        for group in range(groups):

            @pl.when(flags_ref[1] == group)
            def _(chosen=gal_refs[group * each : (group + 1) * each]):
                total = chosen[0][...]
                for gal_ref in chosen[1:]:
                    total = total + gal_ref[...]
                sum_ref[...] = total


def factorize(flags, token, messages, groups):
    size = messages[0].shape[1]
    subs, funcs = groups[0][0].shape[0:2]
    parts = [part for group in groups for part in group]
    return pl.pallas_call(
        functools.partial(factor_kernel, parts=len(messages), groups=len(groups)),
        in_specs=[SMEM, ANY] + [VMEM] * (len(messages) + len(parts)),
        out_specs=[VMEM] * 3,
        out_shape=[
            jax.ShapeDtypeStruct((3 * size, size), BF16),
            jax.ShapeDtypeStruct((size, size), F32),
            jax.ShapeDtypeStruct(groups[0][0].shape, F32),
        ],
        scratch_shapes=[pltpu.VMEM((size, 2 * size), F32)],
        cost_estimate=LIGHT,
        name="factorize",
    )(flags, token, *messages, *parts)


def prepare_kernel(flags_ref, token_ref, head_ref, *rest, sources):
    summary_refs = rest[:sources]
    weights_ref, rows_ref, lower_ref, summary, sem = rest[sources:]
    size = head_ref.shape[0]
    choice, mode = flags_ref[0], flags_ref[1]
    for number, summary_ref in enumerate(summary_refs):

        @pl.when(choice == number)
        def _(summary_ref=summary_ref):
            copy = pltpu.make_async_copy(summary_ref, summary, sem)
            copy.start()
            copy.wait()

    def doubled(block):
        nothing = jnp.zeros((size, size), BF16)
        top = jnp.concatenate([block, nothing], axis=1)
        return jnp.concatenate([top, jnp.concatenate([nothing, block], axis=1)], axis=0)

    @pl.when(mode > 0)
    def _():
        weights_ref[0 : 2 * size] = doubled(summary[0:size])
        weights_ref[2 * size : 4 * size] = doubled(summary[size : 2 * size])
        lower_ref[...] = summary[2 * size : 3 * size]

    @pl.when(mode == 2)
    def _():
        inverse = summary[0:size].astype(F32) + summary[size : 2 * size].astype(F32)
        solved = exact_dot(head_ref[...], inverse)
        rows_ref[...] = doubled(solved.T.astype(BF16))


def prepare(flags, token, head, summaries):
    size = head.shape[0]
    return pl.pallas_call(
        functools.partial(prepare_kernel, sources=len(summaries)),
        in_specs=[SMEM, ANY, VMEM] + [ANY] * len(summaries),
        out_specs=[VMEM] * 3,
        out_shape=[
            jax.ShapeDtypeStruct((4 * size, 2 * size), BF16),
            jax.ShapeDtypeStruct((2 * size, 2 * size), BF16),
            jax.ShapeDtypeStruct((size, size), BF16),
        ],
        scratch_shapes=[pltpu.VMEM(summaries[0].shape, BF16), pltpu.SemaphoreType.DMA],
        compiler_params=pltpu.CompilerParams(vmem_limit_bytes=16 * 2**20),
        cost_estimate=LIGHT,
        name="prepare",
    )(flags, token, head, *summaries)


def added_kernel(flags_ref, token_ref, column_ids_ref, row_ids_ref, *rest, sources):
    sum_refs, (added_ref, gal_ref) = rest[:sources], rest[sources:]
    for number, sum_ref in enumerate(sum_refs):

        @pl.when(flags_ref[0] == number)
        def _(sum_ref=sum_ref):
            gal_ref[...] = sum_ref[...]

    @pl.when((flags_ref[1] == 2) & (flags_ref[2] == 1))
    def _():
        added_ref[...] = spread(gal_ref, column_ids_ref, row_ids_ref, added_ref.shape[0])


def added_of(flags, token, ids, sums, size):
    return pl.pallas_call(
        functools.partial(added_kernel, sources=len(sums)),
        in_specs=[SMEM, ANY] + [VMEM] * (2 + len(sums)),
        out_specs=[VMEM] * 2,
        out_shape=[jax.ShapeDtypeStruct((size, size), F32), jax.ShapeDtypeStruct(sums[0].shape, F32)],
        cost_estimate=LIGHT,
        name="added",
    )(flags, token, ids[:, :, None], ids[:, None, :], *sums)


def panel_kernel(
    flags_ref, token_ref, lower_ref, weights_ref, rows_ref, added_ref, slab_ref, *rest, pieces, spans, first
):
    hops = len(pieces) // len(spans)
    others = rest[: len(pieces)]
    out_ref, done_ref, column, factor, sems = rest[-5:]
    done_ref[0] = flags_ref[0]
    tile, size = out_ref.shape
    half = tile // 2
    mode, head, own, which = flags_ref[0], flags_ref[1], flags_ref[2], flags_ref[3]
    step, steps = pl.program_id(0), pl.num_programs(0)
    top = first & (step == 0)

    def copy_of(at, act):
        for number, (begin, end) in enumerate(spans):
            for hop in range(hops):

                @pl.when((mode == 2) & (which == hop) & (at >= begin) & (at < end))
                def _(other_ref=others[number * hops + hop], begin=begin):
                    source = other_ref.at[pl.ds(pl.multiple_of((at - begin) * tile, tile), tile)]
                    act(pltpu.make_async_copy(source, column.at[at % 2], sems.at[at % 2]))

    @pl.when(step == 0)
    def _():
        copy_of(step, lambda copy: copy.start())

    @pl.when(step + 1 < steps)
    def _():
        copy_of(step + 1, lambda copy: copy.start())

    @pl.when(mode == 0)
    def _():
        out_ref[...] = slab_ref[...]

    @pl.when(mode == 1)
    def _():
        column[step % 2] = slab_ref[...]

    @pl.when(mode == 2)
    def _():
        copy_of(step, lambda copy: copy.wait())

    @pl.when(mode > 0)
    def _():
        value = column[step % 2]
        pair = jnp.concatenate([value[0:half], value[half:tile]], axis=1)
        factor[...] = dot(jnp.concatenate([pair, pair], axis=1), weights_ref[...]).astype(BF16)

        @pl.when(top & (head == 1))
        def _():
            factor[0:size, 0:size] = lower_ref[...]

        @pl.when(top & (head == 2))
        def _():
            factor[0:size, 0:size] = jnp.zeros((size, size), BF16)

    @pl.when(mode == 1)
    def _():
        out_ref[0:half] = factor[:, 0:size]
        out_ref[half:tile] = factor[:, size : 2 * size]

    @pl.when(mode == 2)
    def _():
        update = dot(factor[...], rows_ref[...])
        out_ref[0:half] = (slab_ref[0:half].astype(F32) - update[:, 0:size]).astype(BF16)
        out_ref[half:tile] = (slab_ref[half:tile].astype(F32) - update[:, size : 2 * size]).astype(BF16)

        @pl.when(top & (own == 1))
        def _():
            base = slab_ref[0:size].astype(F32) + added_ref[...]
            out_ref[0:size] = (base - update[0:size, 0:size]).astype(BF16)


def panel(flags, token, lower, weights, rows, added, slab, parts, old, start, tile):
    size = slab.shape[1]
    offset = start // tile
    spans, begin, operands = [], 0, []
    for hops in parts:
        end = begin + hops[0].shape[0] // tile
        spans.append((begin, end))
        begin = end
        operands += hops
    blocks = [
        SMEM,
        ANY,
        pl.BlockSpec((size, size), lambda i: (0, 0)),
        pl.BlockSpec(weights.shape, lambda i: (0, 0)),
        pl.BlockSpec(rows.shape, lambda i: (0, 0)),
        pl.BlockSpec((size, size), lambda i: (0, 0)),
        pl.BlockSpec((tile, size), lambda i: (i + offset, 0)),
    ] + [ANY] * len(operands)
    pieces = len(operands)
    operands = [flags, token, lower, weights, rows, added, slab] + operands
    aliases = {}
    if old is not None:
        aliases = {len(operands): 0}
        blocks.append(ANY)
        operands.append(old)
    return pl.pallas_call(
        functools.partial(panel_kernel, pieces=range(pieces), spans=spans, first=start == 0),
        grid=(begin,),
        in_specs=blocks,
        out_specs=[pl.BlockSpec((tile, size), lambda i: (i + offset, 0)), SMEM],
        out_shape=[jax.ShapeDtypeStruct(slab.shape, BF16), jax.ShapeDtypeStruct((1,), jnp.int32)],
        input_output_aliases=aliases,
        scratch_shapes=[
            pltpu.VMEM((2, tile, size), BF16),
            pltpu.VMEM((tile // 2, 2 * size), BF16),
            pltpu.SemaphoreType.DMA((2,)),
        ],
        compiler_params=pltpu.CompilerParams(vmem_limit_bytes=16 * 2**20),
        cost_estimate=LIGHT,
        name="panel",
    )(*operands)


def broadcast(value, axis, source):
    kept = jnp.where(lax.axis_index(axis) == source, value, 0).astype(value.dtype)
    return lax.psum(kept, axis)


def settings(*values):
    return jnp.stack([jnp.asarray(value).astype(jnp.int32) for value in values])


def holder_pairs(wide, narrow, distance):
    stride = wide // narrow
    found = []
    for n in range(narrow):
        for start in range(0, wide, 2 * distance):
            source = (n * stride) ^ start
            found.append((source * narrow + n, (source ^ distance) * narrow + n))
    return found


class Order:
    def __init__(self, token):
        self.token = token

    def after(self, value):
        value, self.token = lax.optimization_barrier((value, self.token))
        return value


def known_owner(owner, coarse_basis, material_ids, lame_table, coarse_ids, coarse_slab):
    narrow, wide = lax.axis_size("narrow"), lax.axis_size("wide")
    stride = wide // narrow
    wide_index, narrow_index = lax.axis_index("wide"), lax.axis_index("narrow")
    height, block = coarse_slab.shape
    own = wide_index == narrow_index * stride
    later = narrow_index > owner
    which = jnp.where(later, narrow_index - owner - 1, -1)
    mode = jnp.where(narrow_index == owner, 1, jnp.where(later, 2, 0))
    earlier = (wide_index % stride == 0) & (wide_index // stride < owner)
    kind = jnp.where(wide_index == owner * stride, 1, jnp.where(earlier, 2, 0))
    table = lame_table.astype(F32)
    hops = narrow - 1 - owner
    units, joined, plan = PLANS[hops]
    unit = height // sum(units)
    count = len(units)
    bounds, low = [], 0
    for number in units:
        bounds.append((low, low + number * unit))
        low += number * unit
    axes = ("wide", "narrow")

    def rows_of(number):
        low, high = bounds[number]
        return coarse_slab[low:high]

    def send(value, source, target):
        return lax.ppermute(value, "narrow", [(owner + source, owner + target)])

    order = Order(settings(mode))

    ways = [((n * stride) * narrow + owner, (n * stride) * narrow + n) for n in range(owner + 1, narrow)]
    head = order.after(lax.ppermute(coarse_slab[:block], axes, ways))
    moved = {}

    groups = [[w for w in range(wide) if w % stride == 0], [w for w in range(wide) if w % stride]]
    groups = [group for group in groups if group]
    member = jnp.where(wide_index % stride == 0, 0, 1)

    def within(group, pairs):
        return [(w * narrow + one, w * narrow + two) for w in group for one, two in pairs]

    def halo_of(group, message):
        return lax.ppermute(message, axes, within(group, [(i + 1, i) for i in range(narrow - 1)]))

    spans = [bounds[0], (bounds[joined[0]][0], bounds[joined[-1]][1]) if joined else bounds[1]]
    first, last, *begun = halo_message(table, material_ids, order.token, coarse_basis, coarse_slab, spans)
    first = order.after(first)
    halos = [halo_of(groups[0], first)]
    moved[0] = [send(order.after(begun[0]), 0, hops)]
    edge = (narrow_index == 0).astype(jnp.int32).reshape(1)
    inner = order.after(interior(edge, table, material_ids, coarse_basis, order.token))
    halos[0] = order.after(halos[0])
    for group in groups[1:]:
        halos.append(halo_of(group, order.after(first)))

    def nearest(base, extent):
        return min(range(base, min(base + extent, narrow)), key=lambda n: abs(n - owner))

    def summed(parts, distance, group):
        total = parts[0] if len(parts) == 1 else parts[0] + parts[1]
        pairs = []
        for base in range(0, narrow - distance, 2 * distance):
            one, two = nearest(base, distance), nearest(base + distance, distance)
            pairs.append((two, one) if nearest(base, 2 * distance) == one else (one, two))
        return [total, lax.ppermute(total, axes, within(group, pairs))], 2 * distance

    def faces_of(number):
        flag = settings(member == number)
        return [order.after(face(flag, table, material_ids, last, halos[number], order.token, inner))]

    sums, reach = [faces_of(0)], [1]
    while reach[0] < narrow:
        sums[0], reach[0] = summed(sums[0], reach[0], groups[0])
    sums[0][1] = order.after(sums[0][1])
    distance, messages, left = wide // 2, [], plan.count("spread")
    result, prepared = None, None
    choice = (narrow_index - owner) % narrow
    flags = settings(mode, kind, own, which)
    for step in plan:
        if step[0] == "panel":
            if prepared is None:
                prepared = prepare(settings(choice, mode), order.token, head, summaries)
                added, galerkin = added_of(
                    settings(choice, mode, own), prepared[0], coarse_ids, galerkins, block
                )
            weights, rows, lower = prepared
            begin, end = step[1:]
            parts = [moved[number][:: 1 if number else -1] for number in range(begin, end)]
            result, order.token = panel(
                flags, order.token, lower, weights, rows, added if begin == 0 else head, coarse_slab, parts, result, bounds[begin][0], 2 * unit
            )
        elif step == "next":
            if joined:
                whole = send(order.after(begun[1]), 0, 1)
            else:
                moved[1] = [send(order.after(begun[1]), 0, 1)]
                for number in range(2, count - 1):
                    moved[number] = [send(order.after(rows_of(number)), 0, 1)]
        elif step == "assemble":
            message = assemble(settings(mode, own), order.token, coarse_ids, coarse_slab, head, sums[0])
            message = order.after(message)
        elif step == "others":
            for number in range(1, len(groups)):
                halos[number] = order.after(halos[number])
                parts, far = summed(faces_of(number), 1, groups[number])
                sums.append(parts)
                reach.append(far)
        elif step == "more":
            for number in range(1, len(groups)):
                while reach[number] < narrow:
                    sums[number][1] = order.after(sums[number][1])
                    sums[number], reach[number] = summed(sums[number], reach[number], groups[number])
        elif step == "spread":
            left -= 1
            while distance:
                received = order.after(lax.ppermute(message, axes, holder_pairs(wide, narrow, distance)))
                messages = [message, received]
                if distance > 1:
                    message = message + received
                distance //= 2
                if left:
                    break
        elif step == "factor":
            summary, head, galerkin = factorize(settings(mode, member), order.token, messages, sums)
            summary = order.after(summary)
            ways = [[(owner, (owner + place) % narrow)] for place in range(1, narrow)]
            summaries = [summary] + [lax.ppermute(summary, "narrow", way) for way in ways]
            moved[count - 1] = [send(order.after(rows_of(count - 1)), 0, 1)]
            for place in range(1, narrow):
                summaries[place] = order.after(summaries[place])
            galerkin = order.after(galerkin)
            galerkins = [galerkin] + [lax.ppermute(galerkin, "narrow", way) for way in ways]
        else:
            number, hop = step
            if joined and step == (joined[0], 0):
                whole = order.after(whole)
                for part in joined:
                    low, high = (bound - bounds[joined[0]][0] for bound in bounds[part])
                    moved[part] = [whole[low:high]]
            moving = moved[number][hop] = order.after(moved[number][hop])
            if number == 0 and hop + 1 < hops:
                moved[number].append(send(moving, hops - hop, hops - hop - 1))
            elif number != 0 and hop + 1 < hops:
                moved[number].append(send(moving, hop + 1, hop + 2))
    return result, galerkin


def any_owner(owner, coarse_basis, material_ids, lame_table, coarse_ids, coarse_slab):
    narrow, wide = lax.axis_size("narrow"), lax.axis_size("wide")
    stride = wide // narrow
    wide_index, narrow_index = lax.axis_index("wide"), lax.axis_index("narrow")
    own = wide_index == narrow_index * stride
    later = narrow_index > owner
    which = jnp.where(later, 0, -1)
    mode = jnp.where(narrow_index == owner, 1, jnp.where(later, 2, 0))
    earlier = (wide_index % stride == 0) & (wide_index // stride < owner)
    kind = jnp.where(wide_index == owner * stride, 1, jnp.where(earlier, 2, 0))
    table = lame_table.astype(F32)
    column = broadcast(coarse_slab, "narrow", owner)
    first, last = halo_message(table, material_ids, table, coarse_basis, coarse_slab, ())
    halo = lax.ppermute(first, "narrow", [(i + 1, i) for i in range(narrow - 1)])
    edge = (narrow_index == 0).astype(jnp.int32).reshape(1)
    inner = interior(edge, table, material_ids, coarse_basis, first)
    partial = face(settings(1), table, material_ids, last, halo, first, inner)
    parts = [lax.psum(partial, "narrow")]
    message = assemble(settings(mode, own), first, coarse_ids, coarse_slab, column, parts)
    at_owner = (wide_index == owner * stride) & (narrow_index == owner)
    diagonal = lax.psum(jnp.where(at_owner, message, 0.0), ("wide", "narrow"))
    summary, _, galerkin = factorize(settings(1, 0), first, [diagonal], [parts])
    head = broadcast(message, "wide", narrow_index * stride)
    weights, rows, lower = prepare(settings(0, mode), settings(mode), head, [summary])
    added, galerkin = added_of(settings(0, mode, own), weights, coarse_ids, [galerkin], head.shape[0])
    flags = settings(mode, kind, own, which)
    tile = coarse_slab.shape[0] // 12
    result, _ = panel(flags, flags, lower, weights, rows, added, coarse_slab, [[column]], None, 0, tile)
    return result, galerkin


def on_device(coarse_basis, material_ids, lame_table, coarse_ids, coarse_slab, panel_owner):
    narrow, wide = lax.axis_size("narrow"), lax.axis_size("wide")
    arrays = (coarse_basis, material_ids, lame_table, coarse_ids, coarse_slab)
    owner = panel_owner[0]
    if narrow - 1 > len(PLANS) or wide & (wide - 1):
        return any_owner(owner, *arrays)
    branches = [functools.partial(known_owner, place) for place in range(narrow - 1)]
    return lax.switch(owner, branches, *arrays)


def solution(mesh):
    return jax.shard_map(
        on_device,
        mesh=mesh,
        in_specs=(
            P("wide", None, None, "narrow", None, None),
            P("wide", "narrow", None, None),
            P(),
            P("wide", None),
            P("wide", "narrow"),
            P(),
        ),
        out_specs=(P("wide", "narrow"), P("wide", None, None)),
        check_vma=False,
    )
```

```python
import functools

import jax
import jax.numpy as jnp
from jax import lax
from jax.experimental import pallas as pl
from jax.experimental.pallas import tpu as pltpu
from jax.sharding import PartitionSpec as P

F32, BF16 = jnp.float32, jnp.bfloat16
NT = (((1,), (1,)), ((), ()))
TN = (((0,), (0,)), ((), ()))
VMEM = pl.BlockSpec(memory_space=pltpu.VMEM)
ANY = pl.BlockSpec(memory_space=pl.ANY)
SMEM = pl.BlockSpec(memory_space=pltpu.SMEM)
PLANS = {
    1: (
        (12, 6, 6),
        (),
        (
            "assemble", "next", "spread", "others", "spread", "more", "spread", (0, 0), "factor", "summary",
            "sums", ("panel", 0, 2), ("panel", 2, 3),
        ),
    ),
    2: (
        (12, 6, 4, 2),
        (),
        (
            "assemble", "next", "spread", "others", "spread", "more", "spread", (0, 0), (1, 0), "factor", (2, 0),
            "summary", ("panel", 1, 2), (3, 0), "sums", ("panel", 0, 1), ("panel", 2, 4),
        ),
    ),
    3: (
        (12, 6, 4, 2),
        (1, 2),
        (
            "assemble", "next", "spread", "others", "spread", "more", "spread", (0, 0), "factor", (1, 0), "summary",
            (0, 1), (1, 1), (2, 0), "sums", ("panel", 1, 2), (2, 1), (3, 0), ("panel", 0, 1), (3, 1), ("panel", 2, 4),
        ),
    ),
}
BLOCK = 16
LIGHT = pl.CostEstimate(flops=1, bytes_accessed=1, transcendentals=0)


def exact_dot(left, right, dims=(((1,), (0,)), ((), ()))):
    return lax.dot_general(
        left, right, dims, precision=lax.Precision.HIGHEST, preferred_element_type=F32
    )


def dot(left, right, dims=(((1,), (0,)), ((), ()))):
    return lax.dot_general(left, right, dims, preferred_element_type=F32)


def split_two(value):
    high = value.astype(BF16)
    return high, (value - high.astype(F32)).astype(BF16)


def lame_of(ids, table_ref):
    shear = jnp.zeros(ids.shape, F32)
    dilate = jnp.zeros(ids.shape, F32)
    for material in range(table_ref.shape[1]):
        chosen = ids == material
        shear = jnp.where(chosen, table_ref[0, material], shear)
        dilate = jnp.where(chosen, table_ref[1, material], dilate)
    return shear, dilate


def halo_kernel(table_ref, ids_ref, token_ref, basis_ref, slab_ref, out_ref, last_ref, *rest, spans):
    piece_refs, sems = rest[:-1], rest[-1]
    subs, funcs, comps, layers = basis_ref.shape[0:4]
    copies = []
    for number, ((low, high), piece_ref) in enumerate(zip(spans, piece_refs)):
        copies.append(pltpu.make_async_copy(slab_ref.at[pl.ds(low, high - low)], piece_ref, sems.at[number]))
        copies[-1].start()
    for sub in range(subs):
        for comp in range(comps):
            out_ref[sub, comp * funcs : (comp + 1) * funcs] = basis_ref[sub, :, comp, 0]
            last_ref[sub, comp * funcs : (comp + 1) * funcs] = basis_ref[sub, :, comp, layers - 1]
        shear, dilate = lame_of(ids_ref[sub, 0], table_ref)
        out_ref[sub, comps * funcs] = shear.astype(BF16)
        out_ref[sub, comps * funcs + 1] = dilate.astype(BF16)
    for copy in copies:
        copy.wait()


def halo_message(table, ids, token, basis, slab, spans):
    subs, funcs, comps, layers, ny, nz = basis.shape
    return pl.pallas_call(
        functools.partial(halo_kernel, spans=spans),
        in_specs=[SMEM, VMEM, ANY, VMEM, ANY],
        out_specs=[VMEM] * (2 + len(spans)),
        out_shape=[
            jax.ShapeDtypeStruct((subs, comps * funcs + 2, ny, nz), BF16),
            jax.ShapeDtypeStruct((subs, comps * funcs, ny, nz), BF16),
        ]
        + [jax.ShapeDtypeStruct((high - low, slab.shape[1]), BF16) for low, high in spans],
        scratch_shapes=[pltpu.SemaphoreType.DMA((max(1, len(spans)),))],
        compiler_params=pltpu.CompilerParams(vmem_limit_bytes=16 * 2**20),
        cost_estimate=LIGHT,
        name="halo_message",
    )(table, ids, token, basis, slab)


def interior_kernel(edge_ref, table_ref, ids_ref, basis_ref, token_ref, out_ref, fields, turned, coef, left, right, acc):
    sub, comp = pl.program_id(0), pl.program_id(1)
    layers, ny, nz = basis_ref.shape[3:]
    funcs = basis_ref.shape[1]
    row = lax.broadcasted_iota(jnp.int32, (ny, nz), 0)
    lane = lax.broadcasted_iota(jnp.int32, (ny, nz), 1)
    table = [lame_of(ids_ref[sub, x], table_ref) for x in range(layers)]

    def weight(one, two, direction):
        shear = 0.5 * (one[0] + two[0])
        dilate = 0.5 * (one[1] + two[1])
        return shear + jnp.where(comp == direction, shear + dilate, 0.0)

    def ahead(field, axis):
        size = field.shape[axis]
        index = row if axis == 0 else lane
        return jnp.where(index == size - 1, 0.0, pltpu.roll(field, size - 1, axis=axis))

    def behind(field, axis):
        index = row if axis == 0 else lane
        return jnp.where(index == 0, 0.0, pltpu.roll(field, 1, axis=axis))

    nothing = (jnp.zeros((ny, nz), F32),) * 2
    previous = weight(table[0], nothing, 0) * edge_ref[0].astype(F32)
    for x in range(layers):
        diagonal = previous
        forward = []
        if x + 1 < layers:
            face = weight(table[x], table[x + 1], 0)
            diagonal = diagonal + face
            previous = face
            forward.append(face)
        else:
            forward.append(jnp.zeros((ny, nz), F32))
        for axis in (0, 1):
            index, size = (row, ny) if axis == 0 else (lane, nz)
            other = tuple(ahead(value, axis) for value in table[x])
            face = weight(table[x], other, axis + 1)
            before = tuple(behind(value, axis) for value in table[x])
            diagonal = diagonal + face + weight(table[x], before, axis + 1)
            forward.append(jnp.where(index == size - 1, 0.0, face))
        coef[x, 0] = 0.5 * diagonal
        for kind in range(3):
            coef[x, kind + 1] = forward[kind]
        fields[x] = basis_ref[sub, :, comp, x].astype(F32).reshape(funcs * ny, nz)

    total = None
    for x in reversed(range(layers)):
        values = [fields[x, pl.ds(y, funcs, stride=ny), :] for y in range(ny)]
        for y in range(ny):
            value = values[y]
            turned[x % 2, y] = value
            image = coef[x, 0, y : y + 1, :] * value
            image = image - coef[x, 3, y : y + 1, :] * pltpu.roll(value, nz - 1, axis=1)
            if y + 1 < ny:
                image = image - coef[x, 2, y : y + 1, :] * values[y + 1]
            if x + 1 < layers:
                image = image - coef[x, 1, y : y + 1, :] * turned[(x + 1) % 2, y]
            high, low = split_two(image)
            left[:, y * nz : (y + 1) * nz] = value.astype(BF16)
            right[0:funcs, y * nz : (y + 1) * nz] = high
            right[funcs : 2 * funcs, y * nz : (y + 1) * nz] = low
        product = dot(right[...], left[...], NT)
        total = product if total is None else total + product

    @pl.when(comp == 0)
    def _():
        acc[...] = total

    @pl.when(comp > 0)
    def _():
        acc[...] += total

    @pl.when(comp == pl.num_programs(1) - 1)
    def _():
        out_ref[0] = acc[0:funcs] + acc[funcs : 2 * funcs]


def interior(edge, table, ids, basis, token):
    subs, funcs, comps, layers, ny, nz = basis.shape
    return pl.pallas_call(
        interior_kernel,
        grid=(subs, comps),
        in_specs=[SMEM, SMEM, VMEM, VMEM, ANY],
        out_specs=pl.BlockSpec((1, funcs, funcs), lambda s, c: (s, 0, 0)),
        out_shape=jax.ShapeDtypeStruct((subs, funcs, funcs), F32),
        scratch_shapes=[
            pltpu.VMEM((layers, funcs * ny, nz), F32),
            pltpu.VMEM((2, ny, funcs, nz), F32),
            pltpu.VMEM((layers, 4, ny, nz), F32),
            pltpu.VMEM((funcs, ny * nz), BF16),
            pltpu.VMEM((2 * funcs, ny * nz), BF16),
            pltpu.VMEM((2 * funcs, funcs), F32),
        ],
        compiler_params=pltpu.CompilerParams(vmem_limit_bytes=16 * 2**20),
        cost_estimate=LIGHT,
        name="interior",
    )(edge, table, ids, basis, token)


def face_kernel(flags_ref, table_ref, ids_ref, last_ref, halo_ref, token_ref, inner_ref, out_ref, *scratch):
    @pl.when(flags_ref[0] == 1)
    def _():
        last, halo, sems = scratch[-3:]
        copies = [
            pltpu.make_async_copy(last_ref, last, sems.at[0]),
            pltpu.make_async_copy(halo_ref, halo, sems.at[1]),
        ]
        for copy in copies:
            copy.start()
        for copy in copies:
            copy.wait()
        face_sums(table_ref, ids_ref, last, halo, inner_ref, out_ref, *scratch[:-3])


def face_sums(table_ref, ids_ref, last_ref, halo_ref, inner_ref, out_ref, mine, theirs, left, right, weights, acc):
    subs, layers, ny, nz = ids_ref.shape
    funcs = inner_ref.shape[1]
    comps = last_ref.shape[1] // funcs

    @pl.loop(0, subs)
    def _(sub):
        shear, dilate = lame_of(ids_ref[sub, layers - 1], table_ref)
        weights[0] = 0.5 * (shear + halo_ref[sub, comps * funcs].astype(F32))
        weights[1] = 0.5 * (dilate + halo_ref[sub, comps * funcs + 1].astype(F32))

        @pl.loop(0, comps)
        def _(comp):
            weight = weights[0] + jnp.where(comp == 0, weights[0] + weights[1], 0.0)
            rows = pl.ds(comp * funcs, funcs)
            mine[...] = last_ref[sub, rows].astype(F32).reshape(funcs * ny, nz)
            theirs[...] = halo_ref[sub, rows].astype(F32).reshape(funcs * ny, nz)
            for y in range(ny):
                here = mine[pl.ds(y, funcs, stride=ny), :]
                there = theirs[pl.ds(y, funcs, stride=ny), :]
                high, low = split_two(weight[y : y + 1, :] * (here - there))
                left[0:funcs, y * nz : (y + 1) * nz] = here.astype(BF16)
                left[funcs : 2 * funcs, y * nz : (y + 1) * nz] = there.astype(BF16)
                right[0:funcs, y * nz : (y + 1) * nz] = high
                right[funcs : 2 * funcs, y * nz : (y + 1) * nz] = low
            product = dot(right[...], left[...], NT)

            @pl.when(comp == 0)
            def _():
                acc[...] = product

            @pl.when(comp > 0)
            def _():
                acc[...] += product

        total = acc[:, 0:funcs] - acc[:, funcs : 2 * funcs]
        half = inner_ref[sub] + 0.5 * (total[0:funcs] + total[funcs : 2 * funcs])
        out_ref[sub] = half + half.T


def face(flags, table, ids, last, halo, token, inner):
    subs, layers, ny, nz = ids.shape
    funcs = inner.shape[1]
    return pl.pallas_call(
        face_kernel,
        in_specs=[SMEM, SMEM, VMEM, ANY, ANY, ANY, VMEM],
        out_specs=VMEM,
        out_shape=jax.ShapeDtypeStruct((subs, funcs, funcs), F32),
        scratch_shapes=[
            pltpu.VMEM((funcs * ny, nz), F32),
            pltpu.VMEM((funcs * ny, nz), F32),
            pltpu.VMEM((2 * funcs, ny * nz), BF16),
            pltpu.VMEM((2 * funcs, ny * nz), BF16),
            pltpu.VMEM((2, ny, nz), F32),
            pltpu.VMEM((2 * funcs, 2 * funcs), F32),
            pltpu.VMEM(last.shape, BF16),
            pltpu.VMEM(halo.shape, BF16),
            pltpu.SemaphoreType.DMA((2,)),
        ],
        compiler_params=pltpu.CompilerParams(vmem_limit_bytes=16 * 2**20),
        cost_estimate=LIGHT,
        name="face",
    )(flags, table, ids, last, halo, token, inner)


def spread(gal_ref, column_ids_ref, row_ids_ref, size):
    subs, funcs = column_ids_ref.shape[0:2]
    added = jnp.zeros((size, size), F32)
    lane = lax.broadcasted_iota(jnp.int32, (funcs, size), 1)
    row = lax.broadcasted_iota(jnp.int32, (size, funcs), 0)
    for sub in range(subs):
        slots = (column_ids_ref[sub] == lane).astype(F32)
        slots_t = (row_ids_ref[sub] == row).astype(F32)
        added = added + exact_dot(slots_t, exact_dot(gal_ref[sub], slots))
    return added


def assemble_kernel(flags_ref, token_ref, column_ids_ref, row_ids_ref, slab_ref, head_ref, *rest):
    gal_refs, (message_ref, sum_ref) = rest[:-2], rest[-2:]
    size = message_ref.shape[0]
    mode, own = flags_ref[0], flags_ref[1]
    message_ref[...] = jnp.zeros_like(message_ref)

    @pl.when((mode == 1) & (own == 1))
    def _():
        total = gal_refs[0][...]
        for gal_ref in gal_refs[1:]:
            total = total + gal_ref[...]
        sum_ref[...] = total
        added = spread(sum_ref, column_ids_ref, row_ids_ref, size)
        message_ref[...] = added + slab_ref[...].astype(F32)

    @pl.when((mode == 2) & (own == 1))
    def _():
        message_ref[...] = head_ref[...].astype(F32)


def assemble(flags, token, ids, slab, head, parts):
    size = slab.shape[1]
    block = pl.BlockSpec((size, size), lambda i: (0, 0))
    return pl.pallas_call(
        assemble_kernel,
        grid=(1,),
        in_specs=[SMEM, ANY, VMEM, VMEM, block, block] + [VMEM] * len(parts),
        out_specs=VMEM,
        out_shape=jax.ShapeDtypeStruct((size, size), F32),
        scratch_shapes=[pltpu.VMEM(parts[0].shape, F32)],
        cost_estimate=LIGHT,
        name="assemble",
    )(flags, token, ids[:, :, None], ids[:, None, :], slab, head, *parts)


def factor_kernel(flags_ref, token_ref, *refs, parts, groups):
    message_refs, gal_refs = refs[:parts], refs[parts:-4]
    summary_ref, block_ref, sum_ref, work = refs[-4:]
    subs, funcs = gal_refs[0].shape[0:2]
    size = summary_ref.shape[1]
    diagonal = message_refs[0][...]
    for message_ref in message_refs[1:]:
        diagonal = diagonal + message_ref[...]
    block_ref[...] = diagonal

    @pl.when(flags_ref[0] == 1)
    def _():
        row = lax.broadcasted_iota(jnp.int32, (size, size), 0)
        lane = lax.broadcasted_iota(jnp.int32, (size, size), 1)
        work[:, 0:size] = 0.5 * (diagonal + diagonal.T)
        work[:, size : 2 * size] = (row == lane).astype(F32)
        index = lax.broadcasted_iota(jnp.int32, (BLOCK, size), 0)
        for start in range(0, size, BLOCK):
            panel = work[start : start + BLOCK, 0:size]
            extra = work[start : start + BLOCK, size : 2 * size]
            columns = [
                jnp.broadcast_to(panel[:, start + step : start + step + 1], (BLOCK, size))
                for step in range(BLOCK)
            ]
            for step in range(BLOCK):
                scale = lax.rsqrt(columns[step][step : step + 1, :])
                column = jnp.where(index > step, columns[step] * scale, 0.0)
                for later in range(step + 1, BLOCK):
                    columns[later] = columns[later] - column * column[later : later + 1, :]
                pivot = panel[step : step + 1, :] * scale
                panel = jnp.where(index == step, pivot, panel - column * pivot)
                pivot = extra[step : step + 1, :] * scale
                extra = jnp.where(index == step, pivot, extra - column * pivot)
            work[start : start + BLOCK, 0:size] = panel
            work[start : start + BLOCK, size : 2 * size] = extra
            rest = start + BLOCK
            if rest < size:
                both = jnp.concatenate([panel, extra], axis=1)
                work[rest:size, :] -= exact_dot(panel[:, rest:size], both, TN)
        upper = jnp.where(row <= lane, work[:, 0:size], 0.0)
        inverse = jnp.where(row >= lane, work[:, size : 2 * size], 0.0).T
        high = inverse.astype(BF16)
        summary_ref[0:size] = high
        summary_ref[size : 2 * size] = (inverse - high.astype(F32)).astype(BF16)
        summary_ref[2 * size : 3 * size] = upper.T.astype(BF16)
        each = len(gal_refs) // groups
        for group in range(groups):

            @pl.when(flags_ref[1] == group)
            def _(chosen=gal_refs[group * each : (group + 1) * each]):
                total = chosen[0][...]
                for gal_ref in chosen[1:]:
                    total = total + gal_ref[...]
                sum_ref[...] = total


def factorize(flags, token, messages, groups):
    size = messages[0].shape[1]
    subs, funcs = groups[0][0].shape[0:2]
    parts = [part for group in groups for part in group]
    return pl.pallas_call(
        functools.partial(factor_kernel, parts=len(messages), groups=len(groups)),
        in_specs=[SMEM, ANY] + [VMEM] * (len(messages) + len(parts)),
        out_specs=[VMEM] * 3,
        out_shape=[
            jax.ShapeDtypeStruct((3 * size, size), BF16),
            jax.ShapeDtypeStruct((size, size), F32),
            jax.ShapeDtypeStruct(groups[0][0].shape, F32),
        ],
        scratch_shapes=[pltpu.VMEM((size, 2 * size), F32)],
        cost_estimate=LIGHT,
        name="factorize",
    )(flags, token, *messages, *parts)


def prepare_kernel(flags_ref, token_ref, head_ref, *rest, sources):
    summary_refs = rest[:sources]
    weights_ref, rows_ref, lower_ref, summary, sem = rest[sources:]
    size = head_ref.shape[0]
    choice, mode = flags_ref[0], flags_ref[1]
    for number, summary_ref in enumerate(summary_refs):

        @pl.when(choice == number)
        def _(summary_ref=summary_ref):
            copy = pltpu.make_async_copy(summary_ref, summary, sem)
            copy.start()
            copy.wait()

    def doubled(block):
        nothing = jnp.zeros((size, size), BF16)
        top = jnp.concatenate([block, nothing], axis=1)
        return jnp.concatenate([top, jnp.concatenate([nothing, block], axis=1)], axis=0)

    @pl.when(mode > 0)
    def _():
        weights_ref[0 : 2 * size] = doubled(summary[0:size])
        weights_ref[2 * size : 4 * size] = doubled(summary[size : 2 * size])
        lower_ref[...] = summary[2 * size : 3 * size]

    @pl.when(mode == 2)
    def _():
        inverse = summary[0:size].astype(F32) + summary[size : 2 * size].astype(F32)
        solved = exact_dot(head_ref[...], inverse)
        rows_ref[...] = doubled(solved.T.astype(BF16))


def prepare(flags, token, head, summaries):
    size = head.shape[0]
    return pl.pallas_call(
        functools.partial(prepare_kernel, sources=len(summaries)),
        in_specs=[SMEM, ANY, VMEM] + [ANY] * len(summaries),
        out_specs=[VMEM] * 3,
        out_shape=[
            jax.ShapeDtypeStruct((4 * size, 2 * size), BF16),
            jax.ShapeDtypeStruct((2 * size, 2 * size), BF16),
            jax.ShapeDtypeStruct((size, size), BF16),
        ],
        scratch_shapes=[pltpu.VMEM(summaries[0].shape, BF16), pltpu.SemaphoreType.DMA],
        compiler_params=pltpu.CompilerParams(vmem_limit_bytes=16 * 2**20),
        cost_estimate=LIGHT,
        name="prepare",
    )(flags, token, head, *summaries)


def added_kernel(flags_ref, token_ref, column_ids_ref, row_ids_ref, *rest, sources):
    sum_refs, (added_ref, gal_ref) = rest[:sources], rest[sources:]
    for number, sum_ref in enumerate(sum_refs):

        @pl.when(flags_ref[0] == number)
        def _(sum_ref=sum_ref):
            gal_ref[...] = sum_ref[...]

    @pl.when((flags_ref[1] == 2) & (flags_ref[2] == 1))
    def _():
        added_ref[...] = spread(gal_ref, column_ids_ref, row_ids_ref, added_ref.shape[0])


def added_of(flags, token, ids, sums, size):
    return pl.pallas_call(
        functools.partial(added_kernel, sources=len(sums)),
        in_specs=[SMEM, ANY] + [VMEM] * (2 + len(sums)),
        out_specs=[VMEM] * 2,
        out_shape=[jax.ShapeDtypeStruct((size, size), F32), jax.ShapeDtypeStruct(sums[0].shape, F32)],
        cost_estimate=LIGHT,
        name="added",
    )(flags, token, ids[:, :, None], ids[:, None, :], *sums)


def panel_kernel(
    flags_ref, token_ref, lower_ref, weights_ref, rows_ref, added_ref, slab_ref, *rest, pieces, spans, first
):
    hops = len(pieces) // len(spans)
    others = rest[: len(pieces)]
    out_ref, done_ref, column, factor, sems = rest[-5:]
    done_ref[0] = flags_ref[0]
    tile, size = out_ref.shape
    half = tile // 2
    mode, head, own, which = flags_ref[0], flags_ref[1], flags_ref[2], flags_ref[3]
    step, steps = pl.program_id(0), pl.num_programs(0)
    top = first & (step == 0)

    def copy_of(at, act):
        for number, (begin, end) in enumerate(spans):
            for hop in range(hops):

                @pl.when((mode == 2) & (which == hop) & (at >= begin) & (at < end))
                def _(other_ref=others[number * hops + hop], begin=begin):
                    source = other_ref.at[pl.ds(pl.multiple_of((at - begin) * tile, tile), tile)]
                    act(pltpu.make_async_copy(source, column.at[at % 2], sems.at[at % 2]))

    @pl.when(step == 0)
    def _():
        copy_of(step, lambda copy: copy.start())

    @pl.when(step + 1 < steps)
    def _():
        copy_of(step + 1, lambda copy: copy.start())

    @pl.when(mode == 0)
    def _():
        out_ref[...] = slab_ref[...]

    @pl.when(mode == 1)
    def _():
        column[step % 2] = slab_ref[...]

    @pl.when(mode == 2)
    def _():
        copy_of(step, lambda copy: copy.wait())

    @pl.when(mode > 0)
    def _():
        value = column[step % 2]
        pair = jnp.concatenate([value[0:half], value[half:tile]], axis=1)
        factor[...] = dot(jnp.concatenate([pair, pair], axis=1), weights_ref[...]).astype(BF16)

        @pl.when(top & (head == 1))
        def _():
            factor[0:size, 0:size] = lower_ref[...]

        @pl.when(top & (head == 2))
        def _():
            factor[0:size, 0:size] = jnp.zeros((size, size), BF16)

    @pl.when(mode == 1)
    def _():
        out_ref[0:half] = factor[:, 0:size]
        out_ref[half:tile] = factor[:, size : 2 * size]

    @pl.when(mode == 2)
    def _():
        update = dot(factor[...], rows_ref[...])
        out_ref[0:half] = (slab_ref[0:half].astype(F32) - update[:, 0:size]).astype(BF16)
        out_ref[half:tile] = (slab_ref[half:tile].astype(F32) - update[:, size : 2 * size]).astype(BF16)

        @pl.when(top & (own == 1))
        def _():
            base = slab_ref[0:size].astype(F32) + added_ref[...]
            out_ref[0:size] = (base - update[0:size, 0:size]).astype(BF16)


def panel(flags, token, lower, weights, rows, added, slab, parts, old, start, tile):
    size = slab.shape[1]
    offset = start // tile
    spans, begin, operands = [], 0, []
    for hops in parts:
        end = begin + hops[0].shape[0] // tile
        spans.append((begin, end))
        begin = end
        operands += hops
    blocks = [
        SMEM,
        ANY,
        pl.BlockSpec((size, size), lambda i: (0, 0)),
        pl.BlockSpec(weights.shape, lambda i: (0, 0)),
        pl.BlockSpec(rows.shape, lambda i: (0, 0)),
        pl.BlockSpec((size, size), lambda i: (0, 0)),
        pl.BlockSpec((tile, size), lambda i: (i + offset, 0)),
    ] + [ANY] * len(operands)
    pieces = len(operands)
    operands = [flags, token, lower, weights, rows, added, slab] + operands
    aliases = {}
    if old is not None:
        aliases = {len(operands): 0}
        blocks.append(ANY)
        operands.append(old)
    return pl.pallas_call(
        functools.partial(panel_kernel, pieces=range(pieces), spans=spans, first=start == 0),
        grid=(begin,),
        in_specs=blocks,
        out_specs=[pl.BlockSpec((tile, size), lambda i: (i + offset, 0)), SMEM],
        out_shape=[jax.ShapeDtypeStruct(slab.shape, BF16), jax.ShapeDtypeStruct((1,), jnp.int32)],
        input_output_aliases=aliases,
        scratch_shapes=[
            pltpu.VMEM((2, tile, size), BF16),
            pltpu.VMEM((tile // 2, 2 * size), BF16),
            pltpu.SemaphoreType.DMA((2,)),
        ],
        compiler_params=pltpu.CompilerParams(vmem_limit_bytes=16 * 2**20),
        cost_estimate=LIGHT,
        name="panel",
    )(*operands)


def broadcast(value, axis, source):
    kept = jnp.where(lax.axis_index(axis) == source, value, 0).astype(value.dtype)
    return lax.psum(kept, axis)


def settings(*values):
    return jnp.stack([jnp.asarray(value).astype(jnp.int32) for value in values])


def holder_pairs(wide, narrow, distance):
    stride = wide // narrow
    found = []
    for n in range(narrow):
        for start in range(0, wide, 2 * distance):
            source = (n * stride) ^ start
            found.append((source * narrow + n, (source ^ distance) * narrow + n))
    return found


class Order:
    def __init__(self, token):
        self.token = token

    def after(self, value):
        value, self.token = lax.optimization_barrier((value, self.token))
        return value


def known_owner(owner, coarse_basis, material_ids, lame_table, coarse_ids, coarse_slab):
    narrow, wide = lax.axis_size("narrow"), lax.axis_size("wide")
    stride = wide // narrow
    wide_index, narrow_index = lax.axis_index("wide"), lax.axis_index("narrow")
    height, block = coarse_slab.shape
    own = wide_index == narrow_index * stride
    later = narrow_index > owner
    which = jnp.where(later, narrow_index - owner - 1, -1)
    mode = jnp.where(narrow_index == owner, 1, jnp.where(later, 2, 0))
    earlier = (wide_index % stride == 0) & (wide_index // stride < owner)
    kind = jnp.where(wide_index == owner * stride, 1, jnp.where(earlier, 2, 0))
    table = lame_table.astype(F32)
    hops = narrow - 1 - owner
    units, joined, plan = PLANS[hops]
    unit = height // sum(units)
    count = len(units)
    bounds, low = [], 0
    for number in units:
        bounds.append((low, low + number * unit))
        low += number * unit
    axes = ("wide", "narrow")

    def rows_of(number):
        low, high = bounds[number]
        return coarse_slab[low:high]

    def send(value, source, target):
        return lax.ppermute(value, "narrow", [(owner + source, owner + target)])

    order = Order(settings(mode))

    ways = [((n * stride) * narrow + owner, (n * stride) * narrow + n) for n in range(owner + 1, narrow)]
    head = order.after(lax.ppermute(coarse_slab[:block], axes, ways))
    moved = {}

    groups = [[w for w in range(wide) if w % stride == 0], [w for w in range(wide) if w % stride]]
    groups = [group for group in groups if group]
    member = jnp.where(wide_index % stride == 0, 0, 1)

    def within(group, pairs):
        return [(w * narrow + one, w * narrow + two) for w in group for one, two in pairs]

    def halo_of(group, message):
        return lax.ppermute(message, axes, within(group, [(i + 1, i) for i in range(narrow - 1)]))

    spans = [bounds[0], (bounds[joined[0]][0], bounds[joined[-1]][1]) if joined else bounds[1]]
    first, last, *begun = halo_message(table, material_ids, order.token, coarse_basis, coarse_slab, spans)
    first = order.after(first)
    halos = [halo_of(groups[0], first)]
    edge = (narrow_index == 0).astype(jnp.int32).reshape(1)
    inner = order.after(interior(edge, table, material_ids, coarse_basis, order.token))
    halos[0] = order.after(halos[0])
    moved[0] = [send(order.after(begun[0]), 0, hops)]
    for group in groups[1:]:
        halos.append(halo_of(group, order.after(first)))

    def nearest(base, extent):
        return min(range(base, min(base + extent, narrow)), key=lambda n: abs(n - owner))

    def summed(parts, distance, group):
        total = parts[0] if len(parts) == 1 else parts[0] + parts[1]
        pairs = []
        for base in range(0, narrow - distance, 2 * distance):
            one, two = nearest(base, distance), nearest(base + distance, distance)
            pairs.append((two, one) if nearest(base, 2 * distance) == one else (one, two))
        return [total, lax.ppermute(total, axes, within(group, pairs))], 2 * distance

    def faces_of(number):
        flag = settings(member == number)
        return [order.after(face(flag, table, material_ids, last, halos[number], order.token, inner))]

    sums, reach = [faces_of(0)], [1]
    while reach[0] < narrow:
        sums[0], reach[0] = summed(sums[0], reach[0], groups[0])
    sums[0][1] = order.after(sums[0][1])
    distance, messages, left = wide // 2, [], plan.count("spread")
    result, prepared = None, None
    choice = (narrow_index - owner) % narrow
    flags = settings(mode, kind, own, which)
    for step in plan:
        if step[0] == "panel":
            if prepared is None:
                prepared = prepare(settings(choice, mode), order.token, head, summaries)
            weights, rows, lower = prepared
            begin, end = step[1:]
            parts = [moved[number][:: 1 if number else -1] for number in range(begin, end)]
            result, order.token = panel(
                flags, order.token, lower, weights, rows, added if begin == 0 else head, coarse_slab, parts, result, bounds[begin][0], 2 * unit
            )
        elif step == "sums":
            for place in range(1, narrow):
                galerkins[place] = order.after(galerkins[place])
            added, galerkin = added_of(settings(choice, mode, own), order.token, coarse_ids, galerkins, block)
            added = order.after(added)
        elif step == "next":
            if joined:
                whole = send(order.after(begun[1]), 0, 1)
            else:
                moved[1] = [send(order.after(begun[1]), 0, 1)]
                for number in range(2, count - 1):
                    moved[number] = [send(order.after(rows_of(number)), 0, 1)]
        elif step == "assemble":
            message = assemble(settings(mode, own), order.token, coarse_ids, coarse_slab, head, sums[0])
            message = order.after(message)
        elif step == "others":
            for number in range(1, len(groups)):
                halos[number] = order.after(halos[number])
                parts, far = summed(faces_of(number), 1, groups[number])
                sums.append(parts)
                reach.append(far)
        elif step == "more":
            for number in range(1, len(groups)):
                while reach[number] < narrow:
                    sums[number][1] = order.after(sums[number][1])
                    sums[number], reach[number] = summed(sums[number], reach[number], groups[number])
        elif step == "spread":
            left -= 1
            while distance:
                received = order.after(lax.ppermute(message, axes, holder_pairs(wide, narrow, distance)))
                messages = [message, received]
                if distance > 1:
                    message = message + received
                distance //= 2
                if left:
                    break
        elif step == "factor":
            summary, head, galerkin = factorize(settings(mode, member), order.token, messages, sums)
            summary = order.after(summary)
            ways = [[(owner, (owner + place) % narrow)] for place in range(1, narrow)]
            summaries = [summary] + [lax.ppermute(summary, "narrow", way) for way in ways]
        elif step == "summary":
            for place in range(1, narrow):
                summaries[place] = order.after(summaries[place])
            moved[count - 1] = [send(order.after(rows_of(count - 1)), 0, 1)]
            galerkin = order.after(galerkin)
            galerkins = [galerkin] + [lax.ppermute(galerkin, "narrow", way) for way in ways]
        else:
            number, hop = step
            if joined and step == (joined[0], 0):
                whole = order.after(whole)
                for part in joined:
                    low, high = (bound - bounds[joined[0]][0] for bound in bounds[part])
                    moved[part] = [whole[low:high]]
            moving = moved[number][hop] = order.after(moved[number][hop])
            if number == 0 and hop + 1 < hops:
                moved[number].append(send(moving, hops - hop, hops - hop - 1))
            elif number != 0 and hop + 1 < hops:
                moved[number].append(send(moving, hop + 1, hop + 2))
    return result, galerkin


def any_owner(owner, coarse_basis, material_ids, lame_table, coarse_ids, coarse_slab):
    narrow, wide = lax.axis_size("narrow"), lax.axis_size("wide")
    stride = wide // narrow
    wide_index, narrow_index = lax.axis_index("wide"), lax.axis_index("narrow")
    own = wide_index == narrow_index * stride
    later = narrow_index > owner
    which = jnp.where(later, 0, -1)
    mode = jnp.where(narrow_index == owner, 1, jnp.where(later, 2, 0))
    earlier = (wide_index % stride == 0) & (wide_index // stride < owner)
    kind = jnp.where(wide_index == owner * stride, 1, jnp.where(earlier, 2, 0))
    table = lame_table.astype(F32)
    column = broadcast(coarse_slab, "narrow", owner)
    first, last = halo_message(table, material_ids, table, coarse_basis, coarse_slab, ())
    halo = lax.ppermute(first, "narrow", [(i + 1, i) for i in range(narrow - 1)])
    edge = (narrow_index == 0).astype(jnp.int32).reshape(1)
    inner = interior(edge, table, material_ids, coarse_basis, first)
    partial = face(settings(1), table, material_ids, last, halo, first, inner)
    parts = [lax.psum(partial, "narrow")]
    message = assemble(settings(mode, own), first, coarse_ids, coarse_slab, column, parts)
    at_owner = (wide_index == owner * stride) & (narrow_index == owner)
    diagonal = lax.psum(jnp.where(at_owner, message, 0.0), ("wide", "narrow"))
    summary, _, galerkin = factorize(settings(1, 0), first, [diagonal], [parts])
    head = broadcast(message, "wide", narrow_index * stride)
    weights, rows, lower = prepare(settings(0, mode), settings(mode), head, [summary])
    added, galerkin = added_of(settings(0, mode, own), weights, coarse_ids, [galerkin], head.shape[0])
    flags = settings(mode, kind, own, which)
    tile = coarse_slab.shape[0] // 12
    result, _ = panel(flags, flags, lower, weights, rows, added, coarse_slab, [[column]], None, 0, tile)
    return result, galerkin


def on_device(coarse_basis, material_ids, lame_table, coarse_ids, coarse_slab, panel_owner):
    narrow, wide = lax.axis_size("narrow"), lax.axis_size("wide")
    arrays = (coarse_basis, material_ids, lame_table, coarse_ids, coarse_slab)
    owner = panel_owner[0]
    if narrow - 1 > len(PLANS) or wide & (wide - 1):
        return any_owner(owner, *arrays)
    branches = [functools.partial(known_owner, place) for place in range(narrow - 1)]
    return lax.switch(owner, branches, *arrays)


def solution(mesh):
    return jax.shard_map(
        on_device,
        mesh=mesh,
        in_specs=(
            P("wide", None, None, "narrow", None, None),
            P("wide", "narrow", None, None),
            P(),
            P("wide", None),
            P("wide", "narrow"),
            P(),
        ),
        out_specs=(P("wide", "narrow"), P("wide", None, None)),
        check_vma=False,
    )
```

```python
import functools

import jax
import jax.numpy as jnp
from jax import lax
from jax.experimental import pallas as pl
from jax.experimental.pallas import tpu as pltpu
from jax.sharding import PartitionSpec as P

F32, BF16 = jnp.float32, jnp.bfloat16
NT = (((1,), (1,)), ((), ()))
TN = (((0,), (0,)), ((), ()))
VMEM = pl.BlockSpec(memory_space=pltpu.VMEM)
ANY = pl.BlockSpec(memory_space=pl.ANY)
SMEM = pl.BlockSpec(memory_space=pltpu.SMEM)
PLANS = {
    1: (
        (12, 6, 6),
        (),
        (
            "assemble", "next", "spread", "others", "spread", "more", "spread", (0, 0), "factor", "summary",
            "sums", ("panel", 0, 2), ("panel", 2, 3),
        ),
    ),
    2: (
        (12, 6, 4, 2),
        (),
        (
            "assemble", "next", "spread", "others", "spread", "more", "spread", (0, 0), (1, 0), "factor", (2, 0),
            "summary", ("panel", 1, 2), (3, 0), "sums", ("panel", 0, 1), ("panel", 2, 4),
        ),
    ),
    3: (
        (12, 6, 4, 2),
        (1, 2),
        (
            "assemble", "next", "spread", "others", "spread", "more", "spread", (0, 0), "factor", (1, 0), "summary",
            (0, 1), (1, 1), (2, 0), (2, 1), ("panel", 1, 2), (3, 0), (3, 1), "sums", ("panel", 0, 1), ("panel", 2, 4),
        ),
    ),
}
BLOCK = 16
LIGHT = pl.CostEstimate(flops=1, bytes_accessed=1, transcendentals=0)


def exact_dot(left, right, dims=(((1,), (0,)), ((), ()))):
    return lax.dot_general(
        left, right, dims, precision=lax.Precision.HIGHEST, preferred_element_type=F32
    )


def dot(left, right, dims=(((1,), (0,)), ((), ()))):
    return lax.dot_general(left, right, dims, preferred_element_type=F32)


def split_two(value):
    high = value.astype(BF16)
    return high, (value - high.astype(F32)).astype(BF16)


def lame_of(ids, table_ref):
    shear = jnp.zeros(ids.shape, F32)
    dilate = jnp.zeros(ids.shape, F32)
    for material in range(table_ref.shape[1]):
        chosen = ids == material
        shear = jnp.where(chosen, table_ref[0, material], shear)
        dilate = jnp.where(chosen, table_ref[1, material], dilate)
    return shear, dilate


def halo_kernel(table_ref, ids_ref, token_ref, basis_ref, slab_ref, out_ref, last_ref, *rest, spans):
    piece_refs, sems = rest[:-1], rest[-1]
    subs, funcs, comps, layers = basis_ref.shape[0:4]
    copies = []
    for number, ((low, high), piece_ref) in enumerate(zip(spans, piece_refs)):
        copies.append(pltpu.make_async_copy(slab_ref.at[pl.ds(low, high - low)], piece_ref, sems.at[number]))
        copies[-1].start()
    for sub in range(subs):
        for comp in range(comps):
            out_ref[sub, comp * funcs : (comp + 1) * funcs] = basis_ref[sub, :, comp, 0]
            last_ref[sub, comp * funcs : (comp + 1) * funcs] = basis_ref[sub, :, comp, layers - 1]
        shear, dilate = lame_of(ids_ref[sub, 0], table_ref)
        out_ref[sub, comps * funcs] = shear.astype(BF16)
        out_ref[sub, comps * funcs + 1] = dilate.astype(BF16)
    for copy in copies:
        copy.wait()


def halo_message(table, ids, token, basis, slab, spans):
    subs, funcs, comps, layers, ny, nz = basis.shape
    return pl.pallas_call(
        functools.partial(halo_kernel, spans=spans),
        in_specs=[SMEM, VMEM, ANY, VMEM, ANY],
        out_specs=[VMEM] * (2 + len(spans)),
        out_shape=[
            jax.ShapeDtypeStruct((subs, comps * funcs + 2, ny, nz), BF16),
            jax.ShapeDtypeStruct((subs, comps * funcs, ny, nz), BF16),
        ]
        + [jax.ShapeDtypeStruct((high - low, slab.shape[1]), BF16) for low, high in spans],
        scratch_shapes=[pltpu.SemaphoreType.DMA((max(1, len(spans)),))],
        compiler_params=pltpu.CompilerParams(vmem_limit_bytes=16 * 2**20),
        cost_estimate=LIGHT,
        name="halo_message",
    )(table, ids, token, basis, slab)


def interior_kernel(edge_ref, table_ref, ids_ref, basis_ref, token_ref, out_ref, fields, turned, coef, left, right, acc):
    sub, comp = pl.program_id(0), pl.program_id(1)
    layers, ny, nz = basis_ref.shape[3:]
    funcs = basis_ref.shape[1]
    row = lax.broadcasted_iota(jnp.int32, (ny, nz), 0)
    lane = lax.broadcasted_iota(jnp.int32, (ny, nz), 1)
    table = [lame_of(ids_ref[sub, x], table_ref) for x in range(layers)]

    def weight(one, two, direction):
        shear = 0.5 * (one[0] + two[0])
        dilate = 0.5 * (one[1] + two[1])
        return shear + jnp.where(comp == direction, shear + dilate, 0.0)

    def ahead(field, axis):
        size = field.shape[axis]
        index = row if axis == 0 else lane
        return jnp.where(index == size - 1, 0.0, pltpu.roll(field, size - 1, axis=axis))

    def behind(field, axis):
        index = row if axis == 0 else lane
        return jnp.where(index == 0, 0.0, pltpu.roll(field, 1, axis=axis))

    nothing = (jnp.zeros((ny, nz), F32),) * 2
    previous = weight(table[0], nothing, 0) * edge_ref[0].astype(F32)
    for x in range(layers):
        diagonal = previous
        forward = []
        if x + 1 < layers:
            face = weight(table[x], table[x + 1], 0)
            diagonal = diagonal + face
            previous = face
            forward.append(face)
        else:
            forward.append(jnp.zeros((ny, nz), F32))
        for axis in (0, 1):
            index, size = (row, ny) if axis == 0 else (lane, nz)
            other = tuple(ahead(value, axis) for value in table[x])
            face = weight(table[x], other, axis + 1)
            before = tuple(behind(value, axis) for value in table[x])
            diagonal = diagonal + face + weight(table[x], before, axis + 1)
            forward.append(jnp.where(index == size - 1, 0.0, face))
        coef[x, 0] = 0.5 * diagonal
        for kind in range(3):
            coef[x, kind + 1] = forward[kind]
        fields[x] = basis_ref[sub, :, comp, x].astype(F32).reshape(funcs * ny, nz)

    total = None
    for x in reversed(range(layers)):
        values = [fields[x, pl.ds(y, funcs, stride=ny), :] for y in range(ny)]
        for y in range(ny):
            value = values[y]
            turned[x % 2, y] = value
            image = coef[x, 0, y : y + 1, :] * value
            image = image - coef[x, 3, y : y + 1, :] * pltpu.roll(value, nz - 1, axis=1)
            if y + 1 < ny:
                image = image - coef[x, 2, y : y + 1, :] * values[y + 1]
            if x + 1 < layers:
                image = image - coef[x, 1, y : y + 1, :] * turned[(x + 1) % 2, y]
            high, low = split_two(image)
            left[:, y * nz : (y + 1) * nz] = value.astype(BF16)
            right[0:funcs, y * nz : (y + 1) * nz] = high
            right[funcs : 2 * funcs, y * nz : (y + 1) * nz] = low
        product = dot(right[...], left[...], NT)
        total = product if total is None else total + product

    @pl.when(comp == 0)
    def _():
        acc[...] = total

    @pl.when(comp > 0)
    def _():
        acc[...] += total

    @pl.when(comp == pl.num_programs(1) - 1)
    def _():
        out_ref[0] = acc[0:funcs] + acc[funcs : 2 * funcs]


def interior(edge, table, ids, basis, token):
    subs, funcs, comps, layers, ny, nz = basis.shape
    return pl.pallas_call(
        interior_kernel,
        grid=(subs, comps),
        in_specs=[SMEM, SMEM, VMEM, VMEM, ANY],
        out_specs=pl.BlockSpec((1, funcs, funcs), lambda s, c: (s, 0, 0)),
        out_shape=jax.ShapeDtypeStruct((subs, funcs, funcs), F32),
        scratch_shapes=[
            pltpu.VMEM((layers, funcs * ny, nz), F32),
            pltpu.VMEM((2, ny, funcs, nz), F32),
            pltpu.VMEM((layers, 4, ny, nz), F32),
            pltpu.VMEM((funcs, ny * nz), BF16),
            pltpu.VMEM((2 * funcs, ny * nz), BF16),
            pltpu.VMEM((2 * funcs, funcs), F32),
        ],
        compiler_params=pltpu.CompilerParams(vmem_limit_bytes=16 * 2**20),
        cost_estimate=LIGHT,
        name="interior",
    )(edge, table, ids, basis, token)


def face_kernel(flags_ref, table_ref, ids_ref, last_ref, halo_ref, token_ref, inner_ref, out_ref, *scratch):
    @pl.when(flags_ref[0] == 1)
    def _():
        last, halo, sems = scratch[-3:]
        copies = [
            pltpu.make_async_copy(last_ref, last, sems.at[0]),
            pltpu.make_async_copy(halo_ref, halo, sems.at[1]),
        ]
        for copy in copies:
            copy.start()
        for copy in copies:
            copy.wait()
        face_sums(table_ref, ids_ref, last, halo, inner_ref, out_ref, *scratch[:-3])


def face_sums(table_ref, ids_ref, last_ref, halo_ref, inner_ref, out_ref, mine, theirs, left, right, weights, acc):
    subs, layers, ny, nz = ids_ref.shape
    funcs = inner_ref.shape[1]
    comps = last_ref.shape[1] // funcs

    @pl.loop(0, subs)
    def _(sub):
        shear, dilate = lame_of(ids_ref[sub, layers - 1], table_ref)
        weights[0] = 0.5 * (shear + halo_ref[sub, comps * funcs].astype(F32))
        weights[1] = 0.5 * (dilate + halo_ref[sub, comps * funcs + 1].astype(F32))

        @pl.loop(0, comps)
        def _(comp):
            weight = weights[0] + jnp.where(comp == 0, weights[0] + weights[1], 0.0)
            rows = pl.ds(comp * funcs, funcs)
            mine[...] = last_ref[sub, rows].astype(F32).reshape(funcs * ny, nz)
            theirs[...] = halo_ref[sub, rows].astype(F32).reshape(funcs * ny, nz)
            for y in range(ny):
                here = mine[pl.ds(y, funcs, stride=ny), :]
                there = theirs[pl.ds(y, funcs, stride=ny), :]
                high, low = split_two(weight[y : y + 1, :] * (here - there))
                left[0:funcs, y * nz : (y + 1) * nz] = here.astype(BF16)
                left[funcs : 2 * funcs, y * nz : (y + 1) * nz] = there.astype(BF16)
                right[0:funcs, y * nz : (y + 1) * nz] = high
                right[funcs : 2 * funcs, y * nz : (y + 1) * nz] = low
            product = dot(right[...], left[...], NT)

            @pl.when(comp == 0)
            def _():
                acc[...] = product

            @pl.when(comp > 0)
            def _():
                acc[...] += product

        total = acc[:, 0:funcs] - acc[:, funcs : 2 * funcs]
        half = inner_ref[sub] + 0.5 * (total[0:funcs] + total[funcs : 2 * funcs])
        out_ref[sub] = half + half.T


def face(flags, table, ids, last, halo, token, inner):
    subs, layers, ny, nz = ids.shape
    funcs = inner.shape[1]
    return pl.pallas_call(
        face_kernel,
        in_specs=[SMEM, SMEM, VMEM, ANY, ANY, ANY, VMEM],
        out_specs=VMEM,
        out_shape=jax.ShapeDtypeStruct((subs, funcs, funcs), F32),
        scratch_shapes=[
            pltpu.VMEM((funcs * ny, nz), F32),
            pltpu.VMEM((funcs * ny, nz), F32),
            pltpu.VMEM((2 * funcs, ny * nz), BF16),
            pltpu.VMEM((2 * funcs, ny * nz), BF16),
            pltpu.VMEM((2, ny, nz), F32),
            pltpu.VMEM((2 * funcs, 2 * funcs), F32),
            pltpu.VMEM(last.shape, BF16),
            pltpu.VMEM(halo.shape, BF16),
            pltpu.SemaphoreType.DMA((2,)),
        ],
        compiler_params=pltpu.CompilerParams(vmem_limit_bytes=16 * 2**20),
        cost_estimate=LIGHT,
        name="face",
    )(flags, table, ids, last, halo, token, inner)


def spread(gal_ref, column_ids_ref, row_ids_ref, size):
    subs, funcs = column_ids_ref.shape[0:2]
    added = jnp.zeros((size, size), F32)
    lane = lax.broadcasted_iota(jnp.int32, (funcs, size), 1)
    row = lax.broadcasted_iota(jnp.int32, (size, funcs), 0)
    for sub in range(subs):
        slots = (column_ids_ref[sub] == lane).astype(F32)
        slots_t = (row_ids_ref[sub] == row).astype(F32)
        added = added + exact_dot(slots_t, exact_dot(gal_ref[sub], slots))
    return added


def assemble_kernel(flags_ref, token_ref, column_ids_ref, row_ids_ref, slab_ref, head_ref, *rest):
    gal_refs, (message_ref, sum_ref) = rest[:-2], rest[-2:]
    size = message_ref.shape[0]
    mode, own = flags_ref[0], flags_ref[1]
    message_ref[...] = jnp.zeros_like(message_ref)

    @pl.when((mode == 1) & (own == 1))
    def _():
        total = gal_refs[0][...]
        for gal_ref in gal_refs[1:]:
            total = total + gal_ref[...]
        sum_ref[...] = total
        added = spread(sum_ref, column_ids_ref, row_ids_ref, size)
        message_ref[...] = added + slab_ref[...].astype(F32)

    @pl.when((mode == 2) & (own == 1))
    def _():
        message_ref[...] = head_ref[...].astype(F32)


def assemble(flags, token, ids, slab, head, parts):
    size = slab.shape[1]
    block = pl.BlockSpec((size, size), lambda i: (0, 0))
    return pl.pallas_call(
        assemble_kernel,
        grid=(1,),
        in_specs=[SMEM, ANY, VMEM, VMEM, block, block] + [VMEM] * len(parts),
        out_specs=VMEM,
        out_shape=jax.ShapeDtypeStruct((size, size), F32),
        scratch_shapes=[pltpu.VMEM(parts[0].shape, F32)],
        cost_estimate=LIGHT,
        name="assemble",
    )(flags, token, ids[:, :, None], ids[:, None, :], slab, head, *parts)


def factor_kernel(flags_ref, token_ref, *refs, parts, groups):
    message_refs, gal_refs = refs[:parts], refs[parts:-4]
    summary_ref, block_ref, sum_ref, work = refs[-4:]
    subs, funcs = gal_refs[0].shape[0:2]
    size = summary_ref.shape[1]
    diagonal = message_refs[0][...]
    for message_ref in message_refs[1:]:
        diagonal = diagonal + message_ref[...]
    block_ref[...] = diagonal

    @pl.when(flags_ref[0] == 1)
    def _():
        row = lax.broadcasted_iota(jnp.int32, (size, size), 0)
        lane = lax.broadcasted_iota(jnp.int32, (size, size), 1)
        work[:, 0:size] = 0.5 * (diagonal + diagonal.T)
        work[:, size : 2 * size] = (row == lane).astype(F32)
        index = lax.broadcasted_iota(jnp.int32, (BLOCK, size), 0)
        for start in range(0, size, BLOCK):
            panel = work[start : start + BLOCK, 0:size]
            extra = work[start : start + BLOCK, size : 2 * size]
            columns = [
                jnp.broadcast_to(panel[:, start + step : start + step + 1], (BLOCK, size))
                for step in range(BLOCK)
            ]
            for step in range(BLOCK):
                scale = lax.rsqrt(columns[step][step : step + 1, :])
                column = jnp.where(index > step, columns[step] * scale, 0.0)
                for later in range(step + 1, BLOCK):
                    columns[later] = columns[later] - column * column[later : later + 1, :]
                pivot = panel[step : step + 1, :] * scale
                panel = jnp.where(index == step, pivot, panel - column * pivot)
                pivot = extra[step : step + 1, :] * scale
                extra = jnp.where(index == step, pivot, extra - column * pivot)
            work[start : start + BLOCK, 0:size] = panel
            work[start : start + BLOCK, size : 2 * size] = extra
            rest = start + BLOCK
            if rest < size:
                both = jnp.concatenate([panel, extra], axis=1)
                work[rest:size, :] -= exact_dot(panel[:, rest:size], both, TN)
        upper = jnp.where(row <= lane, work[:, 0:size], 0.0)
        inverse = jnp.where(row >= lane, work[:, size : 2 * size], 0.0).T
        high = inverse.astype(BF16)
        summary_ref[0:size] = high
        summary_ref[size : 2 * size] = (inverse - high.astype(F32)).astype(BF16)
        summary_ref[2 * size : 3 * size] = upper.T.astype(BF16)
        each = len(gal_refs) // groups
        for group in range(groups):

            @pl.when(flags_ref[1] == group)
            def _(chosen=gal_refs[group * each : (group + 1) * each]):
                total = chosen[0][...]
                for gal_ref in chosen[1:]:
                    total = total + gal_ref[...]
                sum_ref[...] = total


def factorize(flags, token, messages, groups):
    size = messages[0].shape[1]
    subs, funcs = groups[0][0].shape[0:2]
    parts = [part for group in groups for part in group]
    return pl.pallas_call(
        functools.partial(factor_kernel, parts=len(messages), groups=len(groups)),
        in_specs=[SMEM, ANY] + [VMEM] * (len(messages) + len(parts)),
        out_specs=[VMEM] * 3,
        out_shape=[
            jax.ShapeDtypeStruct((3 * size, size), BF16),
            jax.ShapeDtypeStruct((size, size), F32),
            jax.ShapeDtypeStruct(groups[0][0].shape, F32),
        ],
        scratch_shapes=[pltpu.VMEM((size, 2 * size), F32)],
        cost_estimate=LIGHT,
        name="factorize",
    )(flags, token, *messages, *parts)


def prepare_kernel(flags_ref, token_ref, head_ref, *rest, sources):
    summary_refs = rest[:sources]
    weights_ref, rows_ref, lower_ref, summary, sem = rest[sources:]
    size = head_ref.shape[0]
    choice, mode = flags_ref[0], flags_ref[1]
    for number, summary_ref in enumerate(summary_refs):

        @pl.when(choice == number)
        def _(summary_ref=summary_ref):
            copy = pltpu.make_async_copy(summary_ref, summary, sem)
            copy.start()
            copy.wait()

    def doubled(block):
        nothing = jnp.zeros((size, size), BF16)
        top = jnp.concatenate([block, nothing], axis=1)
        return jnp.concatenate([top, jnp.concatenate([nothing, block], axis=1)], axis=0)

    @pl.when(mode > 0)
    def _():
        weights_ref[0 : 2 * size] = doubled(summary[0:size])
        weights_ref[2 * size : 4 * size] = doubled(summary[size : 2 * size])
        lower_ref[...] = summary[2 * size : 3 * size]

    @pl.when(mode == 2)
    def _():
        inverse = summary[0:size].astype(F32) + summary[size : 2 * size].astype(F32)
        solved = exact_dot(head_ref[...], inverse)
        rows_ref[...] = doubled(solved.T.astype(BF16))


def prepare(flags, token, head, summaries):
    size = head.shape[0]
    return pl.pallas_call(
        functools.partial(prepare_kernel, sources=len(summaries)),
        in_specs=[SMEM, ANY, VMEM] + [ANY] * len(summaries),
        out_specs=[VMEM] * 3,
        out_shape=[
            jax.ShapeDtypeStruct((4 * size, 2 * size), BF16),
            jax.ShapeDtypeStruct((2 * size, 2 * size), BF16),
            jax.ShapeDtypeStruct((size, size), BF16),
        ],
        scratch_shapes=[pltpu.VMEM(summaries[0].shape, BF16), pltpu.SemaphoreType.DMA],
        compiler_params=pltpu.CompilerParams(vmem_limit_bytes=16 * 2**20),
        cost_estimate=LIGHT,
        name="prepare",
    )(flags, token, head, *summaries)


def added_kernel(flags_ref, token_ref, column_ids_ref, row_ids_ref, *rest, sources):
    sum_refs, (added_ref, gal_ref) = rest[:sources], rest[sources:]
    for number, sum_ref in enumerate(sum_refs):

        @pl.when(flags_ref[0] == number)
        def _(sum_ref=sum_ref):
            gal_ref[...] = sum_ref[...]

    @pl.when((flags_ref[1] == 2) & (flags_ref[2] == 1))
    def _():
        added_ref[...] = spread(gal_ref, column_ids_ref, row_ids_ref, added_ref.shape[0])


def added_of(flags, token, ids, sums, size):
    return pl.pallas_call(
        functools.partial(added_kernel, sources=len(sums)),
        in_specs=[SMEM, ANY] + [VMEM] * (2 + len(sums)),
        out_specs=[VMEM] * 2,
        out_shape=[jax.ShapeDtypeStruct((size, size), F32), jax.ShapeDtypeStruct(sums[0].shape, F32)],
        cost_estimate=LIGHT,
        name="added",
    )(flags, token, ids[:, :, None], ids[:, None, :], *sums)


def panel_kernel(
    flags_ref, token_ref, lower_ref, weights_ref, rows_ref, added_ref, slab_ref, *rest, pieces, spans, first
):
    hops = len(pieces) // len(spans)
    others = rest[: len(pieces)]
    out_ref, done_ref, column, factor, sems = rest[-5:]
    done_ref[0] = flags_ref[0]
    tile, size = out_ref.shape
    half = tile // 2
    mode, head, own, which = flags_ref[0], flags_ref[1], flags_ref[2], flags_ref[3]
    step, steps = pl.program_id(0), pl.num_programs(0)
    top = first & (step == 0)

    def copy_of(at, act):
        for number, (begin, end) in enumerate(spans):
            for hop in range(hops):

                @pl.when((mode == 2) & (which == hop) & (at >= begin) & (at < end))
                def _(other_ref=others[number * hops + hop], begin=begin):
                    source = other_ref.at[pl.ds(pl.multiple_of((at - begin) * tile, tile), tile)]
                    act(pltpu.make_async_copy(source, column.at[at % 2], sems.at[at % 2]))

    @pl.when(step == 0)
    def _():
        copy_of(step, lambda copy: copy.start())

    @pl.when(step + 1 < steps)
    def _():
        copy_of(step + 1, lambda copy: copy.start())

    @pl.when(mode == 0)
    def _():
        out_ref[...] = slab_ref[...]

    @pl.when(mode == 1)
    def _():
        column[step % 2] = slab_ref[...]

    @pl.when(mode == 2)
    def _():
        copy_of(step, lambda copy: copy.wait())

    @pl.when(mode > 0)
    def _():
        value = column[step % 2]
        pair = jnp.concatenate([value[0:half], value[half:tile]], axis=1)
        factor[...] = dot(jnp.concatenate([pair, pair], axis=1), weights_ref[...]).astype(BF16)

        @pl.when(top & (head == 1))
        def _():
            factor[0:size, 0:size] = lower_ref[...]

        @pl.when(top & (head == 2))
        def _():
            factor[0:size, 0:size] = jnp.zeros((size, size), BF16)

    @pl.when(mode == 1)
    def _():
        out_ref[0:half] = factor[:, 0:size]
        out_ref[half:tile] = factor[:, size : 2 * size]

    @pl.when(mode == 2)
    def _():
        update = dot(factor[...], rows_ref[...])
        out_ref[0:half] = (slab_ref[0:half].astype(F32) - update[:, 0:size]).astype(BF16)
        out_ref[half:tile] = (slab_ref[half:tile].astype(F32) - update[:, size : 2 * size]).astype(BF16)

        @pl.when(top & (own == 1))
        def _():
            base = slab_ref[0:size].astype(F32) + added_ref[...]
            out_ref[0:size] = (base - update[0:size, 0:size]).astype(BF16)


def panel(flags, token, lower, weights, rows, added, slab, parts, old, start, tile):
    size = slab.shape[1]
    offset = start // tile
    spans, begin, operands = [], 0, []
    for hops in parts:
        end = begin + hops[0].shape[0] // tile
        spans.append((begin, end))
        begin = end
        operands += hops
    blocks = [
        SMEM,
        ANY,
        pl.BlockSpec((size, size), lambda i: (0, 0)),
        pl.BlockSpec(weights.shape, lambda i: (0, 0)),
        pl.BlockSpec(rows.shape, lambda i: (0, 0)),
        pl.BlockSpec((size, size), lambda i: (0, 0)),
        pl.BlockSpec((tile, size), lambda i: (i + offset, 0)),
    ] + [ANY] * len(operands)
    pieces = len(operands)
    operands = [flags, token, lower, weights, rows, added, slab] + operands
    aliases = {}
    if old is not None:
        aliases = {len(operands): 0}
        blocks.append(ANY)
        operands.append(old)
    return pl.pallas_call(
        functools.partial(panel_kernel, pieces=range(pieces), spans=spans, first=start == 0),
        grid=(begin,),
        in_specs=blocks,
        out_specs=[pl.BlockSpec((tile, size), lambda i: (i + offset, 0)), SMEM],
        out_shape=[jax.ShapeDtypeStruct(slab.shape, BF16), jax.ShapeDtypeStruct((1,), jnp.int32)],
        input_output_aliases=aliases,
        scratch_shapes=[
            pltpu.VMEM((2, tile, size), BF16),
            pltpu.VMEM((tile // 2, 2 * size), BF16),
            pltpu.SemaphoreType.DMA((2,)),
        ],
        compiler_params=pltpu.CompilerParams(vmem_limit_bytes=16 * 2**20),
        cost_estimate=LIGHT,
        name="panel",
    )(*operands)


def broadcast(value, axis, source):
    kept = jnp.where(lax.axis_index(axis) == source, value, 0).astype(value.dtype)
    return lax.psum(kept, axis)


def settings(*values):
    return jnp.stack([jnp.asarray(value).astype(jnp.int32) for value in values])


def holder_pairs(wide, narrow, distance):
    stride = wide // narrow
    found = []
    for n in range(narrow):
        for start in range(0, wide, 2 * distance):
            source = (n * stride) ^ start
            found.append((source * narrow + n, (source ^ distance) * narrow + n))
    return found


class Order:
    def __init__(self, token):
        self.token = token

    def after(self, value):
        value, self.token = lax.optimization_barrier((value, self.token))
        return value


def known_owner(owner, coarse_basis, material_ids, lame_table, coarse_ids, coarse_slab):
    narrow, wide = lax.axis_size("narrow"), lax.axis_size("wide")
    stride = wide // narrow
    wide_index, narrow_index = lax.axis_index("wide"), lax.axis_index("narrow")
    height, block = coarse_slab.shape
    own = wide_index == narrow_index * stride
    later = narrow_index > owner
    which = jnp.where(later, narrow_index - owner - 1, -1)
    mode = jnp.where(narrow_index == owner, 1, jnp.where(later, 2, 0))
    earlier = (wide_index % stride == 0) & (wide_index // stride < owner)
    kind = jnp.where(wide_index == owner * stride, 1, jnp.where(earlier, 2, 0))
    table = lame_table.astype(F32)
    hops = narrow - 1 - owner
    units, joined, plan = PLANS[hops]
    unit = height // sum(units)
    count = len(units)
    bounds, low = [], 0
    for number in units:
        bounds.append((low, low + number * unit))
        low += number * unit
    axes = ("wide", "narrow")

    def rows_of(number):
        low, high = bounds[number]
        return coarse_slab[low:high]

    def send(value, source, target):
        return lax.ppermute(value, "narrow", [(owner + source, owner + target)])

    order = Order(settings(mode))

    ways = [((n * stride) * narrow + owner, (n * stride) * narrow + n) for n in range(owner + 1, narrow)]
    moved = {}

    groups = [[w for w in range(wide) if w % stride == 0], [w for w in range(wide) if w % stride]]
    groups = [group for group in groups if group]
    member = jnp.where(wide_index % stride == 0, 0, 1)

    def within(group, pairs):
        return [(w * narrow + one, w * narrow + two) for w in group for one, two in pairs]

    def halo_of(group, message):
        return lax.ppermute(message, axes, within(group, [(i + 1, i) for i in range(narrow - 1)]))

    spans = [bounds[0], (bounds[joined[0]][0], bounds[joined[-1]][1]) if joined else bounds[1]]
    first, last, *begun = halo_message(table, material_ids, order.token, coarse_basis, coarse_slab, spans)
    first = order.after(first)
    halos = [halo_of(groups[0], first)]
    edge = (narrow_index == 0).astype(jnp.int32).reshape(1)
    inner = order.after(interior(edge, table, material_ids, coarse_basis, order.token))
    head = order.after(lax.ppermute(order.after(coarse_slab[:block]), axes, ways))
    halos[0] = order.after(halos[0])
    moved[0] = [send(order.after(begun[0]), 0, hops)]
    for group in groups[1:]:
        halos.append(halo_of(group, order.after(first)))

    def nearest(base, extent):
        return min(range(base, min(base + extent, narrow)), key=lambda n: abs(n - owner))

    def summed(parts, distance, group):
        total = parts[0] if len(parts) == 1 else parts[0] + parts[1]
        pairs = []
        for base in range(0, narrow - distance, 2 * distance):
            one, two = nearest(base, distance), nearest(base + distance, distance)
            pairs.append((two, one) if nearest(base, 2 * distance) == one else (one, two))
        return [total, lax.ppermute(total, axes, within(group, pairs))], 2 * distance

    def faces_of(number):
        flag = settings(member == number)
        return [order.after(face(flag, table, material_ids, last, halos[number], order.token, inner))]

    sums, reach = [faces_of(0)], [1]
    while reach[0] < narrow:
        sums[0], reach[0] = summed(sums[0], reach[0], groups[0])
    sums[0][1] = order.after(sums[0][1])
    distance, messages, left = wide // 2, [], plan.count("spread")
    result, prepared = None, None
    choice = (narrow_index - owner) % narrow
    flags = settings(mode, kind, own, which)
    for step in plan:
        if step[0] == "panel":
            if prepared is None:
                prepared = prepare(settings(choice, mode), order.token, head, summaries)
            weights, rows, lower = prepared
            begin, end = step[1:]
            parts = [moved[number][:: 1 if number else -1] for number in range(begin, end)]
            result, order.token = panel(
                flags, order.token, lower, weights, rows, added if begin == 0 else head, coarse_slab, parts, result, bounds[begin][0], 2 * unit
            )
        elif step == "sums":
            for place in range(1, narrow):
                galerkins[place] = order.after(galerkins[place])
            added, galerkin = added_of(settings(choice, mode, own), order.token, coarse_ids, galerkins, block)
            added = order.after(added)
        elif step == "next":
            if joined:
                whole = send(order.after(begun[1]), 0, 1)
            else:
                moved[1] = [send(order.after(begun[1]), 0, 1)]
                for number in range(2, count - 1):
                    moved[number] = [send(order.after(rows_of(number)), 0, 1)]
        elif step == "assemble":
            message = assemble(settings(mode, own), order.token, coarse_ids, coarse_slab, head, sums[0])
            message = order.after(message)
        elif step == "others":
            for number in range(1, len(groups)):
                halos[number] = order.after(halos[number])
                parts, far = summed(faces_of(number), 1, groups[number])
                sums.append(parts)
                reach.append(far)
        elif step == "more":
            for number in range(1, len(groups)):
                while reach[number] < narrow:
                    sums[number][1] = order.after(sums[number][1])
                    sums[number], reach[number] = summed(sums[number], reach[number], groups[number])
        elif step == "spread":
            left -= 1
            while distance:
                received = order.after(lax.ppermute(message, axes, holder_pairs(wide, narrow, distance)))
                messages = [message, received]
                if distance > 1:
                    message = message + received
                distance //= 2
                if left:
                    break
        elif step == "factor":
            summary, head, galerkin = factorize(settings(mode, member), order.token, messages, sums)
            summary = order.after(summary)
            ways = [[(owner, (owner + place) % narrow)] for place in range(1, narrow)]
            summaries = [summary] + [lax.ppermute(summary, "narrow", way) for way in ways]
        elif step == "summary":
            for place in range(1, narrow):
                summaries[place] = order.after(summaries[place])
            moved[count - 1] = [send(order.after(rows_of(count - 1)), 0, 1)]
            galerkin = order.after(galerkin)
            galerkins = [galerkin] + [lax.ppermute(galerkin, "narrow", way) for way in ways]
        else:
            number, hop = step
            if joined and step == (joined[0], 0):
                whole = order.after(whole)
                for part in joined:
                    low, high = (bound - bounds[joined[0]][0] for bound in bounds[part])
                    moved[part] = [whole[low:high]]
            moving = moved[number][hop] = order.after(moved[number][hop])
            if number == 0 and hop + 1 < hops:
                moved[number].append(send(moving, hops - hop, hops - hop - 1))
            elif number != 0 and hop + 1 < hops:
                moved[number].append(send(moving, hop + 1, hop + 2))
    return result, galerkin


def any_owner(owner, coarse_basis, material_ids, lame_table, coarse_ids, coarse_slab):
    narrow, wide = lax.axis_size("narrow"), lax.axis_size("wide")
    stride = wide // narrow
    wide_index, narrow_index = lax.axis_index("wide"), lax.axis_index("narrow")
    own = wide_index == narrow_index * stride
    later = narrow_index > owner
    which = jnp.where(later, 0, -1)
    mode = jnp.where(narrow_index == owner, 1, jnp.where(later, 2, 0))
    earlier = (wide_index % stride == 0) & (wide_index // stride < owner)
    kind = jnp.where(wide_index == owner * stride, 1, jnp.where(earlier, 2, 0))
    table = lame_table.astype(F32)
    column = broadcast(coarse_slab, "narrow", owner)
    first, last = halo_message(table, material_ids, table, coarse_basis, coarse_slab, ())
    halo = lax.ppermute(first, "narrow", [(i + 1, i) for i in range(narrow - 1)])
    edge = (narrow_index == 0).astype(jnp.int32).reshape(1)
    inner = interior(edge, table, material_ids, coarse_basis, first)
    partial = face(settings(1), table, material_ids, last, halo, first, inner)
    parts = [lax.psum(partial, "narrow")]
    message = assemble(settings(mode, own), first, coarse_ids, coarse_slab, column, parts)
    at_owner = (wide_index == owner * stride) & (narrow_index == owner)
    diagonal = lax.psum(jnp.where(at_owner, message, 0.0), ("wide", "narrow"))
    summary, _, galerkin = factorize(settings(1, 0), first, [diagonal], [parts])
    head = broadcast(message, "wide", narrow_index * stride)
    weights, rows, lower = prepare(settings(0, mode), settings(mode), head, [summary])
    added, galerkin = added_of(settings(0, mode, own), weights, coarse_ids, [galerkin], head.shape[0])
    flags = settings(mode, kind, own, which)
    tile = coarse_slab.shape[0] // 12
    result, _ = panel(flags, flags, lower, weights, rows, added, coarse_slab, [[column]], None, 0, tile)
    return result, galerkin


def on_device(coarse_basis, material_ids, lame_table, coarse_ids, coarse_slab, panel_owner):
    narrow, wide = lax.axis_size("narrow"), lax.axis_size("wide")
    arrays = (coarse_basis, material_ids, lame_table, coarse_ids, coarse_slab)
    owner = panel_owner[0]
    if narrow - 1 > len(PLANS) or wide & (wide - 1):
        return any_owner(owner, *arrays)
    branches = [functools.partial(known_owner, place) for place in range(narrow - 1)]
    return lax.switch(owner, branches, *arrays)


def solution(mesh):
    return jax.shard_map(
        on_device,
        mesh=mesh,
        in_specs=(
            P("wide", None, None, "narrow", None, None),
            P("wide", "narrow", None, None),
            P(),
            P("wide", None),
            P("wide", "narrow"),
            P(),
        ),
        out_specs=(P("wide", "narrow"), P("wide", None, None)),
        check_vma=False,
    )
```

```python
import functools

import jax
import jax.numpy as jnp
from jax import lax
from jax.experimental import pallas as pl
from jax.experimental.pallas import tpu as pltpu
from jax.sharding import PartitionSpec as P

F32, BF16 = jnp.float32, jnp.bfloat16
NT = (((1,), (1,)), ((), ()))
TN = (((0,), (0,)), ((), ()))
VMEM = pl.BlockSpec(memory_space=pltpu.VMEM)
ANY = pl.BlockSpec(memory_space=pl.ANY)
SMEM = pl.BlockSpec(memory_space=pltpu.SMEM)
PLANS = {
    1: (
        (12, 6, 6),
        False,
        True,
        (
            "assemble", "next", "spread", "others", "spread", "more", "spread", (0, 0), "factor", "summary",
            "sums", ("panel", 0, 2), ("panel", 2, 3),
        ),
    ),
    2: (
        (12, 6, 4, 2),
        False,
        True,
        (
            "assemble", "next", "spread", "others", "spread", "more", "spread", (0, 0), (1, 0), "factor", (2, 0),
            "summary", "sums", ("panel", 1, 2), (3, 0), ("panel", 0, 1), ("panel", 2, 4),
        ),
    ),
    3: (
        (12, 6, 6),
        True,
        False,
        (
            "assemble", "next", "spread", "others", "spread", "more", "spread", (0, 0), "factor", (1, 0), "summary",
            (0, 1), (1, 1), (2, 0), ("panel", 1, 2), (2, 1), "sums", ("panel", 0, 1), ("panel", 2, 3),
        ),
    ),
}
BLOCK = 16
LIGHT = pl.CostEstimate(flops=1, bytes_accessed=1, transcendentals=0)


def exact_dot(left, right, dims=(((1,), (0,)), ((), ()))):
    return lax.dot_general(
        left, right, dims, precision=lax.Precision.HIGHEST, preferred_element_type=F32
    )


def dot(left, right, dims=(((1,), (0,)), ((), ()))):
    return lax.dot_general(left, right, dims, preferred_element_type=F32)


def split_two(value):
    high = value.astype(BF16)
    return high, (value - high.astype(F32)).astype(BF16)


def lame_of(ids, table_ref):
    shear = jnp.zeros(ids.shape, F32)
    dilate = jnp.zeros(ids.shape, F32)
    for material in range(table_ref.shape[1]):
        chosen = ids == material
        shear = jnp.where(chosen, table_ref[0, material], shear)
        dilate = jnp.where(chosen, table_ref[1, material], dilate)
    return shear, dilate


def halo_kernel(table_ref, ids_ref, token_ref, basis_ref, slab_ref, out_ref, last_ref, *rest, spans):
    piece_refs, sems = rest[:-1], rest[-1]
    subs, funcs, comps, layers = basis_ref.shape[0:4]
    copies = []
    for number, ((low, high), piece_ref) in enumerate(zip(spans, piece_refs)):
        copies.append(pltpu.make_async_copy(slab_ref.at[pl.ds(low, high - low)], piece_ref, sems.at[number]))
        copies[-1].start()
    for sub in range(subs):
        for comp in range(comps):
            out_ref[sub, comp * funcs : (comp + 1) * funcs] = basis_ref[sub, :, comp, 0]
            last_ref[sub, comp * funcs : (comp + 1) * funcs] = basis_ref[sub, :, comp, layers - 1]
        shear, dilate = lame_of(ids_ref[sub, 0], table_ref)
        out_ref[sub, comps * funcs] = shear.astype(BF16)
        out_ref[sub, comps * funcs + 1] = dilate.astype(BF16)
    for copy in copies:
        copy.wait()


def halo_message(table, ids, token, basis, slab, spans):
    subs, funcs, comps, layers, ny, nz = basis.shape
    return pl.pallas_call(
        functools.partial(halo_kernel, spans=spans),
        in_specs=[SMEM, VMEM, ANY, VMEM, ANY],
        out_specs=[VMEM] * (2 + len(spans)),
        out_shape=[
            jax.ShapeDtypeStruct((subs, comps * funcs + 2, ny, nz), BF16),
            jax.ShapeDtypeStruct((subs, comps * funcs, ny, nz), BF16),
        ]
        + [jax.ShapeDtypeStruct((high - low, slab.shape[1]), BF16) for low, high in spans],
        scratch_shapes=[pltpu.SemaphoreType.DMA((max(1, len(spans)),))],
        compiler_params=pltpu.CompilerParams(vmem_limit_bytes=16 * 2**20),
        cost_estimate=LIGHT,
        name="halo_message",
    )(table, ids, token, basis, slab)


def interior_kernel(edge_ref, table_ref, ids_ref, basis_ref, token_ref, out_ref, fields, turned, coef, left, right, acc):
    sub, comp = pl.program_id(0), pl.program_id(1)
    layers, ny, nz = basis_ref.shape[3:]
    funcs = basis_ref.shape[1]
    row = lax.broadcasted_iota(jnp.int32, (ny, nz), 0)
    lane = lax.broadcasted_iota(jnp.int32, (ny, nz), 1)
    table = [lame_of(ids_ref[sub, x], table_ref) for x in range(layers)]

    def weight(one, two, direction):
        shear = 0.5 * (one[0] + two[0])
        dilate = 0.5 * (one[1] + two[1])
        return shear + jnp.where(comp == direction, shear + dilate, 0.0)

    def ahead(field, axis):
        size = field.shape[axis]
        index = row if axis == 0 else lane
        return jnp.where(index == size - 1, 0.0, pltpu.roll(field, size - 1, axis=axis))

    def behind(field, axis):
        index = row if axis == 0 else lane
        return jnp.where(index == 0, 0.0, pltpu.roll(field, 1, axis=axis))

    nothing = (jnp.zeros((ny, nz), F32),) * 2
    previous = weight(table[0], nothing, 0) * edge_ref[0].astype(F32)
    for x in range(layers):
        diagonal = previous
        forward = []
        if x + 1 < layers:
            face = weight(table[x], table[x + 1], 0)
            diagonal = diagonal + face
            previous = face
            forward.append(face)
        else:
            forward.append(jnp.zeros((ny, nz), F32))
        for axis in (0, 1):
            index, size = (row, ny) if axis == 0 else (lane, nz)
            other = tuple(ahead(value, axis) for value in table[x])
            face = weight(table[x], other, axis + 1)
            before = tuple(behind(value, axis) for value in table[x])
            diagonal = diagonal + face + weight(table[x], before, axis + 1)
            forward.append(jnp.where(index == size - 1, 0.0, face))
        coef[x, 0] = 0.5 * diagonal
        for kind in range(3):
            coef[x, kind + 1] = forward[kind]
        fields[x] = basis_ref[sub, :, comp, x].astype(F32).reshape(funcs * ny, nz)

    total = None
    for x in reversed(range(layers)):
        values = [fields[x, pl.ds(y, funcs, stride=ny), :] for y in range(ny)]
        for y in range(ny):
            value = values[y]
            turned[x % 2, y] = value
            image = coef[x, 0, y : y + 1, :] * value
            image = image - coef[x, 3, y : y + 1, :] * pltpu.roll(value, nz - 1, axis=1)
            if y + 1 < ny:
                image = image - coef[x, 2, y : y + 1, :] * values[y + 1]
            if x + 1 < layers:
                image = image - coef[x, 1, y : y + 1, :] * turned[(x + 1) % 2, y]
            high, low = split_two(image)
            left[:, y * nz : (y + 1) * nz] = value.astype(BF16)
            right[0:funcs, y * nz : (y + 1) * nz] = high
            right[funcs : 2 * funcs, y * nz : (y + 1) * nz] = low
        product = dot(right[...], left[...], NT)
        total = product if total is None else total + product

    @pl.when(comp == 0)
    def _():
        acc[...] = total

    @pl.when(comp > 0)
    def _():
        acc[...] += total

    @pl.when(comp == pl.num_programs(1) - 1)
    def _():
        out_ref[0] = acc[0:funcs] + acc[funcs : 2 * funcs]


def interior(edge, table, ids, basis, token):
    subs, funcs, comps, layers, ny, nz = basis.shape
    return pl.pallas_call(
        interior_kernel,
        grid=(subs, comps),
        in_specs=[SMEM, SMEM, VMEM, VMEM, ANY],
        out_specs=pl.BlockSpec((1, funcs, funcs), lambda s, c: (s, 0, 0)),
        out_shape=jax.ShapeDtypeStruct((subs, funcs, funcs), F32),
        scratch_shapes=[
            pltpu.VMEM((layers, funcs * ny, nz), F32),
            pltpu.VMEM((2, ny, funcs, nz), F32),
            pltpu.VMEM((layers, 4, ny, nz), F32),
            pltpu.VMEM((funcs, ny * nz), BF16),
            pltpu.VMEM((2 * funcs, ny * nz), BF16),
            pltpu.VMEM((2 * funcs, funcs), F32),
        ],
        compiler_params=pltpu.CompilerParams(vmem_limit_bytes=16 * 2**20),
        cost_estimate=LIGHT,
        name="interior",
    )(edge, table, ids, basis, token)


def face_kernel(flags_ref, table_ref, ids_ref, last_ref, halo_ref, token_ref, inner_ref, out_ref, *scratch):
    @pl.when(flags_ref[0] == 1)
    def _():
        last, halo, sems = scratch[-3:]
        copies = [
            pltpu.make_async_copy(last_ref, last, sems.at[0]),
            pltpu.make_async_copy(halo_ref, halo, sems.at[1]),
        ]
        for copy in copies:
            copy.start()
        for copy in copies:
            copy.wait()
        face_sums(table_ref, ids_ref, last, halo, inner_ref, out_ref, *scratch[:-3])


def face_sums(table_ref, ids_ref, last_ref, halo_ref, inner_ref, out_ref, mine, theirs, left, right, weights, acc):
    subs, layers, ny, nz = ids_ref.shape
    funcs = inner_ref.shape[1]
    comps = last_ref.shape[1] // funcs

    @pl.loop(0, subs)
    def _(sub):
        shear, dilate = lame_of(ids_ref[sub, layers - 1], table_ref)
        weights[0] = 0.5 * (shear + halo_ref[sub, comps * funcs].astype(F32))
        weights[1] = 0.5 * (dilate + halo_ref[sub, comps * funcs + 1].astype(F32))

        @pl.loop(0, comps)
        def _(comp):
            weight = weights[0] + jnp.where(comp == 0, weights[0] + weights[1], 0.0)
            rows = pl.ds(comp * funcs, funcs)
            mine[...] = last_ref[sub, rows].astype(F32).reshape(funcs * ny, nz)
            theirs[...] = halo_ref[sub, rows].astype(F32).reshape(funcs * ny, nz)
            for y in range(ny):
                here = mine[pl.ds(y, funcs, stride=ny), :]
                there = theirs[pl.ds(y, funcs, stride=ny), :]
                high, low = split_two(weight[y : y + 1, :] * (here - there))
                left[0:funcs, y * nz : (y + 1) * nz] = here.astype(BF16)
                left[funcs : 2 * funcs, y * nz : (y + 1) * nz] = there.astype(BF16)
                right[0:funcs, y * nz : (y + 1) * nz] = high
                right[funcs : 2 * funcs, y * nz : (y + 1) * nz] = low
            product = dot(right[...], left[...], NT)

            @pl.when(comp == 0)
            def _():
                acc[...] = product

            @pl.when(comp > 0)
            def _():
                acc[...] += product

        total = acc[:, 0:funcs] - acc[:, funcs : 2 * funcs]
        half = inner_ref[sub] + 0.5 * (total[0:funcs] + total[funcs : 2 * funcs])
        out_ref[sub] = half + half.T


def face(flags, table, ids, last, halo, token, inner):
    subs, layers, ny, nz = ids.shape
    funcs = inner.shape[1]
    return pl.pallas_call(
        face_kernel,
        in_specs=[SMEM, SMEM, VMEM, ANY, ANY, ANY, VMEM],
        out_specs=VMEM,
        out_shape=jax.ShapeDtypeStruct((subs, funcs, funcs), F32),
        scratch_shapes=[
            pltpu.VMEM((funcs * ny, nz), F32),
            pltpu.VMEM((funcs * ny, nz), F32),
            pltpu.VMEM((2 * funcs, ny * nz), BF16),
            pltpu.VMEM((2 * funcs, ny * nz), BF16),
            pltpu.VMEM((2, ny, nz), F32),
            pltpu.VMEM((2 * funcs, 2 * funcs), F32),
            pltpu.VMEM(last.shape, BF16),
            pltpu.VMEM(halo.shape, BF16),
            pltpu.SemaphoreType.DMA((2,)),
        ],
        compiler_params=pltpu.CompilerParams(vmem_limit_bytes=16 * 2**20),
        cost_estimate=LIGHT,
        name="face",
    )(flags, table, ids, last, halo, token, inner)


def spread(gal_ref, column_ids_ref, row_ids_ref, size):
    subs, funcs = column_ids_ref.shape[0:2]
    added = jnp.zeros((size, size), F32)
    lane = lax.broadcasted_iota(jnp.int32, (funcs, size), 1)
    row = lax.broadcasted_iota(jnp.int32, (size, funcs), 0)
    for sub in range(subs):
        slots = (column_ids_ref[sub] == lane).astype(F32)
        slots_t = (row_ids_ref[sub] == row).astype(F32)
        added = added + exact_dot(slots_t, exact_dot(gal_ref[sub], slots))
    return added


def assemble_kernel(flags_ref, token_ref, column_ids_ref, row_ids_ref, slab_ref, head_ref, *rest):
    gal_refs, (message_ref, sum_ref) = rest[:-2], rest[-2:]
    size = message_ref.shape[0]
    mode, own = flags_ref[0], flags_ref[1]
    message_ref[...] = jnp.zeros_like(message_ref)

    @pl.when((mode == 1) & (own == 1))
    def _():
        total = gal_refs[0][...]
        for gal_ref in gal_refs[1:]:
            total = total + gal_ref[...]
        sum_ref[...] = total
        added = spread(sum_ref, column_ids_ref, row_ids_ref, size)
        message_ref[...] = added + slab_ref[...].astype(F32)

    @pl.when((mode == 2) & (own == 1))
    def _():
        message_ref[...] = head_ref[...].astype(F32)


def assemble(flags, token, ids, slab, head, parts):
    size = slab.shape[1]
    block = pl.BlockSpec((size, size), lambda i: (0, 0))
    return pl.pallas_call(
        assemble_kernel,
        grid=(1,),
        in_specs=[SMEM, ANY, VMEM, VMEM, block, block] + [VMEM] * len(parts),
        out_specs=VMEM,
        out_shape=jax.ShapeDtypeStruct((size, size), F32),
        scratch_shapes=[pltpu.VMEM(parts[0].shape, F32)],
        cost_estimate=LIGHT,
        name="assemble",
    )(flags, token, ids[:, :, None], ids[:, None, :], slab, head, *parts)


def factor_kernel(flags_ref, token_ref, *refs, parts, groups):
    message_refs, gal_refs = refs[:parts], refs[parts:-4]
    summary_ref, block_ref, sum_ref, work = refs[-4:]
    subs, funcs = gal_refs[0].shape[0:2]
    size = summary_ref.shape[1]
    diagonal = message_refs[0][...]
    for message_ref in message_refs[1:]:
        diagonal = diagonal + message_ref[...]
    block_ref[...] = diagonal

    @pl.when(flags_ref[0] == 1)
    def _():
        row = lax.broadcasted_iota(jnp.int32, (size, size), 0)
        lane = lax.broadcasted_iota(jnp.int32, (size, size), 1)
        work[:, 0:size] = 0.5 * (diagonal + diagonal.T)
        work[:, size : 2 * size] = (row == lane).astype(F32)
        index = lax.broadcasted_iota(jnp.int32, (BLOCK, size), 0)
        for start in range(0, size, BLOCK):
            panel = work[start : start + BLOCK, 0:size]
            extra = work[start : start + BLOCK, size : 2 * size]
            columns = [
                jnp.broadcast_to(panel[:, start + step : start + step + 1], (BLOCK, size))
                for step in range(BLOCK)
            ]
            for step in range(BLOCK):
                scale = lax.rsqrt(columns[step][step : step + 1, :])
                column = jnp.where(index > step, columns[step] * scale, 0.0)
                for later in range(step + 1, BLOCK):
                    columns[later] = columns[later] - column * column[later : later + 1, :]
                pivot = panel[step : step + 1, :] * scale
                panel = jnp.where(index == step, pivot, panel - column * pivot)
                pivot = extra[step : step + 1, :] * scale
                extra = jnp.where(index == step, pivot, extra - column * pivot)
            work[start : start + BLOCK, 0:size] = panel
            work[start : start + BLOCK, size : 2 * size] = extra
            rest = start + BLOCK
            if rest < size:
                both = jnp.concatenate([panel, extra], axis=1)
                work[rest:size, :] -= exact_dot(panel[:, rest:size], both, TN)
        upper = jnp.where(row <= lane, work[:, 0:size], 0.0)
        inverse = jnp.where(row >= lane, work[:, size : 2 * size], 0.0).T
        high = inverse.astype(BF16)
        summary_ref[0:size] = high
        summary_ref[size : 2 * size] = (inverse - high.astype(F32)).astype(BF16)
        summary_ref[2 * size : 3 * size] = upper.T.astype(BF16)
        each = len(gal_refs) // groups
        for group in range(groups):

            @pl.when(flags_ref[1] == group)
            def _(chosen=gal_refs[group * each : (group + 1) * each]):
                total = chosen[0][...]
                for gal_ref in chosen[1:]:
                    total = total + gal_ref[...]
                sum_ref[...] = total


def factorize(flags, token, messages, groups):
    size = messages[0].shape[1]
    subs, funcs = groups[0][0].shape[0:2]
    parts = [part for group in groups for part in group]
    return pl.pallas_call(
        functools.partial(factor_kernel, parts=len(messages), groups=len(groups)),
        in_specs=[SMEM, ANY] + [VMEM] * (len(messages) + len(parts)),
        out_specs=[VMEM] * 3,
        out_shape=[
            jax.ShapeDtypeStruct((3 * size, size), BF16),
            jax.ShapeDtypeStruct((size, size), F32),
            jax.ShapeDtypeStruct(groups[0][0].shape, F32),
        ],
        scratch_shapes=[pltpu.VMEM((size, 2 * size), F32)],
        cost_estimate=LIGHT,
        name="factorize",
    )(flags, token, *messages, *parts)


def prepare_kernel(flags_ref, token_ref, head_ref, *rest, sources):
    summary_refs = rest[:sources]
    weights_ref, rows_ref, lower_ref, summary, sem = rest[sources:]
    size = head_ref.shape[0]
    choice, mode = flags_ref[0], flags_ref[1]
    for number, summary_ref in enumerate(summary_refs):

        @pl.when(choice == number)
        def _(summary_ref=summary_ref):
            copy = pltpu.make_async_copy(summary_ref, summary, sem)
            copy.start()
            copy.wait()

    def doubled(block):
        nothing = jnp.zeros((size, size), BF16)
        top = jnp.concatenate([block, nothing], axis=1)
        return jnp.concatenate([top, jnp.concatenate([nothing, block], axis=1)], axis=0)

    @pl.when(mode > 0)
    def _():
        weights_ref[0 : 2 * size] = doubled(summary[0:size])
        weights_ref[2 * size : 4 * size] = doubled(summary[size : 2 * size])
        lower_ref[...] = summary[2 * size : 3 * size]

    @pl.when(mode == 2)
    def _():
        inverse = summary[0:size].astype(F32) + summary[size : 2 * size].astype(F32)
        solved = exact_dot(head_ref[...], inverse)
        rows_ref[...] = doubled(solved.T.astype(BF16))


def prepare(flags, token, head, summaries):
    size = head.shape[0]
    return pl.pallas_call(
        functools.partial(prepare_kernel, sources=len(summaries)),
        in_specs=[SMEM, ANY, VMEM] + [ANY] * len(summaries),
        out_specs=[VMEM] * 3,
        out_shape=[
            jax.ShapeDtypeStruct((4 * size, 2 * size), BF16),
            jax.ShapeDtypeStruct((2 * size, 2 * size), BF16),
            jax.ShapeDtypeStruct((size, size), BF16),
        ],
        scratch_shapes=[pltpu.VMEM(summaries[0].shape, BF16), pltpu.SemaphoreType.DMA],
        compiler_params=pltpu.CompilerParams(vmem_limit_bytes=16 * 2**20),
        cost_estimate=LIGHT,
        name="prepare",
    )(flags, token, head, *summaries)


def added_kernel(flags_ref, token_ref, column_ids_ref, row_ids_ref, *rest, sources):
    sum_refs, (added_ref, gal_ref) = rest[:sources], rest[sources:]
    for number, sum_ref in enumerate(sum_refs):

        @pl.when(flags_ref[0] == number)
        def _(sum_ref=sum_ref):
            gal_ref[...] = sum_ref[...]

    @pl.when((flags_ref[1] == 2) & (flags_ref[2] == 1))
    def _():
        added_ref[...] = spread(gal_ref, column_ids_ref, row_ids_ref, added_ref.shape[0])


def added_of(flags, token, ids, sums, size):
    return pl.pallas_call(
        functools.partial(added_kernel, sources=len(sums)),
        in_specs=[SMEM, ANY] + [VMEM] * (2 + len(sums)),
        out_specs=[VMEM] * 2,
        out_shape=[jax.ShapeDtypeStruct((size, size), F32), jax.ShapeDtypeStruct(sums[0].shape, F32)],
        cost_estimate=LIGHT,
        name="added",
    )(flags, token, ids[:, :, None], ids[:, None, :], *sums)


def panel_kernel(
    flags_ref, token_ref, lower_ref, weights_ref, rows_ref, added_ref, slab_ref, *rest, pieces, spans, first
):
    hops = len(pieces) // len(spans)
    others = rest[: len(pieces)]
    out_ref, done_ref, column, factor, sems = rest[-5:]
    done_ref[0] = flags_ref[0]
    tile, size = out_ref.shape
    half = tile // 2
    mode, head, own, which = flags_ref[0], flags_ref[1], flags_ref[2], flags_ref[3]
    step, steps = pl.program_id(0), pl.num_programs(0)
    top = first & (step == 0)

    def copy_of(at, act):
        for number, (begin, end) in enumerate(spans):
            for hop in range(hops):

                @pl.when((mode == 2) & (which == hop) & (at >= begin) & (at < end))
                def _(other_ref=others[number * hops + hop], begin=begin):
                    source = other_ref.at[pl.ds(pl.multiple_of((at - begin) * tile, tile), tile)]
                    act(pltpu.make_async_copy(source, column.at[at % 2], sems.at[at % 2]))

    @pl.when(step == 0)
    def _():
        copy_of(step, lambda copy: copy.start())

    @pl.when(step + 1 < steps)
    def _():
        copy_of(step + 1, lambda copy: copy.start())

    @pl.when(mode == 0)
    def _():
        out_ref[...] = slab_ref[...]

    @pl.when(mode == 1)
    def _():
        column[step % 2] = slab_ref[...]

    @pl.when(mode == 2)
    def _():
        copy_of(step, lambda copy: copy.wait())

    @pl.when(mode > 0)
    def _():
        value = column[step % 2]
        pair = jnp.concatenate([value[0:half], value[half:tile]], axis=1)
        factor[...] = dot(jnp.concatenate([pair, pair], axis=1), weights_ref[...]).astype(BF16)

        @pl.when(top & (head == 1))
        def _():
            factor[0:size, 0:size] = lower_ref[...]

        @pl.when(top & (head == 2))
        def _():
            factor[0:size, 0:size] = jnp.zeros((size, size), BF16)

    @pl.when(mode == 1)
    def _():
        out_ref[0:half] = factor[:, 0:size]
        out_ref[half:tile] = factor[:, size : 2 * size]

    @pl.when(mode == 2)
    def _():
        update = dot(factor[...], rows_ref[...])
        out_ref[0:half] = (slab_ref[0:half].astype(F32) - update[:, 0:size]).astype(BF16)
        out_ref[half:tile] = (slab_ref[half:tile].astype(F32) - update[:, size : 2 * size]).astype(BF16)

        @pl.when(top & (own == 1))
        def _():
            base = slab_ref[0:size].astype(F32) + added_ref[...]
            out_ref[0:size] = (base - update[0:size, 0:size]).astype(BF16)


def panel(flags, token, lower, weights, rows, added, slab, parts, old, start, tile):
    size = slab.shape[1]
    offset = start // tile
    spans, begin, operands = [], 0, []
    for hops in parts:
        end = begin + hops[0].shape[0] // tile
        spans.append((begin, end))
        begin = end
        operands += hops
    blocks = [
        SMEM,
        ANY,
        pl.BlockSpec((size, size), lambda i: (0, 0)),
        pl.BlockSpec(weights.shape, lambda i: (0, 0)),
        pl.BlockSpec(rows.shape, lambda i: (0, 0)),
        pl.BlockSpec((size, size), lambda i: (0, 0)),
        pl.BlockSpec((tile, size), lambda i: (i + offset, 0)),
    ] + [ANY] * len(operands)
    pieces = len(operands)
    operands = [flags, token, lower, weights, rows, added, slab] + operands
    aliases = {}
    if old is not None:
        aliases = {len(operands): 0}
        blocks.append(ANY)
        operands.append(old)
    return pl.pallas_call(
        functools.partial(panel_kernel, pieces=range(pieces), spans=spans, first=start == 0),
        grid=(begin,),
        in_specs=blocks,
        out_specs=[pl.BlockSpec((tile, size), lambda i: (i + offset, 0)), SMEM],
        out_shape=[jax.ShapeDtypeStruct(slab.shape, BF16), jax.ShapeDtypeStruct((1,), jnp.int32)],
        input_output_aliases=aliases,
        scratch_shapes=[
            pltpu.VMEM((2, tile, size), BF16),
            pltpu.VMEM((tile // 2, 2 * size), BF16),
            pltpu.SemaphoreType.DMA((2,)),
        ],
        compiler_params=pltpu.CompilerParams(vmem_limit_bytes=16 * 2**20),
        cost_estimate=LIGHT,
        name="panel",
    )(*operands)


def broadcast(value, axis, source):
    kept = jnp.where(lax.axis_index(axis) == source, value, 0).astype(value.dtype)
    return lax.psum(kept, axis)


def settings(*values):
    return jnp.stack([jnp.asarray(value).astype(jnp.int32) for value in values])


def holder_pairs(wide, narrow, distance):
    stride = wide // narrow
    found = []
    for n in range(narrow):
        for start in range(0, wide, 2 * distance):
            source = (n * stride) ^ start
            found.append((source * narrow + n, (source ^ distance) * narrow + n))
    return found


class Order:
    def __init__(self, token):
        self.token = token

    def after(self, value):
        value, self.token = lax.optimization_barrier((value, self.token))
        return value


def known_owner(owner, coarse_basis, material_ids, lame_table, coarse_ids, coarse_slab):
    narrow, wide = lax.axis_size("narrow"), lax.axis_size("wide")
    stride = wide // narrow
    wide_index, narrow_index = lax.axis_index("wide"), lax.axis_index("narrow")
    height, block = coarse_slab.shape
    own = wide_index == narrow_index * stride
    later = narrow_index > owner
    which = jnp.where(later, narrow_index - owner - 1, -1)
    mode = jnp.where(narrow_index == owner, 1, jnp.where(later, 2, 0))
    earlier = (wide_index % stride == 0) & (wide_index // stride < owner)
    kind = jnp.where(wide_index == owner * stride, 1, jnp.where(earlier, 2, 0))
    table = lame_table.astype(F32)
    hops = narrow - 1 - owner
    units, joined, waits, plan = PLANS[hops]
    unit = height // sum(units)
    count = len(units)
    bounds, low = [], 0
    for number in units:
        bounds.append((low, low + number * unit))
        low += number * unit
    axes = ("wide", "narrow")

    def rows_of(number):
        low, high = bounds[number]
        return coarse_slab[low:high]

    def send(value, source, target):
        return lax.ppermute(value, "narrow", [(owner + source, owner + target)])

    order = Order(settings(mode))

    ways = [((n * stride) * narrow + owner, (n * stride) * narrow + n) for n in range(owner + 1, narrow)]
    moved = {}

    groups = [[w for w in range(wide) if w % stride == 0], [w for w in range(wide) if w % stride]]
    groups = [group for group in groups if group]
    member = jnp.where(wide_index % stride == 0, 0, 1)

    def within(group, pairs):
        return [(w * narrow + one, w * narrow + two) for w in group for one, two in pairs]

    def halo_of(group, message):
        return lax.ppermute(message, axes, within(group, [(i + 1, i) for i in range(narrow - 1)]))

    spans = [bounds[0], (bounds[1][0], height) if joined else bounds[1]]
    first, last, *begun = halo_message(table, material_ids, order.token, coarse_basis, coarse_slab, spans)
    first = order.after(first)
    halos = [halo_of(groups[0], first)]
    edge = (narrow_index == 0).astype(jnp.int32).reshape(1)
    inner = order.after(interior(edge, table, material_ids, coarse_basis, order.token))
    head = order.after(lax.ppermute(order.after(coarse_slab[:block]), axes, ways))
    halos[0] = order.after(halos[0])
    moved[0] = [send(order.after(begun[0]), 0, hops)]
    for group in groups[1:]:
        halos.append(halo_of(group, order.after(first)))

    def nearest(base, extent):
        return min(range(base, min(base + extent, narrow)), key=lambda n: abs(n - owner))

    def summed(parts, distance, group):
        total = parts[0] if len(parts) == 1 else parts[0] + parts[1]
        pairs = []
        for base in range(0, narrow - distance, 2 * distance):
            one, two = nearest(base, distance), nearest(base + distance, distance)
            pairs.append((two, one) if nearest(base, 2 * distance) == one else (one, two))
        return [total, lax.ppermute(total, axes, within(group, pairs))], 2 * distance

    def faces_of(number):
        flag = settings(member == number)
        return [order.after(face(flag, table, material_ids, last, halos[number], order.token, inner))]

    sums, reach = [faces_of(0)], [1]
    while reach[0] < narrow:
        sums[0], reach[0] = summed(sums[0], reach[0], groups[0])
    sums[0][1] = order.after(sums[0][1])
    distance, messages, left = wide // 2, [], plan.count("spread")
    result, prepared = None, None
    choice = (narrow_index - owner) % narrow
    flags = settings(mode, kind, own, which)
    for step in plan:
        if step[0] == "panel":
            if prepared is None:
                prepared = prepare(settings(choice, mode), order.token, head, summaries)
            weights, rows, lower = prepared
            begin, end = step[1:]
            parts = [moved[number][:: 1 if number else -1] for number in range(begin, end)]
            result, order.token = panel(
                flags, order.token, lower, weights, rows, added if begin == 0 else head, coarse_slab, parts, result, bounds[begin][0], 2 * unit
            )
        elif step == "sums":
            for place in range(1, narrow):
                galerkins[place] = order.after(galerkins[place])
            added, galerkin = added_of(settings(choice, mode, own), order.token, coarse_ids, galerkins, block)
            added = order.after(added)
        elif step == "next":
            if joined:
                whole = send(order.after(begun[1]), 0, 1)
            else:
                moved[1] = [send(order.after(begun[1]), 0, 1)]
                for number in range(2, count - waits):
                    moved[number] = [send(order.after(rows_of(number)), 0, 1)]
        elif step == "assemble":
            message = assemble(settings(mode, own), order.token, coarse_ids, coarse_slab, head, sums[0])
            message = order.after(message)
        elif step == "others":
            for number in range(1, len(groups)):
                halos[number] = order.after(halos[number])
                parts, far = summed(faces_of(number), 1, groups[number])
                sums.append(parts)
                reach.append(far)
        elif step == "more":
            for number in range(1, len(groups)):
                while reach[number] < narrow:
                    sums[number][1] = order.after(sums[number][1])
                    sums[number], reach[number] = summed(sums[number], reach[number], groups[number])
        elif step == "spread":
            left -= 1
            while distance:
                received = order.after(lax.ppermute(message, axes, holder_pairs(wide, narrow, distance)))
                messages = [message, received]
                if distance > 1:
                    message = message + received
                distance //= 2
                if left:
                    break
        elif step == "factor":
            summary, head, galerkin = factorize(settings(mode, member), order.token, messages, sums)
            summary = order.after(summary)
            ways = [[(owner, (owner + place) % narrow)] for place in range(1, narrow)]
            summaries = [summary] + [lax.ppermute(summary, "narrow", way) for way in ways]
        elif step == "summary":
            for place in range(1, narrow):
                summaries[place] = order.after(summaries[place])
            if waits:
                moved[count - 1] = [send(order.after(rows_of(count - 1)), 0, 1)]
            galerkin = order.after(galerkin)
            galerkins = [galerkin] + [lax.ppermute(galerkin, "narrow", way) for way in ways]
        else:
            number, hop = step
            if joined and step == (1, 0):
                whole = order.after(whole)
                for part in range(1, count):
                    low, high = (bound - bounds[1][0] for bound in bounds[part])
                    moved[part] = [whole[low:high]]
            moving = moved[number][hop] = order.after(moved[number][hop])
            if number == 0 and hop + 1 < hops:
                moved[number].append(send(moving, hops - hop, hops - hop - 1))
            elif number != 0 and hop + 1 < hops:
                moved[number].append(send(moving, hop + 1, hop + 2))
    return result, galerkin


def any_owner(owner, coarse_basis, material_ids, lame_table, coarse_ids, coarse_slab):
    narrow, wide = lax.axis_size("narrow"), lax.axis_size("wide")
    stride = wide // narrow
    wide_index, narrow_index = lax.axis_index("wide"), lax.axis_index("narrow")
    own = wide_index == narrow_index * stride
    later = narrow_index > owner
    which = jnp.where(later, 0, -1)
    mode = jnp.where(narrow_index == owner, 1, jnp.where(later, 2, 0))
    earlier = (wide_index % stride == 0) & (wide_index // stride < owner)
    kind = jnp.where(wide_index == owner * stride, 1, jnp.where(earlier, 2, 0))
    table = lame_table.astype(F32)
    column = broadcast(coarse_slab, "narrow", owner)
    first, last = halo_message(table, material_ids, table, coarse_basis, coarse_slab, ())
    halo = lax.ppermute(first, "narrow", [(i + 1, i) for i in range(narrow - 1)])
    edge = (narrow_index == 0).astype(jnp.int32).reshape(1)
    inner = interior(edge, table, material_ids, coarse_basis, first)
    partial = face(settings(1), table, material_ids, last, halo, first, inner)
    parts = [lax.psum(partial, "narrow")]
    message = assemble(settings(mode, own), first, coarse_ids, coarse_slab, column, parts)
    at_owner = (wide_index == owner * stride) & (narrow_index == owner)
    diagonal = lax.psum(jnp.where(at_owner, message, 0.0), ("wide", "narrow"))
    summary, _, galerkin = factorize(settings(1, 0), first, [diagonal], [parts])
    head = broadcast(message, "wide", narrow_index * stride)
    weights, rows, lower = prepare(settings(0, mode), settings(mode), head, [summary])
    added, galerkin = added_of(settings(0, mode, own), weights, coarse_ids, [galerkin], head.shape[0])
    flags = settings(mode, kind, own, which)
    tile = coarse_slab.shape[0] // 12
    result, _ = panel(flags, flags, lower, weights, rows, added, coarse_slab, [[column]], None, 0, tile)
    return result, galerkin


def on_device(coarse_basis, material_ids, lame_table, coarse_ids, coarse_slab, panel_owner):
    narrow, wide = lax.axis_size("narrow"), lax.axis_size("wide")
    arrays = (coarse_basis, material_ids, lame_table, coarse_ids, coarse_slab)
    owner = panel_owner[0]
    if narrow - 1 > len(PLANS) or wide & (wide - 1):
        return any_owner(owner, *arrays)
    branches = [functools.partial(known_owner, place) for place in range(narrow - 1)]
    return lax.switch(owner, branches, *arrays)


def solution(mesh):
    return jax.shard_map(
        on_device,
        mesh=mesh,
        in_specs=(
            P("wide", None, None, "narrow", None, None),
            P("wide", "narrow", None, None),
            P(),
            P("wide", None),
            P("wide", "narrow"),
            P(),
        ),
        out_specs=(P("wide", "narrow"), P("wide", None, None)),
        check_vma=False,
    )
```

```python
import functools

import jax
import jax.numpy as jnp
from jax import lax
from jax.experimental import pallas as pl
from jax.experimental.pallas import tpu as pltpu
from jax.sharding import PartitionSpec as P

F32, BF16 = jnp.float32, jnp.bfloat16
NT = (((1,), (1,)), ((), ()))
TN = (((0,), (0,)), ((), ()))
VMEM = pl.BlockSpec(memory_space=pltpu.VMEM)
ANY = pl.BlockSpec(memory_space=pl.ANY)
SMEM = pl.BlockSpec(memory_space=pltpu.SMEM)
PLANS = {
    1: (
        (12, 8, 4),
        False,
        True,
        (
            "assemble", "next", "spread", "others", "spread", "more", "spread", (0, 0), "factor", "summary",
            "added", ("panel", 0, 2), "sums", ("panel", 2, 3),
        ),
    ),
    2: (
        (12, 6, 4, 2),
        False,
        True,
        (
            "assemble", "next", "spread", "others", "spread", "more", "spread", (0, 0), (1, 0), "factor", (2, 0),
            "summary", "added", ("panel", 1, 2), (3, 0), ("panel", 0, 1), "sums", ("panel", 2, 4),
        ),
    ),
    3: (
        (12, 6, 6),
        True,
        False,
        (
            "assemble", "next", "spread", "others", "spread", "more", "spread", (0, 0), "factor", (1, 0), "summary",
            (0, 1), (1, 1), (2, 0), ("panel", 1, 2), (2, 1), "added", ("panel", 0, 1), "sums", ("panel", 2, 3),
        ),
    ),
}
BLOCK = 16
LIGHT = pl.CostEstimate(flops=1, bytes_accessed=1, transcendentals=0)


def exact_dot(left, right, dims=(((1,), (0,)), ((), ()))):
    return lax.dot_general(
        left, right, dims, precision=lax.Precision.HIGHEST, preferred_element_type=F32
    )


def dot(left, right, dims=(((1,), (0,)), ((), ()))):
    return lax.dot_general(left, right, dims, preferred_element_type=F32)


def split_two(value):
    high = value.astype(BF16)
    return high, (value - high.astype(F32)).astype(BF16)


def lame_of(ids, table_ref):
    shear = jnp.zeros(ids.shape, F32)
    dilate = jnp.zeros(ids.shape, F32)
    for material in range(table_ref.shape[1]):
        chosen = ids == material
        shear = jnp.where(chosen, table_ref[0, material], shear)
        dilate = jnp.where(chosen, table_ref[1, material], dilate)
    return shear, dilate


def halo_kernel(table_ref, ids_ref, token_ref, basis_ref, slab_ref, out_ref, last_ref, *rest, spans):
    piece_refs, sems = rest[:-1], rest[-1]
    subs, funcs, comps, layers = basis_ref.shape[0:4]
    copies = []
    for number, ((low, high), piece_ref) in enumerate(zip(spans, piece_refs)):
        copies.append(pltpu.make_async_copy(slab_ref.at[pl.ds(low, high - low)], piece_ref, sems.at[number]))
        copies[-1].start()
    for sub in range(subs):
        for comp in range(comps):
            out_ref[sub, comp * funcs : (comp + 1) * funcs] = basis_ref[sub, :, comp, 0]
            last_ref[sub, comp * funcs : (comp + 1) * funcs] = basis_ref[sub, :, comp, layers - 1]
        shear, dilate = lame_of(ids_ref[sub, 0], table_ref)
        out_ref[sub, comps * funcs] = shear.astype(BF16)
        out_ref[sub, comps * funcs + 1] = dilate.astype(BF16)
    for copy in copies:
        copy.wait()


def halo_message(table, ids, token, basis, slab, spans):
    subs, funcs, comps, layers, ny, nz = basis.shape
    return pl.pallas_call(
        functools.partial(halo_kernel, spans=spans),
        in_specs=[SMEM, VMEM, ANY, VMEM, ANY],
        out_specs=[VMEM] * (2 + len(spans)),
        out_shape=[
            jax.ShapeDtypeStruct((subs, comps * funcs + 2, ny, nz), BF16),
            jax.ShapeDtypeStruct((subs, comps * funcs, ny, nz), BF16),
        ]
        + [jax.ShapeDtypeStruct((high - low, slab.shape[1]), BF16) for low, high in spans],
        scratch_shapes=[pltpu.SemaphoreType.DMA((max(1, len(spans)),))],
        compiler_params=pltpu.CompilerParams(vmem_limit_bytes=16 * 2**20),
        cost_estimate=LIGHT,
        name="halo_message",
    )(table, ids, token, basis, slab)


def interior_kernel(edge_ref, table_ref, ids_ref, basis_ref, token_ref, out_ref, fields, turned, coef, left, right, acc):
    sub, comp = pl.program_id(0), pl.program_id(1)
    layers, ny, nz = basis_ref.shape[3:]
    funcs = basis_ref.shape[1]
    row = lax.broadcasted_iota(jnp.int32, (ny, nz), 0)
    lane = lax.broadcasted_iota(jnp.int32, (ny, nz), 1)
    table = [lame_of(ids_ref[sub, x], table_ref) for x in range(layers)]

    def weight(one, two, direction):
        shear = 0.5 * (one[0] + two[0])
        dilate = 0.5 * (one[1] + two[1])
        return shear + jnp.where(comp == direction, shear + dilate, 0.0)

    def ahead(field, axis):
        size = field.shape[axis]
        index = row if axis == 0 else lane
        return jnp.where(index == size - 1, 0.0, pltpu.roll(field, size - 1, axis=axis))

    def behind(field, axis):
        index = row if axis == 0 else lane
        return jnp.where(index == 0, 0.0, pltpu.roll(field, 1, axis=axis))

    nothing = (jnp.zeros((ny, nz), F32),) * 2
    previous = weight(table[0], nothing, 0) * edge_ref[0].astype(F32)
    for x in range(layers):
        diagonal = previous
        forward = []
        if x + 1 < layers:
            face = weight(table[x], table[x + 1], 0)
            diagonal = diagonal + face
            previous = face
            forward.append(face)
        else:
            forward.append(jnp.zeros((ny, nz), F32))
        for axis in (0, 1):
            index, size = (row, ny) if axis == 0 else (lane, nz)
            other = tuple(ahead(value, axis) for value in table[x])
            face = weight(table[x], other, axis + 1)
            before = tuple(behind(value, axis) for value in table[x])
            diagonal = diagonal + face + weight(table[x], before, axis + 1)
            forward.append(jnp.where(index == size - 1, 0.0, face))
        coef[x, 0] = 0.5 * diagonal
        for kind in range(3):
            coef[x, kind + 1] = forward[kind]
        fields[x] = basis_ref[sub, :, comp, x].astype(F32).reshape(funcs * ny, nz)

    total = None
    for x in reversed(range(layers)):
        values = [fields[x, pl.ds(y, funcs, stride=ny), :] for y in range(ny)]
        for y in range(ny):
            value = values[y]
            turned[x % 2, y] = value
            image = coef[x, 0, y : y + 1, :] * value
            image = image - coef[x, 3, y : y + 1, :] * pltpu.roll(value, nz - 1, axis=1)
            if y + 1 < ny:
                image = image - coef[x, 2, y : y + 1, :] * values[y + 1]
            if x + 1 < layers:
                image = image - coef[x, 1, y : y + 1, :] * turned[(x + 1) % 2, y]
            high, low = split_two(image)
            left[:, y * nz : (y + 1) * nz] = value.astype(BF16)
            right[0:funcs, y * nz : (y + 1) * nz] = high
            right[funcs : 2 * funcs, y * nz : (y + 1) * nz] = low
        product = dot(right[...], left[...], NT)
        total = product if total is None else total + product

    @pl.when(comp == 0)
    def _():
        acc[...] = total

    @pl.when(comp > 0)
    def _():
        acc[...] += total

    @pl.when(comp == pl.num_programs(1) - 1)
    def _():
        out_ref[0] = acc[0:funcs] + acc[funcs : 2 * funcs]


def interior(edge, table, ids, basis, token):
    subs, funcs, comps, layers, ny, nz = basis.shape
    return pl.pallas_call(
        interior_kernel,
        grid=(subs, comps),
        in_specs=[SMEM, SMEM, VMEM, VMEM, ANY],
        out_specs=pl.BlockSpec((1, funcs, funcs), lambda s, c: (s, 0, 0)),
        out_shape=jax.ShapeDtypeStruct((subs, funcs, funcs), F32),
        scratch_shapes=[
            pltpu.VMEM((layers, funcs * ny, nz), F32),
            pltpu.VMEM((2, ny, funcs, nz), F32),
            pltpu.VMEM((layers, 4, ny, nz), F32),
            pltpu.VMEM((funcs, ny * nz), BF16),
            pltpu.VMEM((2 * funcs, ny * nz), BF16),
            pltpu.VMEM((2 * funcs, funcs), F32),
        ],
        compiler_params=pltpu.CompilerParams(vmem_limit_bytes=16 * 2**20),
        cost_estimate=LIGHT,
        name="interior",
    )(edge, table, ids, basis, token)


def face_kernel(flags_ref, table_ref, ids_ref, last_ref, halo_ref, token_ref, inner_ref, out_ref, *scratch):
    @pl.when(flags_ref[0] == 1)
    def _():
        last, halo, sems = scratch[-3:]
        copies = [
            pltpu.make_async_copy(last_ref, last, sems.at[0]),
            pltpu.make_async_copy(halo_ref, halo, sems.at[1]),
        ]
        for copy in copies:
            copy.start()
        for copy in copies:
            copy.wait()
        face_sums(table_ref, ids_ref, last, halo, inner_ref, out_ref, *scratch[:-3])


def face_sums(table_ref, ids_ref, last_ref, halo_ref, inner_ref, out_ref, mine, theirs, left, right, weights, acc):
    subs, layers, ny, nz = ids_ref.shape
    funcs = inner_ref.shape[1]
    comps = last_ref.shape[1] // funcs

    @pl.loop(0, subs)
    def _(sub):
        shear, dilate = lame_of(ids_ref[sub, layers - 1], table_ref)
        weights[0] = 0.5 * (shear + halo_ref[sub, comps * funcs].astype(F32))
        weights[1] = 0.5 * (dilate + halo_ref[sub, comps * funcs + 1].astype(F32))

        @pl.loop(0, comps)
        def _(comp):
            weight = weights[0] + jnp.where(comp == 0, weights[0] + weights[1], 0.0)
            rows = pl.ds(comp * funcs, funcs)
            mine[...] = last_ref[sub, rows].astype(F32).reshape(funcs * ny, nz)
            theirs[...] = halo_ref[sub, rows].astype(F32).reshape(funcs * ny, nz)
            for y in range(ny):
                here = mine[pl.ds(y, funcs, stride=ny), :]
                there = theirs[pl.ds(y, funcs, stride=ny), :]
                high, low = split_two(weight[y : y + 1, :] * (here - there))
                left[0:funcs, y * nz : (y + 1) * nz] = here.astype(BF16)
                left[funcs : 2 * funcs, y * nz : (y + 1) * nz] = there.astype(BF16)
                right[0:funcs, y * nz : (y + 1) * nz] = high
                right[funcs : 2 * funcs, y * nz : (y + 1) * nz] = low
            product = dot(right[...], left[...], NT)

            @pl.when(comp == 0)
            def _():
                acc[...] = product

            @pl.when(comp > 0)
            def _():
                acc[...] += product

        total = acc[:, 0:funcs] - acc[:, funcs : 2 * funcs]
        half = inner_ref[sub] + 0.5 * (total[0:funcs] + total[funcs : 2 * funcs])
        out_ref[sub] = half + half.T


def face(flags, table, ids, last, halo, token, inner):
    subs, layers, ny, nz = ids.shape
    funcs = inner.shape[1]
    return pl.pallas_call(
        face_kernel,
        in_specs=[SMEM, SMEM, VMEM, ANY, ANY, ANY, VMEM],
        out_specs=VMEM,
        out_shape=jax.ShapeDtypeStruct((subs, funcs, funcs), F32),
        scratch_shapes=[
            pltpu.VMEM((funcs * ny, nz), F32),
            pltpu.VMEM((funcs * ny, nz), F32),
            pltpu.VMEM((2 * funcs, ny * nz), BF16),
            pltpu.VMEM((2 * funcs, ny * nz), BF16),
            pltpu.VMEM((2, ny, nz), F32),
            pltpu.VMEM((2 * funcs, 2 * funcs), F32),
            pltpu.VMEM(last.shape, BF16),
            pltpu.VMEM(halo.shape, BF16),
            pltpu.SemaphoreType.DMA((2,)),
        ],
        compiler_params=pltpu.CompilerParams(vmem_limit_bytes=16 * 2**20),
        cost_estimate=LIGHT,
        name="face",
    )(flags, table, ids, last, halo, token, inner)


def spread(gal_ref, column_ids_ref, row_ids_ref, size):
    subs, funcs = column_ids_ref.shape[0:2]
    added = jnp.zeros((size, size), F32)
    lane = lax.broadcasted_iota(jnp.int32, (funcs, size), 1)
    row = lax.broadcasted_iota(jnp.int32, (size, funcs), 0)
    for sub in range(subs):
        slots = (column_ids_ref[sub] == lane).astype(F32)
        slots_t = (row_ids_ref[sub] == row).astype(F32)
        added = added + exact_dot(slots_t, exact_dot(gal_ref[sub], slots))
    return added


def assemble_kernel(flags_ref, token_ref, column_ids_ref, row_ids_ref, slab_ref, head_ref, *rest):
    gal_refs, (message_ref, sum_ref) = rest[:-2], rest[-2:]
    size = message_ref.shape[0]
    mode, own = flags_ref[0], flags_ref[1]
    message_ref[...] = jnp.zeros_like(message_ref)

    @pl.when((mode == 1) & (own == 1))
    def _():
        total = gal_refs[0][...]
        for gal_ref in gal_refs[1:]:
            total = total + gal_ref[...]
        sum_ref[...] = total
        added = spread(sum_ref, column_ids_ref, row_ids_ref, size)
        message_ref[...] = added + slab_ref[...].astype(F32)

    @pl.when((mode == 2) & (own == 1))
    def _():
        message_ref[...] = head_ref[...].astype(F32)


def assemble(flags, token, ids, slab, head, parts):
    size = slab.shape[1]
    block = pl.BlockSpec((size, size), lambda i: (0, 0))
    return pl.pallas_call(
        assemble_kernel,
        grid=(1,),
        in_specs=[SMEM, ANY, VMEM, VMEM, block, block] + [VMEM] * len(parts),
        out_specs=VMEM,
        out_shape=jax.ShapeDtypeStruct((size, size), F32),
        scratch_shapes=[pltpu.VMEM(parts[0].shape, F32)],
        cost_estimate=LIGHT,
        name="assemble",
    )(flags, token, ids[:, :, None], ids[:, None, :], slab, head, *parts)


def factor_kernel(flags_ref, token_ref, *refs, parts, groups):
    message_refs, gal_refs = refs[:parts], refs[parts:-4]
    summary_ref, block_ref, sum_ref, work = refs[-4:]
    subs, funcs = gal_refs[0].shape[0:2]
    size = summary_ref.shape[1]
    diagonal = message_refs[0][...]
    for message_ref in message_refs[1:]:
        diagonal = diagonal + message_ref[...]
    block_ref[...] = diagonal

    @pl.when(flags_ref[0] == 1)
    def _():
        row = lax.broadcasted_iota(jnp.int32, (size, size), 0)
        lane = lax.broadcasted_iota(jnp.int32, (size, size), 1)
        work[:, 0:size] = 0.5 * (diagonal + diagonal.T)
        work[:, size : 2 * size] = (row == lane).astype(F32)
        index = lax.broadcasted_iota(jnp.int32, (BLOCK, size), 0)
        for start in range(0, size, BLOCK):
            panel = work[start : start + BLOCK, 0:size]
            extra = work[start : start + BLOCK, size : 2 * size]
            columns = [
                jnp.broadcast_to(panel[:, start + step : start + step + 1], (BLOCK, size))
                for step in range(BLOCK)
            ]
            for step in range(BLOCK):
                scale = lax.rsqrt(columns[step][step : step + 1, :])
                column = jnp.where(index > step, columns[step] * scale, 0.0)
                for later in range(step + 1, BLOCK):
                    columns[later] = columns[later] - column * column[later : later + 1, :]
                pivot = panel[step : step + 1, :] * scale
                panel = jnp.where(index == step, pivot, panel - column * pivot)
                pivot = extra[step : step + 1, :] * scale
                extra = jnp.where(index == step, pivot, extra - column * pivot)
            work[start : start + BLOCK, 0:size] = panel
            work[start : start + BLOCK, size : 2 * size] = extra
            rest = start + BLOCK
            if rest < size:
                both = jnp.concatenate([panel, extra], axis=1)
                work[rest:size, :] -= exact_dot(panel[:, rest:size], both, TN)
        upper = jnp.where(row <= lane, work[:, 0:size], 0.0)
        inverse = jnp.where(row >= lane, work[:, size : 2 * size], 0.0).T
        high = inverse.astype(BF16)
        summary_ref[0:size] = high
        summary_ref[size : 2 * size] = (inverse - high.astype(F32)).astype(BF16)
        summary_ref[2 * size : 3 * size] = upper.T.astype(BF16)
        each = len(gal_refs) // groups
        for group in range(groups):

            @pl.when(flags_ref[1] == group)
            def _(chosen=gal_refs[group * each : (group + 1) * each]):
                total = chosen[0][...]
                for gal_ref in chosen[1:]:
                    total = total + gal_ref[...]
                sum_ref[...] = total


def factorize(flags, token, messages, groups):
    size = messages[0].shape[1]
    subs, funcs = groups[0][0].shape[0:2]
    parts = [part for group in groups for part in group]
    return pl.pallas_call(
        functools.partial(factor_kernel, parts=len(messages), groups=len(groups)),
        in_specs=[SMEM, ANY] + [VMEM] * (len(messages) + len(parts)),
        out_specs=[VMEM] * 3,
        out_shape=[
            jax.ShapeDtypeStruct((3 * size, size), BF16),
            jax.ShapeDtypeStruct((size, size), F32),
            jax.ShapeDtypeStruct(groups[0][0].shape, F32),
        ],
        scratch_shapes=[pltpu.VMEM((size, 2 * size), F32)],
        cost_estimate=LIGHT,
        name="factorize",
    )(flags, token, *messages, *parts)


def prepare_kernel(flags_ref, token_ref, head_ref, *rest, sources):
    summary_refs = rest[:sources]
    weights_ref, rows_ref, lower_ref, summary, sem = rest[sources:]
    size = head_ref.shape[0]
    choice, mode = flags_ref[0], flags_ref[1]
    for number, summary_ref in enumerate(summary_refs):

        @pl.when(choice == number)
        def _(summary_ref=summary_ref):
            copy = pltpu.make_async_copy(summary_ref, summary, sem)
            copy.start()
            copy.wait()

    def doubled(block):
        nothing = jnp.zeros((size, size), BF16)
        top = jnp.concatenate([block, nothing], axis=1)
        return jnp.concatenate([top, jnp.concatenate([nothing, block], axis=1)], axis=0)

    @pl.when(mode > 0)
    def _():
        weights_ref[0 : 2 * size] = doubled(summary[0:size])
        weights_ref[2 * size : 4 * size] = doubled(summary[size : 2 * size])
        lower_ref[...] = summary[2 * size : 3 * size]

    @pl.when(mode == 2)
    def _():
        inverse = summary[0:size].astype(F32) + summary[size : 2 * size].astype(F32)
        solved = exact_dot(head_ref[...], inverse)
        rows_ref[...] = doubled(solved.T.astype(BF16))


def prepare(flags, token, head, summaries):
    size = head.shape[0]
    return pl.pallas_call(
        functools.partial(prepare_kernel, sources=len(summaries)),
        in_specs=[SMEM, ANY, VMEM] + [ANY] * len(summaries),
        out_specs=[VMEM] * 3,
        out_shape=[
            jax.ShapeDtypeStruct((4 * size, 2 * size), BF16),
            jax.ShapeDtypeStruct((2 * size, 2 * size), BF16),
            jax.ShapeDtypeStruct((size, size), BF16),
        ],
        scratch_shapes=[pltpu.VMEM(summaries[0].shape, BF16), pltpu.SemaphoreType.DMA],
        compiler_params=pltpu.CompilerParams(vmem_limit_bytes=16 * 2**20),
        cost_estimate=LIGHT,
        name="prepare",
    )(flags, token, head, *summaries)


def added_kernel(flags_ref, token_ref, column_ids_ref, row_ids_ref, sum_ref, added_ref):
    @pl.when(flags_ref[0] == 1)
    def _():
        added_ref[...] = spread(sum_ref, column_ids_ref, row_ids_ref, added_ref.shape[0])


def added_of(flags, token, ids, galerkin, size):
    return pl.pallas_call(
        added_kernel,
        in_specs=[SMEM, ANY, VMEM, VMEM, VMEM],
        out_specs=VMEM,
        out_shape=jax.ShapeDtypeStruct((size, size), F32),
        cost_estimate=LIGHT,
        name="added",
    )(flags, token, ids[:, :, None], ids[:, None, :], galerkin)


def panel_kernel(
    flags_ref, token_ref, lower_ref, weights_ref, rows_ref, added_ref, slab_ref, *rest, pieces, spans, first
):
    hops = len(pieces) // len(spans)
    others = rest[: len(pieces)]
    out_ref, done_ref, column, factor, sems = rest[-5:]
    done_ref[0] = flags_ref[0]
    tile, size = out_ref.shape
    half = tile // 2
    mode, head, own, which = flags_ref[0], flags_ref[1], flags_ref[2], flags_ref[3]
    step, steps = pl.program_id(0), pl.num_programs(0)
    top = first & (step == 0)

    def copy_of(at, act):
        for number, (begin, end) in enumerate(spans):
            for hop in range(hops):

                @pl.when((mode == 2) & (which == hop) & (at >= begin) & (at < end))
                def _(other_ref=others[number * hops + hop], begin=begin):
                    source = other_ref.at[pl.ds(pl.multiple_of((at - begin) * tile, tile), tile)]
                    act(pltpu.make_async_copy(source, column.at[at % 2], sems.at[at % 2]))

    @pl.when(step == 0)
    def _():
        copy_of(step, lambda copy: copy.start())

    @pl.when(step + 1 < steps)
    def _():
        copy_of(step + 1, lambda copy: copy.start())

    @pl.when(mode == 0)
    def _():
        out_ref[...] = slab_ref[...]

    @pl.when(mode == 1)
    def _():
        column[step % 2] = slab_ref[...]

    @pl.when(mode == 2)
    def _():
        copy_of(step, lambda copy: copy.wait())

    @pl.when(mode > 0)
    def _():
        value = column[step % 2]
        pair = jnp.concatenate([value[0:half], value[half:tile]], axis=1)
        factor[...] = dot(jnp.concatenate([pair, pair], axis=1), weights_ref[...]).astype(BF16)

        @pl.when(top & (head == 1))
        def _():
            factor[0:size, 0:size] = lower_ref[...]

        @pl.when(top & (head == 2))
        def _():
            factor[0:size, 0:size] = jnp.zeros((size, size), BF16)

    @pl.when(mode == 1)
    def _():
        out_ref[0:half] = factor[:, 0:size]
        out_ref[half:tile] = factor[:, size : 2 * size]

    @pl.when(mode == 2)
    def _():
        update = dot(factor[...], rows_ref[...])
        out_ref[0:half] = (slab_ref[0:half].astype(F32) - update[:, 0:size]).astype(BF16)
        out_ref[half:tile] = (slab_ref[half:tile].astype(F32) - update[:, size : 2 * size]).astype(BF16)

        @pl.when(top & (own == 1))
        def _():
            base = slab_ref[0:size].astype(F32) + added_ref[...]
            out_ref[0:size] = (base - update[0:size, 0:size]).astype(BF16)


def panel(flags, token, lower, weights, rows, added, slab, parts, old, start, tile):
    size = slab.shape[1]
    offset = start // tile
    spans, begin, operands = [], 0, []
    for hops in parts:
        end = begin + hops[0].shape[0] // tile
        spans.append((begin, end))
        begin = end
        operands += hops
    blocks = [
        SMEM,
        ANY,
        pl.BlockSpec((size, size), lambda i: (0, 0)),
        pl.BlockSpec(weights.shape, lambda i: (0, 0)),
        pl.BlockSpec(rows.shape, lambda i: (0, 0)),
        pl.BlockSpec((size, size), lambda i: (0, 0)),
        pl.BlockSpec((tile, size), lambda i: (i + offset, 0)),
    ] + [ANY] * len(operands)
    pieces = len(operands)
    operands = [flags, token, lower, weights, rows, added, slab] + operands
    aliases = {}
    if old is not None:
        aliases = {len(operands): 0}
        blocks.append(ANY)
        operands.append(old)
    return pl.pallas_call(
        functools.partial(panel_kernel, pieces=range(pieces), spans=spans, first=start == 0),
        grid=(begin,),
        in_specs=blocks,
        out_specs=[pl.BlockSpec((tile, size), lambda i: (i + offset, 0)), SMEM],
        out_shape=[jax.ShapeDtypeStruct(slab.shape, BF16), jax.ShapeDtypeStruct((1,), jnp.int32)],
        input_output_aliases=aliases,
        scratch_shapes=[
            pltpu.VMEM((2, tile, size), BF16),
            pltpu.VMEM((tile // 2, 2 * size), BF16),
            pltpu.SemaphoreType.DMA((2,)),
        ],
        compiler_params=pltpu.CompilerParams(vmem_limit_bytes=16 * 2**20),
        cost_estimate=LIGHT,
        name="panel",
    )(*operands)


def broadcast(value, axis, source):
    kept = jnp.where(lax.axis_index(axis) == source, value, 0).astype(value.dtype)
    return lax.psum(kept, axis)


def settings(*values):
    return jnp.stack([jnp.asarray(value).astype(jnp.int32) for value in values])


def holder_pairs(wide, narrow, distance):
    stride = wide // narrow
    found = []
    for n in range(narrow):
        for start in range(0, wide, 2 * distance):
            source = (n * stride) ^ start
            found.append((source * narrow + n, (source ^ distance) * narrow + n))
    return found


class Order:
    def __init__(self, token):
        self.token = token

    def after(self, value):
        value, self.token = lax.optimization_barrier((value, self.token))
        return value


def known_owner(owner, coarse_basis, material_ids, lame_table, coarse_ids, coarse_slab):
    narrow, wide = lax.axis_size("narrow"), lax.axis_size("wide")
    stride = wide // narrow
    wide_index, narrow_index = lax.axis_index("wide"), lax.axis_index("narrow")
    height, block = coarse_slab.shape
    own = wide_index == narrow_index * stride
    later = narrow_index > owner
    which = jnp.where(later, narrow_index - owner - 1, -1)
    mode = jnp.where(narrow_index == owner, 1, jnp.where(later, 2, 0))
    earlier = (wide_index % stride == 0) & (wide_index // stride < owner)
    kind = jnp.where(wide_index == owner * stride, 1, jnp.where(earlier, 2, 0))
    table = lame_table.astype(F32)
    hops = narrow - 1 - owner
    units, joined, waits, plan = PLANS[hops]
    unit = height // sum(units)
    count = len(units)
    bounds, low = [], 0
    for number in units:
        bounds.append((low, low + number * unit))
        low += number * unit
    axes = ("wide", "narrow")

    def rows_of(number):
        low, high = bounds[number]
        return coarse_slab[low:high]

    def send(value, source, target):
        return lax.ppermute(value, "narrow", [(owner + source, owner + target)])

    order = Order(settings(mode))

    holders = [((n * stride) * narrow + owner, (n * stride) * narrow + n) for n in range(owner + 1, narrow)]
    moved = {}

    groups = [[w for w in range(wide) if w % stride == 0], [w for w in range(wide) if w % stride]]
    groups = [group for group in groups if group]
    member = jnp.where(wide_index % stride == 0, 0, 1)

    def within(group, pairs):
        return [(w * narrow + one, w * narrow + two) for w in group for one, two in pairs]

    def halo_of(group, message):
        return lax.ppermute(message, axes, within(group, [(i + 1, i) for i in range(narrow - 1)]))

    spans = [bounds[0], (bounds[1][0], height) if joined else bounds[1]]
    first, last, *begun = halo_message(table, material_ids, order.token, coarse_basis, coarse_slab, spans)
    first = order.after(first)
    halos = [halo_of(groups[0], first)]
    edge = (narrow_index == 0).astype(jnp.int32).reshape(1)
    inner = order.after(interior(edge, table, material_ids, coarse_basis, order.token))
    head = order.after(lax.ppermute(order.after(coarse_slab[:block]), axes, holders))
    halos[0] = order.after(halos[0])
    moved[0] = [send(order.after(begun[0]), 0, hops)]
    for group in groups[1:]:
        halos.append(halo_of(group, order.after(first)))

    def nearest(base, extent):
        return min(range(base, min(base + extent, narrow)), key=lambda n: abs(n - owner))

    def summed(parts, distance, group):
        total = parts[0] if len(parts) == 1 else parts[0] + parts[1]
        pairs = []
        for base in range(0, narrow - distance, 2 * distance):
            one, two = nearest(base, distance), nearest(base + distance, distance)
            pairs.append((two, one) if nearest(base, 2 * distance) == one else (one, two))
        return [total, lax.ppermute(total, axes, within(group, pairs))], 2 * distance

    def faces_of(number):
        flag = settings(member == number)
        return [order.after(face(flag, table, material_ids, last, halos[number], order.token, inner))]

    sums, reach = [faces_of(0)], [1]
    while reach[0] < narrow:
        sums[0], reach[0] = summed(sums[0], reach[0], groups[0])
    sums[0][1] = order.after(sums[0][1])
    distance, messages, left = wide // 2, [], plan.count("spread")
    result, prepared = None, None
    choice = (narrow_index - owner) % narrow
    flags = settings(mode, kind, own, which)
    for step in plan:
        if step[0] == "panel":
            if prepared is None:
                prepared = prepare(settings(choice, mode), order.token, head, summaries)
            weights, rows, lower = prepared
            begin, end = step[1:]
            parts = [moved[number][:: 1 if number else -1] for number in range(begin, end)]
            result, order.token = panel(
                flags, order.token, lower, weights, rows, added if begin == 0 else head, coarse_slab, parts, result, bounds[begin][0], 2 * unit
            )
        elif step == "added":
            added = added_of(settings(mode), order.token, coarse_ids, galerkin, block)
            added = order.after(lax.ppermute(added, axes, holders))
            if waits:
                moved[count - 1] = [send(order.after(rows_of(count - 1)), 0, 1)]
        elif step == "sums":
            galerkins = [order.after(part) for part in galerkins]
            galerkin = jnp.where(narrow_index == owner, galerkin, sum(galerkins))
        elif step == "next":
            if joined:
                whole = send(order.after(begun[1]), 0, 1)
            else:
                moved[1] = [send(order.after(begun[1]), 0, 1)]
                for number in range(2, count - waits):
                    moved[number] = [send(order.after(rows_of(number)), 0, 1)]
        elif step == "assemble":
            message = assemble(settings(mode, own), order.token, coarse_ids, coarse_slab, head, sums[0])
            message = order.after(message)
        elif step == "others":
            for number in range(1, len(groups)):
                halos[number] = order.after(halos[number])
                parts, far = summed(faces_of(number), 1, groups[number])
                sums.append(parts)
                reach.append(far)
        elif step == "more":
            for number in range(1, len(groups)):
                while reach[number] < narrow:
                    sums[number][1] = order.after(sums[number][1])
                    sums[number], reach[number] = summed(sums[number], reach[number], groups[number])
        elif step == "spread":
            left -= 1
            while distance:
                received = order.after(lax.ppermute(message, axes, holder_pairs(wide, narrow, distance)))
                messages = [message, received]
                if distance > 1:
                    message = message + received
                distance //= 2
                if left:
                    break
        elif step == "factor":
            summary, head, galerkin = factorize(settings(mode, member), order.token, messages, sums)
            summary = order.after(summary)
            ways = [[(owner, (owner + place) % narrow)] for place in range(1, narrow)]
            summaries = [summary] + [lax.ppermute(summary, "narrow", way) for way in ways]
        elif step == "summary":
            for place in range(1, narrow):
                summaries[place] = order.after(summaries[place])
            galerkin = order.after(galerkin)
            galerkins = [lax.ppermute(galerkin, "narrow", way) for way in ways]
        else:
            number, hop = step
            if joined and step == (1, 0):
                whole = order.after(whole)
                for part in range(1, count):
                    low, high = (bound - bounds[1][0] for bound in bounds[part])
                    moved[part] = [whole[low:high]]
            moving = moved[number][hop] = order.after(moved[number][hop])
            if number == 0 and hop + 1 < hops:
                moved[number].append(send(moving, hops - hop, hops - hop - 1))
            elif number != 0 and hop + 1 < hops:
                moved[number].append(send(moving, hop + 1, hop + 2))
    return result, galerkin


def any_owner(owner, coarse_basis, material_ids, lame_table, coarse_ids, coarse_slab):
    narrow, wide = lax.axis_size("narrow"), lax.axis_size("wide")
    stride = wide // narrow
    wide_index, narrow_index = lax.axis_index("wide"), lax.axis_index("narrow")
    own = wide_index == narrow_index * stride
    later = narrow_index > owner
    which = jnp.where(later, 0, -1)
    mode = jnp.where(narrow_index == owner, 1, jnp.where(later, 2, 0))
    earlier = (wide_index % stride == 0) & (wide_index // stride < owner)
    kind = jnp.where(wide_index == owner * stride, 1, jnp.where(earlier, 2, 0))
    table = lame_table.astype(F32)
    column = broadcast(coarse_slab, "narrow", owner)
    first, last = halo_message(table, material_ids, table, coarse_basis, coarse_slab, ())
    halo = lax.ppermute(first, "narrow", [(i + 1, i) for i in range(narrow - 1)])
    edge = (narrow_index == 0).astype(jnp.int32).reshape(1)
    inner = interior(edge, table, material_ids, coarse_basis, first)
    partial = face(settings(1), table, material_ids, last, halo, first, inner)
    parts = [lax.psum(partial, "narrow")]
    message = assemble(settings(mode, own), first, coarse_ids, coarse_slab, column, parts)
    at_owner = (wide_index == owner * stride) & (narrow_index == owner)
    diagonal = lax.psum(jnp.where(at_owner, message, 0.0), ("wide", "narrow"))
    summary, _, galerkin = factorize(settings(1, 0), first, [diagonal], [parts])
    head = broadcast(message, "wide", narrow_index * stride)
    weights, rows, lower = prepare(settings(0, mode), settings(mode), head, [summary])
    added = added_of(settings(1), weights, coarse_ids, galerkin, head.shape[0])
    flags = settings(mode, kind, own, which)
    tile = coarse_slab.shape[0] // 12
    result, _ = panel(flags, flags, lower, weights, rows, added, coarse_slab, [[column]], None, 0, tile)
    return result, galerkin


def on_device(coarse_basis, material_ids, lame_table, coarse_ids, coarse_slab, panel_owner):
    narrow, wide = lax.axis_size("narrow"), lax.axis_size("wide")
    arrays = (coarse_basis, material_ids, lame_table, coarse_ids, coarse_slab)
    owner = panel_owner[0]
    if narrow - 1 > len(PLANS) or wide & (wide - 1):
        return any_owner(owner, *arrays)
    branches = [functools.partial(known_owner, place) for place in range(narrow - 1)]
    return lax.switch(owner, branches, *arrays)


def solution(mesh):
    return jax.shard_map(
        on_device,
        mesh=mesh,
        in_specs=(
            P("wide", None, None, "narrow", None, None),
            P("wide", "narrow", None, None),
            P(),
            P("wide", None),
            P("wide", "narrow"),
            P(),
        ),
        out_specs=(P("wide", "narrow"), P("wide", None, None)),
        check_vma=False,
    )
```

```python
import functools

import jax
import jax.numpy as jnp
from jax import lax
from jax.experimental import pallas as pl
from jax.experimental.pallas import tpu as pltpu
from jax.sharding import PartitionSpec as P

F32, BF16 = jnp.float32, jnp.bfloat16
NT = (((1,), (1,)), ((), ()))
TN = (((0,), (0,)), ((), ()))
VMEM = pl.BlockSpec(memory_space=pltpu.VMEM)
ANY = pl.BlockSpec(memory_space=pl.ANY)
SMEM = pl.BlockSpec(memory_space=pltpu.SMEM)
PLANS = {
    1: (
        (12, 8, 4),
        False,
        True,
        (
            "assemble", "next", "spread", "others", "spread", "more", "spread", (0, 0), "factor", "summary",
            "added", ("panel", 0, 2), "sums", ("panel", 2, 3),
        ),
    ),
    2: (
        (12, 6, 4, 2),
        False,
        True,
        (
            "assemble", "next", "spread", "others", "spread", "more", "spread", (0, 0), (1, 0), "factor", (2, 0),
            "summary", "added", ("panel", 1, 2), (3, 0), ("panel", 0, 1), "sums", ("panel", 2, 4),
        ),
    ),
    3: (
        (12, 8, 4),
        False,
        False,
        (
            "assemble", "next", "spread", "others", "spread", "more", "spread", (0, 0), (1, 0), "factor", (0, 1),
            (2, 0), (1, 1), "summary", (2, 1), ("panel", 1, 2), "added", ("panel", 0, 1), "sums", ("panel", 2, 3),
        ),
    ),
}
BLOCK = 16
LIGHT = pl.CostEstimate(flops=1, bytes_accessed=1, transcendentals=0)


def exact_dot(left, right, dims=(((1,), (0,)), ((), ()))):
    return lax.dot_general(
        left, right, dims, precision=lax.Precision.HIGHEST, preferred_element_type=F32
    )


def dot(left, right, dims=(((1,), (0,)), ((), ()))):
    return lax.dot_general(left, right, dims, preferred_element_type=F32)


def split_two(value):
    high = value.astype(BF16)
    return high, (value - high.astype(F32)).astype(BF16)


def lame_of(ids, table_ref):
    shear = jnp.zeros(ids.shape, F32)
    dilate = jnp.zeros(ids.shape, F32)
    for material in range(table_ref.shape[1]):
        chosen = ids == material
        shear = jnp.where(chosen, table_ref[0, material], shear)
        dilate = jnp.where(chosen, table_ref[1, material], dilate)
    return shear, dilate


def halo_kernel(table_ref, ids_ref, token_ref, basis_ref, slab_ref, out_ref, last_ref, *rest, spans):
    piece_refs, sems = rest[:-1], rest[-1]
    subs, funcs, comps, layers = basis_ref.shape[0:4]
    copies = []
    for number, ((low, high), piece_ref) in enumerate(zip(spans, piece_refs)):
        copies.append(pltpu.make_async_copy(slab_ref.at[pl.ds(low, high - low)], piece_ref, sems.at[number]))
        copies[-1].start()
    for sub in range(subs):
        for comp in range(comps):
            out_ref[sub, comp * funcs : (comp + 1) * funcs] = basis_ref[sub, :, comp, 0]
            last_ref[sub, comp * funcs : (comp + 1) * funcs] = basis_ref[sub, :, comp, layers - 1]
        shear, dilate = lame_of(ids_ref[sub, 0], table_ref)
        out_ref[sub, comps * funcs] = shear.astype(BF16)
        out_ref[sub, comps * funcs + 1] = dilate.astype(BF16)
    for copy in copies:
        copy.wait()


def halo_message(table, ids, token, basis, slab, spans):
    subs, funcs, comps, layers, ny, nz = basis.shape
    return pl.pallas_call(
        functools.partial(halo_kernel, spans=spans),
        in_specs=[SMEM, VMEM, ANY, VMEM, ANY],
        out_specs=[VMEM] * (2 + len(spans)),
        out_shape=[
            jax.ShapeDtypeStruct((subs, comps * funcs + 2, ny, nz), BF16),
            jax.ShapeDtypeStruct((subs, comps * funcs, ny, nz), BF16),
        ]
        + [jax.ShapeDtypeStruct((high - low, slab.shape[1]), BF16) for low, high in spans],
        scratch_shapes=[pltpu.SemaphoreType.DMA((max(1, len(spans)),))],
        compiler_params=pltpu.CompilerParams(vmem_limit_bytes=16 * 2**20),
        cost_estimate=LIGHT,
        name="halo_message",
    )(table, ids, token, basis, slab)


def interior_kernel(edge_ref, table_ref, ids_ref, basis_ref, token_ref, out_ref, fields, turned, coef, left, right, acc):
    sub, comp = pl.program_id(0), pl.program_id(1)
    layers, ny, nz = basis_ref.shape[3:]
    funcs = basis_ref.shape[1]
    row = lax.broadcasted_iota(jnp.int32, (ny, nz), 0)
    lane = lax.broadcasted_iota(jnp.int32, (ny, nz), 1)
    table = [lame_of(ids_ref[sub, x], table_ref) for x in range(layers)]

    def weight(one, two, direction):
        shear = 0.5 * (one[0] + two[0])
        dilate = 0.5 * (one[1] + two[1])
        return shear + jnp.where(comp == direction, shear + dilate, 0.0)

    def ahead(field, axis):
        size = field.shape[axis]
        index = row if axis == 0 else lane
        return jnp.where(index == size - 1, 0.0, pltpu.roll(field, size - 1, axis=axis))

    def behind(field, axis):
        index = row if axis == 0 else lane
        return jnp.where(index == 0, 0.0, pltpu.roll(field, 1, axis=axis))

    nothing = (jnp.zeros((ny, nz), F32),) * 2
    previous = weight(table[0], nothing, 0) * edge_ref[0].astype(F32)
    for x in range(layers):
        diagonal = previous
        forward = []
        if x + 1 < layers:
            face = weight(table[x], table[x + 1], 0)
            diagonal = diagonal + face
            previous = face
            forward.append(face)
        else:
            forward.append(jnp.zeros((ny, nz), F32))
        for axis in (0, 1):
            index, size = (row, ny) if axis == 0 else (lane, nz)
            other = tuple(ahead(value, axis) for value in table[x])
            face = weight(table[x], other, axis + 1)
            before = tuple(behind(value, axis) for value in table[x])
            diagonal = diagonal + face + weight(table[x], before, axis + 1)
            forward.append(jnp.where(index == size - 1, 0.0, face))
        coef[x, 0] = 0.5 * diagonal
        for kind in range(3):
            coef[x, kind + 1] = forward[kind]
        fields[x] = basis_ref[sub, :, comp, x].astype(F32).reshape(funcs * ny, nz)

    total = None
    for x in reversed(range(layers)):
        values = [fields[x, pl.ds(y, funcs, stride=ny), :] for y in range(ny)]
        for y in range(ny):
            value = values[y]
            turned[x % 2, y] = value
            image = coef[x, 0, y : y + 1, :] * value
            image = image - coef[x, 3, y : y + 1, :] * pltpu.roll(value, nz - 1, axis=1)
            if y + 1 < ny:
                image = image - coef[x, 2, y : y + 1, :] * values[y + 1]
            if x + 1 < layers:
                image = image - coef[x, 1, y : y + 1, :] * turned[(x + 1) % 2, y]
            high, low = split_two(image)
            left[:, y * nz : (y + 1) * nz] = value.astype(BF16)
            right[0:funcs, y * nz : (y + 1) * nz] = high
            right[funcs : 2 * funcs, y * nz : (y + 1) * nz] = low
        product = dot(right[...], left[...], NT)
        total = product if total is None else total + product

    @pl.when(comp == 0)
    def _():
        acc[...] = total

    @pl.when(comp > 0)
    def _():
        acc[...] += total

    @pl.when(comp == pl.num_programs(1) - 1)
    def _():
        out_ref[0] = acc[0:funcs] + acc[funcs : 2 * funcs]


def interior(edge, table, ids, basis, token):
    subs, funcs, comps, layers, ny, nz = basis.shape
    return pl.pallas_call(
        interior_kernel,
        grid=(subs, comps),
        in_specs=[SMEM, SMEM, VMEM, VMEM, ANY],
        out_specs=pl.BlockSpec((1, funcs, funcs), lambda s, c: (s, 0, 0)),
        out_shape=jax.ShapeDtypeStruct((subs, funcs, funcs), F32),
        scratch_shapes=[
            pltpu.VMEM((layers, funcs * ny, nz), F32),
            pltpu.VMEM((2, ny, funcs, nz), F32),
            pltpu.VMEM((layers, 4, ny, nz), F32),
            pltpu.VMEM((funcs, ny * nz), BF16),
            pltpu.VMEM((2 * funcs, ny * nz), BF16),
            pltpu.VMEM((2 * funcs, funcs), F32),
        ],
        compiler_params=pltpu.CompilerParams(vmem_limit_bytes=16 * 2**20),
        cost_estimate=LIGHT,
        name="interior",
    )(edge, table, ids, basis, token)


def face_kernel(flags_ref, table_ref, ids_ref, last_ref, halo_ref, token_ref, inner_ref, out_ref, *scratch):
    @pl.when(flags_ref[0] == 1)
    def _():
        last, halo, sems = scratch[-3:]
        copies = [
            pltpu.make_async_copy(last_ref, last, sems.at[0]),
            pltpu.make_async_copy(halo_ref, halo, sems.at[1]),
        ]
        for copy in copies:
            copy.start()
        for copy in copies:
            copy.wait()
        face_sums(table_ref, ids_ref, last, halo, inner_ref, out_ref, *scratch[:-3])


def face_sums(table_ref, ids_ref, last_ref, halo_ref, inner_ref, out_ref, mine, theirs, left, right, weights, acc):
    subs, layers, ny, nz = ids_ref.shape
    funcs = inner_ref.shape[1]
    comps = last_ref.shape[1] // funcs

    @pl.loop(0, subs)
    def _(sub):
        shear, dilate = lame_of(ids_ref[sub, layers - 1], table_ref)
        weights[0] = 0.5 * (shear + halo_ref[sub, comps * funcs].astype(F32))
        weights[1] = 0.5 * (dilate + halo_ref[sub, comps * funcs + 1].astype(F32))

        @pl.loop(0, comps)
        def _(comp):
            weight = weights[0] + jnp.where(comp == 0, weights[0] + weights[1], 0.0)
            rows = pl.ds(comp * funcs, funcs)
            mine[...] = last_ref[sub, rows].astype(F32).reshape(funcs * ny, nz)
            theirs[...] = halo_ref[sub, rows].astype(F32).reshape(funcs * ny, nz)
            for y in range(ny):
                here = mine[pl.ds(y, funcs, stride=ny), :]
                there = theirs[pl.ds(y, funcs, stride=ny), :]
                high, low = split_two(weight[y : y + 1, :] * (here - there))
                left[0:funcs, y * nz : (y + 1) * nz] = here.astype(BF16)
                left[funcs : 2 * funcs, y * nz : (y + 1) * nz] = there.astype(BF16)
                right[0:funcs, y * nz : (y + 1) * nz] = high
                right[funcs : 2 * funcs, y * nz : (y + 1) * nz] = low
            product = dot(right[...], left[...], NT)

            @pl.when(comp == 0)
            def _():
                acc[...] = product

            @pl.when(comp > 0)
            def _():
                acc[...] += product

        total = acc[:, 0:funcs] - acc[:, funcs : 2 * funcs]
        half = inner_ref[sub] + 0.5 * (total[0:funcs] + total[funcs : 2 * funcs])
        out_ref[sub] = half + half.T


def face(flags, table, ids, last, halo, token, inner):
    subs, layers, ny, nz = ids.shape
    funcs = inner.shape[1]
    return pl.pallas_call(
        face_kernel,
        in_specs=[SMEM, SMEM, VMEM, ANY, ANY, ANY, VMEM],
        out_specs=VMEM,
        out_shape=jax.ShapeDtypeStruct((subs, funcs, funcs), F32),
        scratch_shapes=[
            pltpu.VMEM((funcs * ny, nz), F32),
            pltpu.VMEM((funcs * ny, nz), F32),
            pltpu.VMEM((2 * funcs, ny * nz), BF16),
            pltpu.VMEM((2 * funcs, ny * nz), BF16),
            pltpu.VMEM((2, ny, nz), F32),
            pltpu.VMEM((2 * funcs, 2 * funcs), F32),
            pltpu.VMEM(last.shape, BF16),
            pltpu.VMEM(halo.shape, BF16),
            pltpu.SemaphoreType.DMA((2,)),
        ],
        compiler_params=pltpu.CompilerParams(vmem_limit_bytes=16 * 2**20),
        cost_estimate=LIGHT,
        name="face",
    )(flags, table, ids, last, halo, token, inner)


def spread(gal_ref, column_ids_ref, row_ids_ref, size):
    subs, funcs = column_ids_ref.shape[0:2]
    added = jnp.zeros((size, size), F32)
    lane = lax.broadcasted_iota(jnp.int32, (funcs, size), 1)
    row = lax.broadcasted_iota(jnp.int32, (size, funcs), 0)
    for sub in range(subs):
        slots = (column_ids_ref[sub] == lane).astype(F32)
        slots_t = (row_ids_ref[sub] == row).astype(F32)
        added = added + exact_dot(slots_t, exact_dot(gal_ref[sub], slots))
    return added


def assemble_kernel(flags_ref, token_ref, column_ids_ref, row_ids_ref, slab_ref, head_ref, *rest):
    gal_refs, (message_ref, sum_ref) = rest[:-2], rest[-2:]
    size = message_ref.shape[0]
    mode, own = flags_ref[0], flags_ref[1]
    message_ref[...] = jnp.zeros_like(message_ref)

    @pl.when((mode == 1) & (own == 1))
    def _():
        total = gal_refs[0][...]
        for gal_ref in gal_refs[1:]:
            total = total + gal_ref[...]
        sum_ref[...] = total
        added = spread(sum_ref, column_ids_ref, row_ids_ref, size)
        message_ref[...] = added + slab_ref[...].astype(F32)

    @pl.when((mode == 2) & (own == 1))
    def _():
        message_ref[...] = head_ref[...].astype(F32)


def assemble(flags, token, ids, slab, head, parts):
    size = slab.shape[1]
    block = pl.BlockSpec((size, size), lambda i: (0, 0))
    return pl.pallas_call(
        assemble_kernel,
        grid=(1,),
        in_specs=[SMEM, ANY, VMEM, VMEM, block, block] + [VMEM] * len(parts),
        out_specs=VMEM,
        out_shape=jax.ShapeDtypeStruct((size, size), F32),
        scratch_shapes=[pltpu.VMEM(parts[0].shape, F32)],
        cost_estimate=LIGHT,
        name="assemble",
    )(flags, token, ids[:, :, None], ids[:, None, :], slab, head, *parts)


def factor_kernel(flags_ref, token_ref, *refs, parts, groups):
    message_refs, gal_refs = refs[:parts], refs[parts:-4]
    summary_ref, block_ref, sum_ref, work = refs[-4:]
    subs, funcs = gal_refs[0].shape[0:2]
    size = summary_ref.shape[1]
    diagonal = message_refs[0][...]
    for message_ref in message_refs[1:]:
        diagonal = diagonal + message_ref[...]
    block_ref[...] = diagonal

    @pl.when(flags_ref[0] == 1)
    def _():
        row = lax.broadcasted_iota(jnp.int32, (size, size), 0)
        lane = lax.broadcasted_iota(jnp.int32, (size, size), 1)
        work[:, 0:size] = 0.5 * (diagonal + diagonal.T)
        work[:, size : 2 * size] = (row == lane).astype(F32)
        index = lax.broadcasted_iota(jnp.int32, (BLOCK, size), 0)
        for start in range(0, size, BLOCK):
            panel = work[start : start + BLOCK, 0:size]
            extra = work[start : start + BLOCK, size : 2 * size]
            columns = [
                jnp.broadcast_to(panel[:, start + step : start + step + 1], (BLOCK, size))
                for step in range(BLOCK)
            ]
            for step in range(BLOCK):
                scale = lax.rsqrt(columns[step][step : step + 1, :])
                column = jnp.where(index > step, columns[step] * scale, 0.0)
                for later in range(step + 1, BLOCK):
                    columns[later] = columns[later] - column * column[later : later + 1, :]
                pivot = panel[step : step + 1, :] * scale
                panel = jnp.where(index == step, pivot, panel - column * pivot)
                pivot = extra[step : step + 1, :] * scale
                extra = jnp.where(index == step, pivot, extra - column * pivot)
            work[start : start + BLOCK, 0:size] = panel
            work[start : start + BLOCK, size : 2 * size] = extra
            rest = start + BLOCK
            if rest < size:
                both = jnp.concatenate([panel, extra], axis=1)
                work[rest:size, :] -= exact_dot(panel[:, rest:size], both, TN)
        upper = jnp.where(row <= lane, work[:, 0:size], 0.0)
        inverse = jnp.where(row >= lane, work[:, size : 2 * size], 0.0).T
        high = inverse.astype(BF16)
        summary_ref[0:size] = high
        summary_ref[size : 2 * size] = (inverse - high.astype(F32)).astype(BF16)
        summary_ref[2 * size : 3 * size] = upper.T.astype(BF16)
        each = len(gal_refs) // groups
        for group in range(groups):

            @pl.when(flags_ref[1] == group)
            def _(chosen=gal_refs[group * each : (group + 1) * each]):
                total = chosen[0][...]
                for gal_ref in chosen[1:]:
                    total = total + gal_ref[...]
                sum_ref[...] = total


def factorize(flags, token, messages, groups):
    size = messages[0].shape[1]
    subs, funcs = groups[0][0].shape[0:2]
    parts = [part for group in groups for part in group]
    return pl.pallas_call(
        functools.partial(factor_kernel, parts=len(messages), groups=len(groups)),
        in_specs=[SMEM, ANY] + [VMEM] * (len(messages) + len(parts)),
        out_specs=[VMEM] * 3,
        out_shape=[
            jax.ShapeDtypeStruct((3 * size, size), BF16),
            jax.ShapeDtypeStruct((size, size), F32),
            jax.ShapeDtypeStruct(groups[0][0].shape, F32),
        ],
        scratch_shapes=[pltpu.VMEM((size, 2 * size), F32)],
        cost_estimate=LIGHT,
        name="factorize",
    )(flags, token, *messages, *parts)


def prepare_kernel(flags_ref, token_ref, head_ref, *rest, sources):
    summary_refs = rest[:sources]
    weights_ref, rows_ref, lower_ref, summary, sem = rest[sources:]
    size = head_ref.shape[0]
    choice, mode = flags_ref[0], flags_ref[1]
    for number, summary_ref in enumerate(summary_refs):

        @pl.when(choice == number)
        def _(summary_ref=summary_ref):
            copy = pltpu.make_async_copy(summary_ref, summary, sem)
            copy.start()
            copy.wait()

    def doubled(block):
        nothing = jnp.zeros((size, size), BF16)
        top = jnp.concatenate([block, nothing], axis=1)
        return jnp.concatenate([top, jnp.concatenate([nothing, block], axis=1)], axis=0)

    @pl.when(mode > 0)
    def _():
        weights_ref[0 : 2 * size] = doubled(summary[0:size])
        weights_ref[2 * size : 4 * size] = doubled(summary[size : 2 * size])
        lower_ref[...] = summary[2 * size : 3 * size]

    @pl.when(mode == 2)
    def _():
        inverse = summary[0:size].astype(F32) + summary[size : 2 * size].astype(F32)
        solved = exact_dot(head_ref[...], inverse)
        rows_ref[...] = doubled(solved.T.astype(BF16))


def prepare(flags, token, head, summaries):
    size = head.shape[0]
    return pl.pallas_call(
        functools.partial(prepare_kernel, sources=len(summaries)),
        in_specs=[SMEM, ANY, VMEM] + [ANY] * len(summaries),
        out_specs=[VMEM] * 3,
        out_shape=[
            jax.ShapeDtypeStruct((4 * size, 2 * size), BF16),
            jax.ShapeDtypeStruct((2 * size, 2 * size), BF16),
            jax.ShapeDtypeStruct((size, size), BF16),
        ],
        scratch_shapes=[pltpu.VMEM(summaries[0].shape, BF16), pltpu.SemaphoreType.DMA],
        compiler_params=pltpu.CompilerParams(vmem_limit_bytes=16 * 2**20),
        cost_estimate=LIGHT,
        name="prepare",
    )(flags, token, head, *summaries)


def added_kernel(flags_ref, token_ref, column_ids_ref, row_ids_ref, sum_ref, added_ref):
    @pl.when(flags_ref[0] == 1)
    def _():
        added_ref[...] = spread(sum_ref, column_ids_ref, row_ids_ref, added_ref.shape[0])


def added_of(flags, token, ids, galerkin, size):
    return pl.pallas_call(
        added_kernel,
        in_specs=[SMEM, ANY, VMEM, VMEM, VMEM],
        out_specs=VMEM,
        out_shape=jax.ShapeDtypeStruct((size, size), F32),
        cost_estimate=LIGHT,
        name="added",
    )(flags, token, ids[:, :, None], ids[:, None, :], galerkin)


def panel_kernel(
    flags_ref, token_ref, lower_ref, weights_ref, rows_ref, added_ref, slab_ref, *rest, pieces, spans, first
):
    hops = len(pieces) // len(spans)
    others = rest[: len(pieces)]
    out_ref, done_ref, column, factor, sems = rest[-5:]
    done_ref[0] = flags_ref[0]
    tile, size = out_ref.shape
    half = tile // 2
    mode, head, own, which = flags_ref[0], flags_ref[1], flags_ref[2], flags_ref[3]
    step, steps = pl.program_id(0), pl.num_programs(0)
    top = first & (step == 0)

    def copy_of(at, act):
        for number, (begin, end) in enumerate(spans):
            for hop in range(hops):

                @pl.when((mode == 2) & (which == hop) & (at >= begin) & (at < end))
                def _(other_ref=others[number * hops + hop], begin=begin):
                    source = other_ref.at[pl.ds(pl.multiple_of((at - begin) * tile, tile), tile)]
                    act(pltpu.make_async_copy(source, column.at[at % 2], sems.at[at % 2]))

    @pl.when(step == 0)
    def _():
        copy_of(step, lambda copy: copy.start())

    @pl.when(step + 1 < steps)
    def _():
        copy_of(step + 1, lambda copy: copy.start())

    @pl.when(mode == 0)
    def _():
        out_ref[...] = slab_ref[...]

    @pl.when(mode == 1)
    def _():
        column[step % 2] = slab_ref[...]

    @pl.when(mode == 2)
    def _():
        copy_of(step, lambda copy: copy.wait())

    @pl.when(mode > 0)
    def _():
        value = column[step % 2]
        pair = jnp.concatenate([value[0:half], value[half:tile]], axis=1)
        factor[...] = dot(jnp.concatenate([pair, pair], axis=1), weights_ref[...]).astype(BF16)

        @pl.when(top & (head == 1))
        def _():
            factor[0:size, 0:size] = lower_ref[...]

        @pl.when(top & (head == 2))
        def _():
            factor[0:size, 0:size] = jnp.zeros((size, size), BF16)

    @pl.when(mode == 1)
    def _():
        out_ref[0:half] = factor[:, 0:size]
        out_ref[half:tile] = factor[:, size : 2 * size]

    @pl.when(mode == 2)
    def _():
        update = dot(factor[...], rows_ref[...])
        out_ref[0:half] = (slab_ref[0:half].astype(F32) - update[:, 0:size]).astype(BF16)
        out_ref[half:tile] = (slab_ref[half:tile].astype(F32) - update[:, size : 2 * size]).astype(BF16)

        @pl.when(top & (own == 1))
        def _():
            base = slab_ref[0:size].astype(F32) + added_ref[...]
            out_ref[0:size] = (base - update[0:size, 0:size]).astype(BF16)


def panel(flags, token, lower, weights, rows, added, slab, parts, old, start, tile):
    size = slab.shape[1]
    offset = start // tile
    spans, begin, operands = [], 0, []
    for hops in parts:
        end = begin + hops[0].shape[0] // tile
        spans.append((begin, end))
        begin = end
        operands += hops
    blocks = [
        SMEM,
        ANY,
        pl.BlockSpec((size, size), lambda i: (0, 0)),
        pl.BlockSpec(weights.shape, lambda i: (0, 0)),
        pl.BlockSpec(rows.shape, lambda i: (0, 0)),
        pl.BlockSpec((size, size), lambda i: (0, 0)),
        pl.BlockSpec((tile, size), lambda i: (i + offset, 0)),
    ] + [ANY] * len(operands)
    pieces = len(operands)
    operands = [flags, token, lower, weights, rows, added, slab] + operands
    aliases = {}
    if old is not None:
        aliases = {len(operands): 0}
        blocks.append(ANY)
        operands.append(old)
    return pl.pallas_call(
        functools.partial(panel_kernel, pieces=range(pieces), spans=spans, first=start == 0),
        grid=(begin,),
        in_specs=blocks,
        out_specs=[pl.BlockSpec((tile, size), lambda i: (i + offset, 0)), SMEM],
        out_shape=[jax.ShapeDtypeStruct(slab.shape, BF16), jax.ShapeDtypeStruct((1,), jnp.int32)],
        input_output_aliases=aliases,
        scratch_shapes=[
            pltpu.VMEM((2, tile, size), BF16),
            pltpu.VMEM((tile // 2, 2 * size), BF16),
            pltpu.SemaphoreType.DMA((2,)),
        ],
        compiler_params=pltpu.CompilerParams(vmem_limit_bytes=16 * 2**20),
        cost_estimate=LIGHT,
        name="panel",
    )(*operands)


def broadcast(value, axis, source):
    kept = jnp.where(lax.axis_index(axis) == source, value, 0).astype(value.dtype)
    return lax.psum(kept, axis)


def settings(*values):
    return jnp.stack([jnp.asarray(value).astype(jnp.int32) for value in values])


def holder_pairs(wide, narrow, distance):
    stride = wide // narrow
    found = []
    for n in range(narrow):
        for start in range(0, wide, 2 * distance):
            source = (n * stride) ^ start
            found.append((source * narrow + n, (source ^ distance) * narrow + n))
    return found


class Order:
    def __init__(self, token):
        self.token = token

    def after(self, value):
        value, self.token = lax.optimization_barrier((value, self.token))
        return value


def known_owner(owner, coarse_basis, material_ids, lame_table, coarse_ids, coarse_slab):
    narrow, wide = lax.axis_size("narrow"), lax.axis_size("wide")
    stride = wide // narrow
    wide_index, narrow_index = lax.axis_index("wide"), lax.axis_index("narrow")
    height, block = coarse_slab.shape
    own = wide_index == narrow_index * stride
    later = narrow_index > owner
    which = jnp.where(later, narrow_index - owner - 1, -1)
    mode = jnp.where(narrow_index == owner, 1, jnp.where(later, 2, 0))
    earlier = (wide_index % stride == 0) & (wide_index // stride < owner)
    kind = jnp.where(wide_index == owner * stride, 1, jnp.where(earlier, 2, 0))
    table = lame_table.astype(F32)
    hops = narrow - 1 - owner
    units, joined, waits, plan = PLANS[hops]
    unit = height // sum(units)
    count = len(units)
    bounds, low = [], 0
    for number in units:
        bounds.append((low, low + number * unit))
        low += number * unit
    axes = ("wide", "narrow")

    def rows_of(number):
        low, high = bounds[number]
        return coarse_slab[low:high]

    def send(value, source, target):
        return lax.ppermute(value, "narrow", [(owner + source, owner + target)])

    order = Order(settings(mode))

    holders = [((n * stride) * narrow + owner, (n * stride) * narrow + n) for n in range(owner + 1, narrow)]
    moved = {}

    groups = [[w for w in range(wide) if w % stride == 0], [w for w in range(wide) if w % stride]]
    groups = [group for group in groups if group]
    member = jnp.where(wide_index % stride == 0, 0, 1)

    def within(group, pairs):
        return [(w * narrow + one, w * narrow + two) for w in group for one, two in pairs]

    def halo_of(group, message):
        return lax.ppermute(message, axes, within(group, [(i + 1, i) for i in range(narrow - 1)]))

    spans = [bounds[0], (bounds[1][0], height) if joined else bounds[1]]
    first, last, *begun = halo_message(table, material_ids, order.token, coarse_basis, coarse_slab, spans)
    first = order.after(first)
    halos = [halo_of(groups[0], first)]
    edge = (narrow_index == 0).astype(jnp.int32).reshape(1)
    inner = order.after(interior(edge, table, material_ids, coarse_basis, order.token))
    head = order.after(lax.ppermute(order.after(coarse_slab[:block]), axes, holders))
    halos[0] = order.after(halos[0])
    moved[0] = [send(order.after(begun[0]), 0, hops)]
    for group in groups[1:]:
        halos.append(halo_of(group, order.after(first)))

    def nearest(base, extent):
        return min(range(base, min(base + extent, narrow)), key=lambda n: abs(n - owner))

    def summed(parts, distance, group):
        total = parts[0] if len(parts) == 1 else parts[0] + parts[1]
        pairs = []
        for base in range(0, narrow - distance, 2 * distance):
            one, two = nearest(base, distance), nearest(base + distance, distance)
            pairs.append((two, one) if nearest(base, 2 * distance) == one else (one, two))
        return [total, lax.ppermute(total, axes, within(group, pairs))], 2 * distance

    def faces_of(number):
        flag = settings(member == number)
        return [order.after(face(flag, table, material_ids, last, halos[number], order.token, inner))]

    sums, reach = [faces_of(0)], [1]
    while reach[0] < narrow:
        sums[0], reach[0] = summed(sums[0], reach[0], groups[0])
    sums[0][1] = order.after(sums[0][1])
    distance, messages, left = wide // 2, [], plan.count("spread")
    result, prepared = None, None
    choice = (narrow_index - owner) % narrow
    flags = settings(mode, kind, own, which)
    for step in plan:
        if step[0] == "panel":
            if prepared is None:
                prepared = prepare(settings(choice, mode), order.token, head, summaries)
            weights, rows, lower = prepared
            begin, end = step[1:]
            parts = [moved[number][:: 1 if number else -1] for number in range(begin, end)]
            result, order.token = panel(
                flags, order.token, lower, weights, rows, added if begin == 0 else head, coarse_slab, parts, result, bounds[begin][0], 2 * unit
            )
        elif step == "added":
            added = added_of(settings(mode), order.token, coarse_ids, galerkin, block)
            added = order.after(lax.ppermute(added, axes, holders))
            if waits:
                moved[count - 1] = [send(order.after(rows_of(count - 1)), 0, 1)]
        elif step == "sums":
            galerkins = [order.after(part) for part in galerkins]
            galerkin = jnp.where(narrow_index == owner, galerkin, sum(galerkins))
        elif step == "next":
            if joined:
                whole = send(order.after(begun[1]), 0, 1)
            else:
                moved[1] = [send(order.after(begun[1]), 0, 1)]
                for number in range(2, count - waits):
                    moved[number] = [send(order.after(rows_of(number)), 0, 1)]
        elif step == "assemble":
            message = assemble(settings(mode, own), order.token, coarse_ids, coarse_slab, head, sums[0])
            message = order.after(message)
        elif step == "others":
            for number in range(1, len(groups)):
                halos[number] = order.after(halos[number])
                parts, far = summed(faces_of(number), 1, groups[number])
                sums.append(parts)
                reach.append(far)
        elif step == "more":
            for number in range(1, len(groups)):
                while reach[number] < narrow:
                    sums[number][1] = order.after(sums[number][1])
                    sums[number], reach[number] = summed(sums[number], reach[number], groups[number])
        elif step == "spread":
            left -= 1
            while distance:
                received = order.after(lax.ppermute(message, axes, holder_pairs(wide, narrow, distance)))
                messages = [message, received]
                if distance > 1:
                    message = message + received
                distance //= 2
                if left:
                    break
        elif step == "factor":
            summary, head, galerkin = factorize(settings(mode, member), order.token, messages, sums)
            summary = order.after(summary)
            ways = [[(owner, (owner + place) % narrow)] for place in range(1, narrow)]
            summaries = [summary] + [lax.ppermute(summary, "narrow", way) for way in ways]
        elif step == "summary":
            for place in range(1, narrow):
                summaries[place] = order.after(summaries[place])
            galerkin = order.after(galerkin)
            galerkins = [lax.ppermute(galerkin, "narrow", way) for way in ways]
        else:
            number, hop = step
            if joined and step == (1, 0):
                whole = order.after(whole)
                for part in range(1, count):
                    low, high = (bound - bounds[1][0] for bound in bounds[part])
                    moved[part] = [whole[low:high]]
            moving = moved[number][hop] = order.after(moved[number][hop])
            if number == 0 and hop + 1 < hops:
                moved[number].append(send(moving, hops - hop, hops - hop - 1))
            elif number != 0 and hop + 1 < hops:
                moved[number].append(send(moving, hop + 1, hop + 2))
    return result, galerkin


def any_owner(owner, coarse_basis, material_ids, lame_table, coarse_ids, coarse_slab):
    narrow, wide = lax.axis_size("narrow"), lax.axis_size("wide")
    stride = wide // narrow
    wide_index, narrow_index = lax.axis_index("wide"), lax.axis_index("narrow")
    own = wide_index == narrow_index * stride
    later = narrow_index > owner
    which = jnp.where(later, 0, -1)
    mode = jnp.where(narrow_index == owner, 1, jnp.where(later, 2, 0))
    earlier = (wide_index % stride == 0) & (wide_index // stride < owner)
    kind = jnp.where(wide_index == owner * stride, 1, jnp.where(earlier, 2, 0))
    table = lame_table.astype(F32)
    column = broadcast(coarse_slab, "narrow", owner)
    first, last = halo_message(table, material_ids, table, coarse_basis, coarse_slab, ())
    halo = lax.ppermute(first, "narrow", [(i + 1, i) for i in range(narrow - 1)])
    edge = (narrow_index == 0).astype(jnp.int32).reshape(1)
    inner = interior(edge, table, material_ids, coarse_basis, first)
    partial = face(settings(1), table, material_ids, last, halo, first, inner)
    parts = [lax.psum(partial, "narrow")]
    message = assemble(settings(mode, own), first, coarse_ids, coarse_slab, column, parts)
    at_owner = (wide_index == owner * stride) & (narrow_index == owner)
    diagonal = lax.psum(jnp.where(at_owner, message, 0.0), ("wide", "narrow"))
    summary, _, galerkin = factorize(settings(1, 0), first, [diagonal], [parts])
    head = broadcast(message, "wide", narrow_index * stride)
    weights, rows, lower = prepare(settings(0, mode), settings(mode), head, [summary])
    added = added_of(settings(1), weights, coarse_ids, galerkin, head.shape[0])
    flags = settings(mode, kind, own, which)
    tile = coarse_slab.shape[0] // 12
    result, _ = panel(flags, flags, lower, weights, rows, added, coarse_slab, [[column]], None, 0, tile)
    return result, galerkin


def on_device(coarse_basis, material_ids, lame_table, coarse_ids, coarse_slab, panel_owner):
    narrow, wide = lax.axis_size("narrow"), lax.axis_size("wide")
    arrays = (coarse_basis, material_ids, lame_table, coarse_ids, coarse_slab)
    owner = panel_owner[0]
    if narrow - 1 > len(PLANS) or wide & (wide - 1):
        return any_owner(owner, *arrays)
    branches = [functools.partial(known_owner, place) for place in range(narrow - 1)]
    return lax.switch(owner, branches, *arrays)


def solution(mesh):
    return jax.shard_map(
        on_device,
        mesh=mesh,
        in_specs=(
            P("wide", None, None, "narrow", None, None),
            P("wide", "narrow", None, None),
            P(),
            P("wide", None),
            P("wide", "narrow"),
            P(),
        ),
        out_specs=(P("wide", "narrow"), P("wide", None, None)),
        check_vma=False,
    )
```

```python
import functools

import jax
import jax.numpy as jnp
from jax import lax
from jax.experimental import pallas as pl
from jax.experimental.pallas import tpu as pltpu
from jax.sharding import PartitionSpec as P

F32, BF16 = jnp.float32, jnp.bfloat16
NT = (((1,), (1,)), ((), ()))
TN = (((0,), (0,)), ((), ()))
VMEM = pl.BlockSpec(memory_space=pltpu.VMEM)
ANY = pl.BlockSpec(memory_space=pl.ANY)
SMEM = pl.BlockSpec(memory_space=pltpu.SMEM)
PLANS = {
    1: (
        (12, 8, 4),
        False,
        True,
        (
            "assemble", "next", "spread", "others", "spread", "more", "spread", (0, 0), "factor", "summary",
            "added", ("panel", 0, 2), "sums", ("panel", 2, 3),
        ),
    ),
    2: (
        (12, 6, 4, 2),
        False,
        True,
        (
            "assemble", "next", "spread", "others", "spread", "more", "spread", (0, 0), (1, 0), "factor", (2, 0),
            "summary", "added", ("panel", 1, 2), (3, 0), ("panel", 0, 1), "sums", ("panel", 2, 4),
        ),
    ),
    3: (
        (12, 8, 4),
        False,
        False,
        (
            "assemble", "next", "spread", "others", "spread", "more", "spread", (0, 0), (1, 0), "factor", "summary",
            (2, 0), (0, 1), (1, 1), "added", ("panel", 0, 1), (2, 1), ("panel", 1, 2), "sums", ("panel", 2, 3),
        ),
    ),
}
BLOCK = 16
LIGHT = pl.CostEstimate(flops=1, bytes_accessed=1, transcendentals=0)


def exact_dot(left, right, dims=(((1,), (0,)), ((), ()))):
    return lax.dot_general(
        left, right, dims, precision=lax.Precision.HIGHEST, preferred_element_type=F32
    )


def dot(left, right, dims=(((1,), (0,)), ((), ()))):
    return lax.dot_general(left, right, dims, preferred_element_type=F32)


def split_two(value):
    high = value.astype(BF16)
    return high, (value - high.astype(F32)).astype(BF16)


def lame_of(ids, table_ref):
    shear = jnp.zeros(ids.shape, F32)
    dilate = jnp.zeros(ids.shape, F32)
    for material in range(table_ref.shape[1]):
        chosen = ids == material
        shear = jnp.where(chosen, table_ref[0, material], shear)
        dilate = jnp.where(chosen, table_ref[1, material], dilate)
    return shear, dilate


def halo_kernel(table_ref, ids_ref, token_ref, basis_ref, slab_ref, out_ref, last_ref, *rest, spans):
    piece_refs, sems = rest[:-1], rest[-1]
    subs, funcs, comps, layers = basis_ref.shape[0:4]
    copies = []
    for number, ((low, high), piece_ref) in enumerate(zip(spans, piece_refs)):
        copies.append(pltpu.make_async_copy(slab_ref.at[pl.ds(low, high - low)], piece_ref, sems.at[number]))
        copies[-1].start()
    for sub in range(subs):
        for comp in range(comps):
            out_ref[sub, comp * funcs : (comp + 1) * funcs] = basis_ref[sub, :, comp, 0]
            last_ref[sub, comp * funcs : (comp + 1) * funcs] = basis_ref[sub, :, comp, layers - 1]
        shear, dilate = lame_of(ids_ref[sub, 0], table_ref)
        out_ref[sub, comps * funcs] = shear.astype(BF16)
        out_ref[sub, comps * funcs + 1] = dilate.astype(BF16)
    for copy in copies:
        copy.wait()


def halo_message(table, ids, token, basis, slab, spans):
    subs, funcs, comps, layers, ny, nz = basis.shape
    return pl.pallas_call(
        functools.partial(halo_kernel, spans=spans),
        in_specs=[SMEM, VMEM, ANY, VMEM, ANY],
        out_specs=[VMEM] * (2 + len(spans)),
        out_shape=[
            jax.ShapeDtypeStruct((subs, comps * funcs + 2, ny, nz), BF16),
            jax.ShapeDtypeStruct((subs, comps * funcs, ny, nz), BF16),
        ]
        + [jax.ShapeDtypeStruct((high - low, slab.shape[1]), BF16) for low, high in spans],
        scratch_shapes=[pltpu.SemaphoreType.DMA((max(1, len(spans)),))],
        compiler_params=pltpu.CompilerParams(vmem_limit_bytes=16 * 2**20),
        cost_estimate=LIGHT,
        name="halo_message",
    )(table, ids, token, basis, slab)


def interior_kernel(edge_ref, table_ref, ids_ref, basis_ref, token_ref, out_ref, fields, turned, coef, left, right, acc):
    sub, comp = pl.program_id(0), pl.program_id(1)
    layers, ny, nz = basis_ref.shape[3:]
    funcs = basis_ref.shape[1]
    row = lax.broadcasted_iota(jnp.int32, (ny, nz), 0)
    lane = lax.broadcasted_iota(jnp.int32, (ny, nz), 1)
    table = [lame_of(ids_ref[sub, x], table_ref) for x in range(layers)]

    def weight(one, two, direction):
        shear = 0.5 * (one[0] + two[0])
        dilate = 0.5 * (one[1] + two[1])
        return shear + jnp.where(comp == direction, shear + dilate, 0.0)

    def ahead(field, axis):
        size = field.shape[axis]
        index = row if axis == 0 else lane
        return jnp.where(index == size - 1, 0.0, pltpu.roll(field, size - 1, axis=axis))

    def behind(field, axis):
        index = row if axis == 0 else lane
        return jnp.where(index == 0, 0.0, pltpu.roll(field, 1, axis=axis))

    nothing = (jnp.zeros((ny, nz), F32),) * 2
    previous = weight(table[0], nothing, 0) * edge_ref[0].astype(F32)
    for x in range(layers):
        diagonal = previous
        forward = []
        if x + 1 < layers:
            face = weight(table[x], table[x + 1], 0)
            diagonal = diagonal + face
            previous = face
            forward.append(face)
        else:
            forward.append(jnp.zeros((ny, nz), F32))
        for axis in (0, 1):
            index, size = (row, ny) if axis == 0 else (lane, nz)
            other = tuple(ahead(value, axis) for value in table[x])
            face = weight(table[x], other, axis + 1)
            before = tuple(behind(value, axis) for value in table[x])
            diagonal = diagonal + face + weight(table[x], before, axis + 1)
            forward.append(jnp.where(index == size - 1, 0.0, face))
        coef[x, 0] = 0.5 * diagonal
        for kind in range(3):
            coef[x, kind + 1] = forward[kind]
        fields[x] = basis_ref[sub, :, comp, x].astype(F32).reshape(funcs * ny, nz)

    total = None
    for x in reversed(range(layers)):
        values = [fields[x, pl.ds(y, funcs, stride=ny), :] for y in range(ny)]
        for y in range(ny):
            value = values[y]
            turned[x % 2, y] = value
            image = coef[x, 0, y : y + 1, :] * value
            image = image - coef[x, 3, y : y + 1, :] * pltpu.roll(value, nz - 1, axis=1)
            if y + 1 < ny:
                image = image - coef[x, 2, y : y + 1, :] * values[y + 1]
            if x + 1 < layers:
                image = image - coef[x, 1, y : y + 1, :] * turned[(x + 1) % 2, y]
            high, low = split_two(image)
            left[:, y * nz : (y + 1) * nz] = value.astype(BF16)
            right[0:funcs, y * nz : (y + 1) * nz] = high
            right[funcs : 2 * funcs, y * nz : (y + 1) * nz] = low
        product = dot(right[...], left[...], NT)
        total = product if total is None else total + product

    @pl.when(comp == 0)
    def _():
        acc[...] = total

    @pl.when(comp > 0)
    def _():
        acc[...] += total

    @pl.when(comp == pl.num_programs(1) - 1)
    def _():
        out_ref[0] = acc[0:funcs] + acc[funcs : 2 * funcs]


def interior(edge, table, ids, basis, token):
    subs, funcs, comps, layers, ny, nz = basis.shape
    return pl.pallas_call(
        interior_kernel,
        grid=(subs, comps),
        in_specs=[SMEM, SMEM, VMEM, VMEM, ANY],
        out_specs=pl.BlockSpec((1, funcs, funcs), lambda s, c: (s, 0, 0)),
        out_shape=jax.ShapeDtypeStruct((subs, funcs, funcs), F32),
        scratch_shapes=[
            pltpu.VMEM((layers, funcs * ny, nz), F32),
            pltpu.VMEM((2, ny, funcs, nz), F32),
            pltpu.VMEM((layers, 4, ny, nz), F32),
            pltpu.VMEM((funcs, ny * nz), BF16),
            pltpu.VMEM((2 * funcs, ny * nz), BF16),
            pltpu.VMEM((2 * funcs, funcs), F32),
        ],
        compiler_params=pltpu.CompilerParams(vmem_limit_bytes=16 * 2**20),
        cost_estimate=LIGHT,
        name="interior",
    )(edge, table, ids, basis, token)


def face_kernel(flags_ref, table_ref, ids_ref, last_ref, halo_ref, token_ref, inner_ref, out_ref, *scratch):
    @pl.when(flags_ref[0] == 1)
    def _():
        last, halo, sems = scratch[-3:]
        copies = [
            pltpu.make_async_copy(last_ref, last, sems.at[0]),
            pltpu.make_async_copy(halo_ref, halo, sems.at[1]),
        ]
        for copy in copies:
            copy.start()
        for copy in copies:
            copy.wait()
        face_sums(table_ref, ids_ref, last, halo, inner_ref, out_ref, *scratch[:-3])


def face_sums(table_ref, ids_ref, last_ref, halo_ref, inner_ref, out_ref, mine, theirs, left, right, weights, acc):
    subs, layers, ny, nz = ids_ref.shape
    funcs = inner_ref.shape[1]
    comps = last_ref.shape[1] // funcs

    @pl.loop(0, subs)
    def _(sub):
        shear, dilate = lame_of(ids_ref[sub, layers - 1], table_ref)
        weights[0] = 0.5 * (shear + halo_ref[sub, comps * funcs].astype(F32))
        weights[1] = 0.5 * (dilate + halo_ref[sub, comps * funcs + 1].astype(F32))

        @pl.loop(0, comps)
        def _(comp):
            weight = weights[0] + jnp.where(comp == 0, weights[0] + weights[1], 0.0)
            rows = pl.ds(comp * funcs, funcs)
            mine[...] = last_ref[sub, rows].astype(F32).reshape(funcs * ny, nz)
            theirs[...] = halo_ref[sub, rows].astype(F32).reshape(funcs * ny, nz)
            for y in range(ny):
                here = mine[pl.ds(y, funcs, stride=ny), :]
                there = theirs[pl.ds(y, funcs, stride=ny), :]
                high, low = split_two(weight[y : y + 1, :] * (here - there))
                left[0:funcs, y * nz : (y + 1) * nz] = here.astype(BF16)
                left[funcs : 2 * funcs, y * nz : (y + 1) * nz] = there.astype(BF16)
                right[0:funcs, y * nz : (y + 1) * nz] = high
                right[funcs : 2 * funcs, y * nz : (y + 1) * nz] = low
            product = dot(right[...], left[...], NT)

            @pl.when(comp == 0)
            def _():
                acc[...] = product

            @pl.when(comp > 0)
            def _():
                acc[...] += product

        total = acc[:, 0:funcs] - acc[:, funcs : 2 * funcs]
        half = inner_ref[sub] + 0.5 * (total[0:funcs] + total[funcs : 2 * funcs])
        out_ref[sub] = half + half.T


def face(flags, table, ids, last, halo, token, inner):
    subs, layers, ny, nz = ids.shape
    funcs = inner.shape[1]
    return pl.pallas_call(
        face_kernel,
        in_specs=[SMEM, SMEM, VMEM, ANY, ANY, ANY, VMEM],
        out_specs=VMEM,
        out_shape=jax.ShapeDtypeStruct((subs, funcs, funcs), F32),
        scratch_shapes=[
            pltpu.VMEM((funcs * ny, nz), F32),
            pltpu.VMEM((funcs * ny, nz), F32),
            pltpu.VMEM((2 * funcs, ny * nz), BF16),
            pltpu.VMEM((2 * funcs, ny * nz), BF16),
            pltpu.VMEM((2, ny, nz), F32),
            pltpu.VMEM((2 * funcs, 2 * funcs), F32),
            pltpu.VMEM(last.shape, BF16),
            pltpu.VMEM(halo.shape, BF16),
            pltpu.SemaphoreType.DMA((2,)),
        ],
        compiler_params=pltpu.CompilerParams(vmem_limit_bytes=16 * 2**20),
        cost_estimate=LIGHT,
        name="face",
    )(flags, table, ids, last, halo, token, inner)


def spread(gal_ref, column_ids_ref, row_ids_ref, size):
    subs, funcs = column_ids_ref.shape[0:2]
    added = jnp.zeros((size, size), F32)
    lane = lax.broadcasted_iota(jnp.int32, (funcs, size), 1)
    row = lax.broadcasted_iota(jnp.int32, (size, funcs), 0)
    for sub in range(subs):
        slots = (column_ids_ref[sub] == lane).astype(F32)
        slots_t = (row_ids_ref[sub] == row).astype(F32)
        added = added + exact_dot(slots_t, exact_dot(gal_ref[sub], slots))
    return added


def assemble_kernel(flags_ref, token_ref, column_ids_ref, row_ids_ref, slab_ref, head_ref, *rest):
    gal_refs, (message_ref, sum_ref) = rest[:-2], rest[-2:]
    size = message_ref.shape[0]
    mode, own = flags_ref[0], flags_ref[1]
    message_ref[...] = jnp.zeros_like(message_ref)

    @pl.when((mode == 1) & (own == 1))
    def _():
        total = gal_refs[0][...]
        for gal_ref in gal_refs[1:]:
            total = total + gal_ref[...]
        sum_ref[...] = total
        added = spread(sum_ref, column_ids_ref, row_ids_ref, size)
        message_ref[...] = added + slab_ref[...].astype(F32)

    @pl.when((mode == 2) & (own == 1))
    def _():
        message_ref[...] = head_ref[...].astype(F32)


def assemble(flags, token, ids, slab, head, parts):
    size = slab.shape[1]
    block = pl.BlockSpec((size, size), lambda i: (0, 0))
    return pl.pallas_call(
        assemble_kernel,
        grid=(1,),
        in_specs=[SMEM, ANY, VMEM, VMEM, block, block] + [VMEM] * len(parts),
        out_specs=VMEM,
        out_shape=jax.ShapeDtypeStruct((size, size), F32),
        scratch_shapes=[pltpu.VMEM(parts[0].shape, F32)],
        cost_estimate=LIGHT,
        name="assemble",
    )(flags, token, ids[:, :, None], ids[:, None, :], slab, head, *parts)


def factor_kernel(flags_ref, token_ref, *refs, parts, groups):
    message_refs, gal_refs = refs[:parts], refs[parts:-4]
    summary_ref, block_ref, sum_ref, work = refs[-4:]
    subs, funcs = gal_refs[0].shape[0:2]
    size = summary_ref.shape[1]
    diagonal = message_refs[0][...]
    for message_ref in message_refs[1:]:
        diagonal = diagonal + message_ref[...]
    block_ref[...] = diagonal

    @pl.when(flags_ref[0] == 1)
    def _():
        row = lax.broadcasted_iota(jnp.int32, (size, size), 0)
        lane = lax.broadcasted_iota(jnp.int32, (size, size), 1)
        work[:, 0:size] = 0.5 * (diagonal + diagonal.T)
        work[:, size : 2 * size] = (row == lane).astype(F32)
        index = lax.broadcasted_iota(jnp.int32, (BLOCK, size), 0)
        for start in range(0, size, BLOCK):
            panel = work[start : start + BLOCK, 0:size]
            extra = work[start : start + BLOCK, size : 2 * size]
            columns = [
                jnp.broadcast_to(panel[:, start + step : start + step + 1], (BLOCK, size))
                for step in range(BLOCK)
            ]
            for step in range(BLOCK):
                scale = lax.rsqrt(columns[step][step : step + 1, :])
                column = jnp.where(index > step, columns[step] * scale, 0.0)
                for later in range(step + 1, BLOCK):
                    columns[later] = columns[later] - column * column[later : later + 1, :]
                pivot = panel[step : step + 1, :] * scale
                panel = jnp.where(index == step, pivot, panel - column * pivot)
                pivot = extra[step : step + 1, :] * scale
                extra = jnp.where(index == step, pivot, extra - column * pivot)
            work[start : start + BLOCK, 0:size] = panel
            work[start : start + BLOCK, size : 2 * size] = extra
            rest = start + BLOCK
            if rest < size:
                both = jnp.concatenate([panel, extra], axis=1)
                work[rest:size, :] -= exact_dot(panel[:, rest:size], both, TN)
        upper = jnp.where(row <= lane, work[:, 0:size], 0.0)
        inverse = jnp.where(row >= lane, work[:, size : 2 * size], 0.0).T
        high = inverse.astype(BF16)
        summary_ref[0:size] = high
        summary_ref[size : 2 * size] = (inverse - high.astype(F32)).astype(BF16)
        summary_ref[2 * size : 3 * size] = upper.T.astype(BF16)
        each = len(gal_refs) // groups
        for group in range(groups):

            @pl.when(flags_ref[1] == group)
            def _(chosen=gal_refs[group * each : (group + 1) * each]):
                total = chosen[0][...]
                for gal_ref in chosen[1:]:
                    total = total + gal_ref[...]
                sum_ref[...] = total


def factorize(flags, token, messages, groups):
    size = messages[0].shape[1]
    subs, funcs = groups[0][0].shape[0:2]
    parts = [part for group in groups for part in group]
    return pl.pallas_call(
        functools.partial(factor_kernel, parts=len(messages), groups=len(groups)),
        in_specs=[SMEM, ANY] + [VMEM] * (len(messages) + len(parts)),
        out_specs=[VMEM] * 3,
        out_shape=[
            jax.ShapeDtypeStruct((3 * size, size), BF16),
            jax.ShapeDtypeStruct((size, size), F32),
            jax.ShapeDtypeStruct(groups[0][0].shape, F32),
        ],
        scratch_shapes=[pltpu.VMEM((size, 2 * size), F32)],
        cost_estimate=LIGHT,
        name="factorize",
    )(flags, token, *messages, *parts)


def prepare_kernel(flags_ref, token_ref, head_ref, *rest, sources):
    summary_refs = rest[:sources]
    weights_ref, rows_ref, lower_ref, summary, sem = rest[sources:]
    size = head_ref.shape[0]
    choice, mode = flags_ref[0], flags_ref[1]
    for number, summary_ref in enumerate(summary_refs):

        @pl.when(choice == number)
        def _(summary_ref=summary_ref):
            copy = pltpu.make_async_copy(summary_ref, summary, sem)
            copy.start()
            copy.wait()

    def doubled(block):
        nothing = jnp.zeros((size, size), BF16)
        top = jnp.concatenate([block, nothing], axis=1)
        return jnp.concatenate([top, jnp.concatenate([nothing, block], axis=1)], axis=0)

    @pl.when(mode > 0)
    def _():
        weights_ref[0 : 2 * size] = doubled(summary[0:size])
        weights_ref[2 * size : 4 * size] = doubled(summary[size : 2 * size])
        lower_ref[...] = summary[2 * size : 3 * size]

    @pl.when(mode == 2)
    def _():
        inverse = summary[0:size].astype(F32) + summary[size : 2 * size].astype(F32)
        solved = exact_dot(head_ref[...], inverse)
        rows_ref[...] = doubled(solved.T.astype(BF16))


def prepare(flags, token, head, summaries):
    size = head.shape[0]
    return pl.pallas_call(
        functools.partial(prepare_kernel, sources=len(summaries)),
        in_specs=[SMEM, ANY, VMEM] + [ANY] * len(summaries),
        out_specs=[VMEM] * 3,
        out_shape=[
            jax.ShapeDtypeStruct((4 * size, 2 * size), BF16),
            jax.ShapeDtypeStruct((2 * size, 2 * size), BF16),
            jax.ShapeDtypeStruct((size, size), BF16),
        ],
        scratch_shapes=[pltpu.VMEM(summaries[0].shape, BF16), pltpu.SemaphoreType.DMA],
        compiler_params=pltpu.CompilerParams(vmem_limit_bytes=16 * 2**20),
        cost_estimate=LIGHT,
        name="prepare",
    )(flags, token, head, *summaries)


def added_kernel(flags_ref, token_ref, column_ids_ref, row_ids_ref, sum_ref, added_ref):
    @pl.when(flags_ref[0] == 1)
    def _():
        added_ref[...] = spread(sum_ref, column_ids_ref, row_ids_ref, added_ref.shape[0])


def added_of(flags, token, ids, galerkin, size):
    return pl.pallas_call(
        added_kernel,
        in_specs=[SMEM, ANY, VMEM, VMEM, VMEM],
        out_specs=VMEM,
        out_shape=jax.ShapeDtypeStruct((size, size), F32),
        cost_estimate=LIGHT,
        name="added",
    )(flags, token, ids[:, :, None], ids[:, None, :], galerkin)


def panel_kernel(
    flags_ref, token_ref, lower_ref, weights_ref, rows_ref, added_ref, slab_ref, *rest, pieces, spans, first
):
    hops = len(pieces) // len(spans)
    others = rest[: len(pieces)]
    out_ref, done_ref, column, factor, sems = rest[-5:]
    done_ref[0] = flags_ref[0]
    tile, size = out_ref.shape
    half = tile // 2
    mode, head, own, which = flags_ref[0], flags_ref[1], flags_ref[2], flags_ref[3]
    step, steps = pl.program_id(0), pl.num_programs(0)
    top = first & (step == 0)

    def copy_of(at, act):
        for number, (begin, end) in enumerate(spans):
            for hop in range(hops):

                @pl.when((mode == 2) & (which == hop) & (at >= begin) & (at < end))
                def _(other_ref=others[number * hops + hop], begin=begin):
                    source = other_ref.at[pl.ds(pl.multiple_of((at - begin) * tile, tile), tile)]
                    act(pltpu.make_async_copy(source, column.at[at % 2], sems.at[at % 2]))

    @pl.when(step == 0)
    def _():
        copy_of(step, lambda copy: copy.start())

    @pl.when(step + 1 < steps)
    def _():
        copy_of(step + 1, lambda copy: copy.start())

    @pl.when(mode == 0)
    def _():
        out_ref[...] = slab_ref[...]

    @pl.when(mode == 1)
    def _():
        column[step % 2] = slab_ref[...]

    @pl.when(mode == 2)
    def _():
        copy_of(step, lambda copy: copy.wait())

    @pl.when(mode > 0)
    def _():
        value = column[step % 2]
        pair = jnp.concatenate([value[0:half], value[half:tile]], axis=1)
        factor[...] = dot(jnp.concatenate([pair, pair], axis=1), weights_ref[...]).astype(BF16)

        @pl.when(top & (head == 1))
        def _():
            factor[0:size, 0:size] = lower_ref[...]

        @pl.when(top & (head == 2))
        def _():
            factor[0:size, 0:size] = jnp.zeros((size, size), BF16)

    @pl.when(mode == 1)
    def _():
        out_ref[0:half] = factor[:, 0:size]
        out_ref[half:tile] = factor[:, size : 2 * size]

    @pl.when(mode == 2)
    def _():
        update = dot(factor[...], rows_ref[...])
        out_ref[0:half] = (slab_ref[0:half].astype(F32) - update[:, 0:size]).astype(BF16)
        out_ref[half:tile] = (slab_ref[half:tile].astype(F32) - update[:, size : 2 * size]).astype(BF16)

        @pl.when(top & (own == 1))
        def _():
            base = slab_ref[0:size].astype(F32) + added_ref[...]
            out_ref[0:size] = (base - update[0:size, 0:size]).astype(BF16)


def panel(flags, token, lower, weights, rows, added, slab, parts, old, start, tile):
    size = slab.shape[1]
    offset = start // tile
    spans, begin, operands = [], 0, []
    for hops in parts:
        end = begin + hops[0].shape[0] // tile
        spans.append((begin, end))
        begin = end
        operands += hops
    blocks = [
        SMEM,
        ANY,
        pl.BlockSpec((size, size), lambda i: (0, 0)),
        pl.BlockSpec(weights.shape, lambda i: (0, 0)),
        pl.BlockSpec(rows.shape, lambda i: (0, 0)),
        pl.BlockSpec((size, size), lambda i: (0, 0)),
        pl.BlockSpec((tile, size), lambda i: (i + offset, 0)),
    ] + [ANY] * len(operands)
    pieces = len(operands)
    operands = [flags, token, lower, weights, rows, added, slab] + operands
    aliases = {}
    if old is not None:
        aliases = {len(operands): 0}
        blocks.append(ANY)
        operands.append(old)
    return pl.pallas_call(
        functools.partial(panel_kernel, pieces=range(pieces), spans=spans, first=start == 0),
        grid=(begin,),
        in_specs=blocks,
        out_specs=[pl.BlockSpec((tile, size), lambda i: (i + offset, 0)), SMEM],
        out_shape=[jax.ShapeDtypeStruct(slab.shape, BF16), jax.ShapeDtypeStruct((1,), jnp.int32)],
        input_output_aliases=aliases,
        scratch_shapes=[
            pltpu.VMEM((2, tile, size), BF16),
            pltpu.VMEM((tile // 2, 2 * size), BF16),
            pltpu.SemaphoreType.DMA((2,)),
        ],
        compiler_params=pltpu.CompilerParams(vmem_limit_bytes=16 * 2**20),
        cost_estimate=LIGHT,
        name="panel",
    )(*operands)


def broadcast(value, axis, source):
    kept = jnp.where(lax.axis_index(axis) == source, value, 0).astype(value.dtype)
    return lax.psum(kept, axis)


def settings(*values):
    return jnp.stack([jnp.asarray(value).astype(jnp.int32) for value in values])


def holder_pairs(wide, narrow, distance):
    stride = wide // narrow
    found = []
    for n in range(narrow):
        for start in range(0, wide, 2 * distance):
            source = (n * stride) ^ start
            found.append((source * narrow + n, (source ^ distance) * narrow + n))
    return found


class Order:
    def __init__(self, token):
        self.token = token

    def after(self, value):
        value, self.token = lax.optimization_barrier((value, self.token))
        return value


def known_owner(owner, coarse_basis, material_ids, lame_table, coarse_ids, coarse_slab):
    narrow, wide = lax.axis_size("narrow"), lax.axis_size("wide")
    stride = wide // narrow
    wide_index, narrow_index = lax.axis_index("wide"), lax.axis_index("narrow")
    height, block = coarse_slab.shape
    own = wide_index == narrow_index * stride
    later = narrow_index > owner
    which = jnp.where(later, narrow_index - owner - 1, -1)
    mode = jnp.where(narrow_index == owner, 1, jnp.where(later, 2, 0))
    earlier = (wide_index % stride == 0) & (wide_index // stride < owner)
    kind = jnp.where(wide_index == owner * stride, 1, jnp.where(earlier, 2, 0))
    table = lame_table.astype(F32)
    hops = narrow - 1 - owner
    units, joined, waits, plan = PLANS[hops]
    unit = height // sum(units)
    count = len(units)
    bounds, low = [], 0
    for number in units:
        bounds.append((low, low + number * unit))
        low += number * unit
    axes = ("wide", "narrow")

    def rows_of(number):
        low, high = bounds[number]
        return coarse_slab[low:high]

    def send(value, source, target):
        return lax.ppermute(value, "narrow", [(owner + source, owner + target)])

    order = Order(settings(mode))

    holders = [((n * stride) * narrow + owner, (n * stride) * narrow + n) for n in range(owner + 1, narrow)]
    moved = {}

    groups = [[w for w in range(wide) if w % stride == 0], [w for w in range(wide) if w % stride]]
    groups = [group for group in groups if group]
    member = jnp.where(wide_index % stride == 0, 0, 1)

    def within(group, pairs):
        return [(w * narrow + one, w * narrow + two) for w in group for one, two in pairs]

    def halo_of(group, message):
        return lax.ppermute(message, axes, within(group, [(i + 1, i) for i in range(narrow - 1)]))

    spans = [bounds[0], (bounds[1][0], height) if joined else bounds[1]]
    first, last, *begun = halo_message(table, material_ids, order.token, coarse_basis, coarse_slab, spans)
    first = order.after(first)
    halos = [halo_of(groups[0], first)]
    edge = (narrow_index == 0).astype(jnp.int32).reshape(1)
    inner = order.after(interior(edge, table, material_ids, coarse_basis, order.token))
    head = order.after(lax.ppermute(order.after(coarse_slab[:block]), axes, holders))
    halos[0] = order.after(halos[0])
    moved[0] = [send(order.after(begun[0]), 0, hops)]
    for group in groups[1:]:
        halos.append(halo_of(group, order.after(first)))

    def nearest(base, extent):
        return min(range(base, min(base + extent, narrow)), key=lambda n: abs(n - owner))

    def summed(parts, distance, group):
        total = parts[0] if len(parts) == 1 else parts[0] + parts[1]
        pairs = []
        for base in range(0, narrow - distance, 2 * distance):
            one, two = nearest(base, distance), nearest(base + distance, distance)
            pairs.append((two, one) if nearest(base, 2 * distance) == one else (one, two))
        return [total, lax.ppermute(total, axes, within(group, pairs))], 2 * distance

    def faces_of(number):
        flag = settings(member == number)
        return [order.after(face(flag, table, material_ids, last, halos[number], order.token, inner))]

    sums, reach = [faces_of(0)], [1]
    while reach[0] < narrow:
        sums[0], reach[0] = summed(sums[0], reach[0], groups[0])
    sums[0][1] = order.after(sums[0][1])
    distance, messages, left = wide // 2, [], plan.count("spread")
    result, prepared = None, None
    choice = (narrow_index - owner) % narrow
    flags = settings(mode, kind, own, which)
    for step in plan:
        if step[0] == "panel":
            if prepared is None:
                prepared = prepare(settings(choice, mode), order.token, head, summaries)
            weights, rows, lower = prepared
            begin, end = step[1:]
            parts = [moved[number][:: 1 if number else -1] for number in range(begin, end)]
            result, order.token = panel(
                flags, order.token, lower, weights, rows, added if begin == 0 else head, coarse_slab, parts, result, bounds[begin][0], 2 * unit
            )
        elif step == "added":
            added = added_of(settings(mode), order.token, coarse_ids, galerkin, block)
            added = order.after(lax.ppermute(added, axes, holders))
            if waits:
                moved[count - 1] = [send(order.after(rows_of(count - 1)), 0, 1)]
        elif step == "sums":
            galerkins = [order.after(part) for part in galerkins]
            galerkin = jnp.where(narrow_index == owner, galerkin, sum(galerkins))
        elif step == "next":
            if joined:
                whole = send(order.after(begun[1]), 0, 1)
            else:
                moved[1] = [send(order.after(begun[1]), 0, 1)]
                for number in range(2, count - waits):
                    moved[number] = [send(order.after(rows_of(number)), 0, 1)]
        elif step == "assemble":
            message = assemble(settings(mode, own), order.token, coarse_ids, coarse_slab, head, sums[0])
            message = order.after(message)
        elif step == "others":
            for number in range(1, len(groups)):
                halos[number] = order.after(halos[number])
                parts, far = summed(faces_of(number), 1, groups[number])
                sums.append(parts)
                reach.append(far)
        elif step == "more":
            for number in range(1, len(groups)):
                while reach[number] < narrow:
                    sums[number][1] = order.after(sums[number][1])
                    sums[number], reach[number] = summed(sums[number], reach[number], groups[number])
        elif step == "spread":
            left -= 1
            while distance:
                received = order.after(lax.ppermute(message, axes, holder_pairs(wide, narrow, distance)))
                messages = [message, received]
                if distance > 1:
                    message = message + received
                distance //= 2
                if left:
                    break
        elif step == "factor":
            summary, head, galerkin = factorize(settings(mode, member), order.token, messages, sums)
            summary = order.after(summary)
            ways = [[(owner, (owner + place) % narrow)] for place in range(1, narrow)]
            summaries = [summary] + [lax.ppermute(summary, "narrow", way) for way in ways]
        elif step == "summary":
            for place in range(1, narrow):
                summaries[place] = order.after(summaries[place])
            galerkin = order.after(galerkin)
            galerkins = [lax.ppermute(galerkin, "narrow", way) for way in ways]
        else:
            number, hop = step
            if joined and step == (1, 0):
                whole = order.after(whole)
                for part in range(1, count):
                    low, high = (bound - bounds[1][0] for bound in bounds[part])
                    moved[part] = [whole[low:high]]
            moving = moved[number][hop] = order.after(moved[number][hop])
            if number == 0 and hop + 1 < hops:
                moved[number].append(send(moving, hops - hop, hops - hop - 1))
            elif number != 0 and hop + 1 < hops:
                moved[number].append(send(moving, hop + 1, hop + 2))
    return result, galerkin


def any_owner(owner, coarse_basis, material_ids, lame_table, coarse_ids, coarse_slab):
    narrow, wide = lax.axis_size("narrow"), lax.axis_size("wide")
    stride = wide // narrow
    wide_index, narrow_index = lax.axis_index("wide"), lax.axis_index("narrow")
    own = wide_index == narrow_index * stride
    later = narrow_index > owner
    which = jnp.where(later, 0, -1)
    mode = jnp.where(narrow_index == owner, 1, jnp.where(later, 2, 0))
    earlier = (wide_index % stride == 0) & (wide_index // stride < owner)
    kind = jnp.where(wide_index == owner * stride, 1, jnp.where(earlier, 2, 0))
    table = lame_table.astype(F32)
    column = broadcast(coarse_slab, "narrow", owner)
    first, last = halo_message(table, material_ids, table, coarse_basis, coarse_slab, ())
    halo = lax.ppermute(first, "narrow", [(i + 1, i) for i in range(narrow - 1)])
    edge = (narrow_index == 0).astype(jnp.int32).reshape(1)
    inner = interior(edge, table, material_ids, coarse_basis, first)
    partial = face(settings(1), table, material_ids, last, halo, first, inner)
    parts = [lax.psum(partial, "narrow")]
    message = assemble(settings(mode, own), first, coarse_ids, coarse_slab, column, parts)
    at_owner = (wide_index == owner * stride) & (narrow_index == owner)
    diagonal = lax.psum(jnp.where(at_owner, message, 0.0), ("wide", "narrow"))
    summary, _, galerkin = factorize(settings(1, 0), first, [diagonal], [parts])
    head = broadcast(message, "wide", narrow_index * stride)
    weights, rows, lower = prepare(settings(0, mode), settings(mode), head, [summary])
    added = added_of(settings(1), weights, coarse_ids, galerkin, head.shape[0])
    flags = settings(mode, kind, own, which)
    tile = coarse_slab.shape[0] // 12
    result, _ = panel(flags, flags, lower, weights, rows, added, coarse_slab, [[column]], None, 0, tile)
    return result, galerkin


def on_device(coarse_basis, material_ids, lame_table, coarse_ids, coarse_slab, panel_owner):
    narrow, wide = lax.axis_size("narrow"), lax.axis_size("wide")
    arrays = (coarse_basis, material_ids, lame_table, coarse_ids, coarse_slab)
    owner = panel_owner[0]
    if narrow - 1 > len(PLANS) or wide & (wide - 1):
        return any_owner(owner, *arrays)
    branches = [functools.partial(known_owner, place) for place in range(narrow - 1)]
    return lax.switch(owner, branches, *arrays)


def solution(mesh):
    return jax.shard_map(
        on_device,
        mesh=mesh,
        in_specs=(
            P("wide", None, None, "narrow", None, None),
            P("wide", "narrow", None, None),
            P(),
            P("wide", None),
            P("wide", "narrow"),
            P(),
        ),
        out_specs=(P("wide", "narrow"), P("wide", None, None)),
        check_vma=False,
    )
```

```python
import functools

import jax
import jax.numpy as jnp
from jax import lax
from jax.experimental import pallas as pl
from jax.experimental.pallas import tpu as pltpu
from jax.sharding import PartitionSpec as P

F32, BF16 = jnp.float32, jnp.bfloat16
NT = (((1,), (1,)), ((), ()))
TN = (((0,), (0,)), ((), ()))
VMEM = pl.BlockSpec(memory_space=pltpu.VMEM)
ANY = pl.BlockSpec(memory_space=pl.ANY)
SMEM = pl.BlockSpec(memory_space=pltpu.SMEM)
PLANS = {
    1: (
        (12, 8, 4),
        False,
        True,
        (
            "assemble", "next", "spread", "others", "spread", "more", "spread", (0, 0), "factor", "summary",
            "added", ("panel", 0, 2), "sums", ("panel", 2, 3),
        ),
    ),
    2: (
        (12, 6, 4, 2),
        False,
        True,
        (
            "assemble", "next", "spread", "others", "spread", "more", "spread", (0, 0), (1, 0), "factor", (2, 0),
            "summary", "added", ("panel", 1, 2), (3, 0), ("panel", 0, 1), "sums", ("panel", 2, 4),
        ),
    ),
    3: (
        (12, 8, 4),
        False,
        False,
        (
            "assemble", "next", "spread", "others", "spread", "more", "spread", (0, 0), (1, 0), "factor", (0, 1),
            (2, 0), (1, 1), "summary", "added", (2, 1), ("panel", 1, 2), ("panel", 0, 1), "sums", ("panel", 2, 3),
        ),
    ),
}
BLOCK = 16
LIGHT = pl.CostEstimate(flops=1, bytes_accessed=1, transcendentals=0)


def exact_dot(left, right, dims=(((1,), (0,)), ((), ()))):
    return lax.dot_general(
        left, right, dims, precision=lax.Precision.HIGHEST, preferred_element_type=F32
    )


def dot(left, right, dims=(((1,), (0,)), ((), ()))):
    return lax.dot_general(left, right, dims, preferred_element_type=F32)


def split_two(value):
    high = value.astype(BF16)
    return high, (value - high.astype(F32)).astype(BF16)


def lame_of(ids, table_ref):
    shear = jnp.zeros(ids.shape, F32)
    dilate = jnp.zeros(ids.shape, F32)
    for material in range(table_ref.shape[1]):
        chosen = ids == material
        shear = jnp.where(chosen, table_ref[0, material], shear)
        dilate = jnp.where(chosen, table_ref[1, material], dilate)
    return shear, dilate


def halo_kernel(table_ref, ids_ref, token_ref, basis_ref, slab_ref, out_ref, last_ref, *rest, spans):
    piece_refs, sems = rest[:-1], rest[-1]
    subs, funcs, comps, layers = basis_ref.shape[0:4]
    copies = []
    for number, ((low, high), piece_ref) in enumerate(zip(spans, piece_refs)):
        copies.append(pltpu.make_async_copy(slab_ref.at[pl.ds(low, high - low)], piece_ref, sems.at[number]))
        copies[-1].start()
    for sub in range(subs):
        for comp in range(comps):
            out_ref[sub, comp * funcs : (comp + 1) * funcs] = basis_ref[sub, :, comp, 0]
            last_ref[sub, comp * funcs : (comp + 1) * funcs] = basis_ref[sub, :, comp, layers - 1]
        shear, dilate = lame_of(ids_ref[sub, 0], table_ref)
        out_ref[sub, comps * funcs] = shear.astype(BF16)
        out_ref[sub, comps * funcs + 1] = dilate.astype(BF16)
    for copy in copies:
        copy.wait()


def halo_message(table, ids, token, basis, slab, spans):
    subs, funcs, comps, layers, ny, nz = basis.shape
    return pl.pallas_call(
        functools.partial(halo_kernel, spans=spans),
        in_specs=[SMEM, VMEM, ANY, VMEM, ANY],
        out_specs=[VMEM] * (2 + len(spans)),
        out_shape=[
            jax.ShapeDtypeStruct((subs, comps * funcs + 2, ny, nz), BF16),
            jax.ShapeDtypeStruct((subs, comps * funcs, ny, nz), BF16),
        ]
        + [jax.ShapeDtypeStruct((high - low, slab.shape[1]), BF16) for low, high in spans],
        scratch_shapes=[pltpu.SemaphoreType.DMA((max(1, len(spans)),))],
        compiler_params=pltpu.CompilerParams(vmem_limit_bytes=16 * 2**20),
        cost_estimate=LIGHT,
        name="halo_message",
    )(table, ids, token, basis, slab)


def interior_kernel(edge_ref, table_ref, ids_ref, basis_ref, token_ref, out_ref, fields, turned, coef, left, right, acc):
    sub, comp = pl.program_id(0), pl.program_id(1)
    layers, ny, nz = basis_ref.shape[3:]
    funcs = basis_ref.shape[1]
    row = lax.broadcasted_iota(jnp.int32, (ny, nz), 0)
    lane = lax.broadcasted_iota(jnp.int32, (ny, nz), 1)
    table = [lame_of(ids_ref[sub, x], table_ref) for x in range(layers)]

    def weight(one, two, direction):
        shear = 0.5 * (one[0] + two[0])
        dilate = 0.5 * (one[1] + two[1])
        return shear + jnp.where(comp == direction, shear + dilate, 0.0)

    def ahead(field, axis):
        size = field.shape[axis]
        index = row if axis == 0 else lane
        return jnp.where(index == size - 1, 0.0, pltpu.roll(field, size - 1, axis=axis))

    def behind(field, axis):
        index = row if axis == 0 else lane
        return jnp.where(index == 0, 0.0, pltpu.roll(field, 1, axis=axis))

    nothing = (jnp.zeros((ny, nz), F32),) * 2
    previous = weight(table[0], nothing, 0) * edge_ref[0].astype(F32)
    for x in range(layers):
        diagonal = previous
        forward = []
        if x + 1 < layers:
            face = weight(table[x], table[x + 1], 0)
            diagonal = diagonal + face
            previous = face
            forward.append(face)
        else:
            forward.append(jnp.zeros((ny, nz), F32))
        for axis in (0, 1):
            index, size = (row, ny) if axis == 0 else (lane, nz)
            other = tuple(ahead(value, axis) for value in table[x])
            face = weight(table[x], other, axis + 1)
            before = tuple(behind(value, axis) for value in table[x])
            diagonal = diagonal + face + weight(table[x], before, axis + 1)
            forward.append(jnp.where(index == size - 1, 0.0, face))
        coef[x, 0] = 0.5 * diagonal
        for kind in range(3):
            coef[x, kind + 1] = forward[kind]
        fields[x] = basis_ref[sub, :, comp, x].astype(F32).reshape(funcs * ny, nz)

    total = None
    for x in reversed(range(layers)):
        values = [fields[x, pl.ds(y, funcs, stride=ny), :] for y in range(ny)]
        for y in range(ny):
            value = values[y]
            turned[x % 2, y] = value
            image = coef[x, 0, y : y + 1, :] * value
            image = image - coef[x, 3, y : y + 1, :] * pltpu.roll(value, nz - 1, axis=1)
            if y + 1 < ny:
                image = image - coef[x, 2, y : y + 1, :] * values[y + 1]
            if x + 1 < layers:
                image = image - coef[x, 1, y : y + 1, :] * turned[(x + 1) % 2, y]
            high, low = split_two(image)
            left[:, y * nz : (y + 1) * nz] = value.astype(BF16)
            right[0:funcs, y * nz : (y + 1) * nz] = high
            right[funcs : 2 * funcs, y * nz : (y + 1) * nz] = low
        product = dot(right[...], left[...], NT)
        total = product if total is None else total + product

    @pl.when(comp == 0)
    def _():
        acc[...] = total

    @pl.when(comp > 0)
    def _():
        acc[...] += total

    @pl.when(comp == pl.num_programs(1) - 1)
    def _():
        out_ref[0] = acc[0:funcs] + acc[funcs : 2 * funcs]


def interior(edge, table, ids, basis, token):
    subs, funcs, comps, layers, ny, nz = basis.shape
    return pl.pallas_call(
        interior_kernel,
        grid=(subs, comps),
        in_specs=[SMEM, SMEM, VMEM, VMEM, ANY],
        out_specs=pl.BlockSpec((1, funcs, funcs), lambda s, c: (s, 0, 0)),
        out_shape=jax.ShapeDtypeStruct((subs, funcs, funcs), F32),
        scratch_shapes=[
            pltpu.VMEM((layers, funcs * ny, nz), F32),
            pltpu.VMEM((2, ny, funcs, nz), F32),
            pltpu.VMEM((layers, 4, ny, nz), F32),
            pltpu.VMEM((funcs, ny * nz), BF16),
            pltpu.VMEM((2 * funcs, ny * nz), BF16),
            pltpu.VMEM((2 * funcs, funcs), F32),
        ],
        compiler_params=pltpu.CompilerParams(vmem_limit_bytes=16 * 2**20),
        cost_estimate=LIGHT,
        name="interior",
    )(edge, table, ids, basis, token)


def face_kernel(flags_ref, table_ref, ids_ref, last_ref, halo_ref, token_ref, inner_ref, out_ref, *scratch):
    @pl.when(flags_ref[0] == 1)
    def _():
        last, halo, sems = scratch[-3:]
        copies = [
            pltpu.make_async_copy(last_ref, last, sems.at[0]),
            pltpu.make_async_copy(halo_ref, halo, sems.at[1]),
        ]
        for copy in copies:
            copy.start()
        for copy in copies:
            copy.wait()
        face_sums(table_ref, ids_ref, last, halo, inner_ref, out_ref, *scratch[:-3])


def face_sums(table_ref, ids_ref, last_ref, halo_ref, inner_ref, out_ref, mine, theirs, left, right, weights, acc):
    subs, layers, ny, nz = ids_ref.shape
    funcs = inner_ref.shape[1]
    comps = last_ref.shape[1] // funcs

    @pl.loop(0, subs)
    def _(sub):
        shear, dilate = lame_of(ids_ref[sub, layers - 1], table_ref)
        weights[0] = 0.5 * (shear + halo_ref[sub, comps * funcs].astype(F32))
        weights[1] = 0.5 * (dilate + halo_ref[sub, comps * funcs + 1].astype(F32))

        @pl.loop(0, comps)
        def _(comp):
            weight = weights[0] + jnp.where(comp == 0, weights[0] + weights[1], 0.0)
            rows = pl.ds(comp * funcs, funcs)
            mine[...] = last_ref[sub, rows].astype(F32).reshape(funcs * ny, nz)
            theirs[...] = halo_ref[sub, rows].astype(F32).reshape(funcs * ny, nz)
            for y in range(ny):
                here = mine[pl.ds(y, funcs, stride=ny), :]
                there = theirs[pl.ds(y, funcs, stride=ny), :]
                high, low = split_two(weight[y : y + 1, :] * (here - there))
                left[0:funcs, y * nz : (y + 1) * nz] = here.astype(BF16)
                left[funcs : 2 * funcs, y * nz : (y + 1) * nz] = there.astype(BF16)
                right[0:funcs, y * nz : (y + 1) * nz] = high
                right[funcs : 2 * funcs, y * nz : (y + 1) * nz] = low
            product = dot(right[...], left[...], NT)

            @pl.when(comp == 0)
            def _():
                acc[...] = product

            @pl.when(comp > 0)
            def _():
                acc[...] += product

        total = acc[:, 0:funcs] - acc[:, funcs : 2 * funcs]
        half = inner_ref[sub] + 0.5 * (total[0:funcs] + total[funcs : 2 * funcs])
        out_ref[sub] = half + half.T


def face(flags, table, ids, last, halo, token, inner):
    subs, layers, ny, nz = ids.shape
    funcs = inner.shape[1]
    return pl.pallas_call(
        face_kernel,
        in_specs=[SMEM, SMEM, VMEM, ANY, ANY, ANY, VMEM],
        out_specs=VMEM,
        out_shape=jax.ShapeDtypeStruct((subs, funcs, funcs), F32),
        scratch_shapes=[
            pltpu.VMEM((funcs * ny, nz), F32),
            pltpu.VMEM((funcs * ny, nz), F32),
            pltpu.VMEM((2 * funcs, ny * nz), BF16),
            pltpu.VMEM((2 * funcs, ny * nz), BF16),
            pltpu.VMEM((2, ny, nz), F32),
            pltpu.VMEM((2 * funcs, 2 * funcs), F32),
            pltpu.VMEM(last.shape, BF16),
            pltpu.VMEM(halo.shape, BF16),
            pltpu.SemaphoreType.DMA((2,)),
        ],
        compiler_params=pltpu.CompilerParams(vmem_limit_bytes=16 * 2**20),
        cost_estimate=LIGHT,
        name="face",
    )(flags, table, ids, last, halo, token, inner)


def spread(gal_ref, column_ids_ref, row_ids_ref, size):
    subs, funcs = column_ids_ref.shape[0:2]
    added = jnp.zeros((size, size), F32)
    lane = lax.broadcasted_iota(jnp.int32, (funcs, size), 1)
    row = lax.broadcasted_iota(jnp.int32, (size, funcs), 0)
    for sub in range(subs):
        slots = (column_ids_ref[sub] == lane).astype(F32)
        slots_t = (row_ids_ref[sub] == row).astype(F32)
        added = added + exact_dot(slots_t, exact_dot(gal_ref[sub], slots))
    return added


def assemble_kernel(flags_ref, token_ref, column_ids_ref, row_ids_ref, slab_ref, head_ref, *rest):
    gal_refs, (message_ref, sum_ref) = rest[:-2], rest[-2:]
    size = message_ref.shape[0]
    mode, own = flags_ref[0], flags_ref[1]
    message_ref[...] = jnp.zeros_like(message_ref)

    @pl.when((mode == 1) & (own == 1))
    def _():
        total = gal_refs[0][...]
        for gal_ref in gal_refs[1:]:
            total = total + gal_ref[...]
        sum_ref[...] = total
        added = spread(sum_ref, column_ids_ref, row_ids_ref, size)
        message_ref[...] = added + slab_ref[...].astype(F32)

    @pl.when((mode == 2) & (own == 1))
    def _():
        message_ref[...] = head_ref[...].astype(F32)


def assemble(flags, token, ids, slab, head, parts):
    size = slab.shape[1]
    block = pl.BlockSpec((size, size), lambda i: (0, 0))
    return pl.pallas_call(
        assemble_kernel,
        grid=(1,),
        in_specs=[SMEM, ANY, VMEM, VMEM, block, block] + [VMEM] * len(parts),
        out_specs=VMEM,
        out_shape=jax.ShapeDtypeStruct((size, size), F32),
        scratch_shapes=[pltpu.VMEM(parts[0].shape, F32)],
        cost_estimate=LIGHT,
        name="assemble",
    )(flags, token, ids[:, :, None], ids[:, None, :], slab, head, *parts)


def factor_kernel(flags_ref, token_ref, *refs, parts, groups):
    message_refs, gal_refs = refs[:parts], refs[parts:-4]
    summary_ref, block_ref, sum_ref, work = refs[-4:]
    subs, funcs = gal_refs[0].shape[0:2]
    size = summary_ref.shape[1]
    diagonal = message_refs[0][...]
    for message_ref in message_refs[1:]:
        diagonal = diagonal + message_ref[...]
    block_ref[...] = diagonal

    @pl.when(flags_ref[0] == 1)
    def _():
        row = lax.broadcasted_iota(jnp.int32, (size, size), 0)
        lane = lax.broadcasted_iota(jnp.int32, (size, size), 1)
        work[:, 0:size] = 0.5 * (diagonal + diagonal.T)
        work[:, size : 2 * size] = (row == lane).astype(F32)
        index = lax.broadcasted_iota(jnp.int32, (BLOCK, size), 0)
        for start in range(0, size, BLOCK):
            panel = work[start : start + BLOCK, 0:size]
            extra = work[start : start + BLOCK, size : 2 * size]
            columns = [
                jnp.broadcast_to(panel[:, start + step : start + step + 1], (BLOCK, size))
                for step in range(BLOCK)
            ]
            for step in range(BLOCK):
                scale = lax.rsqrt(columns[step][step : step + 1, :])
                column = jnp.where(index > step, columns[step] * scale, 0.0)
                for later in range(step + 1, BLOCK):
                    columns[later] = columns[later] - column * column[later : later + 1, :]
                pivot = panel[step : step + 1, :] * scale
                panel = jnp.where(index == step, pivot, panel - column * pivot)
                pivot = extra[step : step + 1, :] * scale
                extra = jnp.where(index == step, pivot, extra - column * pivot)
            work[start : start + BLOCK, 0:size] = panel
            work[start : start + BLOCK, size : 2 * size] = extra
            rest = start + BLOCK
            if rest < size:
                both = jnp.concatenate([panel, extra], axis=1)
                work[rest:size, :] -= exact_dot(panel[:, rest:size], both, TN)
        upper = jnp.where(row <= lane, work[:, 0:size], 0.0)
        inverse = jnp.where(row >= lane, work[:, size : 2 * size], 0.0).T
        high = inverse.astype(BF16)
        summary_ref[0:size] = high
        summary_ref[size : 2 * size] = (inverse - high.astype(F32)).astype(BF16)
        summary_ref[2 * size : 3 * size] = upper.T.astype(BF16)
        each = len(gal_refs) // groups
        for group in range(groups):

            @pl.when(flags_ref[1] == group)
            def _(chosen=gal_refs[group * each : (group + 1) * each]):
                total = chosen[0][...]
                for gal_ref in chosen[1:]:
                    total = total + gal_ref[...]
                sum_ref[...] = total


def factorize(flags, token, messages, groups):
    size = messages[0].shape[1]
    subs, funcs = groups[0][0].shape[0:2]
    parts = [part for group in groups for part in group]
    return pl.pallas_call(
        functools.partial(factor_kernel, parts=len(messages), groups=len(groups)),
        in_specs=[SMEM, ANY] + [VMEM] * (len(messages) + len(parts)),
        out_specs=[VMEM] * 3,
        out_shape=[
            jax.ShapeDtypeStruct((3 * size, size), BF16),
            jax.ShapeDtypeStruct((size, size), F32),
            jax.ShapeDtypeStruct(groups[0][0].shape, F32),
        ],
        scratch_shapes=[pltpu.VMEM((size, 2 * size), F32)],
        cost_estimate=LIGHT,
        name="factorize",
    )(flags, token, *messages, *parts)


def prepare_kernel(flags_ref, token_ref, head_ref, *rest, sources):
    summary_refs = rest[:sources]
    weights_ref, rows_ref, lower_ref, summary, sem = rest[sources:]
    size = head_ref.shape[0]
    choice, mode = flags_ref[0], flags_ref[1]
    for number, summary_ref in enumerate(summary_refs):

        @pl.when(choice == number)
        def _(summary_ref=summary_ref):
            copy = pltpu.make_async_copy(summary_ref, summary, sem)
            copy.start()
            copy.wait()

    def doubled(block):
        nothing = jnp.zeros((size, size), BF16)
        top = jnp.concatenate([block, nothing], axis=1)
        return jnp.concatenate([top, jnp.concatenate([nothing, block], axis=1)], axis=0)

    @pl.when(mode > 0)
    def _():
        weights_ref[0 : 2 * size] = doubled(summary[0:size])
        weights_ref[2 * size : 4 * size] = doubled(summary[size : 2 * size])
        lower_ref[...] = summary[2 * size : 3 * size]

    @pl.when(mode == 2)
    def _():
        inverse = summary[0:size].astype(F32) + summary[size : 2 * size].astype(F32)
        solved = exact_dot(head_ref[...], inverse)
        rows_ref[...] = doubled(solved.T.astype(BF16))


def prepare(flags, token, head, summaries):
    size = head.shape[0]
    return pl.pallas_call(
        functools.partial(prepare_kernel, sources=len(summaries)),
        in_specs=[SMEM, ANY, VMEM] + [ANY] * len(summaries),
        out_specs=[VMEM] * 3,
        out_shape=[
            jax.ShapeDtypeStruct((4 * size, 2 * size), BF16),
            jax.ShapeDtypeStruct((2 * size, 2 * size), BF16),
            jax.ShapeDtypeStruct((size, size), BF16),
        ],
        scratch_shapes=[pltpu.VMEM(summaries[0].shape, BF16), pltpu.SemaphoreType.DMA],
        compiler_params=pltpu.CompilerParams(vmem_limit_bytes=16 * 2**20),
        cost_estimate=LIGHT,
        name="prepare",
    )(flags, token, head, *summaries)


def added_kernel(flags_ref, token_ref, column_ids_ref, row_ids_ref, sum_ref, added_ref):
    @pl.when(flags_ref[0] == 1)
    def _():
        added_ref[...] = spread(sum_ref, column_ids_ref, row_ids_ref, added_ref.shape[0])


def added_of(flags, token, ids, galerkin, size):
    return pl.pallas_call(
        added_kernel,
        in_specs=[SMEM, ANY, VMEM, VMEM, VMEM],
        out_specs=VMEM,
        out_shape=jax.ShapeDtypeStruct((size, size), F32),
        cost_estimate=LIGHT,
        name="added",
    )(flags, token, ids[:, :, None], ids[:, None, :], galerkin)


def panel_kernel(
    flags_ref, token_ref, lower_ref, weights_ref, rows_ref, added_ref, slab_ref, *rest, pieces, spans, first
):
    hops = len(pieces) // len(spans)
    others = rest[: len(pieces)]
    out_ref, done_ref, column, factor, sems = rest[-5:]
    done_ref[0] = flags_ref[0]
    tile, size = out_ref.shape
    half = tile // 2
    mode, head, own, which = flags_ref[0], flags_ref[1], flags_ref[2], flags_ref[3]
    step, steps = pl.program_id(0), pl.num_programs(0)
    top = first & (step == 0)

    def copy_of(at, act):
        for number, (begin, end) in enumerate(spans):
            for hop in range(hops):

                @pl.when((mode == 2) & (which == hop) & (at >= begin) & (at < end))
                def _(other_ref=others[number * hops + hop], begin=begin):
                    source = other_ref.at[pl.ds(pl.multiple_of((at - begin) * tile, tile), tile)]
                    act(pltpu.make_async_copy(source, column.at[at % 2], sems.at[at % 2]))

    @pl.when(step == 0)
    def _():
        copy_of(step, lambda copy: copy.start())

    @pl.when(step + 1 < steps)
    def _():
        copy_of(step + 1, lambda copy: copy.start())

    @pl.when(mode == 0)
    def _():
        out_ref[...] = slab_ref[...]

    @pl.when(mode == 1)
    def _():
        column[step % 2] = slab_ref[...]

    @pl.when(mode == 2)
    def _():
        copy_of(step, lambda copy: copy.wait())

    @pl.when(mode > 0)
    def _():
        value = column[step % 2]
        pair = jnp.concatenate([value[0:half], value[half:tile]], axis=1)
        factor[...] = dot(jnp.concatenate([pair, pair], axis=1), weights_ref[...]).astype(BF16)

        @pl.when(top & (head == 1))
        def _():
            factor[0:size, 0:size] = lower_ref[...]

        @pl.when(top & (head == 2))
        def _():
            factor[0:size, 0:size] = jnp.zeros((size, size), BF16)

    @pl.when(mode == 1)
    def _():
        out_ref[0:half] = factor[:, 0:size]
        out_ref[half:tile] = factor[:, size : 2 * size]

    @pl.when(mode == 2)
    def _():
        update = dot(factor[...], rows_ref[...])
        out_ref[0:half] = (slab_ref[0:half].astype(F32) - update[:, 0:size]).astype(BF16)
        out_ref[half:tile] = (slab_ref[half:tile].astype(F32) - update[:, size : 2 * size]).astype(BF16)

        @pl.when(top & (own == 1))
        def _():
            base = slab_ref[0:size].astype(F32) + added_ref[...]
            out_ref[0:size] = (base - update[0:size, 0:size]).astype(BF16)


def panel(flags, token, lower, weights, rows, added, slab, parts, old, start, tile):
    size = slab.shape[1]
    offset = start // tile
    spans, begin, operands = [], 0, []
    for hops in parts:
        end = begin + hops[0].shape[0] // tile
        spans.append((begin, end))
        begin = end
        operands += hops
    blocks = [
        SMEM,
        ANY,
        pl.BlockSpec((size, size), lambda i: (0, 0)),
        pl.BlockSpec(weights.shape, lambda i: (0, 0)),
        pl.BlockSpec(rows.shape, lambda i: (0, 0)),
        pl.BlockSpec((size, size), lambda i: (0, 0)),
        pl.BlockSpec((tile, size), lambda i: (i + offset, 0)),
    ] + [ANY] * len(operands)
    pieces = len(operands)
    operands = [flags, token, lower, weights, rows, added, slab] + operands
    aliases = {}
    if old is not None:
        aliases = {len(operands): 0}
        blocks.append(ANY)
        operands.append(old)
    return pl.pallas_call(
        functools.partial(panel_kernel, pieces=range(pieces), spans=spans, first=start == 0),
        grid=(begin,),
        in_specs=blocks,
        out_specs=[pl.BlockSpec((tile, size), lambda i: (i + offset, 0)), SMEM],
        out_shape=[jax.ShapeDtypeStruct(slab.shape, BF16), jax.ShapeDtypeStruct((1,), jnp.int32)],
        input_output_aliases=aliases,
        scratch_shapes=[
            pltpu.VMEM((2, tile, size), BF16),
            pltpu.VMEM((tile // 2, 2 * size), BF16),
            pltpu.SemaphoreType.DMA((2,)),
        ],
        compiler_params=pltpu.CompilerParams(vmem_limit_bytes=16 * 2**20),
        cost_estimate=LIGHT,
        name="panel",
    )(*operands)


def broadcast(value, axis, source):
    kept = jnp.where(lax.axis_index(axis) == source, value, 0).astype(value.dtype)
    return lax.psum(kept, axis)


def settings(*values):
    return jnp.stack([jnp.asarray(value).astype(jnp.int32) for value in values])


def holder_pairs(wide, narrow, distance):
    stride = wide // narrow
    found = []
    for n in range(narrow):
        for start in range(0, wide, 2 * distance):
            source = (n * stride) ^ start
            found.append((source * narrow + n, (source ^ distance) * narrow + n))
    return found


class Order:
    def __init__(self, token):
        self.token = token

    def after(self, value):
        value, self.token = lax.optimization_barrier((value, self.token))
        return value


def known_owner(owner, coarse_basis, material_ids, lame_table, coarse_ids, coarse_slab):
    narrow, wide = lax.axis_size("narrow"), lax.axis_size("wide")
    stride = wide // narrow
    wide_index, narrow_index = lax.axis_index("wide"), lax.axis_index("narrow")
    height, block = coarse_slab.shape
    own = wide_index == narrow_index * stride
    later = narrow_index > owner
    which = jnp.where(later, narrow_index - owner - 1, -1)
    mode = jnp.where(narrow_index == owner, 1, jnp.where(later, 2, 0))
    earlier = (wide_index % stride == 0) & (wide_index // stride < owner)
    kind = jnp.where(wide_index == owner * stride, 1, jnp.where(earlier, 2, 0))
    table = lame_table.astype(F32)
    hops = narrow - 1 - owner
    units, joined, waits, plan = PLANS[hops]
    unit = height // sum(units)
    count = len(units)
    bounds, low = [], 0
    for number in units:
        bounds.append((low, low + number * unit))
        low += number * unit
    axes = ("wide", "narrow")

    def rows_of(number):
        low, high = bounds[number]
        return coarse_slab[low:high]

    def send(value, source, target):
        return lax.ppermute(value, "narrow", [(owner + source, owner + target)])

    order = Order(settings(mode))

    holders = [((n * stride) * narrow + owner, (n * stride) * narrow + n) for n in range(owner + 1, narrow)]
    moved = {}

    groups = [[w for w in range(wide) if w % stride == 0], [w for w in range(wide) if w % stride]]
    groups = [group for group in groups if group]
    member = jnp.where(wide_index % stride == 0, 0, 1)

    def within(group, pairs):
        return [(w * narrow + one, w * narrow + two) for w in group for one, two in pairs]

    def halo_of(group, message):
        return lax.ppermute(message, axes, within(group, [(i + 1, i) for i in range(narrow - 1)]))

    spans = [bounds[0], (bounds[1][0], height) if joined else bounds[1]]
    first, last, *begun = halo_message(table, material_ids, order.token, coarse_basis, coarse_slab, spans)
    first = order.after(first)
    halos = [halo_of(groups[0], first)]
    edge = (narrow_index == 0).astype(jnp.int32).reshape(1)
    inner = order.after(interior(edge, table, material_ids, coarse_basis, order.token))
    head = order.after(lax.ppermute(order.after(coarse_slab[:block]), axes, holders))
    halos[0] = order.after(halos[0])
    moved[0] = [send(order.after(begun[0]), 0, hops)]
    for group in groups[1:]:
        halos.append(halo_of(group, order.after(first)))

    def nearest(base, extent):
        return min(range(base, min(base + extent, narrow)), key=lambda n: abs(n - owner))

    def summed(parts, distance, group):
        total = parts[0] if len(parts) == 1 else parts[0] + parts[1]
        pairs = []
        for base in range(0, narrow - distance, 2 * distance):
            one, two = nearest(base, distance), nearest(base + distance, distance)
            pairs.append((two, one) if nearest(base, 2 * distance) == one else (one, two))
        return [total, lax.ppermute(total, axes, within(group, pairs))], 2 * distance

    def faces_of(number):
        flag = settings(member == number)
        return [order.after(face(flag, table, material_ids, last, halos[number], order.token, inner))]

    sums, reach = [faces_of(0)], [1]
    while reach[0] < narrow:
        sums[0], reach[0] = summed(sums[0], reach[0], groups[0])
    sums[0][1] = order.after(sums[0][1])
    distance, messages, left = wide // 2, [], plan.count("spread")
    result, prepared = None, None
    choice = (narrow_index - owner) % narrow
    flags = settings(mode, kind, own, which)
    for step in plan:
        if step[0] == "panel":
            if prepared is None:
                prepared = prepare(settings(choice, mode), order.token, head, summaries)
            weights, rows, lower = prepared
            begin, end = step[1:]
            parts = [moved[number][:: 1 if number else -1] for number in range(begin, end)]
            result, order.token = panel(
                flags, order.token, lower, weights, rows, added if begin == 0 else head, coarse_slab, parts, result, bounds[begin][0], 2 * unit
            )
        elif step == "added":
            added = added_of(settings(mode), order.token, coarse_ids, galerkin, block)
            added = order.after(lax.ppermute(added, axes, holders))
            if waits:
                moved[count - 1] = [send(order.after(rows_of(count - 1)), 0, 1)]
        elif step == "sums":
            galerkins = [order.after(part) for part in galerkins]
            galerkin = jnp.where(narrow_index == owner, galerkin, sum(galerkins))
        elif step == "next":
            if joined:
                whole = send(order.after(begun[1]), 0, 1)
            else:
                moved[1] = [send(order.after(begun[1]), 0, 1)]
                for number in range(2, count - waits):
                    moved[number] = [send(order.after(rows_of(number)), 0, 1)]
        elif step == "assemble":
            message = assemble(settings(mode, own), order.token, coarse_ids, coarse_slab, head, sums[0])
            message = order.after(message)
        elif step == "others":
            for number in range(1, len(groups)):
                halos[number] = order.after(halos[number])
                parts, far = summed(faces_of(number), 1, groups[number])
                sums.append(parts)
                reach.append(far)
        elif step == "more":
            for number in range(1, len(groups)):
                while reach[number] < narrow:
                    sums[number][1] = order.after(sums[number][1])
                    sums[number], reach[number] = summed(sums[number], reach[number], groups[number])
        elif step == "spread":
            left -= 1
            while distance:
                received = order.after(lax.ppermute(message, axes, holder_pairs(wide, narrow, distance)))
                messages = [message, received]
                if distance > 1:
                    message = message + received
                distance //= 2
                if left:
                    break
        elif step == "factor":
            summary, head, galerkin = factorize(settings(mode, member), order.token, messages, sums)
            summary = order.after(summary)
            ways = [[(owner, (owner + place) % narrow)] for place in range(1, narrow)]
            summaries = [summary] + [lax.ppermute(summary, "narrow", way) for way in ways]
        elif step == "summary":
            for place in range(1, narrow):
                summaries[place] = order.after(summaries[place])
            galerkin = order.after(galerkin)
            galerkins = [lax.ppermute(galerkin, "narrow", way) for way in ways]
        else:
            number, hop = step
            if joined and step == (1, 0):
                whole = order.after(whole)
                for part in range(1, count):
                    low, high = (bound - bounds[1][0] for bound in bounds[part])
                    moved[part] = [whole[low:high]]
            moving = moved[number][hop] = order.after(moved[number][hop])
            if number == 0 and hop + 1 < hops:
                moved[number].append(send(moving, hops - hop, hops - hop - 1))
            elif number != 0 and hop + 1 < hops:
                moved[number].append(send(moving, hop + 1, hop + 2))
    return result, galerkin


def any_owner(owner, coarse_basis, material_ids, lame_table, coarse_ids, coarse_slab):
    narrow, wide = lax.axis_size("narrow"), lax.axis_size("wide")
    stride = wide // narrow
    wide_index, narrow_index = lax.axis_index("wide"), lax.axis_index("narrow")
    own = wide_index == narrow_index * stride
    later = narrow_index > owner
    which = jnp.where(later, 0, -1)
    mode = jnp.where(narrow_index == owner, 1, jnp.where(later, 2, 0))
    earlier = (wide_index % stride == 0) & (wide_index // stride < owner)
    kind = jnp.where(wide_index == owner * stride, 1, jnp.where(earlier, 2, 0))
    table = lame_table.astype(F32)
    column = broadcast(coarse_slab, "narrow", owner)
    first, last = halo_message(table, material_ids, table, coarse_basis, coarse_slab, ())
    halo = lax.ppermute(first, "narrow", [(i + 1, i) for i in range(narrow - 1)])
    edge = (narrow_index == 0).astype(jnp.int32).reshape(1)
    inner = interior(edge, table, material_ids, coarse_basis, first)
    partial = face(settings(1), table, material_ids, last, halo, first, inner)
    parts = [lax.psum(partial, "narrow")]
    message = assemble(settings(mode, own), first, coarse_ids, coarse_slab, column, parts)
    at_owner = (wide_index == owner * stride) & (narrow_index == owner)
    diagonal = lax.psum(jnp.where(at_owner, message, 0.0), ("wide", "narrow"))
    summary, _, galerkin = factorize(settings(1, 0), first, [diagonal], [parts])
    head = broadcast(message, "wide", narrow_index * stride)
    weights, rows, lower = prepare(settings(0, mode), settings(mode), head, [summary])
    added = added_of(settings(1), weights, coarse_ids, galerkin, head.shape[0])
    flags = settings(mode, kind, own, which)
    tile = coarse_slab.shape[0] // 12
    result, _ = panel(flags, flags, lower, weights, rows, added, coarse_slab, [[column]], None, 0, tile)
    return result, galerkin


def on_device(coarse_basis, material_ids, lame_table, coarse_ids, coarse_slab, panel_owner):
    narrow, wide = lax.axis_size("narrow"), lax.axis_size("wide")
    arrays = (coarse_basis, material_ids, lame_table, coarse_ids, coarse_slab)
    owner = panel_owner[0]
    if narrow - 1 > len(PLANS) or wide & (wide - 1):
        return any_owner(owner, *arrays)
    branches = [functools.partial(known_owner, place) for place in range(narrow - 1)]
    return lax.switch(owner, branches, *arrays)


def solution(mesh):
    return jax.shard_map(
        on_device,
        mesh=mesh,
        in_specs=(
            P("wide", None, None, "narrow", None, None),
            P("wide", "narrow", None, None),
            P(),
            P("wide", None),
            P("wide", "narrow"),
            P(),
        ),
        out_specs=(P("wide", "narrow"), P("wide", None, None)),
        check_vma=False,
    )
```

```python
import functools

import jax
import jax.numpy as jnp
from jax import lax
from jax.experimental import pallas as pl
from jax.experimental.pallas import tpu as pltpu
from jax.sharding import PartitionSpec as P

F32, BF16 = jnp.float32, jnp.bfloat16
NT = (((1,), (1,)), ((), ()))
TN = (((0,), (0,)), ((), ()))
VMEM = pl.BlockSpec(memory_space=pltpu.VMEM)
ANY = pl.BlockSpec(memory_space=pl.ANY)
SMEM = pl.BlockSpec(memory_space=pltpu.SMEM)
PLANS = {
    1: (
        (12, 8, 4),
        False,
        True,
        (
            "assemble", "next", "spread", "others", "spread", "more", "spread", (0, 0), "factor", "summary",
            "added", ("panel", 0, 2), "sums", ("panel", 2, 3),
        ),
    ),
    2: (
        (12, 6, 4, 2),
        False,
        True,
        (
            "assemble", "next", "spread", "others", "spread", "more", "spread", (0, 0), (1, 0), "factor", (2, 0),
            "summary", "added", ("panel", 1, 2), (3, 0), ("panel", 0, 1), "sums", ("panel", 2, 4),
        ),
    ),
    3: (
        (12, 8, 4),
        False,
        False,
        (
            "assemble", "next", "spread", "others", "spread", "more", "spread", (0, 0), (1, 0), "factor", (0, 1),
            (2, 0), (1, 1), "summary", "added", (2, 1), ("panel", 1, 2), ("panel", 0, 1), "sums", ("panel", 2, 3),
        ),
    ),
}
BLOCK = 16
LIGHT = pl.CostEstimate(flops=1, bytes_accessed=1, transcendentals=0)


def exact_dot(left, right, dims=(((1,), (0,)), ((), ()))):
    return lax.dot_general(
        left, right, dims, precision=lax.Precision.HIGHEST, preferred_element_type=F32
    )


def dot(left, right, dims=(((1,), (0,)), ((), ()))):
    return lax.dot_general(left, right, dims, preferred_element_type=F32)


def split_two(value):
    high = value.astype(BF16)
    return high, (value - high.astype(F32)).astype(BF16)


def lame_of(ids, table_ref):
    shear = jnp.zeros(ids.shape, F32)
    dilate = jnp.zeros(ids.shape, F32)
    for material in range(table_ref.shape[1]):
        chosen = ids == material
        shear = jnp.where(chosen, table_ref[0, material], shear)
        dilate = jnp.where(chosen, table_ref[1, material], dilate)
    return shear, dilate


def halo_kernel(table_ref, ids_ref, token_ref, basis_ref, slab_ref, out_ref, last_ref, *rest, spans):
    piece_refs, sems = rest[:-1], rest[-1]
    subs, funcs, comps, layers = basis_ref.shape[0:4]
    copies = []
    for number, ((low, high), piece_ref) in enumerate(zip(spans, piece_refs)):
        copies.append(pltpu.make_async_copy(slab_ref.at[pl.ds(low, high - low)], piece_ref, sems.at[number]))
        copies[-1].start()
    for sub in range(subs):
        for comp in range(comps):
            out_ref[sub, comp * funcs : (comp + 1) * funcs] = basis_ref[sub, :, comp, 0]
            last_ref[sub, comp * funcs : (comp + 1) * funcs] = basis_ref[sub, :, comp, layers - 1]
        shear, dilate = lame_of(ids_ref[sub, 0], table_ref)
        out_ref[sub, comps * funcs] = shear.astype(BF16)
        out_ref[sub, comps * funcs + 1] = dilate.astype(BF16)
    for copy in copies:
        copy.wait()


def halo_message(table, ids, token, basis, slab, spans):
    subs, funcs, comps, layers, ny, nz = basis.shape
    return pl.pallas_call(
        functools.partial(halo_kernel, spans=spans),
        in_specs=[SMEM, VMEM, ANY, VMEM, ANY],
        out_specs=[VMEM] * (2 + len(spans)),
        out_shape=[
            jax.ShapeDtypeStruct((subs, comps * funcs + 2, ny, nz), BF16),
            jax.ShapeDtypeStruct((subs, comps * funcs, ny, nz), BF16),
        ]
        + [jax.ShapeDtypeStruct((high - low, slab.shape[1]), BF16) for low, high in spans],
        scratch_shapes=[pltpu.SemaphoreType.DMA((max(1, len(spans)),))],
        compiler_params=pltpu.CompilerParams(vmem_limit_bytes=16 * 2**20),
        cost_estimate=LIGHT,
        name="halo_message",
    )(table, ids, token, basis, slab)


def interior_kernel(edge_ref, table_ref, ids_ref, basis_ref, token_ref, out_ref, fields, turned, coef, left, right, acc):
    sub, comp = pl.program_id(0), pl.program_id(1)
    layers, ny, nz = basis_ref.shape[3:]
    funcs = basis_ref.shape[1]
    row = lax.broadcasted_iota(jnp.int32, (ny, nz), 0)
    lane = lax.broadcasted_iota(jnp.int32, (ny, nz), 1)
    table = [lame_of(ids_ref[sub, x], table_ref) for x in range(layers)]

    def weight(one, two, direction):
        shear = 0.5 * (one[0] + two[0])
        dilate = 0.5 * (one[1] + two[1])
        return shear + jnp.where(comp == direction, shear + dilate, 0.0)

    def ahead(field, axis):
        size = field.shape[axis]
        index = row if axis == 0 else lane
        return jnp.where(index == size - 1, 0.0, pltpu.roll(field, size - 1, axis=axis))

    def behind(field, axis):
        index = row if axis == 0 else lane
        return jnp.where(index == 0, 0.0, pltpu.roll(field, 1, axis=axis))

    nothing = (jnp.zeros((ny, nz), F32),) * 2
    previous = weight(table[0], nothing, 0) * edge_ref[0].astype(F32)
    for x in range(layers):
        diagonal = previous
        forward = []
        if x + 1 < layers:
            face = weight(table[x], table[x + 1], 0)
            diagonal = diagonal + face
            previous = face
            forward.append(face)
        else:
            forward.append(jnp.zeros((ny, nz), F32))
        for axis in (0, 1):
            index, size = (row, ny) if axis == 0 else (lane, nz)
            other = tuple(ahead(value, axis) for value in table[x])
            face = weight(table[x], other, axis + 1)
            before = tuple(behind(value, axis) for value in table[x])
            diagonal = diagonal + face + weight(table[x], before, axis + 1)
            forward.append(jnp.where(index == size - 1, 0.0, face))
        coef[x, 0] = 0.5 * diagonal
        for kind in range(3):
            coef[x, kind + 1] = forward[kind]
        fields[x] = basis_ref[sub, :, comp, x].astype(F32).reshape(funcs * ny, nz)

    total = None
    for x in reversed(range(layers)):
        values = [fields[x, pl.ds(y, funcs, stride=ny), :] for y in range(ny)]
        for y in range(ny):
            value = values[y]
            turned[x % 2, y] = value
            image = coef[x, 0, y : y + 1, :] * value
            image = image - coef[x, 3, y : y + 1, :] * pltpu.roll(value, nz - 1, axis=1)
            if y + 1 < ny:
                image = image - coef[x, 2, y : y + 1, :] * values[y + 1]
            if x + 1 < layers:
                image = image - coef[x, 1, y : y + 1, :] * turned[(x + 1) % 2, y]
            high, low = split_two(image)
            left[:, y * nz : (y + 1) * nz] = value.astype(BF16)
            right[0:funcs, y * nz : (y + 1) * nz] = high
            right[funcs : 2 * funcs, y * nz : (y + 1) * nz] = low
        product = dot(right[...], left[...], NT)
        total = product if total is None else total + product

    @pl.when(comp == 0)
    def _():
        acc[...] = total

    @pl.when(comp > 0)
    def _():
        acc[...] += total

    @pl.when(comp == pl.num_programs(1) - 1)
    def _():
        out_ref[0] = acc[0:funcs] + acc[funcs : 2 * funcs]


def interior(edge, table, ids, basis, token):
    subs, funcs, comps, layers, ny, nz = basis.shape
    return pl.pallas_call(
        interior_kernel,
        grid=(subs, comps),
        in_specs=[SMEM, SMEM, VMEM, VMEM, ANY],
        out_specs=pl.BlockSpec((1, funcs, funcs), lambda s, c: (s, 0, 0)),
        out_shape=jax.ShapeDtypeStruct((subs, funcs, funcs), F32),
        scratch_shapes=[
            pltpu.VMEM((layers, funcs * ny, nz), F32),
            pltpu.VMEM((2, ny, funcs, nz), F32),
            pltpu.VMEM((layers, 4, ny, nz), F32),
            pltpu.VMEM((funcs, ny * nz), BF16),
            pltpu.VMEM((2 * funcs, ny * nz), BF16),
            pltpu.VMEM((2 * funcs, funcs), F32),
        ],
        compiler_params=pltpu.CompilerParams(vmem_limit_bytes=16 * 2**20),
        cost_estimate=LIGHT,
        name="interior",
    )(edge, table, ids, basis, token)


def face_kernel(flags_ref, table_ref, ids_ref, last_ref, halo_ref, token_ref, inner_ref, out_ref, *scratch):
    @pl.when(flags_ref[0] == 1)
    def _():
        last, halo, sems = scratch[-3:]
        copies = [
            pltpu.make_async_copy(last_ref, last, sems.at[0]),
            pltpu.make_async_copy(halo_ref, halo, sems.at[1]),
        ]
        for copy in copies:
            copy.start()
        for copy in copies:
            copy.wait()
        face_sums(table_ref, ids_ref, last, halo, inner_ref, out_ref, *scratch[:-3])


def face_sums(table_ref, ids_ref, last_ref, halo_ref, inner_ref, out_ref, mine, theirs, left, right, weights, acc):
    subs, layers, ny, nz = ids_ref.shape
    funcs = inner_ref.shape[1]
    comps = last_ref.shape[1] // funcs

    @pl.loop(0, subs)
    def _(sub):
        shear, dilate = lame_of(ids_ref[sub, layers - 1], table_ref)
        weights[0] = 0.5 * (shear + halo_ref[sub, comps * funcs].astype(F32))
        weights[1] = 0.5 * (dilate + halo_ref[sub, comps * funcs + 1].astype(F32))

        @pl.loop(0, comps)
        def _(comp):
            weight = weights[0] + jnp.where(comp == 0, weights[0] + weights[1], 0.0)
            rows = pl.ds(comp * funcs, funcs)
            mine[...] = last_ref[sub, rows].astype(F32).reshape(funcs * ny, nz)
            theirs[...] = halo_ref[sub, rows].astype(F32).reshape(funcs * ny, nz)
            for y in range(ny):
                here = mine[pl.ds(y, funcs, stride=ny), :]
                there = theirs[pl.ds(y, funcs, stride=ny), :]
                high, low = split_two(weight[y : y + 1, :] * (here - there))
                left[0:funcs, y * nz : (y + 1) * nz] = here.astype(BF16)
                left[funcs : 2 * funcs, y * nz : (y + 1) * nz] = there.astype(BF16)
                right[0:funcs, y * nz : (y + 1) * nz] = high
                right[funcs : 2 * funcs, y * nz : (y + 1) * nz] = low
            product = dot(right[...], left[...], NT)

            @pl.when(comp == 0)
            def _():
                acc[...] = product

            @pl.when(comp > 0)
            def _():
                acc[...] += product

        total = acc[:, 0:funcs] - acc[:, funcs : 2 * funcs]
        half = inner_ref[sub] + 0.5 * (total[0:funcs] + total[funcs : 2 * funcs])
        out_ref[sub] = half + half.T


def face(flags, table, ids, last, halo, token, inner):
    subs, layers, ny, nz = ids.shape
    funcs = inner.shape[1]
    return pl.pallas_call(
        face_kernel,
        in_specs=[SMEM, SMEM, VMEM, ANY, ANY, ANY, VMEM],
        out_specs=VMEM,
        out_shape=jax.ShapeDtypeStruct((subs, funcs, funcs), F32),
        scratch_shapes=[
            pltpu.VMEM((funcs * ny, nz), F32),
            pltpu.VMEM((funcs * ny, nz), F32),
            pltpu.VMEM((2 * funcs, ny * nz), BF16),
            pltpu.VMEM((2 * funcs, ny * nz), BF16),
            pltpu.VMEM((2, ny, nz), F32),
            pltpu.VMEM((2 * funcs, 2 * funcs), F32),
            pltpu.VMEM(last.shape, BF16),
            pltpu.VMEM(halo.shape, BF16),
            pltpu.SemaphoreType.DMA((2,)),
        ],
        compiler_params=pltpu.CompilerParams(vmem_limit_bytes=16 * 2**20),
        cost_estimate=LIGHT,
        name="face",
    )(flags, table, ids, last, halo, token, inner)


def spread(gal_ref, column_ids_ref, row_ids_ref, size):
    subs, funcs = column_ids_ref.shape[0:2]
    added = jnp.zeros((size, size), F32)
    lane = lax.broadcasted_iota(jnp.int32, (funcs, size), 1)
    row = lax.broadcasted_iota(jnp.int32, (size, funcs), 0)
    for sub in range(subs):
        slots = (column_ids_ref[sub] == lane).astype(F32)
        slots_t = (row_ids_ref[sub] == row).astype(F32)
        added = added + exact_dot(slots_t, exact_dot(gal_ref[sub], slots))
    return added


def assemble_kernel(flags_ref, token_ref, column_ids_ref, row_ids_ref, slab_ref, head_ref, *rest):
    gal_refs, (message_ref, sum_ref) = rest[:-2], rest[-2:]
    size = message_ref.shape[0]
    mode, own = flags_ref[0], flags_ref[1]
    message_ref[...] = jnp.zeros_like(message_ref)

    @pl.when((mode == 1) & (own == 1))
    def _():
        total = gal_refs[0][...]
        for gal_ref in gal_refs[1:]:
            total = total + gal_ref[...]
        sum_ref[...] = total
        added = spread(sum_ref, column_ids_ref, row_ids_ref, size)
        message_ref[...] = added + slab_ref[...].astype(F32)

    @pl.when((mode == 2) & (own == 1))
    def _():
        message_ref[...] = head_ref[...].astype(F32)


def assemble(flags, token, ids, slab, head, parts):
    size = slab.shape[1]
    block = pl.BlockSpec((size, size), lambda i: (0, 0))
    return pl.pallas_call(
        assemble_kernel,
        grid=(1,),
        in_specs=[SMEM, ANY, VMEM, VMEM, block, block] + [VMEM] * len(parts),
        out_specs=VMEM,
        out_shape=jax.ShapeDtypeStruct((size, size), F32),
        scratch_shapes=[pltpu.VMEM(parts[0].shape, F32)],
        cost_estimate=LIGHT,
        name="assemble",
    )(flags, token, ids[:, :, None], ids[:, None, :], slab, head, *parts)


def factor_kernel(flags_ref, token_ref, *refs, parts, groups):
    message_refs, gal_refs = refs[:parts], refs[parts:-4]
    summary_ref, block_ref, sum_ref, work = refs[-4:]
    subs, funcs = gal_refs[0].shape[0:2]
    size = summary_ref.shape[1]
    diagonal = message_refs[0][...]
    for message_ref in message_refs[1:]:
        diagonal = diagonal + message_ref[...]
    block_ref[...] = diagonal

    @pl.when(flags_ref[0] == 1)
    def _():
        row = lax.broadcasted_iota(jnp.int32, (size, size), 0)
        lane = lax.broadcasted_iota(jnp.int32, (size, size), 1)
        work[:, 0:size] = 0.5 * (diagonal + diagonal.T)
        work[:, size : 2 * size] = (row == lane).astype(F32)
        index = lax.broadcasted_iota(jnp.int32, (BLOCK, size), 0)
        for start in range(0, size, BLOCK):
            panel = work[start : start + BLOCK, 0:size]
            extra = work[start : start + BLOCK, size : 2 * size]
            columns = [
                jnp.broadcast_to(panel[:, start + step : start + step + 1], (BLOCK, size))
                for step in range(BLOCK)
            ]
            for step in range(BLOCK):
                scale = lax.rsqrt(columns[step][step : step + 1, :])
                column = jnp.where(index > step, columns[step] * scale, 0.0)
                for later in range(step + 1, BLOCK):
                    columns[later] = columns[later] - column * column[later : later + 1, :]
                pivot = panel[step : step + 1, :] * scale
                panel = jnp.where(index == step, pivot, panel - column * pivot)
                pivot = extra[step : step + 1, :] * scale
                extra = jnp.where(index == step, pivot, extra - column * pivot)
            work[start : start + BLOCK, 0:size] = panel
            work[start : start + BLOCK, size : 2 * size] = extra
            rest = start + BLOCK
            if rest < size:
                both = jnp.concatenate([panel, extra], axis=1)
                work[rest:size, :] -= exact_dot(panel[:, rest:size], both, TN)
        upper = jnp.where(row <= lane, work[:, 0:size], 0.0)
        inverse = jnp.where(row >= lane, work[:, size : 2 * size], 0.0).T
        high = inverse.astype(BF16)
        summary_ref[0:size] = high
        summary_ref[size : 2 * size] = (inverse - high.astype(F32)).astype(BF16)
        summary_ref[2 * size : 3 * size] = upper.T.astype(BF16)
        each = len(gal_refs) // groups
        for group in range(groups):

            @pl.when(flags_ref[1] == group)
            def _(chosen=gal_refs[group * each : (group + 1) * each]):
                total = chosen[0][...]
                for gal_ref in chosen[1:]:
                    total = total + gal_ref[...]
                sum_ref[...] = total


def factorize(flags, token, messages, groups):
    size = messages[0].shape[1]
    subs, funcs = groups[0][0].shape[0:2]
    parts = [part for group in groups for part in group]
    return pl.pallas_call(
        functools.partial(factor_kernel, parts=len(messages), groups=len(groups)),
        in_specs=[SMEM, ANY] + [VMEM] * (len(messages) + len(parts)),
        out_specs=[VMEM] * 3,
        out_shape=[
            jax.ShapeDtypeStruct((3 * size, size), BF16),
            jax.ShapeDtypeStruct((size, size), F32),
            jax.ShapeDtypeStruct(groups[0][0].shape, F32),
        ],
        scratch_shapes=[pltpu.VMEM((size, 2 * size), F32)],
        cost_estimate=LIGHT,
        name="factorize",
    )(flags, token, *messages, *parts)


def prepare_kernel(flags_ref, token_ref, head_ref, *rest, sources):
    summary_refs = rest[:sources]
    weights_ref, rows_ref, lower_ref, summary, sem = rest[sources:]
    size = head_ref.shape[0]
    choice, mode = flags_ref[0], flags_ref[1]
    for number, summary_ref in enumerate(summary_refs):

        @pl.when(choice == number)
        def _(summary_ref=summary_ref):
            copy = pltpu.make_async_copy(summary_ref, summary, sem)
            copy.start()
            copy.wait()

    def doubled(block):
        nothing = jnp.zeros((size, size), BF16)
        top = jnp.concatenate([block, nothing], axis=1)
        return jnp.concatenate([top, jnp.concatenate([nothing, block], axis=1)], axis=0)

    @pl.when(mode > 0)
    def _():
        weights_ref[0 : 2 * size] = doubled(summary[0:size])
        weights_ref[2 * size : 4 * size] = doubled(summary[size : 2 * size])
        lower_ref[...] = summary[2 * size : 3 * size]

    @pl.when(mode == 2)
    def _():
        inverse = summary[0:size].astype(F32) + summary[size : 2 * size].astype(F32)
        solved = exact_dot(head_ref[...], inverse)
        rows_ref[...] = doubled(solved.T.astype(BF16))


def prepare(flags, token, head, summaries):
    size = head.shape[0]
    return pl.pallas_call(
        functools.partial(prepare_kernel, sources=len(summaries)),
        in_specs=[SMEM, ANY, VMEM] + [ANY] * len(summaries),
        out_specs=[VMEM] * 3,
        out_shape=[
            jax.ShapeDtypeStruct((4 * size, 2 * size), BF16),
            jax.ShapeDtypeStruct((2 * size, 2 * size), BF16),
            jax.ShapeDtypeStruct((size, size), BF16),
        ],
        scratch_shapes=[pltpu.VMEM(summaries[0].shape, BF16), pltpu.SemaphoreType.DMA],
        compiler_params=pltpu.CompilerParams(vmem_limit_bytes=16 * 2**20),
        cost_estimate=LIGHT,
        name="prepare",
    )(flags, token, head, *summaries)


def added_kernel(flags_ref, token_ref, column_ids_ref, row_ids_ref, sum_ref, added_ref):
    @pl.when(flags_ref[0] == 1)
    def _():
        added_ref[...] = spread(sum_ref, column_ids_ref, row_ids_ref, added_ref.shape[0])


def added_of(flags, token, ids, galerkin, size):
    return pl.pallas_call(
        added_kernel,
        in_specs=[SMEM, ANY, VMEM, VMEM, VMEM],
        out_specs=VMEM,
        out_shape=jax.ShapeDtypeStruct((size, size), F32),
        cost_estimate=LIGHT,
        name="added",
    )(flags, token, ids[:, :, None], ids[:, None, :], galerkin)


def panel_kernel(
    flags_ref, token_ref, lower_ref, weights_ref, rows_ref, added_ref, slab_ref, *rest, pieces, spans, first
):
    hops = len(pieces) // len(spans)
    others = rest[: len(pieces)]
    out_ref, done_ref, column, factor, sems = rest[-5:]
    done_ref[0] = flags_ref[0]
    tile, size = out_ref.shape
    half = tile // 2
    mode, head, own, which = flags_ref[0], flags_ref[1], flags_ref[2], flags_ref[3]
    step, steps = pl.program_id(0), pl.num_programs(0)
    top = first & (step == 0)

    def copy_of(at, act):
        for number, (begin, end) in enumerate(spans):
            for hop in range(hops):

                @pl.when((mode == 2) & (which == hop) & (at >= begin) & (at < end))
                def _(other_ref=others[number * hops + hop], begin=begin):
                    source = other_ref.at[pl.ds(pl.multiple_of((at - begin) * tile, tile), tile)]
                    act(pltpu.make_async_copy(source, column.at[at % 2], sems.at[at % 2]))

    @pl.when(step == 0)
    def _():
        copy_of(step, lambda copy: copy.start())

    @pl.when(step + 1 < steps)
    def _():
        copy_of(step + 1, lambda copy: copy.start())

    @pl.when(mode == 0)
    def _():
        out_ref[...] = slab_ref[...]

    @pl.when(mode == 1)
    def _():
        column[step % 2] = slab_ref[...]

    @pl.when(mode == 2)
    def _():
        copy_of(step, lambda copy: copy.wait())

    @pl.when(mode > 0)
    def _():
        value = column[step % 2]
        pair = jnp.concatenate([value[0:half], value[half:tile]], axis=1)
        factor[...] = dot(jnp.concatenate([pair, pair], axis=1), weights_ref[...]).astype(BF16)

        @pl.when(top & (head == 1))
        def _():
            factor[0:size, 0:size] = lower_ref[...]

        @pl.when(top & (head == 2))
        def _():
            factor[0:size, 0:size] = jnp.zeros((size, size), BF16)

    @pl.when(mode == 1)
    def _():
        out_ref[0:half] = factor[:, 0:size]
        out_ref[half:tile] = factor[:, size : 2 * size]

    @pl.when(mode == 2)
    def _():
        update = dot(factor[...], rows_ref[...])
        out_ref[0:half] = (slab_ref[0:half].astype(F32) - update[:, 0:size]).astype(BF16)
        out_ref[half:tile] = (slab_ref[half:tile].astype(F32) - update[:, size : 2 * size]).astype(BF16)

        @pl.when(top & (own == 1))
        def _():
            base = slab_ref[0:size].astype(F32) + added_ref[...]
            out_ref[0:size] = (base - update[0:size, 0:size]).astype(BF16)


def panel(flags, token, lower, weights, rows, added, slab, parts, old, start, tile):
    size = slab.shape[1]
    offset = start // tile
    spans, begin, operands = [], 0, []
    for hops in parts:
        end = begin + hops[0].shape[0] // tile
        spans.append((begin, end))
        begin = end
        operands += hops
    blocks = [
        SMEM,
        ANY,
        pl.BlockSpec((size, size), lambda i: (0, 0)),
        pl.BlockSpec(weights.shape, lambda i: (0, 0)),
        pl.BlockSpec(rows.shape, lambda i: (0, 0)),
        pl.BlockSpec((size, size), lambda i: (0, 0)),
        pl.BlockSpec((tile, size), lambda i: (i + offset, 0)),
    ] + [ANY] * len(operands)
    pieces = len(operands)
    operands = [flags, token, lower, weights, rows, added, slab] + operands
    aliases = {}
    if old is not None:
        aliases = {len(operands): 0}
        blocks.append(ANY)
        operands.append(old)
    return pl.pallas_call(
        functools.partial(panel_kernel, pieces=range(pieces), spans=spans, first=start == 0),
        grid=(begin,),
        in_specs=blocks,
        out_specs=[pl.BlockSpec((tile, size), lambda i: (i + offset, 0)), SMEM],
        out_shape=[pltpu.HBM(slab.shape, BF16), jax.ShapeDtypeStruct((1,), jnp.int32)],
        input_output_aliases=aliases,
        scratch_shapes=[
            pltpu.VMEM((2, tile, size), BF16),
            pltpu.VMEM((tile // 2, 2 * size), BF16),
            pltpu.SemaphoreType.DMA((2,)),
        ],
        compiler_params=pltpu.CompilerParams(vmem_limit_bytes=16 * 2**20),
        cost_estimate=LIGHT,
        name="panel",
    )(*operands)


def broadcast(value, axis, source):
    kept = jnp.where(lax.axis_index(axis) == source, value, 0).astype(value.dtype)
    return lax.psum(kept, axis)


def settings(*values):
    return jnp.stack([jnp.asarray(value).astype(jnp.int32) for value in values])


def holder_pairs(wide, narrow, distance):
    stride = wide // narrow
    found = []
    for n in range(narrow):
        for start in range(0, wide, 2 * distance):
            source = (n * stride) ^ start
            found.append((source * narrow + n, (source ^ distance) * narrow + n))
    return found


class Order:
    def __init__(self, token):
        self.token = token

    def after(self, value):
        value, self.token = lax.optimization_barrier((value, self.token))
        return value


def known_owner(owner, coarse_basis, material_ids, lame_table, coarse_ids, coarse_slab):
    narrow, wide = lax.axis_size("narrow"), lax.axis_size("wide")
    stride = wide // narrow
    wide_index, narrow_index = lax.axis_index("wide"), lax.axis_index("narrow")
    height, block = coarse_slab.shape
    own = wide_index == narrow_index * stride
    later = narrow_index > owner
    which = jnp.where(later, narrow_index - owner - 1, -1)
    mode = jnp.where(narrow_index == owner, 1, jnp.where(later, 2, 0))
    earlier = (wide_index % stride == 0) & (wide_index // stride < owner)
    kind = jnp.where(wide_index == owner * stride, 1, jnp.where(earlier, 2, 0))
    table = lame_table.astype(F32)
    hops = narrow - 1 - owner
    units, joined, waits, plan = PLANS[hops]
    unit = height // sum(units)
    count = len(units)
    bounds, low = [], 0
    for number in units:
        bounds.append((low, low + number * unit))
        low += number * unit
    axes = ("wide", "narrow")

    def rows_of(number):
        low, high = bounds[number]
        return coarse_slab[low:high]

    def send(value, source, target):
        return lax.ppermute(value, "narrow", [(owner + source, owner + target)])

    order = Order(settings(mode))

    holders = [((n * stride) * narrow + owner, (n * stride) * narrow + n) for n in range(owner + 1, narrow)]
    moved = {}

    groups = [[w for w in range(wide) if w % stride == 0], [w for w in range(wide) if w % stride]]
    groups = [group for group in groups if group]
    member = jnp.where(wide_index % stride == 0, 0, 1)

    def within(group, pairs):
        return [(w * narrow + one, w * narrow + two) for w in group for one, two in pairs]

    def halo_of(group, message):
        return lax.ppermute(message, axes, within(group, [(i + 1, i) for i in range(narrow - 1)]))

    spans = [bounds[0], (bounds[1][0], height) if joined else bounds[1]]
    first, last, *begun = halo_message(table, material_ids, order.token, coarse_basis, coarse_slab, spans)
    first = order.after(first)
    halos = [halo_of(groups[0], first)]
    edge = (narrow_index == 0).astype(jnp.int32).reshape(1)
    inner = order.after(interior(edge, table, material_ids, coarse_basis, order.token))
    head = order.after(lax.ppermute(order.after(coarse_slab[:block]), axes, holders))
    halos[0] = order.after(halos[0])
    moved[0] = [send(order.after(begun[0]), 0, hops)]
    for group in groups[1:]:
        halos.append(halo_of(group, order.after(first)))

    def nearest(base, extent):
        return min(range(base, min(base + extent, narrow)), key=lambda n: abs(n - owner))

    def summed(parts, distance, group):
        total = parts[0] if len(parts) == 1 else parts[0] + parts[1]
        pairs = []
        for base in range(0, narrow - distance, 2 * distance):
            one, two = nearest(base, distance), nearest(base + distance, distance)
            pairs.append((two, one) if nearest(base, 2 * distance) == one else (one, two))
        return [total, lax.ppermute(total, axes, within(group, pairs))], 2 * distance

    def faces_of(number):
        flag = settings(member == number)
        return [order.after(face(flag, table, material_ids, last, halos[number], order.token, inner))]

    sums, reach = [faces_of(0)], [1]
    while reach[0] < narrow:
        sums[0], reach[0] = summed(sums[0], reach[0], groups[0])
    sums[0][1] = order.after(sums[0][1])
    distance, messages, left = wide // 2, [], plan.count("spread")
    result, prepared = None, None
    choice = (narrow_index - owner) % narrow
    flags = settings(mode, kind, own, which)
    for step in plan:
        if step[0] == "panel":
            if prepared is None:
                prepared = prepare(settings(choice, mode), order.token, head, summaries)
            weights, rows, lower = prepared
            begin, end = step[1:]
            parts = [moved[number][:: 1 if number else -1] for number in range(begin, end)]
            result, order.token = panel(
                flags, order.token, lower, weights, rows, added if begin == 0 else head, coarse_slab, parts, result, bounds[begin][0], 2 * unit
            )
        elif step == "added":
            added = added_of(settings(mode), order.token, coarse_ids, galerkin, block)
            added = order.after(lax.ppermute(added, axes, holders))
            if waits:
                moved[count - 1] = [send(order.after(rows_of(count - 1)), 0, 1)]
        elif step == "sums":
            galerkins = [order.after(part) for part in galerkins]
            galerkin = jnp.where(narrow_index == owner, galerkin, sum(galerkins))
        elif step == "next":
            if joined:
                whole = send(order.after(begun[1]), 0, 1)
            else:
                moved[1] = [send(order.after(begun[1]), 0, 1)]
                for number in range(2, count - waits):
                    moved[number] = [send(order.after(rows_of(number)), 0, 1)]
        elif step == "assemble":
            message = assemble(settings(mode, own), order.token, coarse_ids, coarse_slab, head, sums[0])
            message = order.after(message)
        elif step == "others":
            for number in range(1, len(groups)):
                halos[number] = order.after(halos[number])
                parts, far = summed(faces_of(number), 1, groups[number])
                sums.append(parts)
                reach.append(far)
        elif step == "more":
            for number in range(1, len(groups)):
                while reach[number] < narrow:
                    sums[number][1] = order.after(sums[number][1])
                    sums[number], reach[number] = summed(sums[number], reach[number], groups[number])
        elif step == "spread":
            left -= 1
            while distance:
                received = order.after(lax.ppermute(message, axes, holder_pairs(wide, narrow, distance)))
                messages = [message, received]
                if distance > 1:
                    message = message + received
                distance //= 2
                if left:
                    break
        elif step == "factor":
            summary, head, galerkin = factorize(settings(mode, member), order.token, messages, sums)
            summary = order.after(summary)
            ways = [[(owner, (owner + place) % narrow)] for place in range(1, narrow)]
            summaries = [summary] + [lax.ppermute(summary, "narrow", way) for way in ways]
        elif step == "summary":
            for place in range(1, narrow):
                summaries[place] = order.after(summaries[place])
            galerkin = order.after(galerkin)
            galerkins = [lax.ppermute(galerkin, "narrow", way) for way in ways]
        else:
            number, hop = step
            if joined and step == (1, 0):
                whole = order.after(whole)
                for part in range(1, count):
                    low, high = (bound - bounds[1][0] for bound in bounds[part])
                    moved[part] = [whole[low:high]]
            moving = moved[number][hop] = order.after(moved[number][hop])
            if number == 0 and hop + 1 < hops:
                moved[number].append(send(moving, hops - hop, hops - hop - 1))
            elif number != 0 and hop + 1 < hops:
                moved[number].append(send(moving, hop + 1, hop + 2))
    return result, galerkin


def any_owner(owner, coarse_basis, material_ids, lame_table, coarse_ids, coarse_slab):
    narrow, wide = lax.axis_size("narrow"), lax.axis_size("wide")
    stride = wide // narrow
    wide_index, narrow_index = lax.axis_index("wide"), lax.axis_index("narrow")
    own = wide_index == narrow_index * stride
    later = narrow_index > owner
    which = jnp.where(later, 0, -1)
    mode = jnp.where(narrow_index == owner, 1, jnp.where(later, 2, 0))
    earlier = (wide_index % stride == 0) & (wide_index // stride < owner)
    kind = jnp.where(wide_index == owner * stride, 1, jnp.where(earlier, 2, 0))
    table = lame_table.astype(F32)
    column = broadcast(coarse_slab, "narrow", owner)
    first, last = halo_message(table, material_ids, table, coarse_basis, coarse_slab, ())
    halo = lax.ppermute(first, "narrow", [(i + 1, i) for i in range(narrow - 1)])
    edge = (narrow_index == 0).astype(jnp.int32).reshape(1)
    inner = interior(edge, table, material_ids, coarse_basis, first)
    partial = face(settings(1), table, material_ids, last, halo, first, inner)
    parts = [lax.psum(partial, "narrow")]
    message = assemble(settings(mode, own), first, coarse_ids, coarse_slab, column, parts)
    at_owner = (wide_index == owner * stride) & (narrow_index == owner)
    diagonal = lax.psum(jnp.where(at_owner, message, 0.0), ("wide", "narrow"))
    summary, _, galerkin = factorize(settings(1, 0), first, [diagonal], [parts])
    head = broadcast(message, "wide", narrow_index * stride)
    weights, rows, lower = prepare(settings(0, mode), settings(mode), head, [summary])
    added = added_of(settings(1), weights, coarse_ids, galerkin, head.shape[0])
    flags = settings(mode, kind, own, which)
    tile = coarse_slab.shape[0] // 12
    result, _ = panel(flags, flags, lower, weights, rows, added, coarse_slab, [[column]], None, 0, tile)
    return result, galerkin


def on_device(coarse_basis, material_ids, lame_table, coarse_ids, coarse_slab, panel_owner):
    narrow, wide = lax.axis_size("narrow"), lax.axis_size("wide")
    arrays = (coarse_basis, material_ids, lame_table, coarse_ids, coarse_slab)
    owner = panel_owner[0]
    if narrow - 1 > len(PLANS) or wide & (wide - 1):
        return any_owner(owner, *arrays)
    branches = [functools.partial(known_owner, place) for place in range(narrow - 1)]
    return lax.switch(owner, branches, *arrays)


def solution(mesh):
    return jax.shard_map(
        on_device,
        mesh=mesh,
        in_specs=(
            P("wide", None, None, "narrow", None, None),
            P("wide", "narrow", None, None),
            P(),
            P("wide", None),
            P("wide", "narrow"),
            P(),
        ),
        out_specs=(P("wide", "narrow"), P("wide", None, None)),
        check_vma=False,
    )
```

```python
import functools

import jax
import jax.numpy as jnp
from jax import lax
from jax.experimental import pallas as pl
from jax.experimental.pallas import tpu as pltpu
from jax.sharding import PartitionSpec as P

F32, BF16 = jnp.float32, jnp.bfloat16
NT = (((1,), (1,)), ((), ()))
TN = (((0,), (0,)), ((), ()))
VMEM = pl.BlockSpec(memory_space=pltpu.VMEM)
ANY = pl.BlockSpec(memory_space=pl.ANY)
SMEM = pl.BlockSpec(memory_space=pltpu.SMEM)
PLANS = {
    1: (
        (12, 8, 4),
        False,
        True,
        (
            "assemble", "next", "spread", "others", "spread", "more", "spread", (0, 0), "factor", "summary",
            "added", ("panel", 0, 2), "sums", ("panel", 2, 3),
        ),
    ),
    2: (
        (12, 6, 4, 2),
        False,
        True,
        (
            "assemble", "next", "spread", "others", "spread", "more", "spread", (0, 0), (1, 0), "factor", (2, 0),
            "summary", "added", ("panel", 1, 2), (3, 0), ("panel", 0, 1), "sums", ("panel", 2, 4),
        ),
    ),
    3: (
        (12, 8, 4),
        False,
        False,
        (
            "assemble", "next", "spread", "others", "spread", "more", "spread", (0, 0), (1, 0), "factor", (0, 1),
            (2, 0), (1, 1), "summary", "added", (2, 1), ("panel", 1, 2), ("panel", 0, 1), "sums", ("panel", 2, 3),
        ),
    ),
}
BLOCK = 16
LIGHT = pl.CostEstimate(flops=1, bytes_accessed=1, transcendentals=0)


def exact_dot(left, right, dims=(((1,), (0,)), ((), ()))):
    return lax.dot_general(
        left, right, dims, precision=lax.Precision.HIGHEST, preferred_element_type=F32
    )


def dot(left, right, dims=(((1,), (0,)), ((), ()))):
    return lax.dot_general(left, right, dims, preferred_element_type=F32)


def split_two(value):
    high = value.astype(BF16)
    return high, (value - high.astype(F32)).astype(BF16)


def lame_of(ids, table_ref):
    shear = jnp.zeros(ids.shape, F32)
    dilate = jnp.zeros(ids.shape, F32)
    for material in range(table_ref.shape[1]):
        chosen = ids == material
        shear = jnp.where(chosen, table_ref[0, material], shear)
        dilate = jnp.where(chosen, table_ref[1, material], dilate)
    return shear, dilate


def halo_kernel(table_ref, ids_ref, token_ref, basis_ref, slab_ref, out_ref, last_ref, *rest, spans):
    piece_refs, sems = rest[:-1], rest[-1]
    subs, funcs, comps, layers = basis_ref.shape[0:4]
    copies = []
    for number, ((low, high), piece_ref) in enumerate(zip(spans, piece_refs)):
        copies.append(pltpu.make_async_copy(slab_ref.at[pl.ds(low, high - low)], piece_ref, sems.at[number]))
        copies[-1].start()
    for sub in range(subs):
        for comp in range(comps):
            out_ref[sub, comp * funcs : (comp + 1) * funcs] = basis_ref[sub, :, comp, 0]
            last_ref[sub, comp * funcs : (comp + 1) * funcs] = basis_ref[sub, :, comp, layers - 1]
        shear, dilate = lame_of(ids_ref[sub, 0], table_ref)
        out_ref[sub, comps * funcs] = shear.astype(BF16)
        out_ref[sub, comps * funcs + 1] = dilate.astype(BF16)
    for copy in copies:
        copy.wait()


def halo_message(table, ids, token, basis, slab, spans):
    subs, funcs, comps, layers, ny, nz = basis.shape
    return pl.pallas_call(
        functools.partial(halo_kernel, spans=spans),
        in_specs=[SMEM, VMEM, ANY, VMEM, ANY],
        out_specs=[VMEM] * (2 + len(spans)),
        out_shape=[
            jax.ShapeDtypeStruct((subs, comps * funcs + 2, ny, nz), BF16),
            jax.ShapeDtypeStruct((subs, comps * funcs, ny, nz), BF16),
        ]
        + [jax.ShapeDtypeStruct((high - low, slab.shape[1]), BF16) for low, high in spans],
        scratch_shapes=[pltpu.SemaphoreType.DMA((max(1, len(spans)),))],
        compiler_params=pltpu.CompilerParams(vmem_limit_bytes=16 * 2**20),
        cost_estimate=LIGHT,
        name="halo_message",
    )(table, ids, token, basis, slab)


def interior_kernel(edge_ref, table_ref, ids_ref, basis_ref, token_ref, out_ref, fields, turned, coef, left, right, acc):
    sub, comp = pl.program_id(0), pl.program_id(1)
    layers, ny, nz = basis_ref.shape[3:]
    funcs = basis_ref.shape[1]
    row = lax.broadcasted_iota(jnp.int32, (ny, nz), 0)
    lane = lax.broadcasted_iota(jnp.int32, (ny, nz), 1)
    table = [lame_of(ids_ref[sub, x], table_ref) for x in range(layers)]

    def weight(one, two, direction):
        shear = 0.5 * (one[0] + two[0])
        dilate = 0.5 * (one[1] + two[1])
        return shear + jnp.where(comp == direction, shear + dilate, 0.0)

    def ahead(field, axis):
        size = field.shape[axis]
        index = row if axis == 0 else lane
        return jnp.where(index == size - 1, 0.0, pltpu.roll(field, size - 1, axis=axis))

    def behind(field, axis):
        index = row if axis == 0 else lane
        return jnp.where(index == 0, 0.0, pltpu.roll(field, 1, axis=axis))

    nothing = (jnp.zeros((ny, nz), F32),) * 2
    previous = weight(table[0], nothing, 0) * edge_ref[0].astype(F32)
    for x in range(layers):
        diagonal = previous
        forward = []
        if x + 1 < layers:
            face = weight(table[x], table[x + 1], 0)
            diagonal = diagonal + face
            previous = face
            forward.append(face)
        else:
            forward.append(jnp.zeros((ny, nz), F32))
        for axis in (0, 1):
            index, size = (row, ny) if axis == 0 else (lane, nz)
            other = tuple(ahead(value, axis) for value in table[x])
            face = weight(table[x], other, axis + 1)
            before = tuple(behind(value, axis) for value in table[x])
            diagonal = diagonal + face + weight(table[x], before, axis + 1)
            forward.append(jnp.where(index == size - 1, 0.0, face))
        coef[x, 0] = 0.5 * diagonal
        for kind in range(3):
            coef[x, kind + 1] = forward[kind]
        fields[x] = basis_ref[sub, :, comp, x].astype(F32).reshape(funcs * ny, nz)

    total = None
    for x in reversed(range(layers)):
        values = [fields[x, pl.ds(y, funcs, stride=ny), :] for y in range(ny)]
        for y in range(ny):
            value = values[y]
            turned[x % 2, y] = value
            image = coef[x, 0, y : y + 1, :] * value
            image = image - coef[x, 3, y : y + 1, :] * pltpu.roll(value, nz - 1, axis=1)
            if y + 1 < ny:
                image = image - coef[x, 2, y : y + 1, :] * values[y + 1]
            if x + 1 < layers:
                image = image - coef[x, 1, y : y + 1, :] * turned[(x + 1) % 2, y]
            high, low = split_two(image)
            left[:, y * nz : (y + 1) * nz] = value.astype(BF16)
            right[0:funcs, y * nz : (y + 1) * nz] = high
            right[funcs : 2 * funcs, y * nz : (y + 1) * nz] = low
        product = dot(right[...], left[...], NT)
        total = product if total is None else total + product

    @pl.when(comp == 0)
    def _():
        acc[...] = total

    @pl.when(comp > 0)
    def _():
        acc[...] += total

    @pl.when(comp == pl.num_programs(1) - 1)
    def _():
        out_ref[0] = acc[0:funcs] + acc[funcs : 2 * funcs]


def interior(edge, table, ids, basis, token):
    subs, funcs, comps, layers, ny, nz = basis.shape
    return pl.pallas_call(
        interior_kernel,
        grid=(subs, comps),
        in_specs=[SMEM, SMEM, VMEM, VMEM, ANY],
        out_specs=pl.BlockSpec((1, funcs, funcs), lambda s, c: (s, 0, 0)),
        out_shape=jax.ShapeDtypeStruct((subs, funcs, funcs), F32),
        scratch_shapes=[
            pltpu.VMEM((layers, funcs * ny, nz), F32),
            pltpu.VMEM((2, ny, funcs, nz), F32),
            pltpu.VMEM((layers, 4, ny, nz), F32),
            pltpu.VMEM((funcs, ny * nz), BF16),
            pltpu.VMEM((2 * funcs, ny * nz), BF16),
            pltpu.VMEM((2 * funcs, funcs), F32),
        ],
        compiler_params=pltpu.CompilerParams(vmem_limit_bytes=16 * 2**20),
        cost_estimate=LIGHT,
        name="interior",
    )(edge, table, ids, basis, token)


def face_kernel(flags_ref, table_ref, ids_ref, last_ref, halo_ref, token_ref, inner_ref, out_ref, *scratch):
    @pl.when(flags_ref[0] == 1)
    def _():
        last, halo, sems = scratch[-3:]
        copies = [
            pltpu.make_async_copy(last_ref, last, sems.at[0]),
            pltpu.make_async_copy(halo_ref, halo, sems.at[1]),
        ]
        for copy in copies:
            copy.start()
        for copy in copies:
            copy.wait()
        face_sums(table_ref, ids_ref, last, halo, inner_ref, out_ref, *scratch[:-3])


def face_sums(table_ref, ids_ref, last_ref, halo_ref, inner_ref, out_ref, mine, theirs, left, right, weights, acc):
    subs, layers, ny, nz = ids_ref.shape
    funcs = inner_ref.shape[1]
    comps = last_ref.shape[1] // funcs

    @pl.loop(0, subs)
    def _(sub):
        shear, dilate = lame_of(ids_ref[sub, layers - 1], table_ref)
        weights[0] = 0.5 * (shear + halo_ref[sub, comps * funcs].astype(F32))
        weights[1] = 0.5 * (dilate + halo_ref[sub, comps * funcs + 1].astype(F32))

        @pl.loop(0, comps)
        def _(comp):
            weight = weights[0] + jnp.where(comp == 0, weights[0] + weights[1], 0.0)
            rows = pl.ds(comp * funcs, funcs)
            mine[...] = last_ref[sub, rows].astype(F32).reshape(funcs * ny, nz)
            theirs[...] = halo_ref[sub, rows].astype(F32).reshape(funcs * ny, nz)
            for y in range(ny):
                here = mine[pl.ds(y, funcs, stride=ny), :]
                there = theirs[pl.ds(y, funcs, stride=ny), :]
                high, low = split_two(weight[y : y + 1, :] * (here - there))
                left[0:funcs, y * nz : (y + 1) * nz] = here.astype(BF16)
                left[funcs : 2 * funcs, y * nz : (y + 1) * nz] = there.astype(BF16)
                right[0:funcs, y * nz : (y + 1) * nz] = high
                right[funcs : 2 * funcs, y * nz : (y + 1) * nz] = low
            product = dot(right[...], left[...], NT)

            @pl.when(comp == 0)
            def _():
                acc[...] = product

            @pl.when(comp > 0)
            def _():
                acc[...] += product

        total = acc[:, 0:funcs] - acc[:, funcs : 2 * funcs]
        half = inner_ref[sub] + 0.5 * (total[0:funcs] + total[funcs : 2 * funcs])
        out_ref[sub] = half + half.T


def face(flags, table, ids, last, halo, token, inner):
    subs, layers, ny, nz = ids.shape
    funcs = inner.shape[1]
    return pl.pallas_call(
        face_kernel,
        in_specs=[SMEM, SMEM, VMEM, ANY, ANY, ANY, VMEM],
        out_specs=VMEM,
        out_shape=jax.ShapeDtypeStruct((subs, funcs, funcs), F32),
        scratch_shapes=[
            pltpu.VMEM((funcs * ny, nz), F32),
            pltpu.VMEM((funcs * ny, nz), F32),
            pltpu.VMEM((2 * funcs, ny * nz), BF16),
            pltpu.VMEM((2 * funcs, ny * nz), BF16),
            pltpu.VMEM((2, ny, nz), F32),
            pltpu.VMEM((2 * funcs, 2 * funcs), F32),
            pltpu.VMEM(last.shape, BF16),
            pltpu.VMEM(halo.shape, BF16),
            pltpu.SemaphoreType.DMA((2,)),
        ],
        compiler_params=pltpu.CompilerParams(vmem_limit_bytes=16 * 2**20),
        cost_estimate=LIGHT,
        name="face",
    )(flags, table, ids, last, halo, token, inner)


def spread(gal_ref, column_ids_ref, row_ids_ref, size):
    subs, funcs = column_ids_ref.shape[0:2]
    added = jnp.zeros((size, size), F32)
    lane = lax.broadcasted_iota(jnp.int32, (funcs, size), 1)
    row = lax.broadcasted_iota(jnp.int32, (size, funcs), 0)
    for sub in range(subs):
        slots = (column_ids_ref[sub] == lane).astype(F32)
        slots_t = (row_ids_ref[sub] == row).astype(F32)
        added = added + exact_dot(slots_t, exact_dot(gal_ref[sub], slots))
    return added


def assemble_kernel(flags_ref, token_ref, column_ids_ref, row_ids_ref, slab_ref, head_ref, *rest):
    gal_refs, (message_ref, sum_ref) = rest[:-2], rest[-2:]
    size = message_ref.shape[0]
    mode, own = flags_ref[0], flags_ref[1]
    message_ref[...] = jnp.zeros_like(message_ref)

    @pl.when((mode == 1) & (own == 1))
    def _():
        total = gal_refs[0][...]
        for gal_ref in gal_refs[1:]:
            total = total + gal_ref[...]
        sum_ref[...] = total
        added = spread(sum_ref, column_ids_ref, row_ids_ref, size)
        message_ref[...] = added + slab_ref[...].astype(F32)

    @pl.when((mode == 2) & (own == 1))
    def _():
        message_ref[...] = head_ref[...].astype(F32)


def assemble(flags, token, ids, slab, head, parts):
    size = slab.shape[1]
    block = pl.BlockSpec((size, size), lambda i: (0, 0))
    return pl.pallas_call(
        assemble_kernel,
        grid=(1,),
        in_specs=[SMEM, ANY, VMEM, VMEM, block, block] + [VMEM] * len(parts),
        out_specs=VMEM,
        out_shape=jax.ShapeDtypeStruct((size, size), F32),
        scratch_shapes=[pltpu.VMEM(parts[0].shape, F32)],
        cost_estimate=LIGHT,
        name="assemble",
    )(flags, token, ids[:, :, None], ids[:, None, :], slab, head, *parts)


def factor_kernel(flags_ref, token_ref, *refs, parts, groups):
    message_refs, gal_refs = refs[:parts], refs[parts:-4]
    summary_ref, block_ref, sum_ref, work = refs[-4:]
    subs, funcs = gal_refs[0].shape[0:2]
    size = summary_ref.shape[1]
    diagonal = message_refs[0][...]
    for message_ref in message_refs[1:]:
        diagonal = diagonal + message_ref[...]
    block_ref[...] = diagonal

    @pl.when(flags_ref[0] == 1)
    def _():
        row = lax.broadcasted_iota(jnp.int32, (size, size), 0)
        lane = lax.broadcasted_iota(jnp.int32, (size, size), 1)
        work[:, 0:size] = 0.5 * (diagonal + diagonal.T)
        work[:, size : 2 * size] = (row == lane).astype(F32)
        index = lax.broadcasted_iota(jnp.int32, (BLOCK, size), 0)
        for start in range(0, size, BLOCK):
            panel = work[start : start + BLOCK, 0:size]
            extra = work[start : start + BLOCK, size : 2 * size]
            columns = [
                jnp.broadcast_to(panel[:, start + step : start + step + 1], (BLOCK, size))
                for step in range(BLOCK)
            ]
            for step in range(BLOCK):
                scale = lax.rsqrt(columns[step][step : step + 1, :])
                column = jnp.where(index > step, columns[step] * scale, 0.0)
                for later in range(step + 1, BLOCK):
                    columns[later] = columns[later] - column * column[later : later + 1, :]
                pivot = panel[step : step + 1, :] * scale
                panel = jnp.where(index == step, pivot, panel - column * pivot)
                pivot = extra[step : step + 1, :] * scale
                extra = jnp.where(index == step, pivot, extra - column * pivot)
            work[start : start + BLOCK, 0:size] = panel
            work[start : start + BLOCK, size : 2 * size] = extra
            rest = start + BLOCK
            if rest < size:
                both = jnp.concatenate([panel, extra], axis=1)
                work[rest:size, :] -= exact_dot(panel[:, rest:size], both, TN)
        upper = jnp.where(row <= lane, work[:, 0:size], 0.0)
        inverse = jnp.where(row >= lane, work[:, size : 2 * size], 0.0).T
        high = inverse.astype(BF16)
        summary_ref[0:size] = high
        summary_ref[size : 2 * size] = (inverse - high.astype(F32)).astype(BF16)
        summary_ref[2 * size : 3 * size] = upper.T.astype(BF16)
        each = len(gal_refs) // groups
        for group in range(groups):

            @pl.when(flags_ref[1] == group)
            def _(chosen=gal_refs[group * each : (group + 1) * each]):
                total = chosen[0][...]
                for gal_ref in chosen[1:]:
                    total = total + gal_ref[...]
                sum_ref[...] = total


def factorize(flags, token, messages, groups):
    size = messages[0].shape[1]
    subs, funcs = groups[0][0].shape[0:2]
    parts = [part for group in groups for part in group]
    return pl.pallas_call(
        functools.partial(factor_kernel, parts=len(messages), groups=len(groups)),
        in_specs=[SMEM, ANY] + [VMEM] * (len(messages) + len(parts)),
        out_specs=[VMEM] * 3,
        out_shape=[
            jax.ShapeDtypeStruct((3 * size, size), BF16),
            jax.ShapeDtypeStruct((size, size), F32),
            jax.ShapeDtypeStruct(groups[0][0].shape, F32),
        ],
        scratch_shapes=[pltpu.VMEM((size, 2 * size), F32)],
        cost_estimate=LIGHT,
        name="factorize",
    )(flags, token, *messages, *parts)


def prepare_kernel(flags_ref, token_ref, head_ref, *rest, sources):
    summary_refs = rest[:sources]
    weights_ref, rows_ref, lower_ref, summary, sem = rest[sources:]
    size = head_ref.shape[0]
    choice, mode = flags_ref[0], flags_ref[1]
    for number, summary_ref in enumerate(summary_refs):

        @pl.when(choice == number)
        def _(summary_ref=summary_ref):
            copy = pltpu.make_async_copy(summary_ref, summary, sem)
            copy.start()
            copy.wait()

    def doubled(block):
        nothing = jnp.zeros((size, size), BF16)
        top = jnp.concatenate([block, nothing], axis=1)
        return jnp.concatenate([top, jnp.concatenate([nothing, block], axis=1)], axis=0)

    @pl.when(mode > 0)
    def _():
        weights_ref[0 : 2 * size] = doubled(summary[0:size])
        weights_ref[2 * size : 4 * size] = doubled(summary[size : 2 * size])
        lower_ref[...] = summary[2 * size : 3 * size]

    @pl.when(mode == 2)
    def _():
        inverse = summary[0:size].astype(F32) + summary[size : 2 * size].astype(F32)
        solved = exact_dot(head_ref[...], inverse)
        rows_ref[...] = doubled(solved.T.astype(BF16))


def prepare(flags, token, head, summaries):
    size = head.shape[0]
    return pl.pallas_call(
        functools.partial(prepare_kernel, sources=len(summaries)),
        in_specs=[SMEM, ANY, VMEM] + [ANY] * len(summaries),
        out_specs=[VMEM] * 3,
        out_shape=[
            jax.ShapeDtypeStruct((4 * size, 2 * size), BF16),
            jax.ShapeDtypeStruct((2 * size, 2 * size), BF16),
            jax.ShapeDtypeStruct((size, size), BF16),
        ],
        scratch_shapes=[pltpu.VMEM(summaries[0].shape, BF16), pltpu.SemaphoreType.DMA],
        compiler_params=pltpu.CompilerParams(vmem_limit_bytes=16 * 2**20),
        cost_estimate=LIGHT,
        name="prepare",
    )(flags, token, head, *summaries)


def added_kernel(flags_ref, token_ref, column_ids_ref, row_ids_ref, sum_ref, added_ref):
    @pl.when(flags_ref[0] == 1)
    def _():
        added_ref[...] = spread(sum_ref, column_ids_ref, row_ids_ref, added_ref.shape[0])


def added_of(flags, token, ids, galerkin, size):
    return pl.pallas_call(
        added_kernel,
        in_specs=[SMEM, ANY, VMEM, VMEM, VMEM],
        out_specs=VMEM,
        out_shape=jax.ShapeDtypeStruct((size, size), F32),
        cost_estimate=LIGHT,
        name="added",
    )(flags, token, ids[:, :, None], ids[:, None, :], galerkin)


def panel_kernel(
    flags_ref, token_ref, lower_ref, weights_ref, rows_ref, added_ref, slab_ref, *rest, pieces, spans, first
):
    hops = len(pieces) // len(spans)
    others = rest[: len(pieces)]
    out_ref, done_ref, column, factor, sems = rest[-5:]
    done_ref[0] = flags_ref[0]
    tile, size = out_ref.shape
    half = tile // 2
    mode, head, own, which = flags_ref[0], flags_ref[1], flags_ref[2], flags_ref[3]
    step, steps = pl.program_id(0), pl.num_programs(0)
    top = first & (step == 0)

    def copy_of(at, act):
        for number, (begin, end) in enumerate(spans):
            for hop in range(hops):

                @pl.when((mode == 2) & (which == hop) & (at >= begin) & (at < end))
                def _(other_ref=others[number * hops + hop], begin=begin):
                    source = other_ref.at[pl.ds(pl.multiple_of((at - begin) * tile, tile), tile)]
                    act(pltpu.make_async_copy(source, column.at[at % 2], sems.at[at % 2]))

    @pl.when(step == 0)
    def _():
        copy_of(step, lambda copy: copy.start())

    @pl.when(step + 1 < steps)
    def _():
        copy_of(step + 1, lambda copy: copy.start())

    @pl.when(mode == 0)
    def _():
        out_ref[...] = slab_ref[...]

    @pl.when(mode == 1)
    def _():
        column[step % 2] = slab_ref[...]

    @pl.when(mode == 2)
    def _():
        copy_of(step, lambda copy: copy.wait())

    @pl.when(mode > 0)
    def _():
        value = column[step % 2]
        pair = jnp.concatenate([value[0:half], value[half:tile]], axis=1)
        factor[...] = dot(jnp.concatenate([pair, pair], axis=1), weights_ref[...]).astype(BF16)

        @pl.when(top & (head == 1))
        def _():
            factor[0:size, 0:size] = lower_ref[...]

        @pl.when(top & (head == 2))
        def _():
            factor[0:size, 0:size] = jnp.zeros((size, size), BF16)

    @pl.when(mode == 1)
    def _():
        out_ref[0:half] = factor[:, 0:size]
        out_ref[half:tile] = factor[:, size : 2 * size]

    @pl.when(mode == 2)
    def _():
        update = dot(factor[...], rows_ref[...])
        out_ref[0:half] = (slab_ref[0:half].astype(F32) - update[:, 0:size]).astype(BF16)
        out_ref[half:tile] = (slab_ref[half:tile].astype(F32) - update[:, size : 2 * size]).astype(BF16)

        @pl.when(top & (own == 1))
        def _():
            base = slab_ref[0:size].astype(F32) + added_ref[...]
            out_ref[0:size] = (base - update[0:size, 0:size]).astype(BF16)


def panel(flags, token, lower, weights, rows, added, slab, parts, old, start, tile):
    size = slab.shape[1]
    offset = start // tile
    spans, begin, operands = [], 0, []
    for hops in parts:
        end = begin + hops[0].shape[0] // tile
        spans.append((begin, end))
        begin = end
        operands += hops
    blocks = [
        SMEM,
        ANY,
        pl.BlockSpec((size, size), lambda i: (0, 0)),
        pl.BlockSpec(weights.shape, lambda i: (0, 0)),
        pl.BlockSpec(rows.shape, lambda i: (0, 0)),
        pl.BlockSpec((size, size), lambda i: (0, 0)),
        pl.BlockSpec((tile, size), lambda i: (i + offset, 0)),
    ] + [ANY] * len(operands)
    pieces = len(operands)
    operands = [flags, token, lower, weights, rows, added, slab] + operands
    aliases = {}
    if old is not None:
        aliases = {len(operands): 0}
        blocks.append(ANY)
        operands.append(old)
    return pl.pallas_call(
        functools.partial(panel_kernel, pieces=range(pieces), spans=spans, first=start == 0),
        grid=(begin,),
        in_specs=blocks,
        out_specs=[pl.BlockSpec((tile, size), lambda i: (i + offset, 0)), SMEM],
        out_shape=[pltpu.HBM(slab.shape, BF16), jax.ShapeDtypeStruct((1,), jnp.int32)],
        input_output_aliases=aliases,
        scratch_shapes=[
            pltpu.VMEM((2, tile, size), BF16),
            pltpu.VMEM((tile // 2, 2 * size), BF16),
            pltpu.SemaphoreType.DMA((2,)),
        ],
        compiler_params=pltpu.CompilerParams(vmem_limit_bytes=16 * 2**20),
        cost_estimate=LIGHT,
        name="panel",
    )(*operands)


def broadcast(value, axis, source):
    kept = jnp.where(lax.axis_index(axis) == source, value, 0).astype(value.dtype)
    return lax.psum(kept, axis)


def settings(*values):
    return jnp.stack([jnp.asarray(value).astype(jnp.int32) for value in values])


def holder_pairs(wide, narrow, distance):
    stride = wide // narrow
    found = []
    for n in range(narrow):
        for start in range(0, wide, 2 * distance):
            source = (n * stride) ^ start
            found.append((source * narrow + n, (source ^ distance) * narrow + n))
    return found


class Order:
    def __init__(self, token):
        self.token = token

    def after(self, value):
        value, self.token = lax.optimization_barrier((value, self.token))
        return value


def known_owner(owner, coarse_basis, material_ids, lame_table, coarse_ids, coarse_slab):
    narrow, wide = lax.axis_size("narrow"), lax.axis_size("wide")
    stride = wide // narrow
    wide_index, narrow_index = lax.axis_index("wide"), lax.axis_index("narrow")
    height, block = coarse_slab.shape
    own = wide_index == narrow_index * stride
    later = narrow_index > owner
    which = jnp.where(later, narrow_index - owner - 1, -1)
    mode = jnp.where(narrow_index == owner, 1, jnp.where(later, 2, 0))
    earlier = (wide_index % stride == 0) & (wide_index // stride < owner)
    kind = jnp.where(wide_index == owner * stride, 1, jnp.where(earlier, 2, 0))
    table = lame_table.astype(F32)
    hops = narrow - 1 - owner
    units, joined, waits, plan = PLANS[hops]
    unit = height // sum(units)
    tile = (2 if any(number % 4 for number in units) else 4) * unit
    count = len(units)
    bounds, low = [], 0
    for number in units:
        bounds.append((low, low + number * unit))
        low += number * unit
    axes = ("wide", "narrow")

    def rows_of(number):
        low, high = bounds[number]
        return coarse_slab[low:high]

    def send(value, source, target):
        return lax.ppermute(value, "narrow", [(owner + source, owner + target)])

    order = Order(settings(mode))

    holders = [((n * stride) * narrow + owner, (n * stride) * narrow + n) for n in range(owner + 1, narrow)]
    moved = {}

    groups = [[w for w in range(wide) if w % stride == 0], [w for w in range(wide) if w % stride]]
    groups = [group for group in groups if group]
    member = jnp.where(wide_index % stride == 0, 0, 1)

    def within(group, pairs):
        return [(w * narrow + one, w * narrow + two) for w in group for one, two in pairs]

    def halo_of(group, message):
        return lax.ppermute(message, axes, within(group, [(i + 1, i) for i in range(narrow - 1)]))

    spans = [bounds[0], (bounds[1][0], height) if joined else bounds[1]]
    first, last, *begun = halo_message(table, material_ids, order.token, coarse_basis, coarse_slab, spans)
    first = order.after(first)
    halos = [halo_of(groups[0], first)]
    edge = (narrow_index == 0).astype(jnp.int32).reshape(1)
    inner = order.after(interior(edge, table, material_ids, coarse_basis, order.token))
    head = order.after(lax.ppermute(order.after(coarse_slab[:block]), axes, holders))
    halos[0] = order.after(halos[0])
    moved[0] = [send(order.after(begun[0]), 0, hops)]
    for group in groups[1:]:
        halos.append(halo_of(group, order.after(first)))

    def nearest(base, extent):
        return min(range(base, min(base + extent, narrow)), key=lambda n: abs(n - owner))

    def summed(parts, distance, group):
        total = parts[0] if len(parts) == 1 else parts[0] + parts[1]
        pairs = []
        for base in range(0, narrow - distance, 2 * distance):
            one, two = nearest(base, distance), nearest(base + distance, distance)
            pairs.append((two, one) if nearest(base, 2 * distance) == one else (one, two))
        return [total, lax.ppermute(total, axes, within(group, pairs))], 2 * distance

    def faces_of(number):
        flag = settings(member == number)
        return [order.after(face(flag, table, material_ids, last, halos[number], order.token, inner))]

    sums, reach = [faces_of(0)], [1]
    while reach[0] < narrow:
        sums[0], reach[0] = summed(sums[0], reach[0], groups[0])
    sums[0][1] = order.after(sums[0][1])
    distance, messages, left = wide // 2, [], plan.count("spread")
    result, prepared = None, None
    choice = (narrow_index - owner) % narrow
    flags = settings(mode, kind, own, which)
    for step in plan:
        if step[0] == "panel":
            if prepared is None:
                prepared = prepare(settings(choice, mode), order.token, head, summaries)
            weights, rows, lower = prepared
            begin, end = step[1:]
            parts = [moved[number][:: 1 if number else -1] for number in range(begin, end)]
            result, order.token = panel(
                flags, order.token, lower, weights, rows, added if begin == 0 else head, coarse_slab, parts, result, bounds[begin][0], tile
            )
        elif step == "added":
            added = added_of(settings(mode), order.token, coarse_ids, galerkin, block)
            added = order.after(lax.ppermute(added, axes, holders))
            if waits:
                moved[count - 1] = [send(order.after(rows_of(count - 1)), 0, 1)]
        elif step == "sums":
            galerkins = [order.after(part) for part in galerkins]
            galerkin = jnp.where(narrow_index == owner, galerkin, sum(galerkins))
        elif step == "next":
            if joined:
                whole = send(order.after(begun[1]), 0, 1)
            else:
                moved[1] = [send(order.after(begun[1]), 0, 1)]
                for number in range(2, count - waits):
                    moved[number] = [send(order.after(rows_of(number)), 0, 1)]
        elif step == "assemble":
            message = assemble(settings(mode, own), order.token, coarse_ids, coarse_slab, head, sums[0])
            message = order.after(message)
        elif step == "others":
            for number in range(1, len(groups)):
                halos[number] = order.after(halos[number])
                parts, far = summed(faces_of(number), 1, groups[number])
                sums.append(parts)
                reach.append(far)
        elif step == "more":
            for number in range(1, len(groups)):
                while reach[number] < narrow:
                    sums[number][1] = order.after(sums[number][1])
                    sums[number], reach[number] = summed(sums[number], reach[number], groups[number])
        elif step == "spread":
            left -= 1
            while distance:
                received = order.after(lax.ppermute(message, axes, holder_pairs(wide, narrow, distance)))
                messages = [message, received]
                if distance > 1:
                    message = message + received
                distance //= 2
                if left:
                    break
        elif step == "factor":
            summary, head, galerkin = factorize(settings(mode, member), order.token, messages, sums)
            summary = order.after(summary)
            ways = [[(owner, (owner + place) % narrow)] for place in range(1, narrow)]
            summaries = [summary] + [lax.ppermute(summary, "narrow", way) for way in ways]
        elif step == "summary":
            for place in range(1, narrow):
                summaries[place] = order.after(summaries[place])
            galerkin = order.after(galerkin)
            galerkins = [lax.ppermute(galerkin, "narrow", way) for way in ways]
        else:
            number, hop = step
            if joined and step == (1, 0):
                whole = order.after(whole)
                for part in range(1, count):
                    low, high = (bound - bounds[1][0] for bound in bounds[part])
                    moved[part] = [whole[low:high]]
            moving = moved[number][hop] = order.after(moved[number][hop])
            if number == 0 and hop + 1 < hops:
                moved[number].append(send(moving, hops - hop, hops - hop - 1))
            elif number != 0 and hop + 1 < hops:
                moved[number].append(send(moving, hop + 1, hop + 2))
    return result, galerkin


def any_owner(owner, coarse_basis, material_ids, lame_table, coarse_ids, coarse_slab):
    narrow, wide = lax.axis_size("narrow"), lax.axis_size("wide")
    stride = wide // narrow
    wide_index, narrow_index = lax.axis_index("wide"), lax.axis_index("narrow")
    own = wide_index == narrow_index * stride
    later = narrow_index > owner
    which = jnp.where(later, 0, -1)
    mode = jnp.where(narrow_index == owner, 1, jnp.where(later, 2, 0))
    earlier = (wide_index % stride == 0) & (wide_index // stride < owner)
    kind = jnp.where(wide_index == owner * stride, 1, jnp.where(earlier, 2, 0))
    table = lame_table.astype(F32)
    column = broadcast(coarse_slab, "narrow", owner)
    first, last = halo_message(table, material_ids, table, coarse_basis, coarse_slab, ())
    halo = lax.ppermute(first, "narrow", [(i + 1, i) for i in range(narrow - 1)])
    edge = (narrow_index == 0).astype(jnp.int32).reshape(1)
    inner = interior(edge, table, material_ids, coarse_basis, first)
    partial = face(settings(1), table, material_ids, last, halo, first, inner)
    parts = [lax.psum(partial, "narrow")]
    message = assemble(settings(mode, own), first, coarse_ids, coarse_slab, column, parts)
    at_owner = (wide_index == owner * stride) & (narrow_index == owner)
    diagonal = lax.psum(jnp.where(at_owner, message, 0.0), ("wide", "narrow"))
    summary, _, galerkin = factorize(settings(1, 0), first, [diagonal], [parts])
    head = broadcast(message, "wide", narrow_index * stride)
    weights, rows, lower = prepare(settings(0, mode), settings(mode), head, [summary])
    added = added_of(settings(1), weights, coarse_ids, galerkin, head.shape[0])
    flags = settings(mode, kind, own, which)
    tile = coarse_slab.shape[0] // 12
    result, _ = panel(flags, flags, lower, weights, rows, added, coarse_slab, [[column]], None, 0, tile)
    return result, galerkin


def on_device(coarse_basis, material_ids, lame_table, coarse_ids, coarse_slab, panel_owner):
    narrow, wide = lax.axis_size("narrow"), lax.axis_size("wide")
    arrays = (coarse_basis, material_ids, lame_table, coarse_ids, coarse_slab)
    owner = panel_owner[0]
    if narrow - 1 > len(PLANS) or wide & (wide - 1):
        return any_owner(owner, *arrays)
    branches = [functools.partial(known_owner, place) for place in range(narrow - 1)]
    return lax.switch(owner, branches, *arrays)


def solution(mesh):
    return jax.shard_map(
        on_device,
        mesh=mesh,
        in_specs=(
            P("wide", None, None, "narrow", None, None),
            P("wide", "narrow", None, None),
            P(),
            P("wide", None),
            P("wide", "narrow"),
            P(),
        ),
        out_specs=(P("wide", "narrow"), P("wide", None, None)),
        check_vma=False,
    )
```
